32 devices in a mesh: tm: 16 (over z, y, x), head: 2 (over core).
Axes of the slice: x: 2, y: 2, z: 4, core: 2. Of those that a mesh axis runs over, the one named last changes fastest.
Arguments:
- frames: bfloat16 [4096, 1024], P('tm'), may hold values from -6 to 6
- x_weight: bfloat16 [1024, 2048], P('tm', 'head'), may hold values from -0.1875 to 0.1875
- z_weight: bfloat16 [1024, 2048], P('tm', 'head'), may hold values from -0.1875 to 0.1875
- bc_weight: bfloat16 [1024, 256], P('tm'), may hold values from -0.1875 to 0.1875
- log_decay: float32 [32, 4096], P('head', 'tm'), may hold values from -0.9 to 0
- norm_gain: float32 [2048], P('head'), may hold values from 0.1 to 1.9
- conv_weight: float32 [31, 2048], P(None, 'head'), may hold values from -1 to 1
- out_weight: bfloat16 [2048, 1024], P('head', 'tm'), may hold values from -0.125 to 0.125
- record_lengths: int32 [8], replicated, may hold values from 1 to 3072, 4096 in all
Outputs:
- mixed: bfloat16 [4096, 1024], P('tm', 'head')
The draws below stay inside these ranges and needn't reach their ends.
Inputs may be any that keep to these rules, and one draw needn't show every extreme that they name: `record_lengths`: 8 recording lengths that sum to 4096; the longest has exactly 3072 frames.
All inputs are finite; a program needn't handle non-finite values.
Results may differ from the reference program's by a relative error of at most 0.02.
Values may be sent and summed in bfloat16 or wider, within the bound.
No kernel may reach another device: no remote copies, remote signals or barrier semaphores. Data moves between devices by JAX's collectives and lax.ppermute only.
A program may use at most 64 MiB of HBM per device.

```python
import math
import jax
import jax.numpy as jnp
import numpy as np
from jax import lax

D = 1024
SCAN_GROUPS = 32
P_SIZE = 64
N = 128
KCONV = 31
SPAN = 128
NREC = 8
TOK_DEV = 256
PACKED_STEPS = 4096
LONGEST = 3072
HALF = 15
HP = 2048
HP_DEV = 1024
N_HEAD = 2


def draw_log_decay(key, part):
    sampler_seeds = [jax.random.fold_in(key, 11 + number) for number in range(8)]
    fast_share = 0.5
    fast = jax.random.bernoulli(sampler_seeds[0], fast_share, (SCAN_GROUPS,))
    fast_rate = jnp.exp(jax.random.uniform(sampler_seeds[1], (SCAN_GROUPS,), jnp.float32, math.log(1.0 / 50.0), math.log(1.0 / 30.0)))
    slow_rate = jnp.exp(jax.random.uniform(sampler_seeds[2], (SCAN_GROUPS,), jnp.float32, math.log(0.3), math.log(1.5))) / PACKED_STEPS
    fading_speed = jnp.where(fast, fast_rate, slow_rate)
    block_count = PACKED_STEPS // TOK_DEV
    tile_factor = jnp.exp(jax.random.uniform(sampler_seeds[3], (SCAN_GROUPS, block_count), jnp.float32, math.log(0.5), math.log(2.0)))
    tile_factor = jnp.repeat(tile_factor, TOK_DEV, axis=1)
    approximate_guess = jnp.exp(jax.random.uniform(sampler_seeds[4], (SCAN_GROUPS, PACKED_STEPS), jnp.float32, math.log(0.5), math.log(2.0)))
    spurt_span = jax.random.bernoulli(sampler_seeds[5], 4.0 / PACKED_STEPS, (SCAN_GROUPS, PACKED_STEPS))
    objective_scalar = jax.random.uniform(sampler_seeds[6], (SCAN_GROUPS, PACKED_STEPS), jnp.float32, 0.2, 0.5)
    return (-(fading_speed[:, None] * tile_factor * approximate_guess) + jnp.where(spurt_span, jnp.log1p(-objective_scalar), 0.0)).astype(jnp.float32)


def steps_of(own_key, extent, split, low, top_value):
    factor_of = 1.0
    for axis_at, parts in split:
        draws = jax.random.uniform(jax.random.fold_in(jax.random.fold_in(own_key, 6), axis_at), (parts,), jnp.float32, low / len(split), top_value / len(split))
        factor_of = factor_of * jnp.repeat(jnp.exp(draws), extent[axis_at] // parts).reshape((-1,) + (1,) * (len(extent) - 1 - axis_at))
    return factor_of


def length_profile(amount, total, most, skew):
    portions = [(1 << 20) // math.isqrt(rank ** skew) + 1 for rank in range(2, amount + 1)]
    surplus, holding = total - most - (amount - 1), [1] * (amount - 1)
    while surplus > 0:
        movable = [i for i in range(amount - 1) if holding[i] < most]
        whole, budget = sum([portions[i] for i in movable]), surplus
        for i in movable:
            addition = min(most - holding[i], max(1, budget * portions[i] // whole), surplus)
            holding[i] = holding[i] + addition
            surplus = surplus - addition
    return np.array([most] + holding)


def uneven(rng, number_of, total, reach, slope):
    if number_of == 2:
        one = jax.random.randint(rng, (), max(1, total - reach), min(reach, total - 1) + 1)
        return jnp.stack([one, total - one])
    tallies = jnp.asarray(length_profile(number_of, total, reach, slope), jnp.int32)
    twos = (number_of - 1) // 2
    source_of, receiver = tallies[1:1 + 2 * twos:2], tallies[2:2 + 2 * twos:2]
    room = jnp.minimum(source_of - 1, reach - receiver)
    shifted = jax.random.randint(jax.random.fold_in(rng, 1), (twos,), 0, 1 << 20) % (room + 1)
    tallies = tallies.at[1:1 + 2 * twos:2].set(source_of - shifted).at[2:2 + 2 * twos:2].set(receiver + shifted)
    return tallies[jax.random.permutation(jax.random.fold_in(rng, 2), number_of)]


def normal_values(rng, dims, scale, bound, split=(), kind=jnp.bfloat16):
    gain = steps_of(rng, dims, split, -0.22, 0.18) if split else 1.0
    drawn = jax.random.normal(rng, dims, jnp.float32) * scale * gain
    return jnp.minimum(jnp.maximum(drawn, -bound), bound).astype(kind)


def setup_inputs(seed: int = 0) -> dict:
    keys = jax.random.split(jax.random.key(seed), 10)
    frames = normal_values(keys[0], (PACKED_STEPS, D), 1.0, 6.0, ((0, 16),))
    x_weight = normal_values(keys[1], (D, HP), D ** -0.5, 0.1875, ((0, 16), (1, 2)))
    z_weight = normal_values(keys[2], (D, HP), D ** -0.5, 0.1875, ((0, 16), (1, 2)))
    bc_weight = normal_values(keys[3], (D, 2 * N), D ** -0.5, 0.1875, ((0, 16),))
    log_decay = draw_log_decay(jax.random.fold_in(keys[9], 71), 0)
    norm_gain = jnp.clip(1.0 + 0.18 * jax.random.normal(keys[5], (HP,), jnp.float32), 0.1, 1.9)
    conv_weight = normal_values(keys[6], (KCONV, HP), KCONV ** -0.5, 1.0, ((1, 2),), jnp.float32)
    out_weight = normal_values(keys[7], (HP, D), HP ** -0.5, 0.125, ((0, 2), (1, 16)))
    record_lengths = uneven(keys[8], NREC, PACKED_STEPS, LONGEST, 2).astype(jnp.int32)
    return dict(frames=frames, x_weight=x_weight, z_weight=z_weight, bc_weight=bc_weight, log_decay=log_decay, norm_gain=norm_gain, conv_weight=conv_weight, out_weight=out_weight, record_lengths=record_lengths)


highest = lax.Precision.HIGHEST

def segment_ids(record_lengths, positions):
    record_ends = jnp.cumsum(record_lengths).astype(jnp.int32)
    return lax.optimization_barrier(jnp.sum((record_ends[None, :] <= positions[:, None]).astype(jnp.int32), axis=1)).astype(jnp.int32)

def span_step(state, inputs):
    x_block, b_block, c_block, log_block, seg_block, seg_before = inputs
    length = seg_block.shape[0]
    cumul = jnp.cumsum(log_block, axis=1)
    lower = jnp.arange(length)[:, None] >= jnp.arange(length)[None, :]
    joined = (seg_block[:, None] == seg_block[None, :]) & lower
    spread = cumul[:, :, None] - cumul[:, None, :]
    mixing = jnp.exp(jnp.where(joined[None], spread, -jnp.inf))
    scores = jnp.dot(c_block, b_block.T, preferred_element_type=jnp.float32)
    x_float = x_block.astype(jnp.float32)
    inner = jnp.einsum('hts,shp->thp', mixing * scores[None], x_float, precision=highest)
    carried = jnp.exp(cumul) * (seg_block == seg_before).astype(jnp.float32)[None, :]
    c_float = c_block.astype(jnp.float32)
    outer = jnp.einsum('tn,hnp->thp', c_float, state, precision=highest) * carried.T[:, :, None]
    tail = jnp.exp(cumul[:, -1:] - cumul) * (seg_block == seg_block[-1]).astype(jnp.float32)[None, :]
    weighted = tail[:, :, None] * b_block.astype(jnp.float32)[None, :, :]
    state_next = carried[:, -1][:, None, None] * state + jnp.einsum('hsn,shp->hnp', weighted, x_float, precision=highest)
    return (state_next, inner + outer)

def run_spans(x_rows, b_rows, c_rows, log_rows, seg_rows, seg_first, state):
    count = x_rows.shape[0] // SPAN
    heads_here = log_rows.shape[0]
    x_blocks = x_rows.reshape(count, SPAN, heads_here, -1)
    b_blocks = b_rows.reshape(count, SPAN, -1)
    c_blocks = c_rows.reshape(count, SPAN, -1)
    log_blocks = log_rows.reshape(heads_here, count, SPAN).transpose(1, 0, 2)
    seg_blocks = seg_rows.reshape(count, SPAN)
    seg_befores = jnp.concatenate([jnp.reshape(seg_first, (1,)).astype(jnp.int32), seg_blocks[:-1, -1].astype(jnp.int32)])
    state, outputs = lax.scan(span_step, state, (x_blocks, b_blocks, c_blocks, log_blocks, seg_blocks, seg_befores))
    return (state, outputs.reshape(count * SPAN, heads_here, -1))

def gate_rows(ssd_out, z_rows, norm_gain):
    square_mean = lax.optimization_barrier(jnp.mean(ssd_out * ssd_out, axis=-1, keepdims=True))
    normed = (ssd_out * lax.rsqrt(square_mean + 1e-05)).reshape(ssd_out.shape[0], -1)
    z_float = z_rows.astype(jnp.float32)
    return (normed * norm_gain[None, :] * z_float * jax.nn.sigmoid(z_float)).astype(jnp.bfloat16)

def conv_rows(extended, seg_extended, seg_rows, conv_weight):
    frame_count = seg_rows.shape[0]
    summed = jnp.zeros((frame_count, extended.shape[1]), jnp.float32)
    for offset in range(conv_weight.shape[0]):
        same = (seg_extended[offset:offset + frame_count] == seg_rows).astype(jnp.float32)
        summed = summed + conv_weight[offset][None, :] * extended[offset:offset + frame_count].astype(jnp.float32) * same[:, None]
    return (summed * jax.nn.sigmoid(summed)).astype(jnp.bfloat16)

def reference(frames, x_weight, z_weight, bc_weight, log_decay, norm_gain, conv_weight, out_weight, record_lengths):
    x_rows = jnp.dot(frames, x_weight, preferred_element_type=jnp.float32).astype(jnp.bfloat16)
    z_rows = jnp.dot(frames, z_weight, preferred_element_type=jnp.float32).astype(jnp.bfloat16)
    bc_rows = jnp.dot(frames, bc_weight, preferred_element_type=jnp.float32).astype(jnp.bfloat16)
    positions = jnp.arange(PACKED_STEPS, dtype=jnp.int32)
    seg_rows = segment_ids(record_lengths, positions)
    start_state = jnp.zeros((SCAN_GROUPS, N, P_SIZE), jnp.float32)
    final_state, ssd_out = run_spans(x_rows, bc_rows[:, :N], bc_rows[:, N:], log_decay, seg_rows, jnp.int32(-1), start_state)
    gated = gate_rows(ssd_out, z_rows, norm_gain)
    extended = jnp.pad(gated, ((HALF, HALF), (0, 0)))
    seg_extended = segment_ids(record_lengths, jnp.arange(PACKED_STEPS + 2 * HALF, dtype=jnp.int32) - HALF)
    act_rows = conv_rows(extended, seg_extended, seg_rows, conv_weight)
    mixed = jnp.zeros((PACKED_STEPS, D), jnp.float32)
    for group in range(N_HEAD):
        lo_row = group * HP_DEV
        partial_sum = jnp.dot(act_rows[:, lo_row:lo_row + HP_DEV], out_weight[lo_row:lo_row + HP_DEV], preferred_element_type=jnp.float32)
        rounded = lax.optimization_barrier(partial_sum.astype(jnp.bfloat16))
        mixed = mixed + rounded.astype(jnp.float32)
    return mixed.astype(jnp.bfloat16)
```

```python
import functools

import jax
import jax.numpy as jnp
from jax import lax
from jax.experimental import pallas as pl
from jax.experimental.pallas import tpu as pltpu
from jax.sharding import PartitionSpec as P

SPAN = 128
LANES = 128
EDGE = 16
BF16 = jnp.bfloat16
F32 = jnp.float32
VMEM_BYTES = 48 * 1024 * 1024


def dot(a, b, dims=((1,), (0,)), precision=None):
    return lax.dot_general(a, b, (dims, ((), ())), precision=precision, preferred_element_type=F32)


def call(kernel, out_shape, operands, scratch=(), flops=0, smem=1):
    in_specs = [pl.BlockSpec(memory_space=pltpu.SMEM)] * smem
    in_specs += [pl.BlockSpec(memory_space=pltpu.VMEM)] * (len(operands) - smem)
    moved = sum(a.size * a.dtype.itemsize for a in operands)
    moved += sum(a.size * a.dtype.itemsize for a in jax.tree.leaves(out_shape))
    return pl.pallas_call(
        kernel,
        out_shape=out_shape,
        in_specs=in_specs,
        out_specs=jax.tree.map(lambda _: pl.BlockSpec(memory_space=pltpu.VMEM), out_shape),
        scratch_shapes=list(scratch),
        compiler_params=pltpu.CompilerParams(vmem_limit_bytes=VMEM_BYTES),
        cost_estimate=pl.CostEstimate(flops=flops, bytes_accessed=moved, transcendentals=0),
    )(*operands)


def plane_place(group):
    index = lax.axis_index("tm")
    return lax.rem(index, group), lax.div(index, group)


def record_starts(len_ref, position):
    start = jnp.zeros_like(position)
    end = jnp.int32(0)
    for record in range(len_ref.shape[0] - 1):
        end = end + len_ref[record]
        start = jnp.where(position >= end, end, start)
    return start


def spread(columns, first, heads, head_of_lane, shape):
    out = jnp.broadcast_to(columns[:, first : first + 1], shape)
    for head in range(1, heads):
        column = jnp.broadcast_to(columns[:, first + head : first + head + 1], shape)
        out = jnp.where(head_of_lane == head, column, out)
    return out


def ssd_kernel(group, heads, state, len_ref, decay_ref, weight_ref, *refs):
    frame_refs = refs[:group]
    c_ref, y_ref, step_ref, carry_ref, keep_ref, send_ref, x_ref, b_ref = refs[group:]
    place, plane = plane_place(group)
    frames = frame_refs[0].shape[0]
    total, width = x_ref.shape
    head_size = width // heads
    count = total // SPAN
    base = plane * total
    for step in range(group):
        rows = pl.ds(pl.multiple_of((place ^ step) * frames, frames), frames)
        product = dot(frame_refs[step][...], weight_ref[...])
        x_ref[rows, :] = product[:, :width].astype(BF16)
        b_ref[rows, :] = product[:, width : width + state].astype(BF16)
        c_ref[rows, :] = product[:, width + state :].astype(BF16)

    decay = decay_ref[...]
    used = decay.shape[0]
    square = (SPAN, SPAN)
    row, lane = (lax.broadcasted_iota(jnp.int32, square, dim) for dim in (0, 1))
    upper = jnp.where(row <= lane, 1.0, 0.0).astype(F32)
    cumul = dot(decay, upper, precision=lax.Precision.HIGHEST)
    whole = dot(decay, jnp.ones(square, F32), precision=lax.Precision.HIGHEST)
    first = base + lax.div(row[:used], heads) * SPAN
    position = first + lane[:used]
    start = record_starts(len_ref, position)
    start_last = record_starts(len_ref, first + (SPAN - 1))
    carried = jnp.where(start < first, jnp.exp(cumul), 0.0)
    tail = jnp.where(position >= start_last, jnp.exp(whole - cumul), 0.0)
    keep = jnp.where(start_last < first, jnp.exp(whole), 0.0)
    parts = [cumul, carried, tail, start.astype(F32)]
    if 4 * used < SPAN:
        parts.append(jnp.zeros((SPAN - 4 * used, SPAN), F32))
    columns = jnp.concatenate(parts, axis=0).T

    head_of_lane = lax.broadcasted_iota(jnp.int32, (SPAN, width), 1) // head_size
    tile_heads = LANES // head_size
    tile_lane = lax.broadcasted_iota(jnp.int32, (1, LANES), 1) // head_size
    lower = row >= lane
    entry = jnp.zeros((state, width), F32)
    through = jnp.ones((1, width), F32)
    for block in range(count):
        rows = slice(block * SPAN, (block + 1) * SPAN)
        at = block * heads
        x, b, c = x_ref[rows, :], b_ref[rows, :], c_ref[rows, :]
        scores = dot(c, b, ((1,), (1,)))
        here = (base + block * SPAN + lane).astype(F32)
        start_here = jnp.broadcast_to(columns[:, 3 * used + at : 3 * used + at + 1], square)
        joined = lower & (here >= start_here)
        keep_lanes = []
        for tile in range(width // LANES):
            mixes, values = [], []
            kept = jnp.zeros((1, LANES), F32)
            for inner in range(tile_heads):
                which = at + tile * tile_heads + inner
                gap = jnp.broadcast_to(columns[:, which : which + 1], square) - cumul[which : which + 1, :]
                mixes.append((jnp.exp(jnp.where(joined, gap, -1e30)) * scores).astype(BF16))
                mask = jnp.where(tile_lane == inner, 1.0, 0.0)
                values.append(x[:, tile * LANES : (tile + 1) * LANES] * mask.astype(BF16))
                kept = kept + mask * keep[which : which + 1, :]
            keep_lanes.append(kept)
            y_ref[rows, tile * LANES : (tile + 1) * LANES] = dot(
                jnp.concatenate(mixes, axis=1), jnp.concatenate(values, axis=0)
            )
        kept = jnp.concatenate(keep_lanes, axis=1)
        carry_ref[rows, :] = spread(columns, used + at, heads, head_of_lane, (SPAN, width))
        weighed = x.astype(F32) * spread(columns, 2 * used + at, heads, head_of_lane, (SPAN, width))
        step = dot(b, weighed.astype(BF16), ((0,), (0,)))
        step_ref[block * state : (block + 1) * state, :] = step
        keep_ref[block * 8 : (block + 1) * 8, :] = jnp.broadcast_to(kept, (8, width))
        entry = kept * entry + step
        through = through * kept
    send_ref[:state, :] = entry.astype(BF16)
    send_ref[state:, :] = jnp.broadcast_to(through, (EDGE, width)).astype(BF16)


def silu_kernel(group, gain_ref, weight_ref, *refs):
    frame_refs, out_ref = refs[:group], refs[group]
    place, _ = plane_place(group)
    frames = frame_refs[0].shape[0]
    width = weight_ref.shape[1]
    gain = gain_ref[:, pl.ds(pl.multiple_of(place * width, LANES), width)]
    for step in range(group):
        rows = pl.ds(pl.multiple_of((place ^ step) * frames, frames), frames)
        z = dot(frame_refs[step][...], weight_ref[...]).astype(BF16).astype(F32)
        out_ref[rows, :] = z / (1.0 + jnp.exp(-z)) * gain


def gate_kernel(heads, state, c_ref, y_ref, step_ref, carry_ref, keep_ref, silu_ref, *refs):
    earlier, (gated_ref, top_ref, bottom_ref) = refs[:-3], refs[-3:]
    total, width = y_ref.shape
    head_size = width // heads
    entry = jnp.zeros((state, width), F32)
    for summary in reversed(earlier):
        through = summary[state : state + EDGE, :].astype(F32)[:1]
        entry = through * entry + summary[:state, :].astype(F32)
    owner = [lax.broadcasted_iota(jnp.int32, (width, width), dim) // head_size for dim in (0, 1)]
    average = jnp.where(owner[0] == owner[1], 1.0 / head_size, 0.0).astype(BF16)
    for block in range(total // SPAN):
        rows = slice(block * SPAN, (block + 1) * SPAN)
        y = y_ref[rows, :] + carry_ref[rows, :] * dot(c_ref[rows, :], entry.astype(BF16))
        square_mean = dot((y * y).astype(BF16), average)
        gated_ref[rows, :] = (y * lax.rsqrt(square_mean + 1e-05) * silu_ref[rows, :]).astype(BF16)
        entry = keep_ref[block * 8 : block * 8 + 1, :] * entry + step_ref[block * state : (block + 1) * state, :]
    top_ref[...] = gated_ref[:EDGE, :]
    bottom_ref[...] = gated_ref[total - EDGE :, :]


def conv_kernel(group, len_ref, taps_ref, before_ref, gated_ref, after_ref, act_ref, ext_ref, ends_ref):
    place, plane = plane_place(group)
    total, width = gated_ref.shape
    taps = taps_ref.shape[0]
    half = (taps - 1) // 2
    base = plane * total
    stream = lax.axis_size("tm") // group * total
    records = len_ref.shape[0]
    ext_ref[:EDGE, :] = before_ref[...].astype(F32)
    ext_ref[EDGE : EDGE + total, :] = gated_ref[...].astype(F32)
    ext_ref[EDGE + total :, :] = after_ref[...].astype(F32)
    ends_ref[0] = 0
    for record in range(records):
        ends_ref[record + 1] = ends_ref[record] + len_ref[record]

    def record_at(position):
        found = jnp.int32(0)
        for record in range(records - 1):
            found = found + (ends_ref[record + 1] <= position).astype(jnp.int32)
        return found

    reach = SPAN + 2 * EDGE
    first_tap = EDGE - half

    def one_block(block, _):
        offset = pl.multiple_of(block * SPAN, SPAN)
        low = record_at(jnp.maximum(base + offset - half, 0))
        high = record_at(jnp.minimum(base + offset + SPAN - 1 + half, stream - 1))
        near = lax.broadcasted_iota(jnp.int32, (reach, LANES), 0) + (base + offset - EDGE)
        for tile in range(width // LANES):
            lanes = slice(tile * LANES, (tile + 1) * LANES)
            weights = taps_ref[:, pl.ds(pl.multiple_of(place * width + tile * LANES, LANES), LANES)]

            def one_record(record, done):
                inside = (near >= ends_ref[record]) & (near < ends_ref[record + 1])
                g = jnp.where(inside, ext_ref[pl.ds(offset, reach), lanes], 0.0)
                out = None
                for phase in range(8):
                    part = None
                    for at in range(phase, reach - SPAN, 8):
                        tap = at - first_tap
                        if 0 <= tap < taps:
                            aligned = at - phase
                            term = weights[tap : tap + 1, :] * g[aligned : aligned + SPAN + 8, :]
                            part = term if part is None else part + term
                    if part is not None:
                        moved = part[phase : phase + SPAN, :]
                        out = moved if out is None else out + moved
                return jnp.where(inside[EDGE : EDGE + SPAN], out, done)

            conv = lax.fori_loop(low, high + 1, one_record, jnp.zeros((SPAN, LANES), F32))
            act_ref[pl.ds(offset, SPAN), lanes] = (conv / (1.0 + jnp.exp(-conv))).astype(BF16)
        return 0

    lax.fori_loop(0, total // SPAN, one_block, 0)


def out_kernel(group, cores, *refs):
    acts, weights, outs = refs[:cores], refs[cores : 2 * cores], refs[2 * cores :]
    place, _ = plane_place(group)
    frames = outs[0].shape[0]
    for step in reversed(range(group)):
        rows = pl.ds(pl.multiple_of((place ^ step) * frames, frames), frames)
        total = None
        for act, weight in zip(acts, weights):
            product = dot(act[rows, :], weight[...], ((1,), (1,)))
            total = product if total is None else total + product
        outs[step][...] = total.astype(outs[step].dtype)


def local(
    frames,
    x_weight,
    z_weight,
    bc_weight,
    log_decay,
    norm_gain,
    conv_weight,
    out_weight,
    record_lengths,
):
    times, cores = lax.axis_size("tm"), lax.axis_size("head")
    frame_count, depth = frames.shape
    heads_here, channels = log_decay.shape[0], x_weight.shape[1]
    state = bc_weight.shape[1] // 2
    group = 4
    while group > 1 and (channels // group % LANES or times % group or heads_here % group):
        group //= 2
    planes = times // group
    width, heads = channels // group, heads_here // group
    total = frame_count * group
    count = total // SPAN
    index, core = lax.axis_index("tm"), lax.axis_index("head")
    place = lax.rem(index, group)

    def in_plane(array, step):
        return lax.ppermute(array, "tm", [(i, i ^ step) for i in range(times)])

    def later(array, step):
        return lax.ppermute(array, "tm", [(i, i + step * group) for i in range(times - step * group)])

    def earlier(array, step):
        return lax.ppermute(array, "tm", [(i + step * group, i) for i in range(times - step * group)])

    def across(array, step):
        return lax.ppermute(array, "head", [(i, i ^ step) for i in range(cores)])

    def to_owners(blocks):
        whole = jnp.broadcast_to(blocks[None], (planes,) + blocks.shape)
        whole = whole.reshape((times,) + blocks.shape[1:])
        moved = lax.all_to_all(whole, "tm", split_axis=0, concat_axis=0, tiled=True)
        return moved.reshape(-1, moved.shape[-1])

    def columns(weight):
        return weight.reshape(weight.shape[0], group, width).transpose(1, 0, 2)

    shared = jnp.broadcast_to(bc_weight[None], (group,) + bc_weight.shape)
    xbc = to_owners(jnp.concatenate([columns(x_weight), shared], axis=2))
    frame_parts = [frames] + [in_plane(frames, step) for step in range(1, group)]
    decay_groups = [[plane * group + q for q in range(group)] for plane in range(planes)]
    decay = lax.all_to_all(
        log_decay.reshape(group, heads, frame_count),
        "tm",
        split_axis=0,
        concat_axis=0,
        axis_index_groups=decay_groups,
        tiled=True,
    )
    decay = decay.reshape(group, heads, -1, SPAN).transpose(0, 2, 1, 3).reshape(-1, SPAN)
    z_columns = to_owners(columns(z_weight))
    out_rows = to_owners(columns(out_weight.T))
    share = depth // cores
    out_parts = [lax.dynamic_slice_in_dim(out_rows, core * share, share, 0)]
    for step in range(1, cores):
        sent = lax.dynamic_slice_in_dim(out_rows, (core ^ step) * share, share, 0)
        out_parts.append(across(sent, step))

    shape = jax.ShapeDtypeStruct
    c_rows, y, steps, carry, keep, summary = call(
        functools.partial(ssd_kernel, group, heads, state),
        (
            shape((total, state), BF16),
            shape((total, width), F32),
            shape((count * state, width), F32),
            shape((total, width), F32),
            shape((count * 8, width), F32),
            shape((state + EDGE, width), BF16),
        ),
        [record_lengths, decay, xbc, *frame_parts],
        [pltpu.VMEM((total, width), BF16), pltpu.VMEM((total, state), BF16)],
        flops=2 * total * depth * (width + 2 * state),
    )
    summaries = [later(summary, step) for step in range(1, planes)]
    silu = call(
        functools.partial(silu_kernel, group),
        shape((total, width), F32),
        [norm_gain[None], z_columns, *frame_parts],
        flops=2 * total * depth * width,
        smem=0,
    )
    gated, top, bottom = call(
        functools.partial(gate_kernel, heads, state),
        (shape((total, width), BF16), shape((EDGE, width), BF16), shape((EDGE, width), BF16)),
        [c_rows, y, steps, carry, keep, silu, *summaries],
        flops=2 * total * state * width,
        smem=0,
    )
    before, after = later(bottom, 1), earlier(top, 1)
    act = call(
        functools.partial(conv_kernel, group),
        shape((total, width), BF16),
        [record_lengths, conv_weight, before, gated, after],
        [pltpu.VMEM((total + 2 * EDGE, width), F32), pltpu.SMEM((record_lengths.shape[0] + 1,), jnp.int32)],
        flops=2 * total * width * conv_weight.shape[0],
    )
    acts = [act] + [across(act, step) for step in range(1, cores)]
    outs = call(
        functools.partial(out_kernel, group, cores),
        tuple(shape((frame_count, share), BF16 if step else F32) for step in range(group)),
        [*acts, *out_parts],
        flops=2 * total * width * cores * share,
        smem=0,
    )
    mixed = outs[0]
    for step in range(1, group):
        mixed = mixed + in_plane(outs[step], step).astype(F32)
    return mixed.astype(BF16)


def solution(mesh):
    in_specs = (
        P("tm", None),
        P("tm", "head"),
        P("tm", "head"),
        P("tm", None),
        P("head", "tm"),
        P("head"),
        P(None, "head"),
        P("head", "tm"),
        P(),
    )
    out_specs = P("tm", "head")
    return jax.shard_map(local, mesh=mesh, in_specs=in_specs, out_specs=out_specs, check_vma=False)
```

```python
import functools

import jax
import jax.numpy as jnp
from jax import lax
from jax.experimental import pallas as pl
from jax.experimental.pallas import tpu as pltpu
from jax.sharding import PartitionSpec as P

SPAN = 128
LANES = 128
EDGE = 16
BF16 = jnp.bfloat16
F32 = jnp.float32
VMEM_BYTES = 48 * 1024 * 1024


def dot(a, b, dims=((1,), (0,)), precision=None):
    return lax.dot_general(a, b, (dims, ((), ())), precision=precision, preferred_element_type=F32)


def call(kernel, out_shape, operands, scratch=(), flops=0, smem=1):
    in_specs = [pl.BlockSpec(memory_space=pltpu.SMEM)] * smem
    in_specs += [pl.BlockSpec(memory_space=pltpu.VMEM)] * (len(operands) - smem)
    moved = sum(a.size * a.dtype.itemsize for a in operands)
    moved += sum(a.size * a.dtype.itemsize for a in jax.tree.leaves(out_shape))
    return pl.pallas_call(
        kernel,
        out_shape=out_shape,
        in_specs=in_specs,
        out_specs=jax.tree.map(lambda _: pl.BlockSpec(memory_space=pltpu.VMEM), out_shape),
        scratch_shapes=list(scratch),
        compiler_params=pltpu.CompilerParams(vmem_limit_bytes=VMEM_BYTES),
        cost_estimate=pl.CostEstimate(flops=flops, bytes_accessed=moved, transcendentals=0),
    )(*operands)


def plane_place(group):
    index = lax.axis_index("tm")
    return lax.rem(index, group), lax.div(index, group)


def record_starts(len_ref, position):
    start = jnp.zeros_like(position)
    end = jnp.int32(0)
    for record in range(len_ref.shape[0] - 1):
        end = end + len_ref[record]
        start = jnp.where(position >= end, end, start)
    return start


def spread(columns, first, heads, head_of_lane, shape):
    out = jnp.broadcast_to(columns[:, first : first + 1], shape)
    for head in range(1, heads):
        column = jnp.broadcast_to(columns[:, first + head : first + head + 1], shape)
        out = jnp.where(head_of_lane == head, column, out)
    return out


def fill_planes(plane, dest_ref, pieces, offsets, lanes=slice(None)):
    rows = pieces[0].shape[0]
    for offset in sorted(set(offsets)):
        same = [piece[:, lanes] for piece, at in zip(pieces, offsets) if at == offset]
        value = same[0] if len(same) == 1 else same[0] + same[1]
        dest_ref[pl.ds(pl.multiple_of((plane ^ offset) * rows, rows), rows), :] = value


def pack_x_kernel(group, decay_ref, x_ref, bc_ref, *out_refs):
    place, _ = plane_place(group)
    rows = x_ref.shape[0]
    width = x_ref.shape[1] // group
    frames = decay_ref.shape[2]
    for step, out_ref in enumerate(out_refs):
        block = place ^ step
        out_ref[:rows, :width] = x_ref[:, pl.ds(pl.multiple_of(block * width, LANES), width)]
        out_ref[:rows, width:] = bc_ref[...]
        left = decay_ref[block]
        terms = []
        for _ in range(3):
            term = left.astype(BF16).astype(F32)
            terms.append(term)
            left = left - term
        terms.append(jnp.zeros_like(left))
        out_ref[rows:, :frames] = jnp.concatenate(terms, axis=0).astype(BF16)
        out_ref[rows:, frames:] = jnp.zeros((4 * 8, out_ref.shape[1] - frames), BF16)


def stack_x_kernel(group, *refs):
    parts, (stack_ref, decay_ref) = refs[:group], refs[group:]
    place, _ = plane_place(group)
    rows = stack_ref.shape[0] // group
    frames = decay_ref.shape[2]
    for step, part in enumerate(parts):
        block = place ^ step
        stack_ref[pl.ds(pl.multiple_of(block * rows, rows), rows), :] = part[:rows, :]
        terms = part[rows:, :frames].astype(F32)
        decay_ref[block] = terms[:8] + terms[8:16] + terms[16:24]


def pack_zo_kernel(group, z_ref, out_w_ref, *out_refs):
    place, _ = plane_place(group)
    width = z_ref.shape[1] // group
    for step, out_ref in enumerate(out_refs):
        lanes = pl.ds(pl.multiple_of((place ^ step) * width, LANES), width)
        out_ref[:, :width] = z_ref[:, lanes]
        out_ref[:, width:] = out_w_ref[:, lanes]


def stack_zo_kernel(group, *refs):
    parts, (z_ref, o_ref) = refs[:group], refs[group:]
    place, _ = plane_place(group)
    rows, width = z_ref.shape[0] // group, z_ref.shape[1]
    for step, part in enumerate(parts):
        at = pl.ds(pl.multiple_of((place ^ step) * rows, rows), rows)
        z_ref[at, :] = part[:, :width]
        o_ref[at, :] = part[:, width:]


def state_kernel(group, heads, state, offsets, len_ref, decay_ref, *refs):
    frame_refs, refs = refs[:group], refs[group:]
    pieces, refs = refs[: len(offsets)], refs[len(offsets) :]
    x_ref, b_ref, c_ref, columns_ref, cumul_ref, step_ref, carry_ref, keep_ref, send_ref, weight_ref = refs
    place, plane = plane_place(group)
    frames = frame_refs[0].shape[0]
    total, width = x_ref.shape
    head_size = width // heads
    count = total // SPAN
    base = plane * total
    fill_planes(plane, weight_ref, pieces, offsets)
    for step in range(group):
        rows = pl.ds(pl.multiple_of((place ^ step) * frames, frames), frames)
        product = dot(frame_refs[step][...], weight_ref[...])
        x_ref[rows, :] = product[:, :width].astype(BF16)
        b_ref[rows, :] = product[:, width : width + state].astype(BF16)
        c_ref[rows, :] = product[:, width + state :].astype(BF16)

    spans = frames // SPAN
    decay = jnp.concatenate(
        [decay_ref[block // spans][:, block % spans * SPAN : (block % spans + 1) * SPAN] for block in range(count)],
        axis=0,
    )
    used = decay.shape[0]
    square = (SPAN, SPAN)
    row, lane = (lax.broadcasted_iota(jnp.int32, square, dim) for dim in (0, 1))
    upper = jnp.where(row <= lane, 1.0, 0.0).astype(F32)
    cumul = dot(decay, upper, precision=lax.Precision.HIGHEST)
    whole = dot(decay, jnp.ones(square, F32), precision=lax.Precision.HIGHEST)
    first = base + lax.broadcasted_iota(jnp.int32, (used, SPAN), 0) // 8 * SPAN
    position = first + lane[:1]
    start = record_starts(len_ref, position)
    start_last = record_starts(len_ref, first + (SPAN - 1))
    carried = jnp.where(start < first, jnp.exp(cumul), 0.0)
    tail = jnp.where(position >= start_last, jnp.exp(whole - cumul), 0.0)
    keep = jnp.where(start_last < first, jnp.exp(whole), 0.0)
    parts = [cumul, carried, tail, start.astype(F32)]
    if 4 * used % SPAN:
        parts.append(jnp.zeros((SPAN - 4 * used % SPAN, SPAN), F32))
    columns = jnp.concatenate(parts, axis=0).T
    columns_ref[...] = columns
    cumul_ref[...] = cumul

    head_of_lane = lax.broadcasted_iota(jnp.int32, (SPAN, width), 1) // head_size
    entry = jnp.zeros((state, width), F32)
    through = jnp.ones((1, width), F32)
    for block in range(count):
        rows = slice(block * SPAN, (block + 1) * SPAN)
        at = block * 8
        kept = jnp.broadcast_to(keep[at : at + 1, :1], (1, width))
        for head in range(1, heads):
            other = jnp.broadcast_to(keep[at + head : at + head + 1, :1], (1, width))
            kept = jnp.where(head_of_lane[:1] == head, other, kept)
        carry_ref[rows, :] = spread(columns, used + at, heads, head_of_lane, (SPAN, width))
        weighed = x_ref[rows, :].astype(F32) * spread(columns, 2 * used + at, heads, head_of_lane, (SPAN, width))
        step = dot(b_ref[rows, :], weighed.astype(BF16), ((0,), (0,)))
        step_ref[block * state : (block + 1) * state, :] = step
        keep_ref[block * 8 : (block + 1) * 8, :] = jnp.broadcast_to(kept, (8, width))
        entry = kept * entry + step
        through = through * kept
    send_ref[:state, :] = entry.astype(BF16)
    send_ref[state:, :] = jnp.broadcast_to(through, (EDGE, width)).astype(BF16)


def inner_kernel(group, heads, x_ref, b_ref, c_ref, columns_ref, cumul_ref, y_ref):
    _, plane = plane_place(group)
    total, width = x_ref.shape
    head_size = width // heads
    count = total // SPAN
    base = plane * total
    used = cumul_ref.shape[0]
    square = (SPAN, SPAN)
    row, lane = (lax.broadcasted_iota(jnp.int32, square, dim) for dim in (0, 1))
    lower = row >= lane
    tile_heads = LANES // head_size
    tile_lane = lax.broadcasted_iota(jnp.int32, (1, LANES), 1) // head_size
    masks = [jnp.where(tile_lane == inner, 1.0, 0.0).astype(BF16) for inner in range(tile_heads)]
    for block in range(count):
        rows = slice(block * SPAN, (block + 1) * SPAN)
        at = block * 8
        x = x_ref[rows, :]
        scores = dot(c_ref[rows, :], b_ref[rows, :], ((1,), (1,)))
        here = (base + block * SPAN + lane).astype(F32)
        start_here = jnp.broadcast_to(columns_ref[:, 3 * used + at : 3 * used + at + 1], square)
        joined = lower & (here >= start_here)
        for tile in range(width // LANES):
            mixes, values = [], []
            for inner in range(tile_heads):
                which = at + tile * tile_heads + inner
                column = jnp.broadcast_to(columns_ref[:, which : which + 1], square)
                gap = jnp.where(joined, column - cumul_ref[which : which + 1, :], -1e30)
                mixes.append((jnp.exp(gap) * scores).astype(BF16))
                values.append(x[:, tile * LANES : (tile + 1) * LANES] * masks[inner])
            y_ref[rows, tile * LANES : (tile + 1) * LANES] = dot(
                jnp.concatenate(mixes, axis=1), jnp.concatenate(values, axis=0)
            )


def silu_kernel(group, offsets, gain_ref, *refs):
    frame_refs, refs = refs[:group], refs[group:]
    pieces, (out_ref, weight_ref) = refs[: len(offsets)], refs[len(offsets) :]
    place, plane = plane_place(group)
    frames = frame_refs[0].shape[0]
    width = weight_ref.shape[1]
    gain = gain_ref[:, pl.ds(pl.multiple_of(place * width, LANES), width)]
    fill_planes(plane, weight_ref, pieces, offsets)
    for step in range(group):
        rows = pl.ds(pl.multiple_of((place ^ step) * frames, frames), frames)
        z = dot(frame_refs[step][...], weight_ref[...]).astype(BF16).astype(F32)
        out_ref[rows, :] = z / (1.0 + jnp.exp(-z)) * gain


def share_kernel(group, cores, offsets, *refs):
    pieces, refs = refs[: len(offsets)], refs[len(offsets) :]
    outs, weight_ref = refs[:cores], refs[cores]
    _, plane = plane_place(group)
    core = lax.axis_index("head")
    fill_planes(plane, weight_ref, pieces, offsets)
    for step, out_ref in enumerate(outs):
        rows = out_ref.shape[0]
        out_ref[...] = weight_ref[pl.ds(pl.multiple_of((core ^ step) * rows, rows), rows), :]


def gate_kernel(heads, state, c_ref, y_ref, step_ref, carry_ref, keep_ref, silu_ref, *refs):
    earlier, (gated_ref, top_ref, bottom_ref) = refs[:-3], refs[-3:]
    total, width = y_ref.shape
    head_size = width // heads
    entry = jnp.zeros((state, width), F32)
    for summary in reversed(earlier):
        through = summary[state : state + EDGE, :].astype(F32)[:1]
        entry = through * entry + summary[:state, :].astype(F32)
    owner = [lax.broadcasted_iota(jnp.int32, (width, width), dim) // head_size for dim in (0, 1)]
    average = jnp.where(owner[0] == owner[1], 1.0 / head_size, 0.0).astype(BF16)
    for block in range(total // SPAN):
        rows = slice(block * SPAN, (block + 1) * SPAN)
        y = y_ref[rows, :] + carry_ref[rows, :] * dot(c_ref[rows, :], entry.astype(BF16))
        square_mean = dot((y * y).astype(BF16), average)
        gated_ref[rows, :] = (y * lax.rsqrt(square_mean + 1e-05) * silu_ref[rows, :]).astype(BF16)
        entry = keep_ref[block * 8 : block * 8 + 1, :] * entry + step_ref[block * state : (block + 1) * state, :]
    top_ref[...] = gated_ref[:EDGE, :]
    bottom_ref[...] = gated_ref[total - EDGE :, :]


def conv_kernel(group, edges, len_ref, taps_ref, gated_ref, *refs):
    if edges:
        before_ref, after_ref, inner_ref, act_ref, ext_ref, ends_ref = refs
    else:
        act_ref, ext_ref, ends_ref = refs
    place, plane = plane_place(group)
    total, width = gated_ref.shape
    count = total // SPAN
    taps = taps_ref.shape[0]
    half = (taps - 1) // 2
    base = plane * total
    stream = lax.axis_size("tm") // group * total
    records = len_ref.shape[0]
    reach = SPAN + 2 * EDGE
    first_tap = EDGE - half
    if edges:
        act_ref[SPAN : total - SPAN, :] = inner_ref[...]
        ext_ref[:EDGE, :] = before_ref[...].astype(F32)
        ext_ref[EDGE:reach, :] = gated_ref[: SPAN + EDGE, :].astype(F32)
        ext_ref[reach : 2 * reach - EDGE, :] = gated_ref[total - SPAN - EDGE :, :].astype(F32)
        ext_ref[2 * reach - EDGE :, :] = after_ref[...].astype(F32)
    else:
        ext_ref[...] = gated_ref[SPAN - EDGE : total - SPAN + EDGE, :].astype(F32)
    ends_ref[0] = 0
    for record in range(records):
        ends_ref[record + 1] = ends_ref[record] + len_ref[record]

    def record_at(position):
        found = jnp.int32(0)
        for record in range(records - 1):
            found = found + (ends_ref[record + 1] <= position).astype(jnp.int32)
        return found

    def one_block(at, source, target):
        low = record_at(jnp.maximum(base + at - half, 0))
        high = record_at(jnp.minimum(base + at + SPAN - 1 + half, stream - 1))
        near = lax.broadcasted_iota(jnp.int32, (reach, LANES), 0) + (base + at - EDGE)
        for tile in range(width // LANES):
            lanes = slice(tile * LANES, (tile + 1) * LANES)
            weights = taps_ref[:, pl.ds(pl.multiple_of(place * width + tile * LANES, LANES), LANES)]

            def one_record(record, done):
                inside = (near >= ends_ref[record]) & (near < ends_ref[record + 1])
                g = jnp.where(inside, ext_ref[pl.ds(source, reach), lanes], 0.0)
                out = None
                for phase in range(8):
                    part = None
                    for offset in range(phase, reach - SPAN, 8):
                        tap = offset - first_tap
                        if 0 <= tap < taps:
                            aligned = offset - phase
                            term = weights[tap : tap + 1, :] * g[aligned : aligned + SPAN + 8, :]
                            part = term if part is None else part + term
                    if part is not None:
                        moved = part[phase : phase + SPAN, :]
                        out = moved if out is None else out + moved
                return jnp.where(inside[EDGE : EDGE + SPAN], out, done)

            conv = lax.fori_loop(low, high + 1, one_record, jnp.zeros((SPAN, LANES), F32))
            act_ref[pl.ds(target, SPAN), lanes] = (conv / (1.0 + jnp.exp(-conv))).astype(BF16)
        return 0

    if edges:

        def edge(number, _):
            at = pl.multiple_of(number * (total - SPAN), SPAN)
            return one_block(at, pl.multiple_of(number * reach, reach), at)

        lax.fori_loop(0, 2, edge, 0)
    else:

        def inner(number, _):
            at = pl.multiple_of(number * SPAN, SPAN)
            return one_block(at + SPAN, at, at)

        lax.fori_loop(0, count - 2, inner, 0)


def out_kernel(group, cores, *refs):
    acts, weights, outs = refs[:cores], refs[cores : 2 * cores], refs[2 * cores :]
    place, _ = plane_place(group)
    frames = outs[0].shape[0]
    for step in reversed(range(group)):
        rows = pl.ds(pl.multiple_of((place ^ step) * frames, frames), frames)
        total = None
        for act, weight in zip(acts, weights):
            product = dot(act[rows, :], weight[...], ((1,), (1,)))
            total = product if total is None else total + product
        outs[step][...] = total.astype(outs[step].dtype)


def local(
    frames,
    x_weight,
    z_weight,
    bc_weight,
    log_decay,
    norm_gain,
    conv_weight,
    out_weight,
    record_lengths,
):
    times, cores = lax.axis_size("tm"), lax.axis_size("head")
    frame_count, depth = frames.shape
    heads_here, channels = log_decay.shape[0], x_weight.shape[1]
    state = bc_weight.shape[1] // 2
    group = 4
    while group > 1 and (channels // group % LANES or times % group or heads_here % group):
        group //= 2
    planes = times // group
    width, heads = channels // group, heads_here // group
    total = frame_count * group
    count = total // SPAN
    index, core = lax.axis_index("tm"), lax.axis_index("head")
    place = lax.rem(index, group)

    def in_plane(array, step):
        return lax.ppermute(array, "tm", [(i, i ^ step) for i in range(times)])

    def later(array, step):
        return lax.ppermute(array, "tm", [(i, i + step * group) for i in range(times - step * group)])

    def earlier(array, step):
        return lax.ppermute(array, "tm", [(i + step * group, i) for i in range(times - step * group)])

    def across(array, step):
        return lax.ppermute(array, "head", [(i, i ^ step) for i in range(cores)])

    def along_planes(stack):
        if planes != 4:
            moved = [
                lax.ppermute(stack, "tm", [(i, i ^ (step * group)) for i in range(times)]) for step in range(1, planes)
            ]
            return [stack, *moved], tuple(range(planes))

        def pairs(chosen):
            return [(a * group + q, b * group + q) for a, b in chosen for q in range(group)]

        second = lax.ppermute(stack, "tm", pairs([(0, 2), (2, 0), (1, 3), (3, 1)]))
        first = lax.ppermute(stack, "tm", pairs([(0, 1), (1, 0), (2, 3), (3, 2)]))
        again, stack_then = lax.optimization_barrier((second, stack))
        third = lax.ppermute(again, "tm", pairs([(1, 0), (2, 3)]))
        middle = lax.ppermute(stack_then, "tm", pairs([(1, 2), (2, 1)]))
        return [stack, first, second, third, middle], (0, 1, 2, 3, 3)

    shape = jax.ShapeDtypeStruct
    rows = x_weight.shape[0]
    decay_blocks = jnp.pad(log_decay.reshape(group, heads, frame_count), ((0, 0), (0, 8 - heads), (0, 0)))
    packed = call(
        functools.partial(pack_x_kernel, group),
        tuple(shape((rows + 32, width + 2 * state), BF16) for _ in range(group)),
        [decay_blocks, x_weight, bc_weight],
        smem=0,
    )
    parts = [packed[0]] + [in_plane(packed[step], step) for step in range(1, group)]
    frame_parts = [frames] + [in_plane(frames, step) for step in range(1, group)]
    stack, decay = call(
        functools.partial(stack_x_kernel, group),
        (shape((group * rows, width + 2 * state), BF16), shape((group, 8, frame_count), F32)),
        parts,
        smem=0,
    )
    x_pieces, offsets = along_planes(stack)

    packed = call(
        functools.partial(pack_zo_kernel, group),
        tuple(shape((rows, 2 * width), BF16) for _ in range(group)),
        [z_weight, out_weight.T],
        smem=0,
    )
    parts = [packed[0]] + [in_plane(packed[step], step) for step in range(1, group)]
    z_stack, o_stack = call(
        functools.partial(stack_zo_kernel, group),
        (shape((group * rows, width), BF16), shape((group * rows, width), BF16)),
        parts,
        smem=0,
    )
    (z_stack, o_stack), x_last = lax.optimization_barrier(((z_stack, o_stack), x_pieces[-1]))
    x_pieces = [*x_pieces[:-1], x_last]
    z_pieces, _ = along_planes(z_stack)

    used = count * 8
    x_rows, b_rows, c_rows, decays, cumul, steps, carry, keep, summary = call(
        functools.partial(state_kernel, group, heads, state, offsets),
        (
            shape((total, width), BF16),
            shape((total, state), BF16),
            shape((total, state), BF16),
            shape((SPAN, -(-4 * used // SPAN) * SPAN), F32),
            shape((used, SPAN), F32),
            shape((count * state, width), F32),
            shape((total, width), F32),
            shape((count * 8, width), F32),
            shape((state + EDGE, width), BF16),
        ),
        [record_lengths, decay, *frame_parts, *x_pieces],
        [pltpu.VMEM((depth, width + 2 * state), BF16)],
        flops=2 * total * depth * (width + 2 * state),
    )
    summaries = [later(summary, step) for step in range(1, planes)]
    y = call(
        functools.partial(inner_kernel, group, heads),
        shape((total, width), F32),
        [x_rows, b_rows, c_rows, decays, cumul],
        flops=4 * total * SPAN * width,
        smem=0,
    )
    silu = call(
        functools.partial(silu_kernel, group, offsets),
        shape((total, width), F32),
        [norm_gain[None], *frame_parts, *z_pieces],
        [pltpu.VMEM((depth, width), BF16)],
        flops=2 * total * depth * width,
        smem=0,
    )
    o_stack, z_last = lax.optimization_barrier((o_stack, z_pieces[-1]))
    o_pieces, _ = along_planes(o_stack)
    gated, top, bottom = call(
        functools.partial(gate_kernel, heads, state),
        (shape((total, width), BF16), shape((EDGE, width), BF16), shape((EDGE, width), BF16)),
        [c_rows, y, steps, carry, keep, silu, *summaries],
        flops=2 * total * state * width,
        smem=0,
    )
    before, after = later(bottom, 1), earlier(top, 1)
    ends = pltpu.SMEM((record_lengths.shape[0] + 1,), jnp.int32)
    inner = call(
        functools.partial(conv_kernel, group, False),
        shape((total - 2 * SPAN, width), BF16),
        [record_lengths, conv_weight, gated],
        [pltpu.VMEM((total - 2 * SPAN + 2 * EDGE, width), F32), ends],
        flops=2 * total * width * conv_weight.shape[0],
    )
    act = call(
        functools.partial(conv_kernel, group, True),
        shape((total, width), BF16),
        [record_lengths, conv_weight, gated, before, after, inner],
        [pltpu.VMEM((2 * SPAN + 4 * EDGE, width), F32), ends],
        flops=4 * SPAN * width * conv_weight.shape[0],
    )
    share = depth // cores
    out_parts = call(
        functools.partial(share_kernel, group, cores, offsets),
        tuple(shape((share, width), BF16) for _ in range(cores)),
        o_pieces,
        [pltpu.VMEM((depth, width), BF16)],
        smem=0,
    )
    out_parts = [out_parts[0]] + [across(out_parts[step], step) for step in range(1, cores)]
    acts = [act] + [across(act, step) for step in range(1, cores)]
    outs = call(
        functools.partial(out_kernel, group, cores),
        tuple(shape((frame_count, share), BF16 if step else F32) for step in range(group)),
        [*acts, *out_parts],
        flops=2 * total * width * cores * share,
        smem=0,
    )
    mixed = outs[0]
    for step in range(1, group):
        mixed = mixed + in_plane(outs[step], step).astype(F32)
    return mixed.astype(BF16)


def solution(mesh):
    in_specs = (
        P("tm", None),
        P("tm", "head"),
        P("tm", "head"),
        P("tm", None),
        P("head", "tm"),
        P("head"),
        P(None, "head"),
        P("head", "tm"),
        P(),
    )
    out_specs = P("tm", "head")
    return jax.shard_map(local, mesh=mesh, in_specs=in_specs, out_specs=out_specs, check_vma=False)
```

```python
import functools

import jax
import jax.numpy as jnp
from jax import lax
from jax.experimental import pallas as pl
from jax.experimental.pallas import tpu as pltpu
from jax.sharding import PartitionSpec as P

SPAN = 128
LANES = 128
EDGE = 16
BF16 = jnp.bfloat16
F32 = jnp.float32
VMEM_BYTES = 48 * 1024 * 1024


def dot(a, b, dims=((1,), (0,)), precision=None):
    return lax.dot_general(a, b, (dims, ((), ())), precision=precision, preferred_element_type=F32)


def call(kernel, out_shape, operands, scratch=(), flops=0, smem=1):
    in_specs = [pl.BlockSpec(memory_space=pltpu.SMEM)] * smem
    in_specs += [pl.BlockSpec(memory_space=pltpu.VMEM)] * (len(operands) - smem)
    moved = sum(a.size * a.dtype.itemsize for a in operands)
    moved += sum(a.size * a.dtype.itemsize for a in jax.tree.leaves(out_shape))
    return pl.pallas_call(
        kernel,
        out_shape=out_shape,
        in_specs=in_specs,
        out_specs=jax.tree.map(lambda _: pl.BlockSpec(memory_space=pltpu.VMEM), out_shape),
        scratch_shapes=list(scratch),
        compiler_params=pltpu.CompilerParams(vmem_limit_bytes=VMEM_BYTES),
        cost_estimate=pl.CostEstimate(flops=flops, bytes_accessed=moved, transcendentals=0),
    )(*operands)


def plane_place(group):
    index = lax.axis_index("tm")
    return lax.rem(index, group), lax.div(index, group)


def record_starts(len_ref, position):
    start = jnp.zeros_like(position)
    end = jnp.int32(0)
    for record in range(len_ref.shape[0] - 1):
        end = end + len_ref[record]
        start = jnp.where(position >= end, end, start)
    return start


def spread(columns, first, heads, head_of_lane, shape):
    out = jnp.broadcast_to(columns[:, first : first + 1], shape)
    for head in range(1, heads):
        column = jnp.broadcast_to(columns[:, first + head : first + head + 1], shape)
        out = jnp.where(head_of_lane == head, column, out)
    return out


def pack_kernel(group, *refs):
    weight_refs, out_ref = refs[:-1], refs[-1]
    width = weight_refs[0].shape[1] // group
    for target in range(out_ref.shape[0]):
        block = target % group
        for number, weight_ref in enumerate(weight_refs):
            columns = weight_ref[:, block * width : (block + 1) * width]
            out_ref[target, :, number * width : (number + 1) * width] = columns


def share_bc_kernel(group, decay_ref, *refs):
    bc_refs, out_refs = refs[:-group], refs[-group:]
    place, _ = plane_place(group)
    rows = bc_refs[0].shape[0]
    below = len(bc_refs) * rows
    for step, out_ref in enumerate(out_refs):
        for number, bc_ref in enumerate(bc_refs):
            out_ref[number * rows : (number + 1) * rows, :] = bc_ref[...]
        left = decay_ref[place ^ step]
        terms = []
        for _ in range(3):
            term = left.astype(BF16).astype(F32)
            terms.append(term)
            left = left - term
        terms.append(jnp.zeros_like(left))
        terms = jnp.concatenate(terms, axis=0).astype(BF16)
        for span in range(terms.shape[1] // SPAN):
            rows_here = slice(below + span * 32, below + (span + 1) * 32)
            out_ref[rows_here, :] = terms[:, span * SPAN : (span + 1) * SPAN]


def swap_kernel(group, rows, *refs):
    part_refs, half_refs = refs[:group], refs[group : 2 * group - 1]
    swap_ref, bc_ref, decay_ref = refs[2 * group - 1 :]
    place, plane = plane_place(group)
    planes = bc_ref.shape[0] // (group * rows)
    below = planes * rows
    spans = (part_refs[0].shape[0] - below) // 32
    for step, part_ref in enumerate(part_refs):
        block = place ^ step
        for offset in range(planes):
            at = pl.multiple_of(((plane ^ offset) * group + block) * rows, rows)
            bc_ref[pl.ds(at, rows), :] = part_ref[offset * rows : (offset + 1) * rows, :]
        for span in range(spans):
            terms = part_ref[below + span * 32 : below + (span + 1) * 32, :].astype(F32)
            at = pl.multiple_of((block * spans + span) * 8, 8)
            decay_ref[pl.ds(at, 8), :] = terms[:8] + terms[8:16] + terms[16:24]
    half = half_refs[0].shape[0]
    for number, half_ref in enumerate(half_refs):
        swap_ref[number * half : (number + 1) * half, :] = half_ref[...]
    top = len(half_refs) * half
    height = swap_ref.shape[0] - top
    for number in range(bc_ref.shape[0] // height):
        lanes = slice(number * LANES, (number + 1) * LANES)
        swap_ref[top:, lanes] = bc_ref[number * height : (number + 1) * height, :]


def state_kernel(group, heads, state, len_ref, decay_ref, xz_ref, bc_half_ref, own_ref, swap_ref, *refs):
    half_refs, refs = refs[: group - 1], refs[group - 1 :]
    frames_ref, x_ref, b_ref, c_ref, columns_ref, cumul_ref, step_ref, carry_ref, keep_ref, send_ref, weight_ref = refs
    place, plane = plane_place(group)
    parity = lax.rem(lax.axis_index("head"), 2)
    total, width = x_ref.shape
    frames = total // group
    half = frames // 2
    head_size = width // heads
    count = total // SPAN
    base = plane * total
    frames_ref[pl.ds(pl.multiple_of(place * frames, frames), frames), :] = own_ref[...]
    for number, half_ref in enumerate(half_refs):
        block = (place ^ (number + 1)) * frames
        mine = pl.ds(pl.multiple_of(block + parity * half, half), half)
        other = pl.ds(pl.multiple_of(block + (1 - parity) * half, half), half)
        frames_ref[mine, :] = half_ref[...]
        frames_ref[other, :] = swap_ref[number * half : (number + 1) * half, :]
    weight_ref[:, :width] = xz_ref[:, :width]
    mine = pl.ds(pl.multiple_of(width + parity * LANES, LANES), LANES)
    other = pl.ds(pl.multiple_of(width + (1 - parity) * LANES, LANES), LANES)
    weight_ref[:, mine] = bc_half_ref[...]
    top = len(half_refs) * half
    height = swap_ref.shape[0] - top
    for number in range(weight_ref.shape[0] // height):
        lanes = slice(number * LANES, (number + 1) * LANES)
        weight_ref[number * height : (number + 1) * height, other] = swap_ref[top:, lanes]
    for block in range(group):
        rows = slice(block * frames, (block + 1) * frames)
        product = dot(frames_ref[rows, :], weight_ref[...])
        x_ref[rows, :] = product[:, :width].astype(BF16)
        b_ref[rows, :] = product[:, width : width + state].astype(BF16)
        c_ref[rows, :] = product[:, width + state :].astype(BF16)

    decay = decay_ref[...]
    used = decay.shape[0]
    square = (SPAN, SPAN)
    row, lane = (lax.broadcasted_iota(jnp.int32, square, dim) for dim in (0, 1))
    upper = jnp.where(row <= lane, 1.0, 0.0).astype(F32)
    cumul = dot(decay, upper, precision=lax.Precision.HIGHEST)
    whole = dot(decay, jnp.ones(square, F32), precision=lax.Precision.HIGHEST)
    first = base + lax.broadcasted_iota(jnp.int32, (used, SPAN), 0) // 8 * SPAN
    position = first + lane[:1]
    start = record_starts(len_ref, position)
    start_last = record_starts(len_ref, first + (SPAN - 1))
    carried = jnp.where(start < first, jnp.exp(cumul), 0.0)
    tail = jnp.where(position >= start_last, jnp.exp(whole - cumul), 0.0)
    keep = jnp.where(start_last < first, jnp.exp(whole), 0.0)
    parts = [cumul, carried, tail, start.astype(F32)]
    if 4 * used % SPAN:
        parts.append(jnp.zeros((SPAN - 4 * used % SPAN, SPAN), F32))
    columns = jnp.concatenate(parts, axis=0).T
    columns_ref[...] = columns
    cumul_ref[...] = cumul

    head_of_lane = lax.broadcasted_iota(jnp.int32, (SPAN, width), 1) // head_size
    entry = jnp.zeros((state, width), F32)
    through = jnp.ones((1, width), F32)
    for block in range(count):
        rows = slice(block * SPAN, (block + 1) * SPAN)
        at = block * 8
        kept = jnp.broadcast_to(keep[at : at + 1, :1], (1, width))
        for head in range(1, heads):
            other = jnp.broadcast_to(keep[at + head : at + head + 1, :1], (1, width))
            kept = jnp.where(head_of_lane[:1] == head, other, kept)
        carry_ref[rows, :] = spread(columns, used + at, heads, head_of_lane, (SPAN, width))
        weighed = x_ref[rows, :].astype(F32) * spread(columns, 2 * used + at, heads, head_of_lane, (SPAN, width))
        step = dot(b_ref[rows, :], weighed.astype(BF16), ((0,), (0,)))
        step_ref[block * state : (block + 1) * state, :] = step
        keep_ref[block * 8 : (block + 1) * 8, :] = jnp.broadcast_to(kept, (8, width))
        entry = kept * entry + step
        through = through * kept
    send_ref[:state, :] = entry.astype(BF16)
    send_ref[state:, :] = jnp.broadcast_to(through, (EDGE, width)).astype(BF16)


def inner_kernel(group, heads, x_ref, b_ref, c_ref, columns_ref, cumul_ref, y_ref):
    _, plane = plane_place(group)
    total, width = x_ref.shape
    head_size = width // heads
    count = total // SPAN
    base = plane * total
    used = cumul_ref.shape[0]
    square = (SPAN, SPAN)
    row, lane = (lax.broadcasted_iota(jnp.int32, square, dim) for dim in (0, 1))
    lower = row >= lane
    tile_heads = LANES // head_size
    tile_lane = lax.broadcasted_iota(jnp.int32, (1, LANES), 1) // head_size
    masks = [jnp.where(tile_lane == inner, 1.0, 0.0).astype(BF16) for inner in range(tile_heads)]
    for block in range(count):
        rows = slice(block * SPAN, (block + 1) * SPAN)
        at = block * 8
        x = x_ref[rows, :]
        scores = dot(c_ref[rows, :], b_ref[rows, :], ((1,), (1,)))
        here = (base + block * SPAN + lane).astype(F32)
        start_here = jnp.broadcast_to(columns_ref[:, 3 * used + at : 3 * used + at + 1], square)
        joined = lower & (here >= start_here)
        for tile in range(width // LANES):
            mixes, values = [], []
            for inner in range(tile_heads):
                which = at + tile * tile_heads + inner
                column = jnp.broadcast_to(columns_ref[:, which : which + 1], square)
                gap = jnp.where(joined, column - cumul_ref[which : which + 1, :], -1e30)
                mixes.append((jnp.exp(gap) * scores).astype(BF16))
                values.append(x[:, tile * LANES : (tile + 1) * LANES] * masks[inner])
            y_ref[rows, tile * LANES : (tile + 1) * LANES] = dot(
                jnp.concatenate(mixes, axis=1), jnp.concatenate(values, axis=0)
            )


def silu_kernel(group, gain_ref, frames_ref, xz_ref, out_ref):
    place, _ = plane_place(group)
    total, width = out_ref.shape
    gain = gain_ref[:, pl.ds(pl.multiple_of(place * width, LANES), width)]
    for block in range(group):
        rows = slice(block * (total // group), (block + 1) * (total // group))
        z = dot(frames_ref[rows, :], xz_ref[:, width:]).astype(BF16).astype(F32)
        out_ref[rows, :] = z / (1.0 + jnp.exp(-z)) * gain


def gate_kernel(heads, state, c_ref, y_ref, step_ref, carry_ref, keep_ref, silu_ref, *refs):
    earlier, (gated_ref, top_ref, bottom_ref) = refs[:-3], refs[-3:]
    total, width = y_ref.shape
    head_size = width // heads
    entry = jnp.zeros((state, width), F32)
    for summary in reversed(earlier):
        through = summary[state : state + EDGE, :].astype(F32)[:1]
        entry = through * entry + summary[:state, :].astype(F32)
    owner = [lax.broadcasted_iota(jnp.int32, (width, width), dim) // head_size for dim in (0, 1)]
    average = jnp.where(owner[0] == owner[1], 1.0 / head_size, 0.0).astype(BF16)
    for block in range(total // SPAN):
        rows = slice(block * SPAN, (block + 1) * SPAN)
        y = y_ref[rows, :] + carry_ref[rows, :] * dot(c_ref[rows, :], entry.astype(BF16))
        square_mean = dot((y * y).astype(BF16), average)
        gated_ref[rows, :] = (y * lax.rsqrt(square_mean + 1e-05) * silu_ref[rows, :]).astype(BF16)
        entry = keep_ref[block * 8 : block * 8 + 1, :] * entry + step_ref[block * state : (block + 1) * state, :]
    top_ref[...] = gated_ref[:EDGE, :]
    bottom_ref[...] = gated_ref[total - EDGE :, :]


def conv_kernel(group, edges, len_ref, taps_ref, gated_ref, *refs):
    if edges:
        before_ref, after_ref, inner_ref, act_ref, ext_ref, ends_ref = refs
    else:
        act_ref, ext_ref, ends_ref = refs
    place, plane = plane_place(group)
    total, width = gated_ref.shape
    count = total // SPAN
    taps = taps_ref.shape[0]
    half = (taps - 1) // 2
    base = plane * total
    stream = lax.axis_size("tm") // group * total
    records = len_ref.shape[0]
    reach = SPAN + 2 * EDGE
    first_tap = EDGE - half
    if edges:
        act_ref[SPAN : total - SPAN, :] = inner_ref[...]
        ext_ref[:EDGE, :] = before_ref[...].astype(F32)
        ext_ref[EDGE:reach, :] = gated_ref[: SPAN + EDGE, :].astype(F32)
        ext_ref[reach : 2 * reach - EDGE, :] = gated_ref[total - SPAN - EDGE :, :].astype(F32)
        ext_ref[2 * reach - EDGE :, :] = after_ref[...].astype(F32)
    else:
        ext_ref[...] = gated_ref[SPAN - EDGE : total - SPAN + EDGE, :].astype(F32)
    ends_ref[0] = 0
    for record in range(records):
        ends_ref[record + 1] = ends_ref[record] + len_ref[record]

    def record_at(position):
        found = jnp.int32(0)
        for record in range(records - 1):
            found = found + (ends_ref[record + 1] <= position).astype(jnp.int32)
        return found

    def one_block(at, source, target):
        low = record_at(jnp.maximum(base + at - half, 0))
        high = record_at(jnp.minimum(base + at + SPAN - 1 + half, stream - 1))
        near = lax.broadcasted_iota(jnp.int32, (reach, LANES), 0) + (base + at - EDGE)
        for tile in range(width // LANES):
            lanes = slice(tile * LANES, (tile + 1) * LANES)
            weights = taps_ref[:, pl.ds(pl.multiple_of(place * width + tile * LANES, LANES), LANES)]

            def one_record(record, done):
                inside = (near >= ends_ref[record]) & (near < ends_ref[record + 1])
                g = jnp.where(inside, ext_ref[pl.ds(source, reach), lanes], 0.0)
                out = None
                for phase in range(8):
                    part = None
                    for offset in range(phase, reach - SPAN, 8):
                        tap = offset - first_tap
                        if 0 <= tap < taps:
                            aligned = offset - phase
                            term = weights[tap : tap + 1, :] * g[aligned : aligned + SPAN + 8, :]
                            part = term if part is None else part + term
                    if part is not None:
                        moved = part[phase : phase + SPAN, :]
                        out = moved if out is None else out + moved
                return jnp.where(inside[EDGE : EDGE + SPAN], out, done)

            conv = lax.fori_loop(low, high + 1, one_record, jnp.zeros((SPAN, LANES), F32))
            act_ref[pl.ds(target, SPAN), lanes] = (conv / (1.0 + jnp.exp(-conv))).astype(BF16)
        return 0

    if edges:

        def edge(number, _):
            at = pl.multiple_of(number * (total - SPAN), SPAN)
            return one_block(at, pl.multiple_of(number * reach, reach), at)

        lax.fori_loop(0, 2, edge, 0)
    else:

        def inner(number, _):
            at = pl.multiple_of(number * SPAN, SPAN)
            return one_block(at + SPAN, at, at)

        lax.fori_loop(0, count - 2, inner, 0)


def out_kernel(group, cores, *refs):
    acts, weights, outs = refs[:cores], refs[cores : 2 * cores], refs[2 * cores :]
    place, _ = plane_place(group)
    frames = outs[0].shape[0]
    for step in reversed(range(group)):
        rows = pl.ds(pl.multiple_of((place ^ step) * frames, frames), frames)
        total = None
        for act, weight in zip(acts, weights):
            product = dot(act[rows, :], weight[...], ((1,), (1,)))
            total = product if total is None else total + product
        outs[step][...] = total.astype(outs[step].dtype)


def local(
    frames,
    x_weight,
    z_weight,
    bc_weight,
    log_decay,
    norm_gain,
    conv_weight,
    out_weight,
    record_lengths,
):
    times, cores = lax.axis_size("tm"), lax.axis_size("head")
    frame_count, depth = frames.shape
    heads_here, channels = log_decay.shape[0], x_weight.shape[1]
    state = bc_weight.shape[1] // 2
    group = 4
    while group > 1 and (channels // group % LANES or times % group or heads_here % group):
        group //= 2
    planes = times // group
    width, heads = channels // group, heads_here // group
    total = frame_count * group
    count = total // SPAN
    index, core = lax.axis_index("tm"), lax.axis_index("head")
    place = lax.rem(index, group)

    def in_plane(array, step):
        return lax.ppermute(array, "tm", [(i, i ^ step) for i in range(times)])

    def later(array, step):
        return lax.ppermute(array, "tm", [(i, i + step * group) for i in range(times - step * group)])

    def earlier(array, step):
        return lax.ppermute(array, "tm", [(i + step * group, i) for i in range(times - step * group)])

    def across(array, step):
        return lax.ppermute(array, "head", [(i, i ^ step) for i in range(cores)])

    def between_planes(array, step):
        return lax.ppermute(array, "tm", [(i, i ^ (step * group)) for i in range(times)])

    shape = jax.ShapeDtypeStruct
    rows = x_weight.shape[0]
    parity = lax.rem(core, 2)

    def to_owners(*weights):
        blocks = call(
            functools.partial(pack_kernel, group),
            shape((times, rows, len(weights) * width), BF16),
            list(weights),
            smem=0,
        )
        moved = lax.all_to_all(blocks, "tm", split_axis=0, concat_axis=0, tiled=True)
        return moved.reshape(times * rows, -1)

    xz = to_owners(x_weight, z_weight)
    bc_half = lax.dynamic_slice_in_dim(bc_weight, parity * LANES, LANES, 1)
    bc_pieces = [bc_half] + [between_planes(bc_half, step) for step in range(1, planes)]
    half_count = frame_count // 2
    frame_half = lax.dynamic_slice_in_dim(frames, parity * half_count, half_count, 0)
    half_parts = [in_plane(frame_half, step) for step in range(1, group)]
    decay_blocks = jnp.pad(log_decay.reshape(group, heads, frame_count), ((0, 0), (0, 8 - heads), (0, 0)))
    bc_parts = call(
        functools.partial(share_bc_kernel, group),
        tuple(shape((planes * rows + frame_count // SPAN * 32, LANES), BF16) for _ in range(group)),
        [decay_blocks, *bc_pieces],
        smem=0,
    )
    bc_parts = [bc_parts[0]] + [in_plane(bc_parts[step], step) for step in range(1, group)]
    height = depth * LANES // depth
    swap, bc_mine, decay = call(
        functools.partial(swap_kernel, group, rows),
        (
            shape(((group - 1) * half_count + height, depth), BF16),
            shape((depth, LANES), BF16),
            shape((count * 8, SPAN), F32),
        ),
        [*bc_parts, *half_parts],
        smem=0,
    )
    swap = across(swap, 1)

    used = count * 8
    frame_rows, x_rows, b_rows, c_rows, decays, cumul, steps, carry, keep, summary = call(
        functools.partial(state_kernel, group, heads, state),
        (
            shape((total, depth), BF16),
            shape((total, width), BF16),
            shape((total, state), BF16),
            shape((total, state), BF16),
            shape((SPAN, -(-4 * used // SPAN) * SPAN), F32),
            shape((used, SPAN), F32),
            shape((count * state, width), F32),
            shape((total, width), F32),
            shape((count * 8, width), F32),
            shape((state + EDGE, width), BF16),
        ),
        [record_lengths, decay, xz, bc_mine, frames, swap, *half_parts],
        [pltpu.VMEM((depth, width + 2 * state), BF16)],
        flops=2 * total * depth * (width + 2 * state),
    )
    summaries = [later(summary, step) for step in range(1, planes)]
    y = call(
        functools.partial(inner_kernel, group, heads),
        shape((total, width), F32),
        [x_rows, b_rows, c_rows, decays, cumul],
        flops=4 * total * SPAN * width,
        smem=0,
    )
    silu = call(
        functools.partial(silu_kernel, group),
        shape((total, width), F32),
        [norm_gain[None], frame_rows, xz],
        flops=2 * total * depth * width,
        smem=0,
    )
    gated, top, bottom = call(
        functools.partial(gate_kernel, heads, state),
        (shape((total, width), BF16), shape((EDGE, width), BF16), shape((EDGE, width), BF16)),
        [c_rows, y, steps, carry, keep, silu, *summaries],
        flops=2 * total * state * width,
        smem=0,
    )
    before, after = later(bottom, 1), earlier(top, 1)
    ends = pltpu.SMEM((record_lengths.shape[0] + 1,), jnp.int32)
    inner = call(
        functools.partial(conv_kernel, group, False),
        shape((total - 2 * SPAN, width), BF16),
        [record_lengths, conv_weight, gated],
        [pltpu.VMEM((total - 2 * SPAN + 2 * EDGE, width), F32), ends],
        flops=2 * total * width * conv_weight.shape[0],
    )
    act = call(
        functools.partial(conv_kernel, group, True),
        shape((total, width), BF16),
        [record_lengths, conv_weight, gated, before, after, inner],
        [pltpu.VMEM((2 * SPAN + 4 * EDGE, width), F32), ends],
        flops=4 * SPAN * width * conv_weight.shape[0],
    )
    out_columns, _ = lax.optimization_barrier((out_weight.T, xz))
    out_rows = to_owners(out_columns)
    share = depth // cores
    out_parts = [lax.dynamic_slice_in_dim(out_rows, core * share, share, 0)]
    for step in range(1, cores):
        sent = lax.dynamic_slice_in_dim(out_rows, (core ^ step) * share, share, 0)
        out_parts.append(across(sent, step))
    acts = [act] + [across(act, step) for step in range(1, cores)]
    outs = call(
        functools.partial(out_kernel, group, cores),
        tuple(shape((frame_count, share), BF16 if step else F32) for step in range(group)),
        [*acts, *out_parts],
        flops=2 * total * width * cores * share,
        smem=0,
    )
    mixed = outs[0]
    for step in range(1, group):
        mixed = mixed + in_plane(outs[step], step).astype(F32)
    return mixed.astype(BF16)


def solution(mesh):
    in_specs = (
        P("tm", None),
        P("tm", "head"),
        P("tm", "head"),
        P("tm", None),
        P("head", "tm"),
        P("head"),
        P(None, "head"),
        P("head", "tm"),
        P(),
    )
    out_specs = P("tm", "head")
    return jax.shard_map(local, mesh=mesh, in_specs=in_specs, out_specs=out_specs, check_vma=False)
```

```python
import functools

import jax
import jax.numpy as jnp
from jax import lax
from jax.experimental import pallas as pl
from jax.experimental.pallas import tpu as pltpu
from jax.sharding import PartitionSpec as P

SPAN = 128
LANES = 128
EDGE = 16
BF16 = jnp.bfloat16
F32 = jnp.float32
VMEM_BYTES = 48 * 1024 * 1024


def dot(a, b, dims=((1,), (0,)), precision=None):
    return lax.dot_general(a, b, (dims, ((), ())), precision=precision, preferred_element_type=F32)


def call(kernel, out_shape, operands, scratch=(), flops=0, smem=1):
    in_specs = [pl.BlockSpec(memory_space=pltpu.SMEM)] * smem
    in_specs += [pl.BlockSpec(memory_space=pltpu.VMEM)] * (len(operands) - smem)
    moved = sum(a.size * a.dtype.itemsize for a in operands)
    moved += sum(a.size * a.dtype.itemsize for a in jax.tree.leaves(out_shape))
    return pl.pallas_call(
        kernel,
        out_shape=out_shape,
        in_specs=in_specs,
        out_specs=jax.tree.map(lambda _: pl.BlockSpec(memory_space=pltpu.VMEM), out_shape),
        scratch_shapes=list(scratch),
        compiler_params=pltpu.CompilerParams(vmem_limit_bytes=VMEM_BYTES),
        cost_estimate=pl.CostEstimate(flops=flops, bytes_accessed=moved, transcendentals=0),
    )(*operands)


def plane_place(group):
    index = lax.axis_index("tm")
    return lax.rem(index, group), lax.div(index, group)


def record_starts(len_ref, position):
    start = jnp.zeros_like(position)
    end = jnp.int32(0)
    for record in range(len_ref.shape[0] - 1):
        end = end + len_ref[record]
        start = jnp.where(position >= end, end, start)
    return start


def spread(columns, first, heads, head_of_lane, shape):
    out = jnp.broadcast_to(columns[:, first : first + 1], shape)
    for head in range(1, heads):
        column = jnp.broadcast_to(columns[:, first + head : first + head + 1], shape)
        out = jnp.where(head_of_lane == head, column, out)
    return out


def fill_planes(plane, dest_ref, pieces, offsets, lanes=slice(None)):
    rows = pieces[0].shape[0]
    for offset in sorted(set(offsets)):
        same = [piece[:, lanes] for piece, at in zip(pieces, offsets) if at == offset]
        value = same[0] if len(same) == 1 else same[0] + same[1]
        dest_ref[pl.ds(pl.multiple_of((plane ^ offset) * rows, rows), rows), : value.shape[1]] = value


def pack_kernel(group, *refs):
    weight_refs, out_refs = refs[:-group], refs[-group:]
    width = weight_refs[0].shape[1] // group
    place, _ = plane_place(group)
    for step, out_ref in enumerate(out_refs):
        lanes = pl.ds(pl.multiple_of((place ^ step) * width, LANES), width)
        for number, weight_ref in enumerate(weight_refs):
            out_ref[:, number * width : (number + 1) * width] = weight_ref[:, lanes]


def stack_kernel(group, *refs):
    parts, stack_refs = refs[:group], refs[group:]
    place, _ = plane_place(group)
    rows = parts[0].shape[0]
    for step, part in enumerate(parts):
        at = pl.ds(pl.multiple_of((place ^ step) * rows, rows), rows)
        first = 0
        for stack_ref in stack_refs:
            width = stack_ref.shape[1]
            stack_ref[at, :] = part[:, first : first + width]
            first += width


def share_bc_kernel(group, decay_ref, *refs):
    bc_refs, out_refs = refs[:-group], refs[-group:]
    place, _ = plane_place(group)
    rows = bc_refs[0].shape[0]
    below = len(bc_refs) * rows
    for step, out_ref in enumerate(out_refs):
        for number, bc_ref in enumerate(bc_refs):
            out_ref[number * rows : (number + 1) * rows, :] = bc_ref[...]
        left = decay_ref[place ^ step]
        terms = []
        for _ in range(3):
            term = left.astype(BF16).astype(F32)
            terms.append(term)
            left = left - term
        terms.append(jnp.zeros_like(left))
        terms = jnp.concatenate(terms, axis=0).astype(BF16)
        for span in range(terms.shape[1] // SPAN):
            rows_here = slice(below + span * 32, below + (span + 1) * 32)
            out_ref[rows_here, :] = terms[:, span * SPAN : (span + 1) * SPAN]


def swap_kernel(group, rows, *refs):
    part_refs, half_refs = refs[:group], refs[group : 2 * group - 1]
    swap_ref, bc_ref, decay_ref = refs[2 * group - 1 :]
    place, plane = plane_place(group)
    planes = bc_ref.shape[0] // (group * rows)
    below = planes * rows
    spans = (part_refs[0].shape[0] - below) // 32
    for step, part_ref in enumerate(part_refs):
        block = place ^ step
        for offset in range(planes):
            at = pl.multiple_of(((plane ^ offset) * group + block) * rows, rows)
            bc_ref[pl.ds(at, rows), :] = part_ref[offset * rows : (offset + 1) * rows, :]
        for span in range(spans):
            terms = part_ref[below + span * 32 : below + (span + 1) * 32, :].astype(F32)
            at = pl.multiple_of((block * spans + span) * 8, 8)
            decay_ref[pl.ds(at, 8), :] = terms[:8] + terms[8:16] + terms[16:24]
    half = half_refs[0].shape[0]
    for number, half_ref in enumerate(half_refs):
        swap_ref[number * half : (number + 1) * half, :] = half_ref[...]
    top = len(half_refs) * half
    height = swap_ref.shape[0] - top
    for number in range(bc_ref.shape[0] // height):
        lanes = slice(number * LANES, (number + 1) * LANES)
        swap_ref[top:, lanes] = bc_ref[number * height : (number + 1) * height, :]


def state_kernel(group, heads, state, offsets, len_ref, decay_ref, bc_half_ref, own_ref, swap_ref, *refs):
    half_refs, refs = refs[: group - 1], refs[group - 1 :]
    pieces, refs = refs[: len(offsets)], refs[len(offsets) :]
    frames_ref, z_ref, x_ref, b_ref, c_ref, columns_ref, cumul_ref, step_ref, carry_ref, keep_ref, send_ref, weight_ref = refs
    place, plane = plane_place(group)
    parity = lax.rem(lax.axis_index("head"), 2)
    total, width = x_ref.shape
    frames = total // group
    half = frames // 2
    head_size = width // heads
    count = total // SPAN
    base = plane * total
    frames_ref[pl.ds(pl.multiple_of(place * frames, frames), frames), :] = own_ref[...]
    for number, half_ref in enumerate(half_refs):
        block = (place ^ (number + 1)) * frames
        mine = pl.ds(pl.multiple_of(block + parity * half, half), half)
        other = pl.ds(pl.multiple_of(block + (1 - parity) * half, half), half)
        frames_ref[mine, :] = half_ref[...]
        frames_ref[other, :] = swap_ref[number * half : (number + 1) * half, :]
    fill_planes(plane, weight_ref, pieces, offsets, slice(0, width))
    fill_planes(plane, z_ref, pieces, offsets, slice(width, 2 * width))
    mine = pl.ds(pl.multiple_of(width + parity * LANES, LANES), LANES)
    other = pl.ds(pl.multiple_of(width + (1 - parity) * LANES, LANES), LANES)
    weight_ref[:, mine] = bc_half_ref[...]
    top = len(half_refs) * half
    height = swap_ref.shape[0] - top
    for number in range(weight_ref.shape[0] // height):
        lanes = slice(number * LANES, (number + 1) * LANES)
        weight_ref[number * height : (number + 1) * height, other] = swap_ref[top:, lanes]
    for block in range(group):
        rows = slice(block * frames, (block + 1) * frames)
        product = dot(frames_ref[rows, :], weight_ref[...])
        x_ref[rows, :] = product[:, :width].astype(BF16)
        b_ref[rows, :] = product[:, width : width + state].astype(BF16)
        c_ref[rows, :] = product[:, width + state :].astype(BF16)

    decay = decay_ref[...]
    used = decay.shape[0]
    square = (SPAN, SPAN)
    row, lane = (lax.broadcasted_iota(jnp.int32, square, dim) for dim in (0, 1))
    upper = jnp.where(row <= lane, 1.0, 0.0).astype(F32)
    cumul = dot(decay, upper, precision=lax.Precision.HIGHEST)
    whole = dot(decay, jnp.ones(square, F32), precision=lax.Precision.HIGHEST)
    first = base + lax.broadcasted_iota(jnp.int32, (used, SPAN), 0) // 8 * SPAN
    position = first + lane[:1]
    start = record_starts(len_ref, position)
    start_last = record_starts(len_ref, first + (SPAN - 1))
    carried = jnp.where(start < first, jnp.exp(cumul), 0.0)
    tail = jnp.where(position >= start_last, jnp.exp(whole - cumul), 0.0)
    keep = jnp.where(start_last < first, jnp.exp(whole), 0.0)
    parts = [cumul, carried, tail, start.astype(F32)]
    if 4 * used % SPAN:
        parts.append(jnp.zeros((SPAN - 4 * used % SPAN, SPAN), F32))
    columns = jnp.concatenate(parts, axis=0).T
    columns_ref[...] = columns
    cumul_ref[...] = cumul

    head_of_lane = lax.broadcasted_iota(jnp.int32, (SPAN, width), 1) // head_size
    entry = jnp.zeros((state, width), F32)
    through = jnp.ones((1, width), F32)
    for block in range(count):
        rows = slice(block * SPAN, (block + 1) * SPAN)
        at = block * 8
        kept = jnp.broadcast_to(keep[at : at + 1, :1], (1, width))
        for head in range(1, heads):
            other = jnp.broadcast_to(keep[at + head : at + head + 1, :1], (1, width))
            kept = jnp.where(head_of_lane[:1] == head, other, kept)
        carry_ref[rows, :] = spread(columns, used + at, heads, head_of_lane, (SPAN, width))
        weighed = x_ref[rows, :].astype(F32) * spread(columns, 2 * used + at, heads, head_of_lane, (SPAN, width))
        step = dot(b_ref[rows, :], weighed.astype(BF16), ((0,), (0,)))
        step_ref[block * state : (block + 1) * state, :] = step
        keep_ref[block * 8 : (block + 1) * 8, :] = jnp.broadcast_to(kept, (8, width))
        entry = kept * entry + step
        through = through * kept
    send_ref[:state, :] = entry.astype(BF16)
    send_ref[state:, :] = jnp.broadcast_to(through, (EDGE, width)).astype(BF16)


def inner_kernel(group, heads, x_ref, b_ref, c_ref, columns_ref, cumul_ref, y_ref):
    _, plane = plane_place(group)
    total, width = x_ref.shape
    head_size = width // heads
    count = total // SPAN
    base = plane * total
    used = cumul_ref.shape[0]
    square = (SPAN, SPAN)
    row, lane = (lax.broadcasted_iota(jnp.int32, square, dim) for dim in (0, 1))
    lower = row >= lane
    tile_heads = LANES // head_size
    tile_lane = lax.broadcasted_iota(jnp.int32, (1, LANES), 1) // head_size
    masks = [jnp.where(tile_lane == inner, 1.0, 0.0).astype(BF16) for inner in range(tile_heads)]
    for block in range(count):
        rows = slice(block * SPAN, (block + 1) * SPAN)
        at = block * 8
        x = x_ref[rows, :]
        scores = dot(c_ref[rows, :], b_ref[rows, :], ((1,), (1,)))
        here = (base + block * SPAN + lane).astype(F32)
        start_here = jnp.broadcast_to(columns_ref[:, 3 * used + at : 3 * used + at + 1], square)
        joined = lower & (here >= start_here)
        for tile in range(width // LANES):
            mixes, values = [], []
            for inner in range(tile_heads):
                which = at + tile * tile_heads + inner
                column = jnp.broadcast_to(columns_ref[:, which : which + 1], square)
                gap = jnp.where(joined, column - cumul_ref[which : which + 1, :], -1e30)
                mixes.append((jnp.exp(gap) * scores).astype(BF16))
                values.append(x[:, tile * LANES : (tile + 1) * LANES] * masks[inner])
            y_ref[rows, tile * LANES : (tile + 1) * LANES] = dot(
                jnp.concatenate(mixes, axis=1), jnp.concatenate(values, axis=0)
            )


def silu_kernel(group, gain_ref, frames_ref, weight_ref, out_ref):
    place, _ = plane_place(group)
    total, width = out_ref.shape
    gain = gain_ref[:, pl.ds(pl.multiple_of(place * width, LANES), width)]
    for block in range(group):
        rows = slice(block * (total // group), (block + 1) * (total // group))
        z = dot(frames_ref[rows, :], weight_ref[...]).astype(BF16).astype(F32)
        out_ref[rows, :] = z / (1.0 + jnp.exp(-z)) * gain


def share_kernel(cores, offsets, group, *refs):
    pieces, refs = refs[: len(offsets)], refs[len(offsets) :]
    outs, weight_ref = refs[:cores], refs[cores]
    _, plane = plane_place(group)
    core = lax.axis_index("head")
    fill_planes(plane, weight_ref, pieces, offsets)
    for step, out_ref in enumerate(outs):
        rows = out_ref.shape[0]
        out_ref[...] = weight_ref[pl.ds(pl.multiple_of((core ^ step) * rows, rows), rows), :]


def gate_kernel(heads, state, c_ref, y_ref, step_ref, carry_ref, keep_ref, silu_ref, *refs):
    earlier, (gated_ref, top_ref, bottom_ref) = refs[:-3], refs[-3:]
    total, width = y_ref.shape
    head_size = width // heads
    entry = jnp.zeros((state, width), F32)
    for summary in reversed(earlier):
        through = summary[state : state + EDGE, :].astype(F32)[:1]
        entry = through * entry + summary[:state, :].astype(F32)
    owner = [lax.broadcasted_iota(jnp.int32, (width, width), dim) // head_size for dim in (0, 1)]
    average = jnp.where(owner[0] == owner[1], 1.0 / head_size, 0.0).astype(BF16)
    for block in range(total // SPAN):
        rows = slice(block * SPAN, (block + 1) * SPAN)
        y = y_ref[rows, :] + carry_ref[rows, :] * dot(c_ref[rows, :], entry.astype(BF16))
        square_mean = dot((y * y).astype(BF16), average)
        gated_ref[rows, :] = (y * lax.rsqrt(square_mean + 1e-05) * silu_ref[rows, :]).astype(BF16)
        entry = keep_ref[block * 8 : block * 8 + 1, :] * entry + step_ref[block * state : (block + 1) * state, :]
    top_ref[...] = gated_ref[:EDGE, :]
    bottom_ref[...] = gated_ref[total - EDGE :, :]


def conv_kernel(group, edges, len_ref, taps_ref, gated_ref, *refs):
    if edges:
        before_ref, after_ref, inner_ref, act_ref, ext_ref, ends_ref = refs
    else:
        act_ref, ext_ref, ends_ref = refs
    place, plane = plane_place(group)
    total, width = gated_ref.shape
    count = total // SPAN
    taps = taps_ref.shape[0]
    half = (taps - 1) // 2
    base = plane * total
    stream = lax.axis_size("tm") // group * total
    records = len_ref.shape[0]
    reach = SPAN + 2 * EDGE
    first_tap = EDGE - half
    if edges:
        act_ref[SPAN : total - SPAN, :] = inner_ref[...]
        ext_ref[:EDGE, :] = before_ref[...].astype(F32)
        ext_ref[EDGE:reach, :] = gated_ref[: SPAN + EDGE, :].astype(F32)
        ext_ref[reach : 2 * reach - EDGE, :] = gated_ref[total - SPAN - EDGE :, :].astype(F32)
        ext_ref[2 * reach - EDGE :, :] = after_ref[...].astype(F32)
    else:
        ext_ref[...] = gated_ref[SPAN - EDGE : total - SPAN + EDGE, :].astype(F32)
    ends_ref[0] = 0
    for record in range(records):
        ends_ref[record + 1] = ends_ref[record] + len_ref[record]

    def record_at(position):
        found = jnp.int32(0)
        for record in range(records - 1):
            found = found + (ends_ref[record + 1] <= position).astype(jnp.int32)
        return found

    def one_block(at, source, target):
        low = record_at(jnp.maximum(base + at - half, 0))
        high = record_at(jnp.minimum(base + at + SPAN - 1 + half, stream - 1))
        near = lax.broadcasted_iota(jnp.int32, (reach, LANES), 0) + (base + at - EDGE)
        for tile in range(width // LANES):
            lanes = slice(tile * LANES, (tile + 1) * LANES)
            weights = taps_ref[:, pl.ds(pl.multiple_of(place * width + tile * LANES, LANES), LANES)]

            def one_record(record, done):
                inside = (near >= ends_ref[record]) & (near < ends_ref[record + 1])
                g = jnp.where(inside, ext_ref[pl.ds(source, reach), lanes], 0.0)
                out = None
                for phase in range(8):
                    part = None
                    for offset in range(phase, reach - SPAN, 8):
                        tap = offset - first_tap
                        if 0 <= tap < taps:
                            aligned = offset - phase
                            term = weights[tap : tap + 1, :] * g[aligned : aligned + SPAN + 8, :]
                            part = term if part is None else part + term
                    if part is not None:
                        moved = part[phase : phase + SPAN, :]
                        out = moved if out is None else out + moved
                return jnp.where(inside[EDGE : EDGE + SPAN], out, done)

            conv = lax.fori_loop(low, high + 1, one_record, jnp.zeros((SPAN, LANES), F32))
            act_ref[pl.ds(target, SPAN), lanes] = (conv / (1.0 + jnp.exp(-conv))).astype(BF16)
        return 0

    if edges:

        def edge(number, _):
            at = pl.multiple_of(number * (total - SPAN), SPAN)
            return one_block(at, pl.multiple_of(number * reach, reach), at)

        lax.fori_loop(0, 2, edge, 0)
    else:

        def inner(number, _):
            at = pl.multiple_of(number * SPAN, SPAN)
            return one_block(at + SPAN, at, at)

        lax.fori_loop(0, count - 2, inner, 0)


def out_kernel(group, cores, *refs):
    acts, weights, outs = refs[:cores], refs[cores : 2 * cores], refs[2 * cores :]
    place, _ = plane_place(group)
    frames = outs[0].shape[0]
    for step in reversed(range(group)):
        rows = pl.ds(pl.multiple_of((place ^ step) * frames, frames), frames)
        total = None
        for act, weight in zip(acts, weights):
            product = dot(act[rows, :], weight[...], ((1,), (1,)))
            total = product if total is None else total + product
        outs[step][...] = total.astype(outs[step].dtype)


def local(
    frames,
    x_weight,
    z_weight,
    bc_weight,
    log_decay,
    norm_gain,
    conv_weight,
    out_weight,
    record_lengths,
):
    times, cores = lax.axis_size("tm"), lax.axis_size("head")
    frame_count, depth = frames.shape
    heads_here, channels = log_decay.shape[0], x_weight.shape[1]
    state = bc_weight.shape[1] // 2
    group = 4
    while group > 1 and (channels // group % LANES or times % group or heads_here % group):
        group //= 2
    planes = times // group
    width, heads = channels // group, heads_here // group
    total = frame_count * group
    count = total // SPAN
    index, core = lax.axis_index("tm"), lax.axis_index("head")
    place = lax.rem(index, group)

    def in_plane(array, step):
        return lax.ppermute(array, "tm", [(i, i ^ step) for i in range(times)])

    def later(array, step):
        return lax.ppermute(array, "tm", [(i, i + step * group) for i in range(times - step * group)])

    def earlier(array, step):
        return lax.ppermute(array, "tm", [(i + step * group, i) for i in range(times - step * group)])

    def across(array, step):
        return lax.ppermute(array, "head", [(i, i ^ step) for i in range(cores)])

    def between_planes(array, step):
        return lax.ppermute(array, "tm", [(i, i ^ (step * group)) for i in range(times)])

    shape = jax.ShapeDtypeStruct
    rows = x_weight.shape[0]
    parity = lax.rem(core, 2)

    def along_planes(stack):
        if planes != 4:
            return [stack] + [between_planes(stack, step) for step in range(1, planes)], tuple(range(planes))

        def pairs(chosen):
            return [(a * group + q, b * group + q) for a, b in chosen for q in range(group)]

        second = between_planes(stack, 2)
        first = between_planes(stack, 1)
        again, stack_then = lax.optimization_barrier((second, stack))
        third = lax.ppermute(again, "tm", pairs([(1, 0), (2, 3)]))
        middle = lax.ppermute(stack_then, "tm", pairs([(1, 2), (2, 1)]))
        return [stack, first, second, third, middle], (0, 1, 2, 3, 3)

    bc_half = lax.dynamic_slice_in_dim(bc_weight, parity * LANES, LANES, 1)
    bc_pieces = [bc_half] + [between_planes(bc_half, step) for step in range(1, planes)]
    packed = call(
        functools.partial(pack_kernel, group),
        tuple(shape((rows, 3 * width), BF16) for _ in range(group)),
        [x_weight, z_weight, out_weight.T],
        smem=0,
    )
    parts = [packed[0]] + [in_plane(packed[step], step) for step in range(1, group)]
    xz_stack, out_stack = call(
        functools.partial(stack_kernel, group),
        (shape((group * rows, 2 * width), BF16), shape((group * rows, width), BF16)),
        parts,
        smem=0,
    )
    xz_pieces, offsets = along_planes(xz_stack)
    decay_blocks = jnp.pad(log_decay.reshape(group, heads, frame_count), ((0, 0), (0, 8 - heads), (0, 0)))
    bc_parts = call(
        functools.partial(share_bc_kernel, group),
        tuple(shape((planes * rows + frame_count // SPAN * 32, LANES), BF16) for _ in range(group)),
        [decay_blocks, *bc_pieces],
        smem=0,
    )
    bc_parts = [bc_parts[0]] + [in_plane(bc_parts[step], step) for step in range(1, group)]
    half_count = frame_count // 2
    frame_half = lax.dynamic_slice_in_dim(frames, parity * half_count, half_count, 0)
    frame_half, out_stack, bc_parts = lax.optimization_barrier((frame_half, out_stack, bc_parts))
    half_parts = [in_plane(frame_half, step) for step in range(1, group)]
    height = depth * LANES // depth
    swap, bc_mine, decay = call(
        functools.partial(swap_kernel, group, rows),
        (
            shape(((group - 1) * half_count + height, depth), BF16),
            shape((depth, LANES), BF16),
            shape((count * 8, SPAN), F32),
        ),
        [*bc_parts, *half_parts],
        smem=0,
    )
    swap = across(swap, 1)

    used = count * 8
    frame_rows, z_columns, x_rows, b_rows, c_rows, decays, cumul, steps, carry, keep, summary = call(
        functools.partial(state_kernel, group, heads, state, offsets),
        (
            shape((total, depth), BF16),
            shape((depth, width), BF16),
            shape((total, width), BF16),
            shape((total, state), BF16),
            shape((total, state), BF16),
            shape((SPAN, -(-4 * used // SPAN) * SPAN), F32),
            shape((used, SPAN), F32),
            shape((count * state, width), F32),
            shape((total, width), F32),
            shape((count * 8, width), F32),
            shape((state + EDGE, width), BF16),
        ),
        [record_lengths, decay, bc_mine, frames, swap, *half_parts, *xz_pieces],
        [pltpu.VMEM((depth, width + 2 * state), BF16)],
        flops=2 * total * depth * (width + 2 * state),
    )
    summaries = [later(summary, step) for step in range(1, planes)]
    y = call(
        functools.partial(inner_kernel, group, heads),
        shape((total, width), F32),
        [x_rows, b_rows, c_rows, decays, cumul],
        flops=4 * total * SPAN * width,
        smem=0,
    )
    out_stack, y = lax.optimization_barrier((out_stack, y))
    out_pieces = [out_stack] + [between_planes(out_stack, step) for step in range(1, planes)]
    silu = call(
        functools.partial(silu_kernel, group),
        shape((total, width), F32),
        [norm_gain[None], frame_rows, z_columns],
        flops=2 * total * depth * width,
        smem=0,
    )
    gated, top, bottom = call(
        functools.partial(gate_kernel, heads, state),
        (shape((total, width), BF16), shape((EDGE, width), BF16), shape((EDGE, width), BF16)),
        [c_rows, y, steps, carry, keep, silu, *summaries],
        flops=2 * total * state * width,
        smem=0,
    )
    before, after = later(bottom, 1), earlier(top, 1)
    ends = pltpu.SMEM((record_lengths.shape[0] + 1,), jnp.int32)
    inner = call(
        functools.partial(conv_kernel, group, False),
        shape((total - 2 * SPAN, width), BF16),
        [record_lengths, conv_weight, gated],
        [pltpu.VMEM((total - 2 * SPAN + 2 * EDGE, width), F32), ends],
        flops=2 * total * width * conv_weight.shape[0],
    )
    act = call(
        functools.partial(conv_kernel, group, True),
        shape((total, width), BF16),
        [record_lengths, conv_weight, gated, before, after, inner],
        [pltpu.VMEM((2 * SPAN + 4 * EDGE, width), F32), ends],
        flops=4 * SPAN * width * conv_weight.shape[0],
    )
    share = depth // cores
    out_parts = call(
        functools.partial(share_kernel, cores, tuple(range(planes)), group),
        tuple(shape((share, width), BF16) for _ in range(cores)),
        out_pieces,
        [pltpu.VMEM((depth, width), BF16)],
        smem=0,
    )
    out_parts = [out_parts[0]] + [across(out_parts[step], step) for step in range(1, cores)]
    acts = [act] + [across(act, step) for step in range(1, cores)]
    outs = call(
        functools.partial(out_kernel, group, cores),
        tuple(shape((frame_count, share), BF16 if step else F32) for step in range(group)),
        [*acts, *out_parts],
        flops=2 * total * width * cores * share,
        smem=0,
    )
    mixed = outs[0]
    for step in range(1, group):
        mixed = mixed + in_plane(outs[step], step).astype(F32)
    return mixed.astype(BF16)


def solution(mesh):
    in_specs = (
        P("tm", None),
        P("tm", "head"),
        P("tm", "head"),
        P("tm", None),
        P("head", "tm"),
        P("head"),
        P(None, "head"),
        P("head", "tm"),
        P(),
    )
    out_specs = P("tm", "head")
    return jax.shard_map(local, mesh=mesh, in_specs=in_specs, out_specs=out_specs, check_vma=False)
```

```python
import functools

import jax
import jax.numpy as jnp
from jax import lax
from jax.experimental import pallas as pl
from jax.experimental.pallas import tpu as pltpu
from jax.sharding import PartitionSpec as P

SPAN = 128
LANES = 128
EDGE = 16
BF16 = jnp.bfloat16
F32 = jnp.float32
VMEM_BYTES = 48 * 1024 * 1024


def dot(a, b, dims=((1,), (0,)), precision=None):
    return lax.dot_general(a, b, (dims, ((), ())), precision=precision, preferred_element_type=F32)


def call(kernel, out_shape, operands, scratch=(), flops=0, smem=1):
    in_specs = [pl.BlockSpec(memory_space=pltpu.SMEM)] * smem
    in_specs += [pl.BlockSpec(memory_space=pltpu.VMEM)] * (len(operands) - smem)
    moved = sum(a.size * a.dtype.itemsize for a in operands)
    moved += sum(a.size * a.dtype.itemsize for a in jax.tree.leaves(out_shape))
    return pl.pallas_call(
        kernel,
        out_shape=out_shape,
        in_specs=in_specs,
        out_specs=jax.tree.map(lambda _: pl.BlockSpec(memory_space=pltpu.VMEM), out_shape),
        scratch_shapes=list(scratch),
        compiler_params=pltpu.CompilerParams(vmem_limit_bytes=VMEM_BYTES),
        cost_estimate=pl.CostEstimate(flops=flops, bytes_accessed=moved, transcendentals=0),
    )(*operands)


def plane_place(group):
    index = lax.axis_index("tm")
    return lax.rem(index, group), lax.div(index, group)


def record_starts(len_ref, position):
    start = jnp.zeros_like(position)
    end = jnp.int32(0)
    for record in range(len_ref.shape[0] - 1):
        end = end + len_ref[record]
        start = jnp.where(position >= end, end, start)
    return start


def fill_planes(plane, dest_ref, pieces, offsets, lanes=slice(None)):
    rows = pieces[0].shape[0]
    for offset in sorted(set(offsets)):
        same = [piece[:, lanes] for piece, at in zip(pieces, offsets) if at == offset]
        value = same[0] if len(same) == 1 else same[0] + same[1]
        dest_ref[pl.ds(pl.multiple_of((plane ^ offset) * rows, rows), rows), : value.shape[1]] = value


def pack_kernel(group, *refs):
    weight_refs, out_refs = refs[:-group], refs[-group:]
    width = weight_refs[0].shape[1] // group
    place, _ = plane_place(group)
    for step, out_ref in enumerate(out_refs):
        lanes = pl.ds(pl.multiple_of((place ^ step) * width, LANES), width)
        for number, weight_ref in enumerate(weight_refs):
            out_ref[:, number * width : (number + 1) * width] = weight_ref[:, lanes]


def pack_all_kernel(group, *refs):
    weight_refs, out_ref = refs[:-1], refs[-1]
    width = weight_refs[0].shape[1] // group
    for target in range(out_ref.shape[0]):
        block = target % group
        for number, weight_ref in enumerate(weight_refs):
            columns = weight_ref[:, block * width : (block + 1) * width]
            out_ref[target, :, number * width : (number + 1) * width] = columns


def stack_kernel(group, *refs):
    parts, stack_refs = refs[:group], refs[group:]
    place, _ = plane_place(group)
    rows = parts[0].shape[0]
    for step, part in enumerate(parts):
        at = pl.ds(pl.multiple_of((place ^ step) * rows, rows), rows)
        first = 0
        for stack_ref in stack_refs:
            width = stack_ref.shape[1]
            stack_ref[at, :] = part[:, first : first + width]
            first += width


def share_bc_kernel(group, decay_ref, *refs):
    bc_refs, out_refs = refs[:-group], refs[-group:]
    place, _ = plane_place(group)
    rows = bc_refs[0].shape[0]
    below = len(bc_refs) * rows
    for step, out_ref in enumerate(out_refs):
        for number, bc_ref in enumerate(bc_refs):
            out_ref[number * rows : (number + 1) * rows, :] = bc_ref[...]
        left = decay_ref[place ^ step]
        terms = []
        for _ in range(3):
            term = left.astype(BF16).astype(F32)
            terms.append(term)
            left = left - term
        terms.append(jnp.zeros_like(left))
        terms = jnp.concatenate(terms, axis=0).astype(BF16)
        for span in range(terms.shape[1] // SPAN):
            rows_here = slice(below + span * 32, below + (span + 1) * 32)
            out_ref[rows_here, :] = terms[:, span * SPAN : (span + 1) * SPAN]


def swap_kernel(group, rows, *refs):
    part_refs, half_refs = refs[:group], refs[group : 2 * group - 1]
    swap_ref, bc_ref, decay_ref = refs[2 * group - 1 :]
    place, plane = plane_place(group)
    planes = bc_ref.shape[0] // (group * rows)
    below = planes * rows
    spans = (part_refs[0].shape[0] - below) // 32
    for step, part_ref in enumerate(part_refs):
        block = place ^ step
        for offset in range(planes):
            at = pl.multiple_of(((plane ^ offset) * group + block) * rows, rows)
            bc_ref[pl.ds(at, rows), :] = part_ref[offset * rows : (offset + 1) * rows, :]
        for span in range(spans):
            terms = part_ref[below + span * 32 : below + (span + 1) * 32, :].astype(F32)
            at = pl.multiple_of((block * spans + span) * 8, 8)
            decay_ref[pl.ds(at, 8), :] = terms[:8] + terms[8:16] + terms[16:24]
    half = half_refs[0].shape[0]
    for number, half_ref in enumerate(half_refs):
        swap_ref[number * half : (number + 1) * half, :] = half_ref[...]
    top = len(half_refs) * half
    height = swap_ref.shape[0] - top
    for number in range(bc_ref.shape[0] // height):
        lanes = slice(number * LANES, (number + 1) * LANES)
        swap_ref[top:, lanes] = bc_ref[number * height : (number + 1) * height, :]


def lanes_of(rows, width, head_size):
    high = rows.astype(BF16)
    low = (rows - high.astype(F32)).astype(BF16)
    owner = lax.broadcasted_iota(jnp.int32, (16, width), 1) // head_size
    chosen = jnp.where((lax.broadcasted_iota(jnp.int32, (16, width), 0) & 7) == owner, 1.0, 0.0).astype(BF16)
    both = jnp.concatenate([high.astype(F32), low.astype(F32)], axis=0).astype(BF16)
    return dot(both, chosen, ((0,), (0,)))


def state_kernel(group, heads, state, len_ref, decay_ref, xz_ref, bc_half_ref, own_ref, swap_ref, *refs):
    half_refs, refs = refs[: group - 1], refs[group - 1 :]
    frames_ref, x_ref, b_ref, c_ref, rows_ref, step_ref, keep_ref, send_ref, weight_ref = refs
    place, plane = plane_place(group)
    parity = lax.rem(lax.axis_index("head"), 2)
    total, width = x_ref.shape
    frames = total // group
    half = frames // 2
    head_size = width // heads
    count = total // SPAN
    base = plane * total
    frames_ref[pl.ds(pl.multiple_of(place * frames, frames), frames), :] = own_ref[...]
    for number, half_ref in enumerate(half_refs):
        block = (place ^ (number + 1)) * frames
        mine = pl.ds(pl.multiple_of(block + parity * half, half), half)
        other = pl.ds(pl.multiple_of(block + (1 - parity) * half, half), half)
        frames_ref[mine, :] = half_ref[...]
        frames_ref[other, :] = swap_ref[number * half : (number + 1) * half, :]
    mine = pl.ds(pl.multiple_of(parity * LANES, LANES), LANES)
    other = pl.ds(pl.multiple_of((1 - parity) * LANES, LANES), LANES)
    weight_ref[:, mine] = bc_half_ref[...]
    top = len(half_refs) * half
    height = swap_ref.shape[0] - top
    for number in range(weight_ref.shape[0] // height):
        lanes = slice(number * LANES, (number + 1) * LANES)
        weight_ref[number * height : (number + 1) * height, other] = swap_ref[top:, lanes]

    decay = decay_ref[...]
    used = decay.shape[0]
    square = (SPAN, SPAN)
    row, lane = (lax.broadcasted_iota(jnp.int32, square, dim) for dim in (0, 1))
    upper = jnp.where(row <= lane, 1.0, 0.0).astype(F32)
    cumul = dot(decay, upper, precision=lax.Precision.HIGHEST)
    whole = dot(decay, jnp.ones(square, F32), precision=lax.Precision.HIGHEST)
    first = base + lax.broadcasted_iota(jnp.int32, (used, SPAN), 0) // 8 * SPAN
    position = first + lane[:1]
    start = record_starts(len_ref, position)
    start_last = record_starts(len_ref, first + (SPAN - 1))
    carried = jnp.where(start < first, jnp.exp(cumul), 0.0)
    tail = jnp.where(position >= start_last, jnp.exp(whole - cumul), 0.0)
    keep = jnp.where(start_last < first, jnp.exp(whole), 0.0)
    rows_ref[:used, :] = cumul
    rows_ref[used : 2 * used, :] = start.astype(F32)
    rows_ref[2 * used :, :] = carried

    for block in range(group):
        rows = slice(block * frames, (block + 1) * frames)
        x_ref[rows, :] = dot(frames_ref[rows, :], xz_ref[:, :width]).astype(BF16)
        product = dot(frames_ref[rows, :], weight_ref[...])
        b_ref[rows, :] = product[:, :state].astype(BF16)
        c_ref[rows, :] = product[:, state:].astype(BF16)

    entry = jnp.zeros((state, width), F32)
    through = jnp.ones((8, width), F32)
    for block in range(count):
        rows = slice(block * SPAN, (block + 1) * SPAN)
        at = slice(block * 8, (block + 1) * 8)
        kept = lanes_of(keep[at], width, head_size)
        weighed = x_ref[rows, :].astype(F32) * lanes_of(tail[at], width, head_size)
        step = dot(b_ref[rows, :], weighed.astype(BF16), ((0,), (0,)))
        step_ref[block * state : (block + 1) * state, :] = step
        keep_ref[at, :] = kept[:8]
        entry = kept[:1] * entry + step
        through = through * kept[:8]
    send_ref[:state, :] = entry.astype(BF16)
    send_ref[state:, :] = jnp.concatenate([through, through], axis=0).astype(BF16)


def inner_kernel(group, heads, x_ref, b_ref, c_ref, rows_ref, y_ref):
    _, plane = plane_place(group)
    total, width = x_ref.shape
    head_size = width // heads
    count = total // SPAN
    base = plane * total
    used = rows_ref.shape[0] // 3
    square = (SPAN, SPAN)
    parts = [rows_ref[: 2 * used, :]]
    if 2 * used % SPAN:
        parts.append(jnp.zeros((SPAN - 2 * used % SPAN, SPAN), F32))
    columns = jnp.concatenate(parts, axis=0).T
    row, lane = (lax.broadcasted_iota(jnp.int32, square, dim) for dim in (0, 1))
    lower = row >= lane
    tile_heads = LANES // head_size
    tile_lane = lax.broadcasted_iota(jnp.int32, (1, LANES), 1) // head_size
    masks = [jnp.where(tile_lane == inner, 1.0, 0.0).astype(BF16) for inner in range(tile_heads)]
    for block in range(count):
        rows = slice(block * SPAN, (block + 1) * SPAN)
        at = block * 8
        x = x_ref[rows, :]
        scores = dot(c_ref[rows, :], b_ref[rows, :], ((1,), (1,)))
        here = (base + block * SPAN + lane).astype(F32)
        start_here = jnp.broadcast_to(columns[:, used + at : used + at + 1], square)
        joined = lower & (here >= start_here)
        for tile in range(width // LANES):
            mixes, values = [], []
            for inner in range(tile_heads):
                which = at + tile * tile_heads + inner
                column = jnp.broadcast_to(columns[:, which : which + 1], square)
                gap = jnp.where(joined, column - rows_ref[which : which + 1, :], -1e30)
                mixes.append((jnp.exp(gap) * scores).astype(BF16))
                values.append(x[:, tile * LANES : (tile + 1) * LANES] * masks[inner])
            y_ref[rows, tile * LANES : (tile + 1) * LANES] = dot(
                jnp.concatenate(mixes, axis=1), jnp.concatenate(values, axis=0)
            )


def silu_kernel(group, gain_ref, frames_ref, xz_ref, out_ref):
    place, _ = plane_place(group)
    total, width = out_ref.shape
    gain = gain_ref[:, pl.ds(pl.multiple_of(place * width, LANES), width)]
    for block in range(group):
        rows = slice(block * (total // group), (block + 1) * (total // group))
        z = dot(frames_ref[rows, :], xz_ref[:, width:]).astype(BF16).astype(F32)
        out_ref[rows, :] = z / (1.0 + jnp.exp(-z)) * gain


def share_kernel(cores, offsets, group, *refs):
    pieces, refs = refs[: len(offsets)], refs[len(offsets) :]
    outs, weight_ref = refs[:cores], refs[cores]
    _, plane = plane_place(group)
    core = lax.axis_index("head")
    fill_planes(plane, weight_ref, pieces, offsets)
    for step, out_ref in enumerate(outs):
        rows = out_ref.shape[0]
        out_ref[...] = weight_ref[pl.ds(pl.multiple_of((core ^ step) * rows, rows), rows), :]


def gate_kernel(heads, state, c_ref, y_ref, step_ref, rows_ref, keep_ref, silu_ref, *refs):
    earlier, (gated_ref, top_ref, bottom_ref) = refs[:-3], refs[-3:]
    total, width = y_ref.shape
    head_size = width // heads
    used = rows_ref.shape[0] // 3
    entry = jnp.zeros((state, width), F32)
    for summary in reversed(earlier):
        through = summary[state : state + EDGE, :].astype(F32)[:1]
        entry = through * entry + summary[:state, :].astype(F32)
    owner = [lax.broadcasted_iota(jnp.int32, (width, width), dim) // head_size for dim in (0, 1)]
    average = jnp.where(owner[0] == owner[1], 1.0 / head_size, 0.0).astype(BF16)
    for block in range(total // SPAN):
        rows = slice(block * SPAN, (block + 1) * SPAN)
        carried = lanes_of(rows_ref[2 * used + block * 8 : 2 * used + (block + 1) * 8, :], width, head_size)
        y = y_ref[rows, :] + carried * dot(c_ref[rows, :], entry.astype(BF16))
        square_mean = dot((y * y).astype(BF16), average)
        gated_ref[rows, :] = (y * lax.rsqrt(square_mean + 1e-05) * silu_ref[rows, :]).astype(BF16)
        entry = keep_ref[block * 8 : block * 8 + 1, :] * entry + step_ref[block * state : (block + 1) * state, :]
    top_ref[...] = gated_ref[:EDGE, :]
    bottom_ref[...] = gated_ref[total - EDGE :, :]


def conv_kernel(group, edges, len_ref, taps_ref, gated_ref, *refs):
    if edges:
        before_ref, after_ref, inner_ref, act_ref, ext_ref, ends_ref = refs
    else:
        act_ref, ext_ref, ends_ref = refs
    place, plane = plane_place(group)
    total, width = gated_ref.shape
    count = total // SPAN
    taps = taps_ref.shape[0]
    half = (taps - 1) // 2
    base = plane * total
    stream = lax.axis_size("tm") // group * total
    records = len_ref.shape[0]
    reach = SPAN + 2 * EDGE
    first_tap = EDGE - half
    if edges:
        act_ref[SPAN : total - SPAN, :] = inner_ref[...]
        ext_ref[:EDGE, :] = before_ref[...].astype(F32)
        ext_ref[EDGE:reach, :] = gated_ref[: SPAN + EDGE, :].astype(F32)
        ext_ref[reach : 2 * reach - EDGE, :] = gated_ref[total - SPAN - EDGE :, :].astype(F32)
        ext_ref[2 * reach - EDGE :, :] = after_ref[...].astype(F32)
    else:
        ext_ref[...] = gated_ref[SPAN - EDGE : total - SPAN + EDGE, :].astype(F32)
    ends_ref[0] = 0
    for record in range(records):
        ends_ref[record + 1] = ends_ref[record] + len_ref[record]

    def record_at(position):
        found = jnp.int32(0)
        for record in range(records - 1):
            found = found + (ends_ref[record + 1] <= position).astype(jnp.int32)
        return found

    def one_block(at, source, target):
        low = record_at(jnp.maximum(base + at - half, 0))
        high = record_at(jnp.minimum(base + at + SPAN - 1 + half, stream - 1))
        near = lax.broadcasted_iota(jnp.int32, (reach, LANES), 0) + (base + at - EDGE)
        for tile in range(width // LANES):
            lanes = slice(tile * LANES, (tile + 1) * LANES)
            weights = taps_ref[:, pl.ds(pl.multiple_of(place * width + tile * LANES, LANES), LANES)]

            def one_record(record, done):
                inside = (near >= ends_ref[record]) & (near < ends_ref[record + 1])
                g = jnp.where(inside, ext_ref[pl.ds(source, reach), lanes], 0.0)
                out = None
                for phase in range(8):
                    part = None
                    for offset in range(phase, reach - SPAN, 8):
                        tap = offset - first_tap
                        if 0 <= tap < taps:
                            aligned = offset - phase
                            term = weights[tap : tap + 1, :] * g[aligned : aligned + SPAN + 8, :]
                            part = term if part is None else part + term
                    if part is not None:
                        moved = part[phase : phase + SPAN, :]
                        out = moved if out is None else out + moved
                return jnp.where(inside[EDGE : EDGE + SPAN], out, done)

            conv = lax.fori_loop(low, high + 1, one_record, jnp.zeros((SPAN, LANES), F32))
            act_ref[pl.ds(target, SPAN), lanes] = (conv / (1.0 + jnp.exp(-conv))).astype(BF16)
        return 0

    if edges:

        def edge(number, _):
            at = pl.multiple_of(number * (total - SPAN), SPAN)
            return one_block(at, pl.multiple_of(number * reach, reach), at)

        lax.fori_loop(0, 2, edge, 0)
    else:

        def inner(number, _):
            at = pl.multiple_of(number * SPAN, SPAN)
            return one_block(at + SPAN, at, at)

        lax.fori_loop(0, count - 2, inner, 0)


def out_kernel(group, cores, *refs):
    acts, weights, outs = refs[:cores], refs[cores : 2 * cores], refs[2 * cores :]
    place, _ = plane_place(group)
    frames = outs[0].shape[0]
    for step in reversed(range(group)):
        rows = pl.ds(pl.multiple_of((place ^ step) * frames, frames), frames)
        total = None
        for act, weight in zip(acts, weights):
            product = dot(act[rows, :], weight[...], ((1,), (1,)))
            total = product if total is None else total + product
        outs[step][...] = total.astype(outs[step].dtype)


def local(
    frames,
    x_weight,
    z_weight,
    bc_weight,
    log_decay,
    norm_gain,
    conv_weight,
    out_weight,
    record_lengths,
):
    times, cores = lax.axis_size("tm"), lax.axis_size("head")
    frame_count, depth = frames.shape
    heads_here, channels = log_decay.shape[0], x_weight.shape[1]
    state = bc_weight.shape[1] // 2
    group = 4
    while group > 1 and (channels // group % LANES or times % group or heads_here % group):
        group //= 2
    planes = times // group
    width, heads = channels // group, heads_here // group
    total = frame_count * group
    count = total // SPAN
    index, core = lax.axis_index("tm"), lax.axis_index("head")
    place = lax.rem(index, group)

    def in_plane(array, step):
        return lax.ppermute(array, "tm", [(i, i ^ step) for i in range(times)])

    def later(array, step):
        return lax.ppermute(array, "tm", [(i, i + step * group) for i in range(times - step * group)])

    def earlier(array, step):
        return lax.ppermute(array, "tm", [(i + step * group, i) for i in range(times - step * group)])

    def across(array, step):
        return lax.ppermute(array, "head", [(i, i ^ step) for i in range(cores)])

    def between_planes(array, step):
        return lax.ppermute(array, "tm", [(i, i ^ (step * group)) for i in range(times)])

    shape = jax.ShapeDtypeStruct
    rows = x_weight.shape[0]
    parity = lax.rem(core, 2)

    bc_half = lax.dynamic_slice_in_dim(bc_weight, parity * LANES, LANES, 1)
    bc_pieces = [bc_half] + [between_planes(bc_half, step) for step in range(1, planes)]
    bc_pieces, x_weight, z_weight = lax.optimization_barrier((bc_pieces, x_weight, z_weight))
    blocks = call(
        functools.partial(pack_all_kernel, group),
        shape((times, rows, 2 * width), BF16),
        [x_weight, z_weight],
        smem=0,
    )
    xz = lax.all_to_all(blocks, "tm", split_axis=0, concat_axis=0, tiled=True).reshape(depth, 2 * width)
    decay_blocks = jnp.pad(log_decay.reshape(group, heads, frame_count), ((0, 0), (0, 8 - heads), (0, 0)))
    bc_parts = call(
        functools.partial(share_bc_kernel, group),
        tuple(shape((planes * rows + frame_count // SPAN * 32, LANES), BF16) for _ in range(group)),
        [decay_blocks, *bc_pieces],
        smem=0,
    )
    bc_parts = [bc_parts[0]] + [in_plane(bc_parts[step], step) for step in range(1, group)]
    half_count = frame_count // 2
    frame_half = lax.dynamic_slice_in_dim(frames, parity * half_count, half_count, 0)
    half_parts = [in_plane(frame_half, step) for step in range(1, group)]
    swap, bc_mine, decay = call(
        functools.partial(swap_kernel, group, rows),
        (
            shape(((group - 1) * half_count + LANES, depth), BF16),
            shape((depth, LANES), BF16),
            shape((count * 8, SPAN), F32),
        ),
        [*bc_parts, *half_parts],
        smem=0,
    )
    out_columns, half_parts = lax.optimization_barrier((out_weight.T, half_parts))
    packed = call(
        functools.partial(pack_kernel, group),
        tuple(shape((rows, width), BF16) for _ in range(group)),
        [out_columns],
        smem=0,
    )
    parts = [packed[0]] + [in_plane(packed[step], step) for step in range(1, group)]
    swap, parts = lax.optimization_barrier((swap, parts))
    swap = across(swap, 1)
    out_stack = call(
        functools.partial(stack_kernel, group),
        shape((group * rows, width), BF16),
        parts,
        smem=0,
    )

    frame_rows, x_rows, b_rows, c_rows, decay_rows, steps, keep, summary = call(
        functools.partial(state_kernel, group, heads, state),
        (
            shape((total, depth), BF16),
            shape((total, width), BF16),
            shape((total, state), BF16),
            shape((total, state), BF16),
            shape((3 * count * 8, SPAN), F32),
            shape((count * state, width), F32),
            shape((count * 8, width), F32),
            shape((state + EDGE, width), BF16),
        ),
        [record_lengths, decay, xz, bc_mine, frames, swap, *half_parts],
        [pltpu.VMEM((depth, 2 * state), BF16)],
        flops=2 * total * depth * (width + 2 * state),
    )
    summaries = [later(summary, step) for step in range(1, planes)]
    y = call(
        functools.partial(inner_kernel, group, heads),
        shape((total, width), F32),
        [x_rows, b_rows, c_rows, decay_rows],
        flops=4 * total * SPAN * width,
        smem=0,
    )
    silu = call(
        functools.partial(silu_kernel, group),
        shape((total, width), F32),
        [norm_gain[None], frame_rows, xz],
        flops=2 * total * depth * width,
        smem=0,
    )
    out_stack, summaries, y = lax.optimization_barrier((out_stack, summaries, y))
    out_pieces = [out_stack] + [between_planes(out_stack, step) for step in range(1, planes)]
    gated, top, bottom = call(
        functools.partial(gate_kernel, heads, state),
        (shape((total, width), BF16), shape((EDGE, width), BF16), shape((EDGE, width), BF16)),
        [c_rows, y, steps, decay_rows, keep, silu, *summaries],
        flops=2 * total * state * width,
        smem=0,
    )
    before, after = later(bottom, 1), earlier(top, 1)
    gated, out_pieces[1] = lax.optimization_barrier((gated, out_pieces[1]))
    ends = pltpu.SMEM((record_lengths.shape[0] + 1,), jnp.int32)
    inner = call(
        functools.partial(conv_kernel, group, False),
        shape((total - 2 * SPAN, width), BF16),
        [record_lengths, conv_weight, gated],
        [pltpu.VMEM((total - 2 * SPAN + 2 * EDGE, width), F32), ends],
        flops=2 * total * width * conv_weight.shape[0],
    )
    inner, out_pieces[2:] = lax.optimization_barrier((inner, out_pieces[2:]))
    act = call(
        functools.partial(conv_kernel, group, True),
        shape((total, width), BF16),
        [record_lengths, conv_weight, gated, before, after, inner],
        [pltpu.VMEM((2 * SPAN + 4 * EDGE, width), F32), ends],
        flops=4 * SPAN * width * conv_weight.shape[0],
    )
    share = depth // cores
    out_parts = call(
        functools.partial(share_kernel, cores, tuple(range(planes)), group),
        tuple(shape((share, width), BF16) for _ in range(cores)),
        out_pieces,
        [pltpu.VMEM((depth, width), BF16)],
        smem=0,
    )
    out_parts = [out_parts[0]] + [across(out_parts[step], step) for step in range(1, cores)]
    acts = [act] + [across(act, step) for step in range(1, cores)]
    outs = call(
        functools.partial(out_kernel, group, cores),
        tuple(shape((frame_count, share), BF16 if step else F32) for step in range(group)),
        [*acts, *out_parts],
        flops=2 * total * width * cores * share,
        smem=0,
    )
    mixed = outs[0]
    for step in range(1, group):
        mixed = mixed + in_plane(outs[step], step).astype(F32)
    return mixed.astype(BF16)


def solution(mesh):
    in_specs = (
        P("tm", None),
        P("tm", "head"),
        P("tm", "head"),
        P("tm", None),
        P("head", "tm"),
        P("head"),
        P(None, "head"),
        P("head", "tm"),
        P(),
    )
    out_specs = P("tm", "head")
    return jax.shard_map(local, mesh=mesh, in_specs=in_specs, out_specs=out_specs, check_vma=False)
```

```python
import functools

import jax
import jax.numpy as jnp
from jax import lax
from jax.experimental import pallas as pl
from jax.experimental.pallas import tpu as pltpu
from jax.sharding import PartitionSpec as P

SPAN = 128
LANES = 128
EDGE = 16
BF16 = jnp.bfloat16
F32 = jnp.float32
STACK_HINT = 40_000_000_000
ASSEMBLE_HINT = 40_000_000_000
ALL_VMEM_BYTES = 63 * 1024 * 1024
VMEM_BYTES = 48 * 1024 * 1024


def dot(a, b, dims=((1,), (0,)), precision=None):
    return lax.dot_general(a, b, (dims, ((), ())), precision=precision, preferred_element_type=F32)


def call(kernel, out_shape, operands, scratch=(), flops=0, smem=1, anywhere=0, vmem=VMEM_BYTES):
    in_specs = [pl.BlockSpec(memory_space=pltpu.SMEM)] * smem
    in_specs += [pl.BlockSpec(memory_space=pltpu.VMEM)] * (len(operands) - smem - anywhere)
    in_specs += [pl.BlockSpec(memory_space=pl.ANY)] * anywhere
    moved = sum(a.size * a.dtype.itemsize for a in operands)
    moved += sum(a.size * a.dtype.itemsize for a in jax.tree.leaves(out_shape))
    return pl.pallas_call(
        kernel,
        out_shape=out_shape,
        in_specs=in_specs,
        out_specs=jax.tree.map(lambda _: pl.BlockSpec(memory_space=pltpu.VMEM), out_shape),
        scratch_shapes=list(scratch),
        compiler_params=pltpu.CompilerParams(vmem_limit_bytes=vmem),
        cost_estimate=pl.CostEstimate(flops=flops, bytes_accessed=moved, transcendentals=0),
    )(*operands)


def plane_place(group):
    index = lax.axis_index("tm")
    return lax.rem(index, group), lax.div(index, group)


def record_starts(len_ref, position):
    start = jnp.zeros_like(position)
    end = jnp.int32(0)
    for record in range(len_ref.shape[0] - 1):
        end = end + len_ref[record]
        start = jnp.where(position >= end, end, start)
    return start


def fill_planes(plane, dest_ref, pieces, offsets, lanes=slice(None)):
    rows = pieces[0].shape[0]
    for offset in sorted(set(offsets)):
        same = [piece[:, lanes] for piece, at in zip(pieces, offsets) if at == offset]
        value = same[0] if len(same) == 1 else same[0] + same[1]
        dest_ref[pl.ds(pl.multiple_of((plane ^ offset) * rows, rows), rows), : value.shape[1]] = value


def cut_kernel(group, bc_ref, *refs):
    weight_refs, refs = refs[:3], refs[3:]
    bc_half_ref, out_refs, sems = refs[0], refs[1:-1], refs[-1]
    place, _ = plane_place(group)
    parity = lax.rem(lax.axis_index("head"), 2)
    width = weight_refs[0].shape[1] // group
    copies = [(bc_ref.at[:, pl.ds(pl.multiple_of(parity * LANES, LANES), LANES)], bc_half_ref)]
    for step, out_ref in enumerate(out_refs):
        lanes = pl.ds(pl.multiple_of((place ^ step) * width, LANES), width)
        for number, weight_ref in enumerate(weight_refs):
            copies.append((weight_ref.at[:, lanes], out_ref.at[:, number * width : (number + 1) * width]))
    started = [pltpu.make_async_copy(a, b, sems.at[number]) for number, (a, b) in enumerate(copies)]
    for copy in started:
        copy.start()
    for copy in started:
        copy.wait()


def stack_kernel(group, *refs):
    parts, stack_refs = refs[:group], refs[group:]
    place, _ = plane_place(group)
    rows = parts[0].shape[0]
    for step, part in enumerate(parts):
        at = pl.ds(pl.multiple_of((place ^ step) * rows, rows), rows)
        first = 0
        for stack_ref in stack_refs:
            width = stack_ref.shape[1]
            stack_ref[at, :] = part[:, first : first + width]
            first += width


def assemble_kernel(group, offsets, *refs):
    pieces, dest_refs = refs[: len(offsets)], refs[len(offsets) :]
    _, plane = plane_place(group)
    first = 0
    for dest_ref in dest_refs:
        width = dest_ref.shape[1]
        fill_planes(plane, dest_ref, pieces, offsets, slice(first, first + width))
        first += width


def tiles_below(half, number):
    return slice(half + number // 8 * 16, half + number // 8 * 16 + 16), slice(number % 8 * LANES, (number % 8 + 1) * LANES)


def payload_kernel(group, decay_ref, frames_ref, *refs):
    bc_refs, out_refs = refs[:-group], refs[-group:]
    place, _ = plane_place(group)
    half, rows = frames_ref.shape[0] // 2, bc_refs[0].shape[0]
    mine = pl.ds(pl.multiple_of(lax.rem(lax.axis_index("head"), 2) * half, half), half)
    for step, out_ref in enumerate(out_refs):
        out_ref[:half, :] = frames_ref[mine, :]
        tile = 0
        for bc_ref in bc_refs:
            for at in range(0, rows, 16):
                out_ref[tiles_below(half, tile)] = bc_ref[at : at + 16, :]
                tile += 1
        left = decay_ref[place ^ step]
        terms = []
        for _ in range(3):
            term = left.astype(BF16).astype(F32)
            terms.append(term)
            left = left - term
        terms.append(jnp.zeros_like(left))
        terms = jnp.concatenate(terms, axis=0).astype(BF16)
        for span in range(terms.shape[1] // SPAN):
            for at in (0, 16):
                out_ref[tiles_below(half, tile)] = terms[at : at + 16, span * SPAN : (span + 1) * SPAN]
                tile += 1


def swap_kernel(group, rows, half, *refs):
    part_refs, (swap_ref, bc_ref, decay_ref) = refs[:group], refs[group:]
    place, plane = plane_place(group)
    planes = bc_ref.shape[0] // (group * rows)
    spans = 2 * half // SPAN
    for step, part_ref in enumerate(part_refs):
        block = place ^ step
        tile = 0
        for offset in range(planes):
            first = ((plane ^ offset) * group + block) * rows
            for at in range(0, rows, 16):
                bc_ref[pl.ds(pl.multiple_of(first + at, 16), 16), :] = part_ref[tiles_below(half, tile)]
                tile += 1
        for span in range(spans):
            top = part_ref[tiles_below(half, tile)].astype(F32)
            bottom = part_ref[tiles_below(half, tile + 1)].astype(F32)
            tile += 2
            at = pl.multiple_of((block * spans + span) * 8, 8)
            decay_ref[pl.ds(at, 8), :] = top[:8] + top[8:] + bottom[:8]
        if step:
            swap_ref[(step - 1) * half : step * half, :] = part_ref[:half, :]
    top = (group - 1) * half
    height = swap_ref.shape[0] - top
    for number in range(bc_ref.shape[0] // height):
        lanes = slice(number * LANES, (number + 1) * LANES)
        swap_ref[top:, lanes] = bc_ref[number * height : (number + 1) * height, :]


def lanes_of(rows, width, head_size):
    high = rows.astype(BF16)
    low = (rows - high.astype(F32)).astype(BF16)
    owner = lax.broadcasted_iota(jnp.int32, (16, width), 1) // head_size
    chosen = jnp.where((lax.broadcasted_iota(jnp.int32, (16, width), 0) & 7) == owner, 1.0, 0.0).astype(BF16)
    both = jnp.concatenate([high.astype(F32), low.astype(F32)], axis=0).astype(BF16)
    return dot(both, chosen, ((0,), (0,)))


def state_kernel(group, heads, state, len_ref, decay_ref, x_weight_ref, bc_half_ref, own_ref, swap_ref, *refs):
    half_refs, refs = refs[: group - 1], refs[group - 1 :]
    frames_ref, x_ref, b_ref, c_ref, rows_ref, step_ref, keep_ref, send_ref, weight_ref = refs
    place, plane = plane_place(group)
    parity = lax.rem(lax.axis_index("head"), 2)
    total, width = x_ref.shape
    frames = total // group
    half = frames // 2
    head_size = width // heads
    count = total // SPAN
    base = plane * total
    frames_ref[pl.ds(pl.multiple_of(place * frames, frames), frames), :] = own_ref[...]
    for number, half_ref in enumerate(half_refs):
        block = (place ^ (number + 1)) * frames
        mine = pl.ds(pl.multiple_of(block + parity * half, half), half)
        other = pl.ds(pl.multiple_of(block + (1 - parity) * half, half), half)
        frames_ref[mine, :] = half_ref[:half, :]
        frames_ref[other, :] = swap_ref[number * half : (number + 1) * half, :]
    mine = pl.ds(pl.multiple_of(parity * LANES, LANES), LANES)
    other = pl.ds(pl.multiple_of((1 - parity) * LANES, LANES), LANES)
    weight_ref[:, mine] = bc_half_ref[...]
    top = len(half_refs) * half
    height = swap_ref.shape[0] - top
    for number in range(weight_ref.shape[0] // height):
        lanes = slice(number * LANES, (number + 1) * LANES)
        weight_ref[number * height : (number + 1) * height, other] = swap_ref[top:, lanes]

    decay = decay_ref[...]
    used = decay.shape[0]
    square = (SPAN, SPAN)
    row, lane = (lax.broadcasted_iota(jnp.int32, square, dim) for dim in (0, 1))
    upper = jnp.where(row <= lane, 1.0, 0.0).astype(F32)
    cumul = dot(decay, upper, precision=lax.Precision.HIGHEST)
    whole = dot(decay, jnp.ones(square, F32), precision=lax.Precision.HIGHEST)
    first = base + lax.broadcasted_iota(jnp.int32, (used, SPAN), 0) // 8 * SPAN
    position = first + lane[:1]
    start = record_starts(len_ref, position)
    start_last = record_starts(len_ref, first + (SPAN - 1))
    carried = jnp.where(start < first, jnp.exp(cumul), 0.0)
    tail = jnp.where(position >= start_last, jnp.exp(whole - cumul), 0.0)
    keep = jnp.where(start_last < first, jnp.exp(whole), 0.0)
    rows_ref[:used, :] = cumul
    rows_ref[used : 2 * used, :] = start.astype(F32)
    rows_ref[2 * used :, :] = carried

    for block in range(group):
        rows = slice(block * frames, (block + 1) * frames)
        x_ref[rows, :] = dot(frames_ref[rows, :], x_weight_ref[...]).astype(BF16)
        product = dot(frames_ref[rows, :], weight_ref[...])
        b_ref[rows, :] = product[:, :state].astype(BF16)
        c_ref[rows, :] = product[:, state:].astype(BF16)

    entry = jnp.zeros((state, width), F32)
    through = jnp.ones((8, width), F32)
    for block in range(count):
        rows = slice(block * SPAN, (block + 1) * SPAN)
        at = slice(block * 8, (block + 1) * 8)
        kept = lanes_of(keep[at], width, head_size)
        weighed = x_ref[rows, :].astype(F32) * lanes_of(tail[at], width, head_size)
        step = dot(b_ref[rows, :], weighed.astype(BF16), ((0,), (0,)))
        step_ref[block * state : (block + 1) * state, :] = step
        keep_ref[at, :] = kept[:8]
        entry = kept[:1] * entry + step
        through = through * kept[:8]
    send_ref[:state, :] = entry.astype(BF16)
    send_ref[state:, :] = jnp.concatenate([through, through], axis=0).astype(BF16)


def inner_kernel(group, heads, x_ref, b_ref, c_ref, rows_ref, y_ref):
    _, plane = plane_place(group)
    total, width = x_ref.shape
    head_size = width // heads
    count = total // SPAN
    base = plane * total
    used = rows_ref.shape[0] // 3
    square = (SPAN, SPAN)
    parts = [rows_ref[: 2 * used, :]]
    if 2 * used % SPAN:
        parts.append(jnp.zeros((SPAN - 2 * used % SPAN, SPAN), F32))
    columns = jnp.concatenate(parts, axis=0).T
    row, lane = (lax.broadcasted_iota(jnp.int32, square, dim) for dim in (0, 1))
    lower = row >= lane
    tile_heads = LANES // head_size
    tile_lane = lax.broadcasted_iota(jnp.int32, (1, LANES), 1) // head_size
    masks = [jnp.where(tile_lane == inner, 1.0, 0.0).astype(BF16) for inner in range(tile_heads)]
    for block in range(count):
        rows = slice(block * SPAN, (block + 1) * SPAN)
        at = block * 8
        x = x_ref[rows, :]
        scores = dot(c_ref[rows, :], b_ref[rows, :], ((1,), (1,)))
        here = (base + block * SPAN + lane).astype(F32)
        start_here = jnp.broadcast_to(columns[:, used + at : used + at + 1], square)
        joined = lower & (here >= start_here)
        for tile in range(width // LANES):
            mixes, values = [], []
            for inner in range(tile_heads):
                which = at + tile * tile_heads + inner
                column = jnp.broadcast_to(columns[:, which : which + 1], square)
                gap = jnp.where(joined, column - rows_ref[which : which + 1, :], -1e30)
                mixes.append((jnp.exp(gap) * scores).astype(BF16))
                values.append(x[:, tile * LANES : (tile + 1) * LANES] * masks[inner])
            y_ref[rows, tile * LANES : (tile + 1) * LANES] = dot(
                jnp.concatenate(mixes, axis=1), jnp.concatenate(values, axis=0)
            )


def silu_kernel(group, gain_ref, frames_ref, weight_ref, out_ref):
    place, _ = plane_place(group)
    total, width = out_ref.shape
    gain = gain_ref[:, pl.ds(pl.multiple_of(place * width, LANES), width)]
    for block in range(group):
        rows = slice(block * (total // group), (block + 1) * (total // group))
        z = dot(frames_ref[rows, :], weight_ref[...]).astype(BF16).astype(F32)
        out_ref[rows, :] = z / (1.0 + jnp.exp(-z)) * gain


def share_kernel(cores, offsets, group, *refs):
    pieces, refs = refs[: len(offsets)], refs[len(offsets) :]
    outs, weight_ref = refs[:cores], refs[cores]
    _, plane = plane_place(group)
    core = lax.axis_index("head")
    fill_planes(plane, weight_ref, pieces, offsets)
    for step, out_ref in enumerate(outs):
        rows = out_ref.shape[0]
        out_ref[...] = weight_ref[pl.ds(pl.multiple_of((core ^ step) * rows, rows), rows), :]


def gate_kernel(heads, state, c_ref, y_ref, step_ref, rows_ref, keep_ref, silu_ref, *refs):
    earlier, (gated_ref, top_ref, bottom_ref) = refs[:-3], refs[-3:]
    total, width = y_ref.shape
    head_size = width // heads
    used = rows_ref.shape[0] // 3
    entry = jnp.zeros((state, width), F32)
    for summary in reversed(earlier):
        through = summary[state : state + EDGE, :].astype(F32)[:1]
        entry = through * entry + summary[:state, :].astype(F32)
    owner = [lax.broadcasted_iota(jnp.int32, (width, width), dim) // head_size for dim in (0, 1)]
    average = jnp.where(owner[0] == owner[1], 1.0 / head_size, 0.0).astype(BF16)
    for block in range(total // SPAN):
        rows = slice(block * SPAN, (block + 1) * SPAN)
        carried = lanes_of(rows_ref[2 * used + block * 8 : 2 * used + (block + 1) * 8, :], width, head_size)
        y = y_ref[rows, :] + carried * dot(c_ref[rows, :], entry.astype(BF16))
        square_mean = dot((y * y).astype(BF16), average)
        gated_ref[rows, :] = (y * lax.rsqrt(square_mean + 1e-05) * silu_ref[rows, :]).astype(BF16)
        entry = keep_ref[block * 8 : block * 8 + 1, :] * entry + step_ref[block * state : (block + 1) * state, :]
    top_ref[...] = gated_ref[:EDGE, :]
    bottom_ref[...] = gated_ref[total - EDGE :, :]


def conv_kernel(group, edges, len_ref, taps_ref, gated_ref, *refs):
    if edges:
        before_ref, after_ref, inner_ref, act_ref, ext_ref, ends_ref = refs
    else:
        act_ref, ext_ref, ends_ref = refs
    place, plane = plane_place(group)
    total, width = gated_ref.shape
    count = total // SPAN
    taps = taps_ref.shape[0]
    half = (taps - 1) // 2
    base = plane * total
    stream = lax.axis_size("tm") // group * total
    records = len_ref.shape[0]
    reach = SPAN + 2 * EDGE
    first_tap = EDGE - half
    if edges:
        act_ref[SPAN : total - SPAN, :] = inner_ref[...]
        ext_ref[:EDGE, :] = before_ref[...].astype(F32)
        ext_ref[EDGE:reach, :] = gated_ref[: SPAN + EDGE, :].astype(F32)
        ext_ref[reach : 2 * reach - EDGE, :] = gated_ref[total - SPAN - EDGE :, :].astype(F32)
        ext_ref[2 * reach - EDGE :, :] = after_ref[...].astype(F32)
    else:
        ext_ref[...] = gated_ref[SPAN - EDGE : total - SPAN + EDGE, :].astype(F32)
    ends_ref[0] = 0
    for record in range(records):
        ends_ref[record + 1] = ends_ref[record] + len_ref[record]

    def record_at(position):
        found = jnp.int32(0)
        for record in range(records - 1):
            found = found + (ends_ref[record + 1] <= position).astype(jnp.int32)
        return found

    def one_block(at, source, target):
        low = record_at(jnp.maximum(base + at - half, 0))
        high = record_at(jnp.minimum(base + at + SPAN - 1 + half, stream - 1))
        near = lax.broadcasted_iota(jnp.int32, (reach, LANES), 0) + (base + at - EDGE)
        for tile in range(width // LANES):
            lanes = slice(tile * LANES, (tile + 1) * LANES)
            weights = taps_ref[:, pl.ds(pl.multiple_of(place * width + tile * LANES, LANES), LANES)]

            def one_record(record, done):
                inside = (near >= ends_ref[record]) & (near < ends_ref[record + 1])
                g = jnp.where(inside, ext_ref[pl.ds(source, reach), lanes], 0.0)
                out = None
                for phase in range(8):
                    part = None
                    for offset in range(phase, reach - SPAN, 8):
                        tap = offset - first_tap
                        if 0 <= tap < taps:
                            aligned = offset - phase
                            term = weights[tap : tap + 1, :] * g[aligned : aligned + SPAN + 8, :]
                            part = term if part is None else part + term
                    if part is not None:
                        moved = part[phase : phase + SPAN, :]
                        out = moved if out is None else out + moved
                return jnp.where(inside[EDGE : EDGE + SPAN], out, done)

            conv = lax.fori_loop(low, high + 1, one_record, jnp.zeros((SPAN, LANES), F32))
            act_ref[pl.ds(target, SPAN), lanes] = (conv / (1.0 + jnp.exp(-conv))).astype(BF16)
        return 0

    if edges:

        def edge(number, _):
            at = pl.multiple_of(number * (total - SPAN), SPAN)
            return one_block(at, pl.multiple_of(number * reach, reach), at)

        lax.fori_loop(0, 2, edge, 0)
    else:

        def inner(number, _):
            at = pl.multiple_of(number * SPAN, SPAN)
            return one_block(at + SPAN, at, at)

        lax.fori_loop(0, count - 2, inner, 0)


def out_kernel(group, cores, *refs):
    acts, weights, outs = refs[:cores], refs[cores : 2 * cores], refs[2 * cores :]
    place, _ = plane_place(group)
    frames = outs[0].shape[0]
    for step in reversed(range(group)):
        rows = pl.ds(pl.multiple_of((place ^ step) * frames, frames), frames)
        total = None
        for act, weight in zip(acts, weights):
            product = dot(act[rows, :], weight[...], ((1,), (1,)))
            total = product if total is None else total + product
        outs[step][...] = total.astype(outs[step].dtype)


def local(
    frames,
    x_weight,
    z_weight,
    bc_weight,
    log_decay,
    norm_gain,
    conv_weight,
    out_weight,
    record_lengths,
):
    times, cores = lax.axis_size("tm"), lax.axis_size("head")
    frame_count, depth = frames.shape
    heads_here, channels = log_decay.shape[0], x_weight.shape[1]
    state = bc_weight.shape[1] // 2
    group = 4
    while group > 1 and (channels // group % LANES or times % group or heads_here % group):
        group //= 2
    planes = times // group
    width, heads = channels // group, heads_here // group
    total = frame_count * group
    count = total // SPAN
    index, core = lax.axis_index("tm"), lax.axis_index("head")
    place = lax.rem(index, group)

    def in_plane(array, step):
        return lax.ppermute(array, "tm", [(i, i ^ step) for i in range(times)])

    def later(array, step):
        return lax.ppermute(array, "tm", [(i, i + step * group) for i in range(times - step * group)])

    def earlier(array, step):
        return lax.ppermute(array, "tm", [(i + step * group, i) for i in range(times - step * group)])

    def across(array, step):
        return lax.ppermute(array, "head", [(i, i ^ step) for i in range(cores)])

    def between_planes(array, step):
        return lax.ppermute(array, "tm", [(i, i ^ (step * group)) for i in range(times)])

    shape = jax.ShapeDtypeStruct
    rows = x_weight.shape[0]
    parity = lax.rem(core, 2)

    def along_planes(stack):
        if planes != 4:
            return [stack] + [between_planes(stack, step) for step in range(1, planes)], tuple(range(planes))

        def pairs(chosen):
            return [(a * group + q, b * group + q) for a, b in chosen for q in range(group)]

        second = between_planes(stack, 2)
        first = between_planes(stack, 1)
        again, stack_then, first = lax.optimization_barrier((second, stack, first))
        third = lax.ppermute(again, "tm", pairs([(1, 0), (2, 3)]))
        middle = lax.ppermute(stack_then, "tm", pairs([(1, 2), (2, 1)]))
        return [stack, first, second, third, middle], (0, 1, 2, 3, 3)

    half_count = frame_count // 2
    bc_half, *packed = call(
        functools.partial(cut_kernel, group),
        (
            shape((rows, LANES), BF16),
            *(shape((rows, 3 * width), BF16) for _ in range(group)),
        ),
        [bc_weight, x_weight, z_weight, out_weight.T],
        [pltpu.SemaphoreType.DMA((1 + 3 * group,))],
        smem=0,
        anywhere=4,
        vmem=ALL_VMEM_BYTES,
    )
    parts = [packed[0]] + [in_plane(packed[step], step) for step in range(1, group)]
    bc_pieces = [bc_half] + [between_planes(bc_half, step) for step in range(1, planes)]
    parts, bc_pieces = lax.optimization_barrier((parts, bc_pieces))
    xz_stack, out_stack = call(
        functools.partial(stack_kernel, group),
        (shape((group * rows, 2 * width), BF16), shape((group * rows, width), BF16)),
        parts,
        flops=STACK_HINT,
        smem=0,
    )
    xz_pieces, offsets = along_planes(xz_stack)
    x_columns, z_columns = call(
        functools.partial(assemble_kernel, group, offsets),
        (shape((depth, width), BF16), shape((depth, width), BF16)),
        xz_pieces,
        flops=ASSEMBLE_HINT,
        smem=0,
    )
    decay_blocks = jnp.pad(log_decay.reshape(group, heads, frame_count), ((0, 0), (0, 8 - heads), (0, 0)))
    tiles = planes * rows // 16 + frame_count // SPAN * 2
    payloads = call(
        functools.partial(payload_kernel, group),
        tuple(shape((half_count + -(-tiles // 8) * 16, depth), BF16) for _ in range(group)),
        [decay_blocks, frames, *bc_pieces],
        smem=0,
    )
    payloads = [payloads[0]] + [in_plane(payloads[step], step) for step in range(1, group)]
    swap, bc_mine, decay = call(
        functools.partial(swap_kernel, group, rows, half_count),
        (
            shape(((group - 1) * half_count + LANES, depth), BF16),
            shape((depth, LANES), BF16),
            shape((count * 8, SPAN), F32),
        ),
        payloads,
        smem=0,
    )
    swap = across(swap, 1)

    frame_rows, x_rows, b_rows, c_rows, decay_rows, steps, keep, summary = call(
        functools.partial(state_kernel, group, heads, state),
        (
            shape((total, depth), BF16),
            shape((total, width), BF16),
            shape((total, state), BF16),
            shape((total, state), BF16),
            shape((3 * count * 8, SPAN), F32),
            shape((count * state, width), F32),
            shape((count * 8, width), F32),
            shape((state + EDGE, width), BF16),
        ),
        [record_lengths, decay, x_columns, bc_mine, frames, swap, *payloads[1:]],
        [pltpu.VMEM((depth, 2 * state), BF16)],
        flops=2 * total * depth * (width + 2 * state),
    )
    summaries = [later(summary, step) for step in range(1, planes)]
    y = call(
        functools.partial(inner_kernel, group, heads),
        shape((total, width), F32),
        [x_rows, b_rows, c_rows, decay_rows],
        flops=4 * total * SPAN * width,
        smem=0,
    )
    silu = call(
        functools.partial(silu_kernel, group),
        shape((total, width), F32),
        [norm_gain[None], frame_rows, z_columns],
        flops=2 * total * depth * width,
        smem=0,
    )
    out_stack, summaries, y = lax.optimization_barrier((out_stack, summaries, y))
    out_pieces = [out_stack] + [between_planes(out_stack, step) for step in range(1, planes)]
    gated, top, bottom = call(
        functools.partial(gate_kernel, heads, state),
        (shape((total, width), BF16), shape((EDGE, width), BF16), shape((EDGE, width), BF16)),
        [c_rows, y, steps, decay_rows, keep, silu, *summaries],
        flops=2 * total * state * width,
        smem=0,
    )
    before, after = later(bottom, 1), earlier(top, 1)
    gated, out_pieces[1] = lax.optimization_barrier((gated, out_pieces[1]))
    ends = pltpu.SMEM((record_lengths.shape[0] + 1,), jnp.int32)
    inner = call(
        functools.partial(conv_kernel, group, False),
        shape((total - 2 * SPAN, width), BF16),
        [record_lengths, conv_weight, gated],
        [pltpu.VMEM((total - 2 * SPAN + 2 * EDGE, width), F32), ends],
        flops=2 * total * width * conv_weight.shape[0],
    )
    inner, out_pieces[2:] = lax.optimization_barrier((inner, out_pieces[2:]))
    act = call(
        functools.partial(conv_kernel, group, True),
        shape((total, width), BF16),
        [record_lengths, conv_weight, gated, before, after, inner],
        [pltpu.VMEM((2 * SPAN + 4 * EDGE, width), F32), ends],
        flops=4 * SPAN * width * conv_weight.shape[0],
    )
    share = depth // cores
    out_parts = call(
        functools.partial(share_kernel, cores, tuple(range(planes)), group),
        tuple(shape((share, width), BF16) for _ in range(cores)),
        out_pieces,
        [pltpu.VMEM((depth, width), BF16)],
        smem=0,
    )
    out_parts = [out_parts[0]] + [across(out_parts[step], step) for step in range(1, cores)]
    acts = [act] + [across(act, step) for step in range(1, cores)]
    outs = call(
        functools.partial(out_kernel, group, cores),
        tuple(shape((frame_count, share), BF16 if step else F32) for step in range(group)),
        [*acts, *out_parts],
        flops=2 * total * width * cores * share,
        smem=0,
    )
    mixed = outs[0]
    for step in range(1, group):
        mixed = mixed + in_plane(outs[step], step).astype(F32)
    return mixed.astype(BF16)


def solution(mesh):
    in_specs = (
        P("tm", None),
        P("tm", "head"),
        P("tm", "head"),
        P("tm", None),
        P("head", "tm"),
        P("head"),
        P(None, "head"),
        P("head", "tm"),
        P(),
    )
    out_specs = P("tm", "head")
    return jax.shard_map(local, mesh=mesh, in_specs=in_specs, out_specs=out_specs, check_vma=False)
```

```python
import functools

import jax
import jax.numpy as jnp
from jax import lax
from jax.experimental import pallas as pl
from jax.experimental.pallas import tpu as pltpu
from jax.sharding import PartitionSpec as P

SPAN = 128
LANES = 128
EDGE = 16
CONV_ROWS = 64
BF16 = jnp.bfloat16
F32 = jnp.float32
STACK_HINT = 40_000_000_000
ASSEMBLE_HINT = 40_000_000_000
ALL_VMEM_BYTES = 63 * 1024 * 1024
VMEM_BYTES = 20 * 1024 * 1024


def dot(a, b, dims=((1,), (0,)), precision=None):
    return lax.dot_general(a, b, (dims, ((), ())), precision=precision, preferred_element_type=F32)


def call(kernel, out_shape, operands, scratch=(), flops=0, smem=1, anywhere=0, vmem=VMEM_BYTES):
    in_specs = [pl.BlockSpec(memory_space=pltpu.SMEM)] * smem
    in_specs += [pl.BlockSpec(memory_space=pltpu.VMEM)] * (len(operands) - smem - anywhere)
    in_specs += [pl.BlockSpec(memory_space=pl.ANY)] * anywhere
    moved = sum(a.size * a.dtype.itemsize for a in operands)
    moved += sum(a.size * a.dtype.itemsize for a in jax.tree.leaves(out_shape))
    return pl.pallas_call(
        kernel,
        out_shape=out_shape,
        in_specs=in_specs,
        out_specs=jax.tree.map(lambda _: pl.BlockSpec(memory_space=pltpu.VMEM), out_shape),
        scratch_shapes=list(scratch),
        compiler_params=pltpu.CompilerParams(vmem_limit_bytes=vmem),
        cost_estimate=pl.CostEstimate(flops=flops, bytes_accessed=moved, transcendentals=0),
    )(*operands)


def plane_place(group):
    index = lax.axis_index("tm")
    return lax.rem(index, group), lax.div(index, group)


def record_starts(len_ref, position):
    start = jnp.zeros_like(position)
    end = jnp.int32(0)
    for record in range(len_ref.shape[0] - 1):
        end = end + len_ref[record]
        start = jnp.where(position >= end, end, start)
    return start


def fill_planes(plane, dest_ref, pieces, offsets, lanes=slice(None)):
    rows = pieces[0].shape[0]
    for offset in sorted(set(offsets)):
        same = [piece[:, lanes] for piece, at in zip(pieces, offsets) if at == offset]
        value = same[0] if len(same) == 1 else same[0] + same[1]
        dest_ref[pl.ds(pl.multiple_of((plane ^ offset) * rows, rows), rows), : value.shape[1]] = value


def cut_kernel(group, bc_ref, *refs):
    weight_refs, refs = refs[:3], refs[3:]
    bc_half_ref, out_refs, sems = refs[0], refs[1:-1], refs[-1]
    place, _ = plane_place(group)
    parity = lax.rem(lax.axis_index("head"), 2)
    width = weight_refs[0].shape[1] // group
    copies = [(bc_ref.at[:, pl.ds(pl.multiple_of(parity * LANES, LANES), LANES)], bc_half_ref)]
    for step, out_ref in enumerate(out_refs):
        lanes = pl.ds(pl.multiple_of((place ^ step) * width, LANES), width)
        for number, weight_ref in enumerate(weight_refs):
            copies.append((weight_ref.at[:, lanes], out_ref.at[:, number * width : (number + 1) * width]))
    started = [pltpu.make_async_copy(a, b, sems.at[number]) for number, (a, b) in enumerate(copies)]
    for copy in started:
        copy.start()
    for copy in started:
        copy.wait()


def stack_kernel(group, *refs):
    parts, stack_refs = refs[:group], refs[group:]
    place, _ = plane_place(group)
    rows = parts[0].shape[0]
    for step, part in enumerate(parts):
        at = pl.ds(pl.multiple_of((place ^ step) * rows, rows), rows)
        first = 0
        for stack_ref in stack_refs:
            width = stack_ref.shape[1]
            stack_ref[at, :] = part[:, first : first + width]
            first += width


def assemble_kernel(group, offsets, *refs):
    pieces, dest_refs = refs[: len(offsets)], refs[len(offsets) :]
    _, plane = plane_place(group)
    first = 0
    for dest_ref in dest_refs:
        width = dest_ref.shape[1]
        fill_planes(plane, dest_ref, pieces, offsets, slice(first, first + width))
        first += width


def tiles_below(half, number):
    return slice(half + number // 8 * 16, half + number // 8 * 16 + 16), slice(number % 8 * LANES, (number % 8 + 1) * LANES)


def payload_kernel(group, decay_ref, frames_ref, *refs):
    bc_refs, out_refs = refs[:-group], refs[-group:]
    place, _ = plane_place(group)
    half, rows = frames_ref.shape[0] // 2, bc_refs[0].shape[0]
    mine = pl.ds(pl.multiple_of(lax.rem(lax.axis_index("head"), 2) * half, half), half)
    for step, out_ref in enumerate(out_refs):
        out_ref[:half, :] = frames_ref[mine, :]
        tile = 0
        for bc_ref in bc_refs:
            for at in range(0, rows, 16):
                out_ref[tiles_below(half, tile)] = bc_ref[at : at + 16, :]
                tile += 1
        left = decay_ref[place ^ step]
        terms = []
        for _ in range(3):
            term = left.astype(BF16).astype(F32)
            terms.append(term)
            left = left - term
        terms.append(jnp.zeros_like(left))
        terms = jnp.concatenate(terms, axis=0).astype(BF16)
        for span in range(terms.shape[1] // SPAN):
            for at in (0, 16):
                out_ref[tiles_below(half, tile)] = terms[at : at + 16, span * SPAN : (span + 1) * SPAN]
                tile += 1


def swap_kernel(group, rows, half, *refs):
    part_refs, (swap_ref, bc_ref, decay_ref) = refs[:group], refs[group:]
    place, plane = plane_place(group)
    planes = bc_ref.shape[0] // (group * rows)
    spans = 2 * half // SPAN
    for step, part_ref in enumerate(part_refs):
        block = place ^ step
        tile = 0
        for offset in range(planes):
            first = ((plane ^ offset) * group + block) * rows
            for at in range(0, rows, 16):
                bc_ref[pl.ds(pl.multiple_of(first + at, 16), 16), :] = part_ref[tiles_below(half, tile)]
                tile += 1
        for span in range(spans):
            top = part_ref[tiles_below(half, tile)].astype(F32)
            bottom = part_ref[tiles_below(half, tile + 1)].astype(F32)
            tile += 2
            at = pl.multiple_of((block * spans + span) * 8, 8)
            decay_ref[pl.ds(at, 8), :] = top[:8] + top[8:] + bottom[:8]
        if step:
            swap_ref[(step - 1) * half : step * half, :] = part_ref[:half, :]
    top = (group - 1) * half
    height = swap_ref.shape[0] - top
    for number in range(bc_ref.shape[0] // height):
        lanes = slice(number * LANES, (number + 1) * LANES)
        swap_ref[top:, lanes] = bc_ref[number * height : (number + 1) * height, :]


def lanes_of(rows, width, head_size):
    high = rows.astype(BF16).astype(F32)
    owner = lax.broadcasted_iota(jnp.int32, (16, width), 1) // head_size
    chosen = jnp.where((lax.broadcasted_iota(jnp.int32, (16, width), 0) & 7) == owner, 1.0, 0.0).astype(BF16)
    return dot(jnp.concatenate([high, rows - high], axis=0).astype(BF16), chosen, ((0,), (0,)))


def spans_in_lanes(rows):
    return jnp.concatenate([rows[at : at + 8] for at in range(0, rows.shape[0], 8)], axis=1)


def state_kernel(group, heads, state, len_ref, decay_ref, x_weight_ref, bc_half_ref, own_ref, swap_ref, *refs):
    half_refs, refs = refs[: group - 1], refs[group - 1 :]
    frames_ref, x_ref, b_ref, c_ref, rows_ref, step_ref, keep_ref, send_ref, weight_ref, tail_ref = refs
    place, plane = plane_place(group)
    parity = lax.rem(lax.axis_index("head"), 2)
    total, width = x_ref.shape
    frames = total // group
    half = frames // 2
    head_size = width // heads
    count = total // SPAN
    base = plane * total
    frames_ref[pl.ds(pl.multiple_of(place * frames, frames), frames), :] = own_ref[...]
    for number, half_ref in enumerate(half_refs):
        block = (place ^ (number + 1)) * frames
        mine = pl.ds(pl.multiple_of(block + parity * half, half), half)
        other = pl.ds(pl.multiple_of(block + (1 - parity) * half, half), half)
        frames_ref[mine, :] = half_ref[:half, :]
        frames_ref[other, :] = swap_ref[number * half : (number + 1) * half, :]
    mine = pl.ds(pl.multiple_of(parity * LANES, LANES), LANES)
    other = pl.ds(pl.multiple_of((1 - parity) * LANES, LANES), LANES)
    weight_ref[:, mine] = bc_half_ref[...]
    top = len(half_refs) * half
    height = swap_ref.shape[0] - top
    for number in range(weight_ref.shape[0] // height):
        lanes = slice(number * LANES, (number + 1) * LANES)
        weight_ref[number * height : (number + 1) * height, other] = swap_ref[top:, lanes]

    decay = decay_ref[...]
    used = decay.shape[0]
    square = (SPAN, SPAN)
    row, lane = (lax.broadcasted_iota(jnp.int32, square, dim) for dim in (0, 1))
    upper = jnp.where(row <= lane, 1.0, 0.0).astype(F32)
    cumul = dot(decay, upper, precision=lax.Precision.HIGHEST)
    whole = dot(decay, jnp.ones(square, F32), precision=lax.Precision.HIGHEST)
    first = base + lax.broadcasted_iota(jnp.int32, (used, SPAN), 0) // 8 * SPAN
    position = first + lane[:1]
    start = record_starts(len_ref, position)
    start_last = record_starts(len_ref, first + (SPAN - 1))
    carried = jnp.where(start < first, jnp.exp(cumul), 0.0)
    tail = jnp.where(position >= start_last, jnp.exp(whole - cumul), 0.0)
    keep = jnp.where(start_last < first, jnp.exp(whole), 0.0)
    rows_ref[:used, :] = cumul
    rows_ref[used : 2 * used, :] = start.astype(F32)
    rows_ref[2 * used :, :] = carried

    for block in range(group):
        rows = slice(block * frames, (block + 1) * frames)
        x_ref[rows, :] = dot(frames_ref[rows, :], x_weight_ref[...]).astype(BF16)
        product = dot(frames_ref[rows, :], weight_ref[...])
        b_ref[rows, :] = product[:, :state].astype(BF16)
        c_ref[rows, :] = product[:, state:].astype(BF16)

    tail_ref[...] = lanes_of(spans_in_lanes(tail), width, head_size)
    by_span = jnp.zeros((8, SPAN), F32)
    for block in range(count):
        by_span = jnp.where(lane[:8] == block, keep[block * 8 : (block + 1) * 8], by_span)
    kept = lanes_of(by_span, width, head_size)[: keep_ref.shape[0]]
    keep_ref[...] = kept
    entry = jnp.zeros((state, width), F32)
    through = jnp.ones((1, width), F32)
    for block in range(count):
        rows = slice(block * SPAN, (block + 1) * SPAN)
        weighed = x_ref[rows, :].astype(F32) * tail_ref[rows, :]
        step = dot(b_ref[rows, :], weighed.astype(BF16), ((0,), (0,)))
        step_ref[block * state : (block + 1) * state, :] = step
        entry = kept[block : block + 1] * entry + step
        through = through * kept[block : block + 1]
    send_ref[:state, :] = entry.astype(BF16)
    send_ref[state:, :] = jnp.broadcast_to(through, (EDGE, width)).astype(BF16)


def inner_kernel(group, heads, x_ref, b_ref, c_ref, rows_ref, y_ref, carry_ref):
    _, plane = plane_place(group)
    total, width = x_ref.shape
    head_size = width // heads
    count = total // SPAN
    base = plane * total
    used = rows_ref.shape[0] // 3
    square = (SPAN, SPAN)
    parts = [rows_ref[: 2 * used, :]]
    if 2 * used % SPAN:
        parts.append(jnp.zeros((SPAN - 2 * used % SPAN, SPAN), F32))
    columns = jnp.concatenate(parts, axis=0).T
    carry_ref[...] = lanes_of(spans_in_lanes(rows_ref[2 * used :, :]), width, head_size)
    row, lane = (lax.broadcasted_iota(jnp.int32, square, dim) for dim in (0, 1))
    lower = row >= lane
    tile_heads = LANES // head_size
    tile_lane = lax.broadcasted_iota(jnp.int32, (1, LANES), 1) // head_size
    masks = [jnp.where(tile_lane == inner, 1.0, 0.0).astype(BF16) for inner in range(tile_heads)]
    for block in range(count):
        rows = slice(block * SPAN, (block + 1) * SPAN)
        at = block * 8
        x = x_ref[rows, :]
        scores = dot(c_ref[rows, :], b_ref[rows, :], ((1,), (1,)))
        here = (base + block * SPAN + lane).astype(F32)
        start_here = jnp.broadcast_to(columns[:, used + at : used + at + 1], square)
        joined = lower & (here >= start_here)
        for tile in range(width // LANES):
            mixes, values = [], []
            for inner in range(tile_heads):
                which = at + tile * tile_heads + inner
                column = jnp.broadcast_to(columns[:, which : which + 1], square)
                gap = jnp.where(joined, column - rows_ref[which : which + 1, :], -1e30)
                mixes.append((jnp.exp(gap) * scores).astype(BF16))
                values.append(x[:, tile * LANES : (tile + 1) * LANES] * masks[inner])
            y_ref[rows, tile * LANES : (tile + 1) * LANES] = dot(
                jnp.concatenate(mixes, axis=1), jnp.concatenate(values, axis=0)
            )


def silu_kernel(group, gain_ref, frames_ref, weight_ref, out_ref):
    place, _ = plane_place(group)
    total, width = out_ref.shape
    gain = gain_ref[:, pl.ds(pl.multiple_of(place * width, LANES), width)]
    for block in range(group):
        rows = slice(block * (total // group), (block + 1) * (total // group))
        z = dot(frames_ref[rows, :], weight_ref[...]).astype(BF16).astype(F32)
        out_ref[rows, :] = z / (1.0 + jnp.exp(-z)) * gain


def share_kernel(cores, offsets, group, *refs):
    pieces, refs = refs[: len(offsets)], refs[len(offsets) :]
    outs, weight_ref = refs[:cores], refs[cores]
    _, plane = plane_place(group)
    core = lax.axis_index("head")
    fill_planes(plane, weight_ref, pieces, offsets)
    for step, out_ref in enumerate(outs):
        rows = out_ref.shape[0]
        out_ref[...] = weight_ref[pl.ds(pl.multiple_of((core ^ step) * rows, rows), rows), :]


def gate_kernel(heads, state, c_ref, y_ref, step_ref, carry_ref, keep_ref, silu_ref, *refs):
    earlier, (gated_ref, top_ref, bottom_ref) = refs[:-3], refs[-3:]
    total, width = y_ref.shape
    head_size = width // heads
    entry = jnp.zeros((state, width), F32)
    for summary in reversed(earlier):
        through = summary[state : state + EDGE, :].astype(F32)[:1]
        entry = through * entry + summary[:state, :].astype(F32)
    owner = [lax.broadcasted_iota(jnp.int32, (width, width), dim) // head_size for dim in (0, 1)]
    average = jnp.where(owner[0] == owner[1], 1.0 / head_size, 0.0).astype(BF16)
    for block in range(total // SPAN):
        rows = slice(block * SPAN, (block + 1) * SPAN)
        y = y_ref[rows, :] + carry_ref[rows, :] * dot(c_ref[rows, :], entry.astype(BF16))
        square_mean = dot((y * y).astype(BF16), average)
        gated_ref[rows, :] = (y * lax.rsqrt(square_mean + 1e-05) * silu_ref[rows, :]).astype(BF16)
        entry = keep_ref[block : block + 1, :] * entry + step_ref[block * state : (block + 1) * state, :]
    top_ref[...] = gated_ref[:EDGE, :]
    bottom_ref[...] = gated_ref[total - EDGE :, :]


def conv_kernel(group, steps, len_ref, taps_ref, gated_ref, before_ref, after_ref, act_ref, ext_ref, ends_ref):
    place, plane = plane_place(group)
    total, width = gated_ref.shape
    frames = total // group
    taps = taps_ref.shape[0]
    half = (taps - 1) // 2
    stream = lax.axis_size("tm") // group * total
    records = len_ref.shape[0]
    reach = CONV_ROWS + 2 * EDGE
    first_tap = EDGE - half
    pitch = frames + 2 * EDGE
    ends_ref[0] = 0
    for record in range(records):
        ends_ref[record + 1] = ends_ref[record] + len_ref[record]
    for number, step in enumerate(steps):
        owner = place ^ step
        first = pl.multiple_of(owner * frames, frames)
        top = gated_ref[pl.ds(pl.multiple_of(jnp.maximum(first - EDGE, 0), EDGE), EDGE), :].astype(F32)
        below = pl.multiple_of(jnp.minimum(first + frames, total - EDGE), EDGE)
        bottom = gated_ref[pl.ds(below, EDGE), :].astype(F32)
        at = number * pitch
        ext_ref[at : at + EDGE, :] = jnp.where(owner == 0, before_ref[...].astype(F32), top)
        ext_ref[at + EDGE : at + EDGE + frames, :] = gated_ref[pl.ds(first, frames), :].astype(F32)
        ext_ref[at + EDGE + frames : at + pitch, :] = jnp.where(owner == group - 1, after_ref[...].astype(F32), bottom)

    def record_at(position):
        found = jnp.int32(0)
        for record in range(records - 1):
            found = found + (ends_ref[record + 1] <= position).astype(jnp.int32)
        return found

    for number, step in enumerate(steps):
        base = plane * total + (place ^ step) * frames

        def one_block(block, _, number=number, base=base):
            inside_part = pl.multiple_of(block * CONV_ROWS, CONV_ROWS)
            source = pl.multiple_of(number * pitch + inside_part, EDGE)
            target = pl.multiple_of(number * frames + inside_part, CONV_ROWS)
            at = base + inside_part
            low = record_at(jnp.maximum(at - half, 0))
            high = record_at(jnp.minimum(at + CONV_ROWS - 1 + half, stream - 1))
            near = lax.broadcasted_iota(jnp.int32, (reach, LANES), 0) + (at - EDGE)
            for tile in range(width // LANES):
                lanes = slice(tile * LANES, (tile + 1) * LANES)
                weights = taps_ref[:, pl.ds(pl.multiple_of(place * width + tile * LANES, LANES), LANES)]

                def one_record(record, done):
                    inside = (near >= ends_ref[record]) & (near < ends_ref[record + 1])
                    g = jnp.where(inside, ext_ref[pl.ds(source, reach), lanes], 0.0)
                    out = None
                    for phase in range(8):
                        part = None
                        for offset in range(phase, reach - CONV_ROWS, 8):
                            tap = offset - first_tap
                            if 0 <= tap < taps:
                                aligned = offset - phase
                                term = weights[tap : tap + 1, :] * g[aligned : aligned + CONV_ROWS + 8, :]
                                part = term if part is None else part + term
                        if part is not None:
                            moved = part[phase : phase + CONV_ROWS, :]
                            out = moved if out is None else out + moved
                    return jnp.where(inside[EDGE : EDGE + CONV_ROWS], out, done)

                conv = lax.fori_loop(low, high + 1, one_record, jnp.zeros((CONV_ROWS, LANES), F32))
                act_ref[pl.ds(target, CONV_ROWS), lanes] = (conv / (1.0 + jnp.exp(-conv))).astype(BF16)
            return 0

        lax.fori_loop(0, frames // CONV_ROWS, one_block, 0)


def out_kernel(cores, *refs):
    acts, weights, outs = refs[:cores], refs[cores : 2 * cores], refs[2 * cores :]
    frames = outs[0].shape[0]
    for number, out_ref in enumerate(outs):
        rows = slice(number * frames, (number + 1) * frames)
        total = None
        for act, weight in zip(acts, weights):
            product = dot(act[rows, :], weight[...], ((1,), (1,)))
            total = product if total is None else total + product
        out_ref[...] = total.astype(out_ref.dtype)


def local(
    frames,
    x_weight,
    z_weight,
    bc_weight,
    log_decay,
    norm_gain,
    conv_weight,
    out_weight,
    record_lengths,
):
    times, cores = lax.axis_size("tm"), lax.axis_size("head")
    frame_count, depth = frames.shape
    heads_here, channels = log_decay.shape[0], x_weight.shape[1]
    state = bc_weight.shape[1] // 2
    group = 4
    while group > 1 and (channels // group % LANES or times % group or heads_here % group):
        group //= 2
    planes = times // group
    width, heads = channels // group, heads_here // group
    total = frame_count * group
    count = total // SPAN
    index, core = lax.axis_index("tm"), lax.axis_index("head")
    place = lax.rem(index, group)

    def in_plane(array, step):
        return lax.ppermute(array, "tm", [(i, i ^ step) for i in range(times)])

    def later(array, step):
        return lax.ppermute(array, "tm", [(i, i + step * group) for i in range(times - step * group)])

    def earlier(array, step):
        return lax.ppermute(array, "tm", [(i + step * group, i) for i in range(times - step * group)])

    def across(array, step):
        return lax.ppermute(array, "head", [(i, i ^ step) for i in range(cores)])

    def between_planes(array, step):
        return lax.ppermute(array, "tm", [(i, i ^ (step * group)) for i in range(times)])

    shape = jax.ShapeDtypeStruct
    rows = x_weight.shape[0]
    parity = lax.rem(core, 2)

    def along_planes(stack):
        if planes != 4:
            return [stack] + [between_planes(stack, step) for step in range(1, planes)], tuple(range(planes))

        def pairs(chosen):
            return [(a * group + q, b * group + q) for a, b in chosen for q in range(group)]

        second = between_planes(stack, 2)
        first = between_planes(stack, 1)
        again, stack_then, first = lax.optimization_barrier((second, stack, first))
        third = lax.ppermute(again, "tm", pairs([(1, 0), (2, 3)]))
        middle = lax.ppermute(stack_then, "tm", pairs([(1, 2), (2, 1)]))
        return [stack, first, second, third, middle], (0, 1, 2, 3, 3)

    half_count = frame_count // 2
    bc_half, *packed = call(
        functools.partial(cut_kernel, group),
        (
            shape((rows, LANES), BF16),
            *(shape((rows, 3 * width), BF16) for _ in range(group)),
        ),
        [bc_weight, x_weight, z_weight, out_weight.T],
        [pltpu.SemaphoreType.DMA((1 + 3 * group,))],
        smem=0,
        anywhere=4,
        vmem=ALL_VMEM_BYTES,
    )
    parts = [packed[0]] + [in_plane(packed[step], step) for step in range(1, group)]
    bc_pieces = [bc_half] + [between_planes(bc_half, step) for step in range(1, planes)]
    parts, bc_pieces = lax.optimization_barrier((parts, bc_pieces))
    xz_stack, out_stack = call(
        functools.partial(stack_kernel, group),
        (shape((group * rows, 2 * width), BF16), shape((group * rows, width), BF16)),
        parts,
        flops=STACK_HINT,
        smem=0,
    )
    xz_pieces, offsets = along_planes(xz_stack)
    x_columns, z_columns = call(
        functools.partial(assemble_kernel, group, offsets),
        (shape((depth, width), BF16), shape((depth, width), BF16)),
        xz_pieces,
        flops=ASSEMBLE_HINT,
        smem=0,
    )
    decay_blocks = jnp.pad(log_decay.reshape(group, heads, frame_count), ((0, 0), (0, 8 - heads), (0, 0)))
    tiles = planes * rows // 16 + frame_count // SPAN * 2
    payloads = call(
        functools.partial(payload_kernel, group),
        tuple(shape((half_count + -(-tiles // 8) * 16, depth), BF16) for _ in range(group)),
        [decay_blocks, frames, *bc_pieces],
        smem=0,
    )
    payloads = [payloads[0]] + [in_plane(payloads[step], step) for step in range(1, group)]
    swap, bc_mine, decay = call(
        functools.partial(swap_kernel, group, rows, half_count),
        (
            shape(((group - 1) * half_count + LANES, depth), BF16),
            shape((depth, LANES), BF16),
            shape((count * 8, SPAN), F32),
        ),
        payloads,
        smem=0,
    )
    swap = across(swap, 1)

    frame_rows, x_rows, b_rows, c_rows, decay_rows, steps, keep, summary = call(
        functools.partial(state_kernel, group, heads, state),
        (
            shape((total, depth), BF16),
            shape((total, width), BF16),
            shape((total, state), BF16),
            shape((total, state), BF16),
            shape((3 * count * 8, SPAN), F32),
            shape((count * state, width), F32),
            shape((-(-count // 8) * 8, width), F32),
            shape((state + EDGE, width), BF16),
        ),
        [record_lengths, decay, x_columns, bc_mine, frames, swap, *payloads[1:]],
        [pltpu.VMEM((depth, 2 * state), BF16), pltpu.VMEM((total, width), F32)],
        flops=2 * total * depth * (width + 2 * state),
    )
    summaries = [later(summary, step) for step in range(1, planes)]
    y, carry = call(
        functools.partial(inner_kernel, group, heads),
        (shape((total, width), F32), shape((total, width), F32)),
        [x_rows, b_rows, c_rows, decay_rows],
        flops=4 * total * SPAN * width,
        smem=0,
    )
    silu = call(
        functools.partial(silu_kernel, group),
        shape((total, width), F32),
        [norm_gain[None], frame_rows, z_columns],
        flops=2 * total * depth * width,
        smem=0,
    )
    silu = call(
        functools.partial(silu_kernel, group),
        shape((total, width), F32),
        [norm_gain[None], frame_rows, z_columns],
        flops=2 * total * depth * width,
        smem=0,
    )
    out_stack, summaries, y = lax.optimization_barrier((out_stack, summaries, y))
    out_pieces = [out_stack] + [between_planes(out_stack, step) for step in range(1, planes)]
    gated, top, bottom = call(
        functools.partial(gate_kernel, heads, state),
        (shape((total, width), BF16), shape((EDGE, width), BF16), shape((EDGE, width), BF16)),
        [c_rows, y, steps, carry, keep, silu, *summaries],
        flops=2 * total * state * width,
        smem=0,
    )
    before, after = later(bottom, 1), earlier(top, 1)
    ends = pltpu.SMEM((record_lengths.shape[0] + 1,), jnp.int32)
    share = depth // cores
    far, near = (group - 1,), (*range(1, group - 1), 0)

    def conv(steps, gated):
        return call(
            functools.partial(conv_kernel, group, steps),
            shape((len(steps) * frame_count, width), BF16),
            [record_lengths, conv_weight, gated, before, after],
            [pltpu.VMEM((len(steps) * (frame_count + 2 * EDGE), width), F32), ends],
            flops=2 * len(steps) * frame_count * width * conv_weight.shape[0],
        )

    def out(steps, act, swapped):
        return call(
            functools.partial(out_kernel, cores),
            tuple(shape((frame_count, share), BF16 if step else F32) for step in steps),
            [act, *swapped, *out_parts],
            flops=2 * len(steps) * frame_count * width * cores * share,
            smem=0,
        )

    far_act = conv(far, gated)
    far_swapped = [across(far_act, step) for step in range(1, cores)]
    far_act, out_pieces = lax.optimization_barrier((far_act, out_pieces))
    out_parts = call(
        functools.partial(share_kernel, cores, tuple(range(planes)), group),
        tuple(shape((share, width), BF16) for _ in range(cores)),
        out_pieces,
        [pltpu.VMEM((depth, width), BF16)],
        smem=0,
    )
    out_parts = [out_parts[0]] + [across(out_parts[step], step) for step in range(1, cores)]
    gated, far_act = lax.optimization_barrier((gated, far_act))
    near_act = conv(near, gated)
    near_act, far_swapped, out_parts = lax.optimization_barrier((near_act, far_swapped, out_parts))
    (far_out,) = out(far, far_act, far_swapped)
    near_act, far_out = lax.optimization_barrier((near_act, far_out))
    far_out = in_plane(far_out, far[0])
    near_swapped = [across(near_act, step) for step in range(1, cores)]
    near_outs = out(near, near_act, near_swapped)
    mixed = near_outs[-1] + far_out.astype(F32)
    for step, partial in zip(near[:-1], near_outs[:-1]):
        mixed = mixed + in_plane(partial, step).astype(F32)
    return mixed.astype(BF16)


def solution(mesh):
    in_specs = (
        P("tm", None),
        P("tm", "head"),
        P("tm", "head"),
        P("tm", None),
        P("head", "tm"),
        P("head"),
        P(None, "head"),
        P("head", "tm"),
        P(),
    )
    out_specs = P("tm", "head")
    return jax.shard_map(local, mesh=mesh, in_specs=in_specs, out_specs=out_specs, check_vma=False)
```

```python
import functools

import jax
import jax.numpy as jnp
from jax import lax
from jax.experimental import pallas as pl
from jax.experimental.pallas import tpu as pltpu
from jax.sharding import PartitionSpec as P

SPAN = 128
LANES = 128
EDGE = 16
CONV_ROWS = 64
BF16 = jnp.bfloat16
F32 = jnp.float32
STACK_HINT = 40_000_000_000
ASSEMBLE_HINT = 40_000_000_000
ALL_VMEM_BYTES = 63 * 1024 * 1024
VMEM_BYTES = 20 * 1024 * 1024


def dot(a, b, dims=((1,), (0,)), precision=None):
    return lax.dot_general(a, b, (dims, ((), ())), precision=precision, preferred_element_type=F32)


def call(kernel, out_shape, operands, scratch=(), flops=0, smem=1, anywhere=0, vmem=VMEM_BYTES):
    in_specs = [pl.BlockSpec(memory_space=pltpu.SMEM)] * smem
    in_specs += [pl.BlockSpec(memory_space=pltpu.VMEM)] * (len(operands) - smem - anywhere)
    in_specs += [pl.BlockSpec(memory_space=pl.ANY)] * anywhere
    moved = sum(a.size * a.dtype.itemsize for a in operands)
    moved += sum(a.size * a.dtype.itemsize for a in jax.tree.leaves(out_shape))
    return pl.pallas_call(
        kernel,
        out_shape=out_shape,
        in_specs=in_specs,
        out_specs=jax.tree.map(lambda _: pl.BlockSpec(memory_space=pltpu.VMEM), out_shape),
        scratch_shapes=list(scratch),
        compiler_params=pltpu.CompilerParams(vmem_limit_bytes=vmem),
        cost_estimate=pl.CostEstimate(flops=flops, bytes_accessed=moved, transcendentals=0),
    )(*operands)


def plane_place(group):
    index = lax.axis_index("tm")
    return lax.rem(index, group), lax.div(index, group)


def record_starts(len_ref, position):
    start = jnp.zeros_like(position)
    end = jnp.int32(0)
    for record in range(len_ref.shape[0] - 1):
        end = end + len_ref[record]
        start = jnp.where(position >= end, end, start)
    return start


def fill_planes(plane, dest_ref, pieces, offsets, lanes=slice(None)):
    rows = pieces[0].shape[0]
    for offset in sorted(set(offsets)):
        same = [piece[:, lanes] for piece, at in zip(pieces, offsets) if at == offset]
        value = same[0] if len(same) == 1 else same[0] + same[1]
        dest_ref[pl.ds(pl.multiple_of((plane ^ offset) * rows, rows), rows), : value.shape[1]] = value


def cut_kernel(group, bc_ref, *refs):
    weight_refs, refs = refs[:3], refs[3:]
    bc_half_ref, out_refs, sems = refs[0], refs[1:-1], refs[-1]
    place, _ = plane_place(group)
    parity = lax.rem(lax.axis_index("head"), 2)
    width = weight_refs[0].shape[1] // group
    copies = [(bc_ref.at[:, pl.ds(pl.multiple_of(parity * LANES, LANES), LANES)], bc_half_ref)]
    for step, out_ref in enumerate(out_refs):
        lanes = pl.ds(pl.multiple_of((place ^ step) * width, LANES), width)
        for number, weight_ref in enumerate(weight_refs):
            copies.append((weight_ref.at[:, lanes], out_ref.at[:, number * width : (number + 1) * width]))
    started = [pltpu.make_async_copy(a, b, sems.at[number]) for number, (a, b) in enumerate(copies)]
    for copy in started:
        copy.start()
    for copy in started:
        copy.wait()


def stack_kernel(group, *refs):
    parts, stack_refs = refs[:group], refs[group:]
    place, _ = plane_place(group)
    rows = parts[0].shape[0]
    for step, part in enumerate(parts):
        at = pl.ds(pl.multiple_of((place ^ step) * rows, rows), rows)
        first = 0
        for stack_ref in stack_refs:
            width = stack_ref.shape[1]
            stack_ref[at, :] = part[:, first : first + width]
            first += width


def assemble_kernel(group, offsets, *refs):
    pieces, dest_refs = refs[: len(offsets)], refs[len(offsets) :]
    _, plane = plane_place(group)
    first = 0
    for dest_ref in dest_refs:
        width = dest_ref.shape[1]
        fill_planes(plane, dest_ref, pieces, offsets, slice(first, first + width))
        first += width


def tiles_below(half, number):
    return slice(half + number // 8 * 16, half + number // 8 * 16 + 16), slice(number % 8 * LANES, (number % 8 + 1) * LANES)


def payload_kernel(group, decay_ref, frames_ref, *refs):
    bc_refs, out_refs = refs[:-group], refs[-group:]
    place, _ = plane_place(group)
    half, rows = frames_ref.shape[0] // 2, bc_refs[0].shape[0]
    mine = pl.ds(pl.multiple_of(lax.rem(lax.axis_index("head"), 2) * half, half), half)
    for step, out_ref in enumerate(out_refs):
        out_ref[:half, :] = frames_ref[mine, :]
        tile = 0
        for bc_ref in bc_refs:
            for at in range(0, rows, 16):
                out_ref[tiles_below(half, tile)] = bc_ref[at : at + 16, :]
                tile += 1
        left = decay_ref[place ^ step]
        terms = []
        for _ in range(3):
            term = left.astype(BF16).astype(F32)
            terms.append(term)
            left = left - term
        terms.append(jnp.zeros_like(left))
        terms = jnp.concatenate(terms, axis=0).astype(BF16)
        for span in range(terms.shape[1] // SPAN):
            for at in (0, 16):
                out_ref[tiles_below(half, tile)] = terms[at : at + 16, span * SPAN : (span + 1) * SPAN]
                tile += 1


def swap_kernel(group, rows, half, *refs):
    part_refs, (swap_ref, bc_ref, decay_ref) = refs[:group], refs[group:]
    place, plane = plane_place(group)
    planes = bc_ref.shape[0] // (group * rows)
    spans = 2 * half // SPAN
    for step, part_ref in enumerate(part_refs):
        block = place ^ step
        tile = 0
        for offset in range(planes):
            first = ((plane ^ offset) * group + block) * rows
            for at in range(0, rows, 16):
                bc_ref[pl.ds(pl.multiple_of(first + at, 16), 16), :] = part_ref[tiles_below(half, tile)]
                tile += 1
        for span in range(spans):
            top = part_ref[tiles_below(half, tile)].astype(F32)
            bottom = part_ref[tiles_below(half, tile + 1)].astype(F32)
            tile += 2
            at = pl.multiple_of((block * spans + span) * 8, 8)
            decay_ref[pl.ds(at, 8), :] = top[:8] + top[8:] + bottom[:8]
        if step:
            swap_ref[(step - 1) * half : step * half, :] = part_ref[:half, :]
    top = (group - 1) * half
    height = swap_ref.shape[0] - top
    for number in range(bc_ref.shape[0] // height):
        lanes = slice(number * LANES, (number + 1) * LANES)
        swap_ref[top:, lanes] = bc_ref[number * height : (number + 1) * height, :]


def lanes_of(rows, width, head_size):
    high = rows.astype(BF16).astype(F32)
    owner = lax.broadcasted_iota(jnp.int32, (16, width), 1) // head_size
    chosen = jnp.where((lax.broadcasted_iota(jnp.int32, (16, width), 0) & 7) == owner, 1.0, 0.0).astype(BF16)
    return dot(jnp.concatenate([high, rows - high], axis=0).astype(BF16), chosen, ((0,), (0,)))


def spans_in_lanes(rows):
    return jnp.concatenate([rows[at : at + 8] for at in range(0, rows.shape[0], 8)], axis=1)


def state_kernel(group, heads, state, len_ref, decay_ref, x_weight_ref, bc_half_ref, own_ref, swap_ref, *refs):
    half_refs, refs = refs[: group - 1], refs[group - 1 :]
    frames_ref, x_ref, b_ref, c_ref, rows_ref, step_ref, keep_ref, send_ref, weight_ref, tail_ref = refs
    place, plane = plane_place(group)
    parity = lax.rem(lax.axis_index("head"), 2)
    total, width = x_ref.shape
    frames = total // group
    half = frames // 2
    head_size = width // heads
    count = total // SPAN
    base = plane * total
    frames_ref[pl.ds(pl.multiple_of(place * frames, frames), frames), :] = own_ref[...]
    for number, half_ref in enumerate(half_refs):
        block = (place ^ (number + 1)) * frames
        mine = pl.ds(pl.multiple_of(block + parity * half, half), half)
        other = pl.ds(pl.multiple_of(block + (1 - parity) * half, half), half)
        frames_ref[mine, :] = half_ref[:half, :]
        frames_ref[other, :] = swap_ref[number * half : (number + 1) * half, :]
    mine = pl.ds(pl.multiple_of(parity * LANES, LANES), LANES)
    other = pl.ds(pl.multiple_of((1 - parity) * LANES, LANES), LANES)
    weight_ref[:, mine] = bc_half_ref[...]
    top = len(half_refs) * half
    height = swap_ref.shape[0] - top
    for number in range(weight_ref.shape[0] // height):
        lanes = slice(number * LANES, (number + 1) * LANES)
        weight_ref[number * height : (number + 1) * height, other] = swap_ref[top:, lanes]

    decay = decay_ref[...]
    used = decay.shape[0]
    square = (SPAN, SPAN)
    row, lane = (lax.broadcasted_iota(jnp.int32, square, dim) for dim in (0, 1))
    upper = jnp.where(row <= lane, 1.0, 0.0).astype(F32)
    cumul = dot(decay, upper, precision=lax.Precision.HIGHEST)
    whole = dot(decay, jnp.ones(square, F32), precision=lax.Precision.HIGHEST)
    first = base + lax.broadcasted_iota(jnp.int32, (used, SPAN), 0) // 8 * SPAN
    position = first + lane[:1]
    start = record_starts(len_ref, position)
    start_last = record_starts(len_ref, first + (SPAN - 1))
    carried = jnp.where(start < first, jnp.exp(cumul), 0.0)
    tail = jnp.where(position >= start_last, jnp.exp(whole - cumul), 0.0)
    keep = jnp.where(start_last < first, jnp.exp(whole), 0.0)
    rows_ref[:used, :] = cumul
    rows_ref[used : 2 * used, :] = start.astype(F32)
    rows_ref[2 * used :, :] = carried

    for block in range(group):
        rows = slice(block * frames, (block + 1) * frames)
        x_ref[rows, :] = dot(frames_ref[rows, :], x_weight_ref[...]).astype(BF16)
        product = dot(frames_ref[rows, :], weight_ref[...])
        b_ref[rows, :] = product[:, :state].astype(BF16)
        c_ref[rows, :] = product[:, state:].astype(BF16)

    tail_ref[...] = lanes_of(spans_in_lanes(tail), width, head_size)
    by_span = jnp.zeros((8, SPAN), F32)
    for block in range(count):
        by_span = jnp.where(lane[:8] == block, keep[block * 8 : (block + 1) * 8], by_span)
    kept = lanes_of(by_span, width, head_size)[: keep_ref.shape[0]]
    keep_ref[...] = kept
    entry = jnp.zeros((state, width), F32)
    through = jnp.ones((1, width), F32)
    for block in range(count):
        rows = slice(block * SPAN, (block + 1) * SPAN)
        weighed = x_ref[rows, :].astype(F32) * tail_ref[rows, :]
        step = dot(b_ref[rows, :], weighed.astype(BF16), ((0,), (0,)))
        step_ref[block * state : (block + 1) * state, :] = step
        entry = kept[block : block + 1] * entry + step
        through = through * kept[block : block + 1]
    send_ref[:state, :] = entry.astype(BF16)
    send_ref[state:, :] = jnp.broadcast_to(through, (EDGE, width)).astype(BF16)


def inner_kernel(group, heads, x_ref, b_ref, c_ref, rows_ref, y_ref, carry_ref):
    _, plane = plane_place(group)
    total, width = x_ref.shape
    head_size = width // heads
    count = total // SPAN
    base = plane * total
    used = rows_ref.shape[0] // 3
    square = (SPAN, SPAN)
    parts = [rows_ref[: 2 * used, :]]
    if 2 * used % SPAN:
        parts.append(jnp.zeros((SPAN - 2 * used % SPAN, SPAN), F32))
    columns = jnp.concatenate(parts, axis=0).T
    carry_ref[...] = lanes_of(spans_in_lanes(rows_ref[2 * used :, :]), width, head_size)
    row, lane = (lax.broadcasted_iota(jnp.int32, square, dim) for dim in (0, 1))
    lower = row >= lane
    tile_heads = LANES // head_size
    tile_lane = lax.broadcasted_iota(jnp.int32, (1, LANES), 1) // head_size
    masks = [jnp.where(tile_lane == inner, 1.0, 0.0).astype(BF16) for inner in range(tile_heads)]
    for block in range(count):
        rows = slice(block * SPAN, (block + 1) * SPAN)
        at = block * 8
        x = x_ref[rows, :]
        scores = dot(c_ref[rows, :], b_ref[rows, :], ((1,), (1,)))
        here = (base + block * SPAN + lane).astype(F32)
        start_here = jnp.broadcast_to(columns[:, used + at : used + at + 1], square)
        joined = lower & (here >= start_here)
        for tile in range(width // LANES):
            mixes, values = [], []
            for inner in range(tile_heads):
                which = at + tile * tile_heads + inner
                column = jnp.broadcast_to(columns[:, which : which + 1], square)
                gap = jnp.where(joined, column - rows_ref[which : which + 1, :], -1e30)
                mixes.append((jnp.exp(gap) * scores).astype(BF16))
                values.append(x[:, tile * LANES : (tile + 1) * LANES] * masks[inner])
            y_ref[rows, tile * LANES : (tile + 1) * LANES] = dot(
                jnp.concatenate(mixes, axis=1), jnp.concatenate(values, axis=0)
            )


def silu_kernel(group, gain_ref, frames_ref, weight_ref, out_ref):
    place, _ = plane_place(group)
    total, width = out_ref.shape
    gain = gain_ref[:, pl.ds(pl.multiple_of(place * width, LANES), width)]
    for block in range(group):
        rows = slice(block * (total // group), (block + 1) * (total // group))
        z = dot(frames_ref[rows, :], weight_ref[...]).astype(BF16).astype(F32)
        out_ref[rows, :] = z / (1.0 + jnp.exp(-z)) * gain


def share_kernel(cores, offsets, group, *refs):
    pieces, refs = refs[: len(offsets)], refs[len(offsets) :]
    outs, weight_ref = refs[:cores], refs[cores]
    _, plane = plane_place(group)
    core = lax.axis_index("head")
    fill_planes(plane, weight_ref, pieces, offsets)
    for step, out_ref in enumerate(outs):
        rows = out_ref.shape[0]
        out_ref[...] = weight_ref[pl.ds(pl.multiple_of((core ^ step) * rows, rows), rows), :]


def gate_kernel(heads, state, c_ref, y_ref, step_ref, carry_ref, keep_ref, silu_ref, *refs):
    earlier, (gated_ref, top_ref, bottom_ref) = refs[:-3], refs[-3:]
    total, width = y_ref.shape
    head_size = width // heads
    entry = jnp.zeros((state, width), F32)
    for summary in reversed(earlier):
        through = summary[state : state + EDGE, :].astype(F32)[:1]
        entry = through * entry + summary[:state, :].astype(F32)
    owner = [lax.broadcasted_iota(jnp.int32, (width, width), dim) // head_size for dim in (0, 1)]
    average = jnp.where(owner[0] == owner[1], 1.0 / head_size, 0.0).astype(BF16)
    for block in range(total // SPAN):
        rows = slice(block * SPAN, (block + 1) * SPAN)
        y = y_ref[rows, :] + carry_ref[rows, :] * dot(c_ref[rows, :], entry.astype(BF16))
        square_mean = dot((y * y).astype(BF16), average)
        gated_ref[rows, :] = (y * lax.rsqrt(square_mean + 1e-05) * silu_ref[rows, :]).astype(BF16)
        entry = keep_ref[block : block + 1, :] * entry + step_ref[block * state : (block + 1) * state, :]
    top_ref[...] = gated_ref[:EDGE, :]
    bottom_ref[...] = gated_ref[total - EDGE :, :]


def conv_kernel(group, steps, len_ref, taps_ref, gated_ref, before_ref, after_ref, act_ref, ext_ref, ends_ref):
    place, plane = plane_place(group)
    total, width = gated_ref.shape
    frames = total // group
    taps = taps_ref.shape[0]
    half = (taps - 1) // 2
    stream = lax.axis_size("tm") // group * total
    records = len_ref.shape[0]
    reach = CONV_ROWS + 2 * EDGE
    first_tap = EDGE - half
    pitch = frames + 2 * EDGE
    ends_ref[0] = 0
    for record in range(records):
        ends_ref[record + 1] = ends_ref[record] + len_ref[record]
    for number, step in enumerate(steps):
        owner = place ^ step
        first = pl.multiple_of(owner * frames, frames)
        top = gated_ref[pl.ds(pl.multiple_of(jnp.maximum(first - EDGE, 0), EDGE), EDGE), :].astype(F32)
        below = pl.multiple_of(jnp.minimum(first + frames, total - EDGE), EDGE)
        bottom = gated_ref[pl.ds(below, EDGE), :].astype(F32)
        at = number * pitch
        ext_ref[at : at + EDGE, :] = jnp.where(owner == 0, before_ref[...].astype(F32), top)
        ext_ref[at + EDGE : at + EDGE + frames, :] = gated_ref[pl.ds(first, frames), :].astype(F32)
        ext_ref[at + EDGE + frames : at + pitch, :] = jnp.where(owner == group - 1, after_ref[...].astype(F32), bottom)

    def record_at(position):
        found = jnp.int32(0)
        for record in range(records - 1):
            found = found + (ends_ref[record + 1] <= position).astype(jnp.int32)
        return found

    for number, step in enumerate(steps):
        base = plane * total + (place ^ step) * frames

        def one_block(block, _, number=number, base=base):
            inside_part = pl.multiple_of(block * CONV_ROWS, CONV_ROWS)
            source = pl.multiple_of(number * pitch + inside_part, EDGE)
            target = pl.multiple_of(number * frames + inside_part, CONV_ROWS)
            at = base + inside_part
            low = record_at(jnp.maximum(at - half, 0))
            high = record_at(jnp.minimum(at + CONV_ROWS - 1 + half, stream - 1))
            near = lax.broadcasted_iota(jnp.int32, (reach, LANES), 0) + (at - EDGE)
            for tile in range(width // LANES):
                lanes = slice(tile * LANES, (tile + 1) * LANES)
                weights = taps_ref[:, pl.ds(pl.multiple_of(place * width + tile * LANES, LANES), LANES)]

                def one_record(record, done):
                    inside = (near >= ends_ref[record]) & (near < ends_ref[record + 1])
                    g = jnp.where(inside, ext_ref[pl.ds(source, reach), lanes], 0.0)
                    out = None
                    for phase in range(8):
                        part = None
                        for offset in range(phase, reach - CONV_ROWS, 8):
                            tap = offset - first_tap
                            if 0 <= tap < taps:
                                aligned = offset - phase
                                term = weights[tap : tap + 1, :] * g[aligned : aligned + CONV_ROWS + 8, :]
                                part = term if part is None else part + term
                        if part is not None:
                            moved = part[phase : phase + CONV_ROWS, :]
                            out = moved if out is None else out + moved
                    return jnp.where(inside[EDGE : EDGE + CONV_ROWS], out, done)

                conv = lax.fori_loop(low, high + 1, one_record, jnp.zeros((CONV_ROWS, LANES), F32))
                act_ref[pl.ds(target, CONV_ROWS), lanes] = (conv / (1.0 + jnp.exp(-conv))).astype(BF16)
            return 0

        lax.fori_loop(0, frames // CONV_ROWS, one_block, 0)


def out_kernel(cores, *refs):
    acts, weights, outs = refs[:cores], refs[cores : 2 * cores], refs[2 * cores :]
    frames = outs[0].shape[0]
    for number, out_ref in enumerate(outs):
        rows = slice(number * frames, (number + 1) * frames)
        total = None
        for act, weight in zip(acts, weights):
            product = dot(act[rows, :], weight[...], ((1,), (1,)))
            total = product if total is None else total + product
        out_ref[...] = total.astype(out_ref.dtype)


def local(
    frames,
    x_weight,
    z_weight,
    bc_weight,
    log_decay,
    norm_gain,
    conv_weight,
    out_weight,
    record_lengths,
):
    times, cores = lax.axis_size("tm"), lax.axis_size("head")
    frame_count, depth = frames.shape
    heads_here, channels = log_decay.shape[0], x_weight.shape[1]
    state = bc_weight.shape[1] // 2
    group = 4
    while group > 1 and (channels // group % LANES or times % group or heads_here % group):
        group //= 2
    planes = times // group
    width, heads = channels // group, heads_here // group
    total = frame_count * group
    count = total // SPAN
    index, core = lax.axis_index("tm"), lax.axis_index("head")
    place = lax.rem(index, group)

    def in_plane(array, step):
        return lax.ppermute(array, "tm", [(i, i ^ step) for i in range(times)])

    def later(array, step):
        return lax.ppermute(array, "tm", [(i, i + step * group) for i in range(times - step * group)])

    def earlier(array, step):
        return lax.ppermute(array, "tm", [(i + step * group, i) for i in range(times - step * group)])

    def across(array, step):
        return lax.ppermute(array, "head", [(i, i ^ step) for i in range(cores)])

    def between_planes(array, step):
        return lax.ppermute(array, "tm", [(i, i ^ (step * group)) for i in range(times)])

    shape = jax.ShapeDtypeStruct
    rows = x_weight.shape[0]
    parity = lax.rem(core, 2)

    offsets = (0, 1, 2, 3, 3) if planes == 4 else tuple(range(planes))

    def first_hops(stack):
        return [stack] + [between_planes(stack, step) for step in range(1, 3 if planes == 4 else planes)]

    def last_hops(pieces, ready):
        if planes != 4:
            return pieces, ready

        def pairs(chosen):
            return [(a * group + q, b * group + q) for a, b in chosen for q in range(group)]

        pieces, ready = lax.optimization_barrier((pieces, ready))
        third = lax.ppermute(pieces[2], "tm", pairs([(1, 0), (2, 3)]))
        middle = lax.ppermute(pieces[0], "tm", pairs([(1, 2), (2, 1)]))
        return [*pieces, third, middle], ready

    half_count = frame_count // 2
    bc_half, *packed = call(
        functools.partial(cut_kernel, group),
        (
            shape((rows, LANES), BF16),
            *(shape((rows, 3 * width), BF16) for _ in range(group)),
        ),
        [bc_weight, x_weight, z_weight, out_weight.T],
        [pltpu.SemaphoreType.DMA((1 + 3 * group,))],
        smem=0,
        anywhere=4,
        vmem=ALL_VMEM_BYTES,
    )
    parts = [packed[0]] + [in_plane(packed[step], step) for step in range(1, group)]
    bc_pieces = [bc_half] + [between_planes(bc_half, step) for step in range(1, planes)]
    parts, bc_pieces = lax.optimization_barrier((parts, bc_pieces))
    xz_stack, out_stack = call(
        functools.partial(stack_kernel, group),
        (shape((group * rows, 2 * width), BF16), shape((group * rows, width), BF16)),
        parts,
        flops=STACK_HINT,
        smem=0,
    )
    xz_pieces, _ = last_hops(first_hops(xz_stack), ())
    out_stack, xz_pieces = lax.optimization_barrier((out_stack, xz_pieces))
    x_columns, z_columns = call(
        functools.partial(assemble_kernel, group, offsets),
        (shape((depth, width), BF16), shape((depth, width), BF16)),
        xz_pieces,
        flops=ASSEMBLE_HINT,
        smem=0,
    )
    decay_blocks = jnp.pad(log_decay.reshape(group, heads, frame_count), ((0, 0), (0, 8 - heads), (0, 0)))
    tiles = planes * rows // 16 + frame_count // SPAN * 2
    payloads = call(
        functools.partial(payload_kernel, group),
        tuple(shape((half_count + -(-tiles // 8) * 16, depth), BF16) for _ in range(group)),
        [decay_blocks, frames, *bc_pieces],
        smem=0,
    )
    payloads = [payloads[0]] + [in_plane(payloads[step], step) for step in range(1, group)]
    swap, bc_mine, decay = call(
        functools.partial(swap_kernel, group, rows, half_count),
        (
            shape(((group - 1) * half_count + LANES, depth), BF16),
            shape((depth, LANES), BF16),
            shape((count * 8, SPAN), F32),
        ),
        payloads,
        smem=0,
    )
    swap = across(swap, 1)

    frame_rows, x_rows, b_rows, c_rows, decay_rows, steps, keep, summary = call(
        functools.partial(state_kernel, group, heads, state),
        (
            shape((total, depth), BF16),
            shape((total, width), BF16),
            shape((total, state), BF16),
            shape((total, state), BF16),
            shape((3 * count * 8, SPAN), F32),
            shape((count * state, width), F32),
            shape((-(-count // 8) * 8, width), F32),
            shape((state + EDGE, width), BF16),
        ),
        [record_lengths, decay, x_columns, bc_mine, frames, swap, *payloads[1:]],
        [pltpu.VMEM((depth, 2 * state), BF16), pltpu.VMEM((total, width), F32)],
        flops=2 * total * depth * (width + 2 * state),
    )
    out_pieces, summary = lax.optimization_barrier((first_hops(out_stack), summary))
    summaries = [later(summary, step) for step in range(1, planes)]
    y, carry = call(
        functools.partial(inner_kernel, group, heads),
        (shape((total, width), F32), shape((total, width), F32)),
        [x_rows, b_rows, c_rows, decay_rows],
        flops=4 * total * SPAN * width,
        smem=0,
    )
    silu = call(
        functools.partial(silu_kernel, group),
        shape((total, width), F32),
        [norm_gain[None], frame_rows, z_columns],
        flops=2 * total * depth * width,
        smem=0,
    )
    out_pieces, (summaries, y) = last_hops(out_pieces, (summaries, y))
    silu, out_pieces[3:] = lax.optimization_barrier((silu, out_pieces[3:]))
    gated, top, bottom = call(
        functools.partial(gate_kernel, heads, state),
        (shape((total, width), BF16), shape((EDGE, width), BF16), shape((EDGE, width), BF16)),
        [c_rows, y, steps, carry, keep, silu, *summaries],
        flops=2 * total * state * width,
        smem=0,
    )
    before, after = later(bottom, 1), earlier(top, 1)
    ends = pltpu.SMEM((record_lengths.shape[0] + 1,), jnp.int32)
    share = depth // cores
    far, near = (group - 1,), (*range(1, group - 1), 0)

    def conv(steps, gated):
        return call(
            functools.partial(conv_kernel, group, steps),
            shape((len(steps) * frame_count, width), BF16),
            [record_lengths, conv_weight, gated, before, after],
            [pltpu.VMEM((len(steps) * (frame_count + 2 * EDGE), width), F32), ends],
            flops=2 * len(steps) * frame_count * width * conv_weight.shape[0],
        )

    def out(steps, act, swapped):
        return call(
            functools.partial(out_kernel, cores),
            tuple(shape((frame_count, share), BF16 if step else F32) for step in steps),
            [act, *swapped, *out_parts],
            flops=2 * len(steps) * frame_count * width * cores * share,
            smem=0,
        )

    far_act = conv(far, gated)
    far_swapped = [across(far_act, step) for step in range(1, cores)]
    far_act, out_pieces = lax.optimization_barrier((far_act, out_pieces))
    out_parts = call(
        functools.partial(share_kernel, cores, offsets, group),
        tuple(shape((share, width), BF16) for _ in range(cores)),
        out_pieces,
        [pltpu.VMEM((depth, width), BF16)],
        smem=0,
    )
    out_parts = [out_parts[0]] + [across(out_parts[step], step) for step in range(1, cores)]
    gated, far_act = lax.optimization_barrier((gated, far_act))
    near_act = conv(near, gated)
    near_act, far_swapped, out_parts = lax.optimization_barrier((near_act, far_swapped, out_parts))
    (far_out,) = out(far, far_act, far_swapped)
    near_act, far_out = lax.optimization_barrier((near_act, far_out))
    far_out = in_plane(far_out, far[0])
    near_swapped = [across(near_act, step) for step in range(1, cores)]
    near_outs = out(near, near_act, near_swapped)
    mixed = near_outs[-1] + far_out.astype(F32)
    for step, partial in zip(near[:-1], near_outs[:-1]):
        mixed = mixed + in_plane(partial, step).astype(F32)
    return mixed.astype(BF16)


def solution(mesh):
    in_specs = (
        P("tm", None),
        P("tm", "head"),
        P("tm", "head"),
        P("tm", None),
        P("head", "tm"),
        P("head"),
        P(None, "head"),
        P("head", "tm"),
        P(),
    )
    out_specs = P("tm", "head")
    return jax.shard_map(local, mesh=mesh, in_specs=in_specs, out_specs=out_specs, check_vma=False)
```

```python
import functools

import jax
import jax.numpy as jnp
from jax import lax
from jax.experimental import pallas as pl
from jax.experimental.pallas import tpu as pltpu
from jax.sharding import PartitionSpec as P

SPAN = 128
LANES = 128
EDGE = 16
CONV_ROWS = 64
BF16 = jnp.bfloat16
F32 = jnp.float32
STACK_HINT = 40_000_000_000
ASSEMBLE_HINT = 40_000_000_000
ALL_VMEM_BYTES = 63 * 1024 * 1024
VMEM_BYTES = 20 * 1024 * 1024


def dot(a, b, dims=((1,), (0,)), precision=None):
    return lax.dot_general(a, b, (dims, ((), ())), precision=precision, preferred_element_type=F32)


def call(kernel, out_shape, operands, scratch=(), flops=0, smem=1, anywhere=0, vmem=VMEM_BYTES):
    in_specs = [pl.BlockSpec(memory_space=pltpu.SMEM)] * smem
    in_specs += [pl.BlockSpec(memory_space=pltpu.VMEM)] * (len(operands) - smem - anywhere)
    in_specs += [pl.BlockSpec(memory_space=pl.ANY)] * anywhere
    moved = sum(a.size * a.dtype.itemsize for a in operands)
    moved += sum(a.size * a.dtype.itemsize for a in jax.tree.leaves(out_shape))
    return pl.pallas_call(
        kernel,
        out_shape=out_shape,
        in_specs=in_specs,
        out_specs=jax.tree.map(lambda _: pl.BlockSpec(memory_space=pltpu.VMEM), out_shape),
        scratch_shapes=list(scratch),
        compiler_params=pltpu.CompilerParams(vmem_limit_bytes=vmem),
        cost_estimate=pl.CostEstimate(flops=flops, bytes_accessed=moved, transcendentals=0),
    )(*operands)


def plane_place(group):
    index = lax.axis_index("tm")
    return lax.rem(index, group), lax.div(index, group)


def record_starts(len_ref, position):
    start = jnp.zeros_like(position)
    end = jnp.int32(0)
    for record in range(len_ref.shape[0] - 1):
        end = end + len_ref[record]
        start = jnp.where(position >= end, end, start)
    return start


def fill_planes(plane, dest_ref, pieces, offsets, lanes=slice(None)):
    rows = pieces[0].shape[0]
    for offset in sorted(set(offsets)):
        same = [piece[:, lanes] for piece, at in zip(pieces, offsets) if at == offset]
        value = same[0] if len(same) == 1 else same[0] + same[1]
        dest_ref[pl.ds(pl.multiple_of((plane ^ offset) * rows, rows), rows), : value.shape[1]] = value


def cut_kernel(group, frames_ref, *refs):
    weight_refs, refs = refs[:2], refs[2:]
    half_ref, out_refs, sems = refs[0], refs[1:-1], refs[-1]
    place, _ = plane_place(group)
    parity = lax.rem(lax.axis_index("head"), 2)
    width = weight_refs[0].shape[1] // group
    half = half_ref.shape[0]
    copies = [(frames_ref.at[pl.ds(pl.multiple_of(parity * half, half), half), :], half_ref)]
    for step, out_ref in enumerate(out_refs):
        lanes = pl.ds(pl.multiple_of((place ^ step) * width, LANES), width)
        for number, weight_ref in enumerate(weight_refs):
            copies.append((weight_ref.at[:, lanes], out_ref.at[:, number * width : (number + 1) * width]))
    started = [pltpu.make_async_copy(a, b, sems.at[number]) for number, (a, b) in enumerate(copies)]
    for copy in started:
        copy.start()
    for copy in started:
        copy.wait()


def stack_kernel(group, *refs):
    parts, stack_refs = refs[:group], refs[group:]
    place, _ = plane_place(group)
    rows = parts[0].shape[0]
    for step, part in enumerate(parts):
        at = pl.ds(pl.multiple_of((place ^ step) * rows, rows), rows)
        first = 0
        for stack_ref in stack_refs:
            width = stack_ref.shape[1]
            stack_ref[at, :] = part[:, first : first + width]
            first += width


def assemble_kernel(group, offsets, *refs):
    pieces, dest_refs = refs[: len(offsets)], refs[len(offsets) :]
    _, plane = plane_place(group)
    first = 0
    for dest_ref in dest_refs:
        width = dest_ref.shape[1]
        fill_planes(plane, dest_ref, pieces, offsets, slice(first, first + width))
        first += width


def tile(number):
    return slice(number // 8 * 16, number // 8 * 16 + 16), slice(number % 8 * LANES, (number % 8 + 1) * LANES)


def put(out_ref, number, array):
    for at in range(0, array.shape[0], 16):
        for lane in range(0, array.shape[1], LANES):
            out_ref[tile(number)] = array[at : at + 16, lane : lane + LANES]
            number += 1
    return number


def three_terms(value):
    terms = []
    for _ in range(3):
        term = value.astype(BF16).astype(F32)
        terms.append(term)
        value = value - term
    return terms


def outward_kernel(group, planes, out_w_ref, bc_ref, frames_ref, decay_ref, *out_refs):
    _, plane = plane_place(group)
    parity = lax.rem(lax.axis_index("head"), 2)
    frames = frames_ref.shape[0]
    lane = lax.broadcasted_iota(jnp.int32, (8, LANES), 1)
    decays = []
    for first in (0, frames - LANES):
        rows = [jnp.zeros((8, LANES), F32), jnp.zeros((8, LANES), F32)]
        for block in range(group):
            for number, term in enumerate(three_terms(decay_ref[block, :, first : first + LANES])):
                slot = number * group + block
                moved = pltpu.roll(term, (slot % 8 * EDGE + (EDGE if first else 0)) % LANES, 1)
                rows[slot // 8] = jnp.where(lane // EDGE == slot % 8, moved, rows[slot // 8])
        decays.append(jnp.concatenate(rows, axis=0))
    for step, out_ref in enumerate(out_refs):
        number = put(out_ref, 0, out_w_ref[...])
        number = put(out_ref, number, bc_ref[:, pl.ds(pl.multiple_of(parity * LANES, LANES), LANES)])
        later = (plane ^ step) > plane
        edge = pl.multiple_of(jnp.where(later, frames - EDGE, 0), EDGE)
        number = put(out_ref, number, frames_ref[pl.ds(edge, EDGE), :])
        put(out_ref, number, jnp.where(later, decays[1], decays[0]).astype(BF16))


def inward_kernel(group, rows, channels, decay_ref, *refs):
    piece_refs, out_refs = refs[:-group], refs[-group:]
    place, plane = plane_place(group)
    width = channels // group
    planes = len(piece_refs)
    wanted = jnp.clip(jnp.where(place == 0, plane + 1, plane - 1), 0, planes - 1)
    depth_tiles = out_refs[0].shape[1] // LANES
    across, down = channels // LANES, rows // 16
    for step, out_ref in enumerate(out_refs):
        block = place ^ step
        number = 0
        for piece_ref in piece_refs:
            for at in range(down):
                for lane in range(width // LANES):
                    if across == 8:
                        lanes = pl.ds(pl.multiple_of(block * width + lane * LANES, LANES), LANES)
                        out_ref[tile(number)] = piece_ref[at * 16 : at * 16 + 16, lanes]
                    else:
                        value = piece_ref[tile(at * across + lane)]
                        for other in range(1, group):
                            there = piece_ref[tile(at * across + other * (width // LANES) + lane)]
                            value = jnp.where(block == other, there, value)
                        out_ref[tile(number)] = value
                    number += 1
            for at in range(down):
                out_ref[tile(number)] = piece_ref[tile(down * across + at)]
                number += 1
        for offset, piece_ref in enumerate(piece_refs):

            @pl.when((plane ^ offset) == wanted)
            def _(piece_ref=piece_ref, number=number):
                for at in range(depth_tiles + 1):
                    out_ref[tile(number + at)] = piece_ref[tile(down * (across + 1) + at)]

        number += depth_tiles + 1
        terms = three_terms(decay_ref[block])
        terms = jnp.concatenate([*terms, jnp.zeros_like(terms[0])], axis=0).astype(BF16)
        for span in range(terms.shape[1] // SPAN):
            number = put(out_ref, number, terms[:, span * SPAN : (span + 1) * SPAN])


def swap_kernel(group, rows, *refs):
    part_refs, half_refs = refs[:group], refs[group : 2 * group - 1]
    swap_ref, bc_ref, halo_ref, decay_ref, own_out_ref, other_out_ref, out_ref, span_ref = refs[2 * group - 1 :]
    place, plane = plane_place(group)
    planes = bc_ref.shape[0] // (group * rows)
    width = out_ref.shape[1]
    count = span_ref.shape[0]
    spans = count // group
    down = rows // 16
    depth_tiles = swap_ref.shape[1] // LANES
    lane = lax.broadcasted_iota(jnp.int32, (8, LANES), 1)
    for step, part_ref in enumerate(part_refs):
        block = place ^ step
        number = 0
        for offset in range(planes):
            first = ((plane ^ offset) * group + block) * rows
            for at in range(down):
                for column in range(width // LANES):
                    lanes = slice(column * LANES, (column + 1) * LANES)
                    out_ref[pl.ds(pl.multiple_of(first + at * 16, 16), 16), lanes] = part_ref[tile(number)]
                    number += 1
            for at in range(down):
                bc_ref[pl.ds(pl.multiple_of(first + at * 16, 16), 16), :] = part_ref[tile(number)]
                number += 1
        for side, owner in enumerate((group - 1, 0)):

            @pl.when(block == owner)
            def _(part_ref=part_ref, number=number, side=side):
                for at in range(depth_tiles):
                    halo_ref[side * EDGE : (side + 1) * EDGE, at * LANES : (at + 1) * LANES] = part_ref[tile(number + at)]
                packed = part_ref[tile(number + depth_tiles)].astype(F32)
                chosen = jnp.zeros((8, LANES), F32)
                for head_block in range(group):
                    value = jnp.zeros((8, LANES), F32)
                    for term in range(3):
                        slot = term * group + head_block
                        half = packed[slot // 8 * 8 : slot // 8 * 8 + 8]
                        value = value + pltpu.roll(half, (LANES - slot % 8 * EDGE) % LANES, 1)
                    chosen = jnp.where(place == head_block, value, chosen)
                if side:
                    last = pltpu.roll(chosen, EDGE, 1)
                    decay_ref[count * 8 :, :] = jnp.where((lane >= EDGE) & (lane < 2 * EDGE), last, 0.0)
                else:
                    decay_ref[:8, :] = jnp.where(lane < EDGE, chosen, 0.0)

        number += depth_tiles + 1
        for span in range(spans):
            top = part_ref[tile(number)].astype(F32)
            bottom = part_ref[tile(number + 1)].astype(F32)
            number += 2
            span_ref[block * spans + span] = top[:8] + top[8:] + bottom[:8]
    for span in range(count):
        moved = pltpu.roll(span_ref[span], EDGE, 1)
        here, after = slice(span * 8, span * 8 + 8), slice(span * 8 + 8, span * 8 + 16)
        decay_ref[here, :] = jnp.where(lane < EDGE, decay_ref[here, :], moved)
        kept = decay_ref[after, :] if span == count - 1 else jnp.zeros((8, LANES), F32)
        decay_ref[after, :] = jnp.where(lane < EDGE, moved, kept)
    core = lax.axis_index("head")
    share = own_out_ref.shape[0]
    own_out_ref[...] = out_ref[pl.ds(pl.multiple_of(core * share, share), share), :]
    for step in range(1, other_out_ref.shape[0] // share + 1):
        at = pl.ds(pl.multiple_of((core ^ step) * share, share), share)
        other_out_ref[(step - 1) * share : step * share, :] = out_ref[at, :]
    half = half_refs[0].shape[0]
    for number, half_ref in enumerate(half_refs):
        swap_ref[number * half : (number + 1) * half, :] = half_ref[...]
    top = len(half_refs) * half
    height = swap_ref.shape[0] - top
    for number in range(bc_ref.shape[0] // height):
        lanes = slice(number * LANES, (number + 1) * LANES)
        swap_ref[top:, lanes] = bc_ref[number * height : (number + 1) * height, :]


def lanes_of(rows, width, head_size):
    high = rows.astype(BF16).astype(F32)
    owner = lax.broadcasted_iota(jnp.int32, (16, width), 1) // head_size
    chosen = jnp.where((lax.broadcasted_iota(jnp.int32, (16, width), 0) & 7) == owner, 1.0, 0.0).astype(BF16)
    return dot(jnp.concatenate([high, rows - high], axis=0).astype(BF16), chosen, ((0,), (0,)))


def spans_in_lanes(rows):
    return jnp.concatenate([rows[at : at + 8] for at in range(0, rows.shape[0], 8)], axis=1)


def row_blocks(total, wide):
    return [slice(at, at + 256) for at in range(0, total, 256)] + [slice(total, wide)]


def state_kernel(group, heads, state, len_ref, decay_ref, x_weight_ref, bc_half_ref, own_ref, swap_ref, halo_ref, *refs):
    half_refs, refs = refs[: group - 1], refs[group - 1 :]
    frames_ref, x_ref, b_ref, c_ref, rows_ref, step_ref, keep_ref, send_ref, weight_ref, tail_ref = refs
    place, plane = plane_place(group)
    parity = lax.rem(lax.axis_index("head"), 2)
    width = x_ref.shape[1]
    frames = own_ref.shape[0]
    total = frames * group
    half = frames // 2
    head_size = width // heads
    count = total // SPAN
    base = plane * total - EDGE
    wide = total + 2 * EDGE
    frames_ref[:EDGE, :] = halo_ref[:EDGE, :]
    frames_ref[total + EDGE : wide, :] = halo_ref[EDGE:, :]
    frames_ref[wide:, :] = jnp.zeros((frames_ref.shape[0] - wide, frames_ref.shape[1]), BF16)
    frames_ref[pl.ds(pl.multiple_of(EDGE + place * frames, EDGE), frames), :] = own_ref[...]
    for number, half_ref in enumerate(half_refs):
        block = EDGE + (place ^ (number + 1)) * frames
        mine = pl.ds(pl.multiple_of(block + parity * half, EDGE), half)
        other = pl.ds(pl.multiple_of(block + (1 - parity) * half, EDGE), half)
        frames_ref[mine, :] = half_ref[...]
        frames_ref[other, :] = swap_ref[number * half : (number + 1) * half, :]
    mine = pl.ds(pl.multiple_of(parity * LANES, LANES), LANES)
    other = pl.ds(pl.multiple_of((1 - parity) * LANES, LANES), LANES)
    weight_ref[:, mine] = bc_half_ref[...]
    top = len(half_refs) * half
    height = swap_ref.shape[0] - top
    for number in range(weight_ref.shape[0] // height):
        lanes = slice(number * LANES, (number + 1) * LANES)
        weight_ref[number * height : (number + 1) * height, other] = swap_ref[top:, lanes]

    decay = decay_ref[...]
    used = decay.shape[0]
    square = (SPAN, SPAN)
    row, lane = (lax.broadcasted_iota(jnp.int32, square, dim) for dim in (0, 1))
    upper = jnp.where(row <= lane, 1.0, 0.0).astype(F32)
    cumul = dot(decay, upper, precision=lax.Precision.HIGHEST)
    whole = dot(decay, jnp.ones(square, F32), precision=lax.Precision.HIGHEST)
    first = base + lax.broadcasted_iota(jnp.int32, (used, SPAN), 0) // 8 * SPAN
    position = first + lane[:1]
    start = record_starts(len_ref, position)
    start_last = record_starts(len_ref, first + (SPAN - 1))
    carried = jnp.where(start < first, jnp.exp(cumul), 0.0)
    tail = jnp.where(position >= start_last, jnp.exp(whole - cumul), 0.0)
    keep = jnp.where(start_last < first, jnp.exp(whole), 0.0)
    rows_ref[:used, :] = cumul
    rows_ref[used : 2 * used, :] = start.astype(F32)
    rows_ref[2 * used :, :] = carried

    for rows in row_blocks(total, wide):
        x_ref[rows, :] = dot(frames_ref[rows, :], x_weight_ref[...]).astype(BF16)
        product = dot(frames_ref[rows, :], weight_ref[...])
        b_ref[rows, :] = product[:, :state].astype(BF16)
        c_ref[rows, :] = product[:, state:].astype(BF16)
    for ref in (x_ref, b_ref, c_ref):
        ref[wide:, :] = jnp.zeros((ref.shape[0] - wide, ref.shape[1]), BF16)

    tail_ref[...] = lanes_of(spans_in_lanes(tail[: count * 8]), width, head_size)
    by_span = jnp.zeros((8, SPAN), F32)
    for block in range(count):
        by_span = jnp.where(lane[:8] == block, keep[block * 8 : (block + 1) * 8], by_span)
    kept = lanes_of(by_span, width, head_size)[: keep_ref.shape[0]]
    keep_ref[...] = kept
    entry = jnp.zeros((state, width), F32)
    through = jnp.ones((1, width), F32)
    for block in range(count):
        rows = slice(block * SPAN, (block + 1) * SPAN)
        weighed = x_ref[rows, :].astype(F32) * tail_ref[rows, :]
        step = dot(b_ref[rows, :], weighed.astype(BF16), ((0,), (0,)))
        step_ref[block * state : (block + 1) * state, :] = step
        entry = kept[block : block + 1] * entry + step
        through = through * kept[block : block + 1]
    send_ref[:state, :] = entry.astype(BF16)
    send_ref[state:, :] = jnp.broadcast_to(through, (EDGE, width)).astype(BF16)


def inner_kernel(group, heads, x_ref, b_ref, c_ref, rows_ref, y_ref, carry_ref):
    _, plane = plane_place(group)
    total, width = x_ref.shape
    head_size = width // heads
    count = total // SPAN
    base = plane * (total - SPAN) - EDGE
    used = rows_ref.shape[0] // 3
    square = (SPAN, SPAN)
    parts = [rows_ref[: 2 * used, :]]
    if 2 * used % SPAN:
        parts.append(jnp.zeros((SPAN - 2 * used % SPAN, SPAN), F32))
    columns = jnp.concatenate(parts, axis=0).T
    carry_ref[...] = lanes_of(spans_in_lanes(rows_ref[2 * used :, :]), width, head_size)
    row, lane = (lax.broadcasted_iota(jnp.int32, square, dim) for dim in (0, 1))
    lower = row >= lane
    tile_heads = LANES // head_size
    tile_lane = lax.broadcasted_iota(jnp.int32, (1, LANES), 1) // head_size
    masks = [jnp.where(tile_lane == inner, 1.0, 0.0).astype(BF16) for inner in range(tile_heads)]
    for block in range(count):
        rows = slice(block * SPAN, (block + 1) * SPAN)
        at = block * 8
        x = x_ref[rows, :]
        scores = dot(c_ref[rows, :], b_ref[rows, :], ((1,), (1,)))
        here = (base + block * SPAN + lane).astype(F32)
        start_here = jnp.broadcast_to(columns[:, used + at : used + at + 1], square)
        joined = lower & (here >= start_here)
        for tile in range(width // LANES):
            mixes, values = [], []
            for inner in range(tile_heads):
                which = at + tile * tile_heads + inner
                column = jnp.broadcast_to(columns[:, which : which + 1], square)
                gap = jnp.where(joined, column - rows_ref[which : which + 1, :], -1e30)
                mixes.append((jnp.exp(gap) * scores).astype(BF16))
                values.append(x[:, tile * LANES : (tile + 1) * LANES] * masks[inner])
            y_ref[rows, tile * LANES : (tile + 1) * LANES] = dot(
                jnp.concatenate(mixes, axis=1), jnp.concatenate(values, axis=0)
            )


def silu_kernel(group, gain_ref, frames_ref, weight_ref, out_ref):
    place, _ = plane_place(group)
    rows_all, width = out_ref.shape
    total = rows_all - SPAN
    wide = total + 2 * EDGE
    gain = gain_ref[:, pl.ds(pl.multiple_of(place * width, LANES), width)]
    for rows in row_blocks(total, wide):
        z = dot(frames_ref[rows, :], weight_ref[...]).astype(BF16).astype(F32)
        out_ref[rows, :] = z / (1.0 + jnp.exp(-z)) * gain
    out_ref[wide:, :] = jnp.zeros((rows_all - wide, width), F32)


def gate_kernel(heads, state, c_ref, y_ref, step_ref, carry_ref, keep_ref, silu_ref, *refs):
    earlier, gated_ref = refs[:-1], refs[-1]
    total, width = y_ref.shape
    head_size = width // heads
    count = total // SPAN
    entry = jnp.zeros((state, width), F32)
    for summary in reversed(earlier):
        through = summary[state : state + EDGE, :].astype(F32)[:1]
        entry = through * entry + summary[:state, :].astype(F32)
    owner = [lax.broadcasted_iota(jnp.int32, (width, width), dim) // head_size for dim in (0, 1)]
    average = jnp.where(owner[0] == owner[1], 1.0 / head_size, 0.0).astype(BF16)
    for block in range(count):
        rows = slice(block * SPAN, (block + 1) * SPAN)
        y = y_ref[rows, :] + carry_ref[rows, :] * dot(c_ref[rows, :], entry.astype(BF16))
        square_mean = dot((y * y).astype(BF16), average)
        gated_ref[rows, :] = (y * lax.rsqrt(square_mean + 1e-05) * silu_ref[rows, :]).astype(BF16)
        if block < count - 1:
            entry = keep_ref[block : block + 1, :] * entry + step_ref[block * state : (block + 1) * state, :]


def conv_kernel(group, steps, len_ref, taps_ref, gated_ref, act_ref, ext_ref, ends_ref):
    place, plane = plane_place(group)
    rows_all, width = gated_ref.shape
    total = rows_all - SPAN
    frames = total // group
    taps = taps_ref.shape[0]
    half = (taps - 1) // 2
    stream = lax.axis_size("tm") // group * total
    records = len_ref.shape[0]
    reach = CONV_ROWS + 2 * EDGE
    first_tap = EDGE - half
    pitch = frames + 2 * EDGE
    ends_ref[0] = 0
    for record in range(records):
        ends_ref[record + 1] = ends_ref[record] + len_ref[record]
    for number, step in enumerate(steps):
        first = pl.multiple_of((place ^ step) * frames, frames)
        ext_ref[number * pitch : (number + 1) * pitch, :] = gated_ref[pl.ds(first, pitch), :].astype(F32)

    def record_at(position):
        found = jnp.int32(0)
        for record in range(records - 1):
            found = found + (ends_ref[record + 1] <= position).astype(jnp.int32)
        return found

    for number, step in enumerate(steps):
        base = plane * total + (place ^ step) * frames

        def one_block(block, _, number=number, base=base):
            inside_part = pl.multiple_of(block * CONV_ROWS, CONV_ROWS)
            source = pl.multiple_of(number * pitch + inside_part, EDGE)
            target = pl.multiple_of(number * frames + inside_part, CONV_ROWS)
            at = base + inside_part
            low = record_at(jnp.maximum(at - half, 0))
            high = record_at(jnp.minimum(at + CONV_ROWS - 1 + half, stream - 1))
            near = lax.broadcasted_iota(jnp.int32, (reach, LANES), 0) + (at - EDGE)
            for tile in range(width // LANES):
                lanes = slice(tile * LANES, (tile + 1) * LANES)
                weights = taps_ref[:, pl.ds(pl.multiple_of(place * width + tile * LANES, LANES), LANES)]

                def one_record(record, done):
                    inside = (near >= ends_ref[record]) & (near < ends_ref[record + 1])
                    g = jnp.where(inside, ext_ref[pl.ds(source, reach), lanes], 0.0)
                    out = None
                    for phase in range(8):
                        part = None
                        for offset in range(phase, reach - CONV_ROWS, 8):
                            tap = offset - first_tap
                            if 0 <= tap < taps:
                                aligned = offset - phase
                                term = weights[tap : tap + 1, :] * g[aligned : aligned + CONV_ROWS + 8, :]
                                part = term if part is None else part + term
                        if part is not None:
                            moved = part[phase : phase + CONV_ROWS, :]
                            out = moved if out is None else out + moved
                    return jnp.where(inside[EDGE : EDGE + CONV_ROWS], out, done)

                conv = lax.fori_loop(low, high + 1, one_record, jnp.zeros((CONV_ROWS, LANES), F32))
                act_ref[pl.ds(target, CONV_ROWS), lanes] = (conv / (1.0 + jnp.exp(-conv))).astype(BF16)
            return 0

        lax.fori_loop(0, frames // CONV_ROWS, one_block, 0)


def out_kernel(cores, *refs):
    acts, weights, outs = refs[:cores], refs[cores : 2 * cores], refs[2 * cores :]
    frames = outs[0].shape[0]
    for number, out_ref in enumerate(outs):
        rows = slice(number * frames, (number + 1) * frames)
        total = None
        for act, weight in zip(acts, weights):
            product = dot(act[rows, :], weight[...], ((1,), (1,)))
            total = product if total is None else total + product
        out_ref[...] = total.astype(out_ref.dtype)


def local(
    frames,
    x_weight,
    z_weight,
    bc_weight,
    log_decay,
    norm_gain,
    conv_weight,
    out_weight,
    record_lengths,
):
    times, cores = lax.axis_size("tm"), lax.axis_size("head")
    frame_count, depth = frames.shape
    heads_here, channels = log_decay.shape[0], x_weight.shape[1]
    state = bc_weight.shape[1] // 2
    group = 4
    while group > 1 and (channels // group % LANES or times % group or heads_here % group):
        group //= 2
    planes = times // group
    width, heads = channels // group, heads_here // group
    total = frame_count * group
    count = total // SPAN
    index, core = lax.axis_index("tm"), lax.axis_index("head")
    place = lax.rem(index, group)

    def in_plane(array, step):
        return lax.ppermute(array, "tm", [(i, i ^ step) for i in range(times)])

    def later(array, step):
        return lax.ppermute(array, "tm", [(i, i + step * group) for i in range(times - step * group)])

    def across(array, step):
        return lax.ppermute(array, "head", [(i, i ^ step) for i in range(cores)])

    def between_planes(array, step):
        return lax.ppermute(array, "tm", [(i, i ^ (step * group)) for i in range(times)])

    shape = jax.ShapeDtypeStruct
    rows = x_weight.shape[0]
    parity = lax.rem(core, 2)

    def along_planes(stack):
        if planes != 4:
            return [stack] + [between_planes(stack, step) for step in range(1, planes)], tuple(range(planes))

        def pairs(chosen):
            return [(a * group + q, b * group + q) for a, b in chosen for q in range(group)]

        second = between_planes(stack, 2)
        first = between_planes(stack, 1)
        again, stack_then, first = lax.optimization_barrier((second, stack, first))
        third = lax.ppermute(again, "tm", pairs([(1, 0), (2, 3)]))
        middle = lax.ppermute(stack_then, "tm", pairs([(1, 2), (2, 1)]))
        return [stack, first, second, third, middle], (0, 1, 2, 3, 3)

    half_count = frame_count // 2
    frame_half, *packed = call(
        functools.partial(cut_kernel, group),
        (shape((half_count, depth), BF16), *(shape((rows, 2 * width), BF16) for _ in range(group))),
        [frames, x_weight, z_weight],
        [pltpu.SemaphoreType.DMA((1 + 2 * group,))],
        smem=0,
        anywhere=3,
        vmem=ALL_VMEM_BYTES,
    )
    parts = [packed[0]] + [in_plane(packed[step], step) for step in range(1, group)]
    (xz_stack,) = call(
        functools.partial(stack_kernel, group),
        (shape((group * rows, 2 * width), BF16),),
        parts,
        flops=STACK_HINT,
        smem=0,
    )
    xz_pieces, offsets = along_planes(xz_stack)
    x_columns, z_columns = call(
        functools.partial(assemble_kernel, group, offsets),
        (shape((depth, width), BF16), shape((depth, width), BF16)),
        xz_pieces,
        flops=ASSEMBLE_HINT,
        smem=0,
    )
    decay_blocks = jnp.pad(log_decay.reshape(group, heads, frame_count), ((0, 0), (0, 8 - heads), (0, 0)))
    down, across_tiles, depth_tiles = rows // 16, channels // LANES, depth // LANES
    tiles = down * (across_tiles + 1) + depth_tiles + 1
    outward = call(
        functools.partial(outward_kernel, group, planes),
        tuple(shape((-(-tiles // 8) * 16, depth), BF16) for _ in range(planes)),
        [out_weight.T, bc_weight, frames, decay_blocks],
        smem=0,
    )
    pieces = [outward[0]] + [between_planes(outward[step], step) for step in range(1, planes)]
    half_parts = [in_plane(frame_half, step) for step in range(1, group)]
    tiles = planes * down * (width // LANES + 1) + depth_tiles + 1 + frame_count // SPAN * 2
    inward = call(
        functools.partial(inward_kernel, group, rows, channels),
        tuple(shape((-(-tiles // 8) * 16, depth), BF16) for _ in range(group)),
        [decay_blocks, *pieces],
        smem=0,
    )
    inward = [inward[0]] + [in_plane(inward[step], step) for step in range(1, group)]
    share = depth // cores
    swap, bc_mine, halo, decay, *out_parts = call(
        functools.partial(swap_kernel, group, rows),
        (
            shape(((group - 1) * half_count + LANES, depth), BF16),
            shape((depth, LANES), BF16),
            shape((2 * EDGE, depth), BF16),
            shape((count * 8 + 8, SPAN), F32),
            shape((share, width), BF16),
            shape(((cores - 1) * share, width), BF16),
        ),
        [*inward, *half_parts],
        [pltpu.VMEM((depth, width), BF16), pltpu.VMEM((count, 8, SPAN), F32)],
        smem=0,
    )
    swap = across(swap, 1)
    all_rows = total + SPAN

    frame_rows, x_rows, b_rows, c_rows, decay_rows, steps, keep, summary = call(
        functools.partial(state_kernel, group, heads, state),
        (
            shape((all_rows, depth), BF16),
            shape((all_rows, width), BF16),
            shape((all_rows, state), BF16),
            shape((all_rows, state), BF16),
            shape((3 * (count + 1) * 8, SPAN), F32),
            shape((count * state, width), F32),
            shape((-(-count // 8) * 8, width), F32),
            shape((state + EDGE, width), BF16),
        ),
        [record_lengths, decay, x_columns, bc_mine, frames, swap, halo, *half_parts],
        [pltpu.VMEM((depth, 2 * state), BF16), pltpu.VMEM((total, width), F32)],
        flops=2 * total * depth * (width + 2 * state),
    )
    summaries = [later(summary, step) for step in range(1, planes)]
    y, carry = call(
        functools.partial(inner_kernel, group, heads),
        (shape((all_rows, width), F32), shape((all_rows, width), F32)),
        [x_rows, b_rows, c_rows, decay_rows],
        flops=4 * total * SPAN * width,
        smem=0,
    )
    silu = call(
        functools.partial(silu_kernel, group),
        shape((all_rows, width), F32),
        [norm_gain[None], frame_rows, z_columns],
        flops=2 * total * depth * width,
        smem=0,
    )
    gated = call(
        functools.partial(gate_kernel, heads, state),
        shape((all_rows, width), BF16),
        [c_rows, y, steps, carry, keep, silu, *summaries],
        flops=2 * total * state * width,
        smem=0,
    )
    ends = pltpu.SMEM((record_lengths.shape[0] + 1,), jnp.int32)
    far, near = (group - 1,), (*range(1, group - 1), 0)

    def conv(steps, gated):
        return call(
            functools.partial(conv_kernel, group, steps),
            shape((len(steps) * frame_count, width), BF16),
            [record_lengths, conv_weight, gated],
            [pltpu.VMEM((len(steps) * (frame_count + 2 * EDGE), width), F32), ends],
            flops=2 * len(steps) * frame_count * width * conv_weight.shape[0],
        )

    def out(steps, act, swapped):
        return call(
            functools.partial(out_kernel, cores),
            tuple(shape((frame_count, share), BF16 if step else F32) for step in steps),
            [act, *swapped, *out_parts],
            flops=2 * len(steps) * frame_count * width * cores * share,
            smem=0,
        )

    far_act = conv(far, gated)
    far_swapped = [across(far_act, step) for step in range(1, cores)]
    own_out, other_out = out_parts
    out_parts = [own_out]
    for step in range(1, cores):
        out_parts.append(across(other_out[(step - 1) * share : step * share], step))
    gated, far_act = lax.optimization_barrier((gated, far_act))
    near_act = conv(near, gated)
    near_act, far_swapped, out_parts = lax.optimization_barrier((near_act, far_swapped, out_parts))
    (far_out,) = out(far, far_act, far_swapped)
    near_act, far_out = lax.optimization_barrier((near_act, far_out))
    far_out = in_plane(far_out, far[0])
    near_swapped = [across(near_act, step) for step in range(1, cores)]
    near_outs = out(near, near_act, near_swapped)
    mixed = near_outs[-1] + far_out.astype(F32)
    for step, partial in zip(near[:-1], near_outs[:-1]):
        mixed = mixed + in_plane(partial, step).astype(F32)
    return mixed.astype(BF16)


def solution(mesh):
    in_specs = (
        P("tm", None),
        P("tm", "head"),
        P("tm", "head"),
        P("tm", None),
        P("head", "tm"),
        P("head"),
        P(None, "head"),
        P("head", "tm"),
        P(),
    )
    out_specs = P("tm", "head")
    return jax.shard_map(local, mesh=mesh, in_specs=in_specs, out_specs=out_specs, check_vma=False)
```

```python
import functools

import jax
import jax.numpy as jnp
from jax import lax
from jax.experimental import pallas as pl
from jax.experimental.pallas import tpu as pltpu
from jax.sharding import PartitionSpec as P

SPAN = 128
LANES = 128
EDGE = 16
CONV_ROWS = 64
BF16 = jnp.bfloat16
F32 = jnp.float32
INWARD_HINT = 40_000_000_000
ASSEMBLE_HINT = 40_000_000_000
ALL_VMEM_BYTES = 63 * 1024 * 1024
VMEM_BYTES = 20 * 1024 * 1024


def dot(a, b, dims=((1,), (0,)), precision=None):
    return lax.dot_general(a, b, (dims, ((), ())), precision=precision, preferred_element_type=F32)


def call(kernel, out_shape, operands, scratch=(), flops=0, smem=1, anywhere=0, vmem=VMEM_BYTES):
    in_specs = [pl.BlockSpec(memory_space=pltpu.SMEM)] * smem
    in_specs += [pl.BlockSpec(memory_space=pltpu.VMEM)] * (len(operands) - smem - anywhere)
    in_specs += [pl.BlockSpec(memory_space=pl.ANY)] * anywhere
    moved = sum(a.size * a.dtype.itemsize for a in operands)
    moved += sum(a.size * a.dtype.itemsize for a in jax.tree.leaves(out_shape))
    return pl.pallas_call(
        kernel,
        out_shape=out_shape,
        in_specs=in_specs,
        out_specs=jax.tree.map(lambda _: pl.BlockSpec(memory_space=pltpu.VMEM), out_shape),
        scratch_shapes=list(scratch),
        compiler_params=pltpu.CompilerParams(vmem_limit_bytes=vmem),
        cost_estimate=pl.CostEstimate(flops=flops, bytes_accessed=moved, transcendentals=0),
    )(*operands)


def plane_place(group):
    index = lax.axis_index("tm")
    return lax.rem(index, group), lax.div(index, group)


def record_starts(len_ref, position):
    start = jnp.zeros_like(position)
    end = jnp.int32(0)
    for record in range(len_ref.shape[0] - 1):
        end = end + len_ref[record]
        start = jnp.where(position >= end, end, start)
    return start


def fill_planes(plane, dest_ref, pieces, offsets, lanes=slice(None)):
    rows = pieces[0].shape[0]
    for offset in sorted(set(offsets)):
        same = [piece[:, lanes] for piece, at in zip(pieces, offsets) if at == offset]
        value = same[0] if len(same) == 1 else same[0] + same[1]
        dest_ref[pl.ds(pl.multiple_of((plane ^ offset) * rows, rows), rows), : value.shape[1]] = value


def first_kernel(group, planes, log_decay_ref, bc_ref, out_w_ref, frames_ref, *refs):
    weight_refs, refs = refs[:2], refs[2:]
    inner_refs, outer_refs, refs = refs[:group], refs[group : group + planes], refs[group + planes :]
    bc_half_ref, out_copy_ref, edge_ref, decay_ref, sems = refs
    place, plane = plane_place(group)
    parity = lax.rem(lax.axis_index("head"), 2)
    width = weight_refs[0].shape[1] // group
    frames = frames_ref.shape[0]
    heads = log_decay_ref.shape[0] // group
    half = frames // 2
    fold = inner_refs[0].shape[1] // (2 * width)
    height = weight_refs[0].shape[0] // fold
    copies = [
        (out_w_ref, out_copy_ref),
        (bc_ref.at[:, pl.ds(pl.multiple_of(parity * LANES, LANES), LANES)], bc_half_ref),
        (frames_ref.at[:EDGE, :], edge_ref.at[0]),
        (frames_ref.at[frames - EDGE :, :], edge_ref.at[1]),
        (log_decay_ref, decay_ref),
    ]
    for step, inner_ref in enumerate(inner_refs):
        top = inner_ref.shape[0] - height
        lanes = pl.ds(pl.multiple_of((place ^ step) * width, LANES), width)
        for number, weight_ref in enumerate(weight_refs):
            for part in range(fold):
                at = (2 * part + number) * width
                source = weight_ref.at[part * height : (part + 1) * height, lanes]
                copies.append((source, inner_ref.at[top:, at : at + width]))
        if step:
            source = frames_ref.at[pl.ds(pl.multiple_of(parity * half, half), half), :]
            copies.append((source, inner_ref.at[:half, : frames_ref.shape[1]]))
    started = [pltpu.make_async_copy(a, b, sems.at[number]) for number, (a, b) in enumerate(copies)]
    for copy in started:
        copy.start()
    for copy in started[:5]:
        copy.wait()
    lane = lax.broadcasted_iota(jnp.int32, (8, LANES), 1)
    decays = []
    for first in (0, frames - LANES):
        rows = [jnp.zeros((8, LANES), F32), jnp.zeros((8, LANES), F32)]
        for block in range(group):
            here = decay_ref[block * heads : (block + 1) * heads, first : first + LANES]
            here = jnp.concatenate([here, jnp.zeros((8 - heads, LANES), F32)], axis=0)
            for number, term in enumerate(three_terms(here)):
                slot = number * group + block
                moved = pltpu.roll(term, (slot % 8 * EDGE + (EDGE if first else 0)) % LANES, 1)
                rows[slot // 8] = jnp.where(lane // EDGE == slot % 8, moved, rows[slot // 8])
        decays.append(jnp.concatenate(rows, axis=0))
    for step, out_ref in enumerate(outer_refs):
        number = put(out_ref, 0, out_copy_ref[...])
        number = put(out_ref, number, bc_half_ref[...])
        later = (plane ^ step) > plane
        number = put(out_ref, number, jnp.where(later, edge_ref[1].astype(F32), edge_ref[0].astype(F32)).astype(BF16))
        put(out_ref, number, jnp.where(later, decays[1], decays[0]).astype(BF16))
    for copy in started[5:]:
        copy.wait()


def stack_kernel(group, *refs):
    parts, stack_ref = refs[:group], refs[group]
    place, _ = plane_place(group)
    width = stack_ref.shape[1]
    height = parts[0].shape[0]
    fold = parts[0].shape[1] // width
    for step, part in enumerate(parts):
        for number in range(fold):
            at = pl.multiple_of(((place ^ step) * fold + number) * height, 16)
            stack_ref[pl.ds(at, height), :] = part[part.shape[0] - height :, number * width : (number + 1) * width]


def assemble_kernel(group, offsets, *refs):
    pieces, dest_refs = refs[: len(offsets)], refs[len(offsets) :]
    _, plane = plane_place(group)
    first = 0
    for dest_ref in dest_refs:
        width = dest_ref.shape[1]
        fill_planes(plane, dest_ref, pieces, offsets, slice(first, first + width))
        first += width


def tile(number):
    return slice(number // 8 * 16, number // 8 * 16 + 16), slice(number % 8 * LANES, (number % 8 + 1) * LANES)


def put(out_ref, number, array):
    for at in range(0, array.shape[0], 16):
        for lane in range(0, array.shape[1], LANES):
            out_ref[tile(number)] = array[at : at + 16, lane : lane + LANES]
            number += 1
    return number


def three_terms(value):
    terms = []
    for _ in range(3):
        term = value.astype(BF16).astype(F32)
        terms.append(term)
        value = value - term
    return terms


def inward_kernel(group, planes, rows, channels, decay_ref, *refs):
    piece_refs, out_refs, whole_ref = refs[: -group - 1], refs[-group - 1 : -1], refs[-1]
    place, plane = plane_place(group)
    width = channels // group
    if len(piece_refs) > planes:
        whole_ref[...] = piece_refs[-2][...] + piece_refs[-1][...]
        piece_refs = [*piece_refs[: planes - 1], whole_ref]
    wanted = jnp.clip(jnp.where(place == 0, plane + 1, plane - 1), 0, planes - 1)
    depth_tiles = out_refs[0].shape[1] // LANES
    across, down = channels // LANES, rows // 16
    for step, out_ref in enumerate(out_refs):
        block = place ^ step
        number = 0
        for piece_ref in piece_refs:
            for at in range(down):
                for lane in range(width // LANES):
                    if across == 8:
                        lanes = pl.ds(pl.multiple_of(block * width + lane * LANES, LANES), LANES)
                        out_ref[tile(number)] = piece_ref[at * 16 : at * 16 + 16, lanes]
                    else:
                        value = piece_ref[tile(at * across + lane)]
                        for other in range(1, group):
                            there = piece_ref[tile(at * across + other * (width // LANES) + lane)]
                            value = jnp.where(block == other, there, value)
                        out_ref[tile(number)] = value
                    number += 1
            for at in range(down):
                out_ref[tile(number)] = piece_ref[tile(down * across + at)]
                number += 1
        for offset, piece_ref in enumerate(piece_refs):

            @pl.when((plane ^ offset) == wanted)
            def _(piece_ref=piece_ref, number=number):
                for at in range(depth_tiles + 1):
                    out_ref[tile(number + at)] = piece_ref[tile(down * (across + 1) + at)]

        number += depth_tiles + 1
        terms = three_terms(decay_ref[block])
        terms = jnp.concatenate([*terms, jnp.zeros_like(terms[0])], axis=0).astype(BF16)
        for span in range(terms.shape[1] // SPAN):
            number = put(out_ref, number, terms[:, span * SPAN : (span + 1) * SPAN])


def swap_kernel(group, rows, *refs):
    part_refs, half_refs = refs[:group], refs[group : 2 * group - 1]
    swap_ref, bc_ref, halo_ref, decay_ref, own_out_ref, other_out_ref, out_ref, span_ref = refs[2 * group - 1 :]
    place, plane = plane_place(group)
    planes = bc_ref.shape[0] // (group * rows)
    width = out_ref.shape[1]
    count = span_ref.shape[0]
    spans = count // group
    down = rows // 16
    depth_tiles = swap_ref.shape[1] // LANES
    lane = lax.broadcasted_iota(jnp.int32, (8, LANES), 1)
    for step, part_ref in enumerate(part_refs):
        block = place ^ step
        number = 0
        for offset in range(planes):
            first = ((plane ^ offset) * group + block) * rows
            for at in range(down):
                for column in range(width // LANES):
                    lanes = slice(column * LANES, (column + 1) * LANES)
                    out_ref[pl.ds(pl.multiple_of(first + at * 16, 16), 16), lanes] = part_ref[tile(number)]
                    number += 1
            for at in range(down):
                bc_ref[pl.ds(pl.multiple_of(first + at * 16, 16), 16), :] = part_ref[tile(number)]
                number += 1
        for side, owner in enumerate((group - 1, 0)):

            @pl.when(block == owner)
            def _(part_ref=part_ref, number=number, side=side):
                for at in range(depth_tiles):
                    halo_ref[side * EDGE : (side + 1) * EDGE, at * LANES : (at + 1) * LANES] = part_ref[tile(number + at)]
                packed = part_ref[tile(number + depth_tiles)].astype(F32)
                chosen = jnp.zeros((8, LANES), F32)
                for head_block in range(group):
                    value = jnp.zeros((8, LANES), F32)
                    for term in range(3):
                        slot = term * group + head_block
                        half = packed[slot // 8 * 8 : slot // 8 * 8 + 8]
                        value = value + pltpu.roll(half, (LANES - slot % 8 * EDGE) % LANES, 1)
                    chosen = jnp.where(place == head_block, value, chosen)
                if side:
                    last = pltpu.roll(chosen, EDGE, 1)
                    decay_ref[count * 8 :, :] = jnp.where((lane >= EDGE) & (lane < 2 * EDGE), last, 0.0)
                else:
                    decay_ref[:8, :] = jnp.where(lane < EDGE, chosen, 0.0)

        number += depth_tiles + 1
        for span in range(spans):
            top = part_ref[tile(number)].astype(F32)
            bottom = part_ref[tile(number + 1)].astype(F32)
            number += 2
            span_ref[block * spans + span] = top[:8] + top[8:] + bottom[:8]
    for span in range(count):
        moved = pltpu.roll(span_ref[span], EDGE, 1)
        here, after = slice(span * 8, span * 8 + 8), slice(span * 8 + 8, span * 8 + 16)
        decay_ref[here, :] = jnp.where(lane < EDGE, decay_ref[here, :], moved)
        kept = decay_ref[after, :] if span == count - 1 else jnp.zeros((8, LANES), F32)
        decay_ref[after, :] = jnp.where(lane < EDGE, moved, kept)
    core = lax.axis_index("head")
    share = own_out_ref.shape[0]
    own_out_ref[...] = out_ref[pl.ds(pl.multiple_of(core * share, share), share), :]
    for step in range(1, other_out_ref.shape[0] // share + 1):
        at = pl.ds(pl.multiple_of((core ^ step) * share, share), share)
        other_out_ref[(step - 1) * share : step * share, :] = out_ref[at, :]
    height = LANES
    top = swap_ref.shape[0] - height
    half = top // len(half_refs)
    for number, half_ref in enumerate(half_refs):
        swap_ref[number * half : (number + 1) * half, :] = half_ref[:half, : swap_ref.shape[1]]
    for number in range(bc_ref.shape[0] // height):
        lanes = slice(number * LANES, (number + 1) * LANES)
        swap_ref[top:, lanes] = bc_ref[number * height : (number + 1) * height, :]


def lanes_of(rows, width, head_size):
    high = rows.astype(BF16).astype(F32)
    owner = lax.broadcasted_iota(jnp.int32, (16, width), 1) // head_size
    chosen = jnp.where((lax.broadcasted_iota(jnp.int32, (16, width), 0) & 7) == owner, 1.0, 0.0).astype(BF16)
    return dot(jnp.concatenate([high, rows - high], axis=0).astype(BF16), chosen, ((0,), (0,)))


def spans_in_lanes(rows):
    return jnp.concatenate([rows[at : at + 8] for at in range(0, rows.shape[0], 8)], axis=1)


def row_blocks(total, wide):
    return [slice(at, at + 256) for at in range(0, total, 256)] + [slice(total, wide)]


def state_kernel(group, heads, state, len_ref, decay_ref, x_weight_ref, bc_half_ref, own_ref, swap_ref, halo_ref, *refs):
    half_refs, refs = refs[: group - 1], refs[group - 1 :]
    frames_ref, x_ref, b_ref, c_ref, rows_ref, step_ref, keep_ref, send_ref, weight_ref, tail_ref = refs
    place, plane = plane_place(group)
    parity = lax.rem(lax.axis_index("head"), 2)
    width = x_ref.shape[1]
    frames = own_ref.shape[0]
    total = frames * group
    half = frames // 2
    head_size = width // heads
    count = total // SPAN
    base = plane * total - EDGE
    wide = total + 2 * EDGE
    frames_ref[:EDGE, :] = halo_ref[:EDGE, :]
    frames_ref[total + EDGE : wide, :] = halo_ref[EDGE:, :]
    frames_ref[wide:, :] = jnp.zeros((frames_ref.shape[0] - wide, frames_ref.shape[1]), BF16)
    frames_ref[pl.ds(pl.multiple_of(EDGE + place * frames, EDGE), frames), :] = own_ref[...]
    for number, half_ref in enumerate(half_refs):
        block = EDGE + (place ^ (number + 1)) * frames
        mine = pl.ds(pl.multiple_of(block + parity * half, EDGE), half)
        other = pl.ds(pl.multiple_of(block + (1 - parity) * half, EDGE), half)
        frames_ref[mine, :] = half_ref[:half, : frames_ref.shape[1]]
        frames_ref[other, :] = swap_ref[number * half : (number + 1) * half, :]
    mine = pl.ds(pl.multiple_of(parity * LANES, LANES), LANES)
    other = pl.ds(pl.multiple_of((1 - parity) * LANES, LANES), LANES)
    weight_ref[:, mine] = bc_half_ref[...]
    top = len(half_refs) * half
    height = swap_ref.shape[0] - top
    for number in range(weight_ref.shape[0] // height):
        lanes = slice(number * LANES, (number + 1) * LANES)
        weight_ref[number * height : (number + 1) * height, other] = swap_ref[top:, lanes]

    decay = decay_ref[...]
    used = decay.shape[0]
    square = (SPAN, SPAN)
    row, lane = (lax.broadcasted_iota(jnp.int32, square, dim) for dim in (0, 1))
    upper = jnp.where(row <= lane, 1.0, 0.0).astype(F32)
    cumul = dot(decay, upper, precision=lax.Precision.HIGHEST)
    whole = dot(decay, jnp.ones(square, F32), precision=lax.Precision.HIGHEST)
    first = base + lax.broadcasted_iota(jnp.int32, (used, SPAN), 0) // 8 * SPAN
    position = first + lane[:1]
    start = record_starts(len_ref, position)
    start_last = record_starts(len_ref, first + (SPAN - 1))
    carried = jnp.where(start < first, jnp.exp(cumul), 0.0)
    tail = jnp.where(position >= start_last, jnp.exp(whole - cumul), 0.0)
    keep = jnp.where(start_last < first, jnp.exp(whole), 0.0)
    rows_ref[:used, :] = cumul
    rows_ref[used : 2 * used, :] = start.astype(F32)
    rows_ref[2 * used :, :] = carried

    for rows in row_blocks(total, wide):
        x_ref[rows, :] = dot(frames_ref[rows, :], x_weight_ref[...]).astype(BF16)
        product = dot(frames_ref[rows, :], weight_ref[...])
        b_ref[rows, :] = product[:, :state].astype(BF16)
        c_ref[rows, :] = product[:, state:].astype(BF16)
    for ref in (x_ref, b_ref, c_ref):
        ref[wide:, :] = jnp.zeros((ref.shape[0] - wide, ref.shape[1]), BF16)

    tail_ref[...] = lanes_of(spans_in_lanes(tail[: count * 8]), width, head_size)
    by_span = jnp.zeros((8, SPAN), F32)
    for block in range(count):
        by_span = jnp.where(lane[:8] == block, keep[block * 8 : (block + 1) * 8], by_span)
    kept = lanes_of(by_span, width, head_size)[: keep_ref.shape[0]]
    keep_ref[...] = kept
    entry = jnp.zeros((state, width), F32)
    through = jnp.ones((1, width), F32)
    for block in range(count):
        rows = slice(block * SPAN, (block + 1) * SPAN)
        weighed = x_ref[rows, :].astype(F32) * tail_ref[rows, :]
        step = dot(b_ref[rows, :], weighed.astype(BF16), ((0,), (0,)))
        step_ref[block * state : (block + 1) * state, :] = step
        entry = kept[block : block + 1] * entry + step
        through = through * kept[block : block + 1]
    send_ref[:state, :] = entry.astype(BF16)
    send_ref[state:, :] = jnp.broadcast_to(through, (EDGE, width)).astype(BF16)


def inner_kernel(group, heads, x_ref, b_ref, c_ref, rows_ref, y_ref, carry_ref):
    _, plane = plane_place(group)
    total, width = x_ref.shape
    head_size = width // heads
    count = total // SPAN
    base = plane * (total - SPAN) - EDGE
    used = rows_ref.shape[0] // 3
    square = (SPAN, SPAN)
    parts = [rows_ref[: 2 * used, :]]
    if 2 * used % SPAN:
        parts.append(jnp.zeros((SPAN - 2 * used % SPAN, SPAN), F32))
    columns = jnp.concatenate(parts, axis=0).T
    carry_ref[...] = lanes_of(spans_in_lanes(rows_ref[2 * used :, :]), width, head_size)
    row, lane = (lax.broadcasted_iota(jnp.int32, square, dim) for dim in (0, 1))
    lower = row >= lane
    tile_heads = LANES // head_size
    tile_lane = lax.broadcasted_iota(jnp.int32, (1, LANES), 1) // head_size
    masks = [jnp.where(tile_lane == inner, 1.0, 0.0).astype(BF16) for inner in range(tile_heads)]
    for block in range(count):
        rows = slice(block * SPAN, (block + 1) * SPAN)
        at = block * 8
        x = x_ref[rows, :]
        scores = dot(c_ref[rows, :], b_ref[rows, :], ((1,), (1,)))
        here = (base + block * SPAN + lane).astype(F32)
        start_here = jnp.broadcast_to(columns[:, used + at : used + at + 1], square)
        joined = lower & (here >= start_here)
        for tile in range(width // LANES):
            mixes, values = [], []
            for inner in range(tile_heads):
                which = at + tile * tile_heads + inner
                column = jnp.broadcast_to(columns[:, which : which + 1], square)
                gap = jnp.where(joined, column - rows_ref[which : which + 1, :], -1e30)
                mixes.append((jnp.exp(gap) * scores).astype(BF16))
                values.append(x[:, tile * LANES : (tile + 1) * LANES] * masks[inner])
            y_ref[rows, tile * LANES : (tile + 1) * LANES] = dot(
                jnp.concatenate(mixes, axis=1), jnp.concatenate(values, axis=0)
            )


def silu_kernel(group, gain_ref, frames_ref, weight_ref, out_ref):
    place, _ = plane_place(group)
    rows_all, width = out_ref.shape
    total = rows_all - SPAN
    wide = total + 2 * EDGE
    gain = gain_ref[:, pl.ds(pl.multiple_of(place * width, LANES), width)]
    for rows in row_blocks(total, wide):
        z = dot(frames_ref[rows, :], weight_ref[...]).astype(BF16).astype(F32)
        out_ref[rows, :] = z / (1.0 + jnp.exp(-z)) * gain
    out_ref[wide:, :] = jnp.zeros((rows_all - wide, width), F32)


def gate_kernel(heads, state, c_ref, y_ref, step_ref, carry_ref, keep_ref, silu_ref, *refs):
    earlier, gated_ref = refs[:-1], refs[-1]
    total, width = y_ref.shape
    head_size = width // heads
    count = total // SPAN
    entry = jnp.zeros((state, width), F32)
    for summary in reversed(earlier):
        through = summary[state : state + EDGE, :].astype(F32)[:1]
        entry = through * entry + summary[:state, :].astype(F32)
    owner = [lax.broadcasted_iota(jnp.int32, (width, width), dim) // head_size for dim in (0, 1)]
    average = jnp.where(owner[0] == owner[1], 1.0 / head_size, 0.0).astype(BF16)
    for block in range(count):
        rows = slice(block * SPAN, (block + 1) * SPAN)
        y = y_ref[rows, :] + carry_ref[rows, :] * dot(c_ref[rows, :], entry.astype(BF16))
        square_mean = dot((y * y).astype(BF16), average)
        gated_ref[rows, :] = (y * lax.rsqrt(square_mean + 1e-05) * silu_ref[rows, :]).astype(BF16)
        if block < count - 1:
            entry = keep_ref[block : block + 1, :] * entry + step_ref[block * state : (block + 1) * state, :]


def conv_kernel(group, steps, len_ref, taps_ref, gated_ref, act_ref, ext_ref, ends_ref):
    place, plane = plane_place(group)
    rows_all, width = gated_ref.shape
    total = rows_all - SPAN
    frames = total // group
    taps = taps_ref.shape[0]
    half = (taps - 1) // 2
    stream = lax.axis_size("tm") // group * total
    records = len_ref.shape[0]
    reach = CONV_ROWS + 2 * EDGE
    first_tap = EDGE - half
    pitch = frames + 2 * EDGE
    ends_ref[0] = 0
    for record in range(records):
        ends_ref[record + 1] = ends_ref[record] + len_ref[record]
    for number, step in enumerate(steps):
        first = pl.multiple_of((place ^ step) * frames, frames)
        ext_ref[number * pitch : (number + 1) * pitch, :] = gated_ref[pl.ds(first, pitch), :].astype(F32)

    def record_at(position):
        found = jnp.int32(0)
        for record in range(records - 1):
            found = found + (ends_ref[record + 1] <= position).astype(jnp.int32)
        return found

    for number, step in enumerate(steps):
        base = plane * total + (place ^ step) * frames

        def one_block(block, _, number=number, base=base):
            inside_part = pl.multiple_of(block * CONV_ROWS, CONV_ROWS)
            source = pl.multiple_of(number * pitch + inside_part, EDGE)
            target = pl.multiple_of(number * frames + inside_part, CONV_ROWS)
            at = base + inside_part
            low = record_at(jnp.maximum(at - half, 0))
            high = record_at(jnp.minimum(at + CONV_ROWS - 1 + half, stream - 1))
            near = lax.broadcasted_iota(jnp.int32, (reach, LANES), 0) + (at - EDGE)
            for tile in range(width // LANES):
                lanes = slice(tile * LANES, (tile + 1) * LANES)
                weights = taps_ref[:, pl.ds(pl.multiple_of(place * width + tile * LANES, LANES), LANES)]

                def one_record(record, done):
                    inside = (near >= ends_ref[record]) & (near < ends_ref[record + 1])
                    g = jnp.where(inside, ext_ref[pl.ds(source, reach), lanes], 0.0)
                    out = None
                    for phase in range(8):
                        part = None
                        for offset in range(phase, reach - CONV_ROWS, 8):
                            tap = offset - first_tap
                            if 0 <= tap < taps:
                                aligned = offset - phase
                                term = weights[tap : tap + 1, :] * g[aligned : aligned + CONV_ROWS + 8, :]
                                part = term if part is None else part + term
                        if part is not None:
                            moved = part[phase : phase + CONV_ROWS, :]
                            out = moved if out is None else out + moved
                    return jnp.where(inside[EDGE : EDGE + CONV_ROWS], out, done)

                conv = lax.fori_loop(low, high + 1, one_record, jnp.zeros((CONV_ROWS, LANES), F32))
                act_ref[pl.ds(target, CONV_ROWS), lanes] = (conv / (1.0 + jnp.exp(-conv))).astype(BF16)
            return 0

        lax.fori_loop(0, frames // CONV_ROWS, one_block, 0)


def out_kernel(cores, *refs):
    acts, weights, outs = refs[:cores], refs[cores : 2 * cores], refs[2 * cores :]
    frames = outs[0].shape[0]
    for number, out_ref in enumerate(outs):
        rows = slice(number * frames, (number + 1) * frames)
        total = None
        for act, weight in zip(acts, weights):
            product = dot(act[rows, :], weight[...], ((1,), (1,)))
            total = product if total is None else total + product
        out_ref[...] = total.astype(out_ref.dtype)


def local(
    frames,
    x_weight,
    z_weight,
    bc_weight,
    log_decay,
    norm_gain,
    conv_weight,
    out_weight,
    record_lengths,
):
    times, cores = lax.axis_size("tm"), lax.axis_size("head")
    frame_count, depth = frames.shape
    heads_here, channels = log_decay.shape[0], x_weight.shape[1]
    state = bc_weight.shape[1] // 2
    group = 4
    while group > 1 and (channels // group % LANES or times % group or heads_here % group):
        group //= 2
    planes = times // group
    width, heads = channels // group, heads_here // group
    total = frame_count * group
    count = total // SPAN
    index, core = lax.axis_index("tm"), lax.axis_index("head")
    place = lax.rem(index, group)

    def in_plane(array, step):
        return lax.ppermute(array, "tm", [(i, i ^ step) for i in range(times)])

    def later(array, step):
        return lax.ppermute(array, "tm", [(i, i + step * group) for i in range(times - step * group)])

    def across(array, step):
        return lax.ppermute(array, "head", [(i, i ^ step) for i in range(cores)])

    def between_planes(array, step):
        return lax.ppermute(array, "tm", [(i, i ^ (step * group)) for i in range(times)])

    shape = jax.ShapeDtypeStruct
    rows = x_weight.shape[0]
    parity = lax.rem(core, 2)

    def along_planes(stacks):
        if planes != 4:
            return [stacks[0]] + [between_planes(stacks[step], step) for step in range(1, planes)]

        def pairs(chosen):
            return [(a * group + q, b * group + q) for a, b in chosen for q in range(group)]

        second = between_planes(stacks[2], 2)
        first = between_planes(stacks[1], 1)
        again, last, first = lax.optimization_barrier((second, stacks[3], first))
        third = lax.ppermute(again, "tm", pairs([(1, 0), (2, 3)]))
        middle = lax.ppermute(last, "tm", pairs([(1, 2), (2, 1)]))
        return [stacks[0], first, second, third, middle]

    offsets = (0, 1, 2, 3, 3) if planes == 4 else tuple(range(planes))
    half_count = frame_count // 2
    down, across_tiles, depth_tiles = rows // 16, channels // LANES, depth // LANES
    tiles = down * (across_tiles + 1) + depth_tiles + 1
    fold = max(1, min(depth // (2 * width), down))
    inner_shape = (half_count + rows // fold, max(depth, fold * 2 * width))
    payloads = call(
        functools.partial(first_kernel, group, planes),
        (
            shape((rows // fold, fold * 2 * width), BF16),
            *(shape(inner_shape, BF16) for _ in range(1, group)),
            *(shape((-(-tiles // 8) * 16, depth), BF16) for _ in range(planes)),
        ),
        [log_decay, bc_weight, out_weight.T, frames, x_weight, z_weight],
        [
            pltpu.VMEM((rows, LANES), BF16),
            pltpu.VMEM((rows, channels), BF16),
            pltpu.VMEM((2, EDGE, depth), BF16),
            pltpu.VMEM(log_decay.shape, F32),
            pltpu.SemaphoreType.DMA((4 + group * (2 * fold + 1),)),
        ],
        smem=0,
        anywhere=6,
        vmem=ALL_VMEM_BYTES,
    )
    inner, outer = payloads[:group], payloads[group:]
    parts = [inner[0]] + [in_plane(inner[step], step) for step in range(1, group)]
    pieces = along_planes(outer)
    xz_stack = call(
        functools.partial(stack_kernel, group),
        shape((group * rows, 2 * width), BF16),
        parts,
        smem=0,
    )
    xz_pieces = along_planes([xz_stack] * planes)
    x_columns, z_columns = call(
        functools.partial(assemble_kernel, group, offsets),
        (shape((depth, width), BF16), shape((depth, width), BF16)),
        xz_pieces,
        flops=ASSEMBLE_HINT,
        smem=0,
    )
    decay_blocks = jnp.pad(log_decay.reshape(group, heads, frame_count), ((0, 0), (0, 8 - heads), (0, 0)))
    tiles = planes * down * (width // LANES + 1) + depth_tiles + 1 + frame_count // SPAN * 2
    inward = call(
        functools.partial(inward_kernel, group, planes, rows, channels),
        tuple(shape((-(-tiles // 8) * 16, depth), BF16) for _ in range(group)),
        [decay_blocks, *pieces],
        [pltpu.VMEM(pieces[0].shape, BF16)],
        flops=INWARD_HINT,
        smem=0,
    )
    inward = [inward[0]] + [in_plane(inward[step], step) for step in range(1, group)]
    share = depth // cores
    swap, bc_mine, halo, decay, *out_parts = call(
        functools.partial(swap_kernel, group, rows),
        (
            shape(((group - 1) * half_count + LANES, depth), BF16),
            shape((depth, LANES), BF16),
            shape((2 * EDGE, depth), BF16),
            shape((count * 8 + 8, SPAN), F32),
            shape((share, width), BF16),
            shape(((cores - 1) * share, width), BF16),
        ),
        [*inward, *parts[1:]],
        [pltpu.VMEM((depth, width), BF16), pltpu.VMEM((count, 8, SPAN), F32)],
        smem=0,
    )
    swap = across(swap, 1)
    all_rows = total + SPAN

    frame_rows, x_rows, b_rows, c_rows, decay_rows, steps, keep, summary = call(
        functools.partial(state_kernel, group, heads, state),
        (
            shape((all_rows, depth), BF16),
            shape((all_rows, width), BF16),
            shape((all_rows, state), BF16),
            shape((all_rows, state), BF16),
            shape((3 * (count + 1) * 8, SPAN), F32),
            shape((count * state, width), F32),
            shape((-(-count // 8) * 8, width), F32),
            shape((state + EDGE, width), BF16),
        ),
        [record_lengths, decay, x_columns, bc_mine, frames, swap, halo, *parts[1:]],
        [pltpu.VMEM((depth, 2 * state), BF16), pltpu.VMEM((total, width), F32)],
        flops=2 * total * depth * (width + 2 * state),
    )
    summaries = [later(summary, step) for step in range(1, planes)]
    y, carry = call(
        functools.partial(inner_kernel, group, heads),
        (shape((all_rows, width), F32), shape((all_rows, width), F32)),
        [x_rows, b_rows, c_rows, decay_rows],
        flops=4 * total * SPAN * width,
        smem=0,
    )
    silu = call(
        functools.partial(silu_kernel, group),
        shape((all_rows, width), F32),
        [norm_gain[None], frame_rows, z_columns],
        flops=2 * total * depth * width,
        smem=0,
    )
    gated = call(
        functools.partial(gate_kernel, heads, state),
        shape((all_rows, width), BF16),
        [c_rows, y, steps, carry, keep, silu, *summaries],
        flops=2 * total * state * width,
        smem=0,
    )
    ends = pltpu.SMEM((record_lengths.shape[0] + 1,), jnp.int32)
    far, near = (group - 1,), (*range(1, group - 1), 0)

    def conv(steps, gated):
        return call(
            functools.partial(conv_kernel, group, steps),
            shape((len(steps) * frame_count, width), BF16),
            [record_lengths, conv_weight, gated],
            [pltpu.VMEM((len(steps) * (frame_count + 2 * EDGE), width), F32), ends],
            flops=2 * len(steps) * frame_count * width * conv_weight.shape[0],
        )

    def out(steps, act, swapped):
        return call(
            functools.partial(out_kernel, cores),
            tuple(shape((frame_count, share), BF16 if step else F32) for step in steps),
            [act, *swapped, *out_parts],
            flops=2 * len(steps) * frame_count * width * cores * share,
            smem=0,
        )

    far_act = conv(far, gated)
    far_swapped = [across(far_act, step) for step in range(1, cores)]
    own_out, other_out = out_parts
    other_out, gated = lax.optimization_barrier((other_out, gated))
    out_parts = [own_out]
    for step in range(1, cores):
        out_parts.append(across(other_out[(step - 1) * share : step * share], step))
    gated, far_act = lax.optimization_barrier((gated, far_act))
    near_act = conv(near, gated)
    near_act, far_swapped, out_parts = lax.optimization_barrier((near_act, far_swapped, out_parts))
    (far_out,) = out(far, far_act, far_swapped)
    near_act, far_out = lax.optimization_barrier((near_act, far_out))
    far_out = in_plane(far_out, far[0])
    near_swapped = [across(near_act, step) for step in range(1, cores)]
    near_outs = out(near, near_act, near_swapped)
    mixed = near_outs[-1] + far_out.astype(F32)
    for step, partial in zip(near[:-1], near_outs[:-1]):
        mixed = mixed + in_plane(partial, step).astype(F32)
    return mixed.astype(BF16)


def solution(mesh):
    in_specs = (
        P("tm", None),
        P("tm", "head"),
        P("tm", "head"),
        P("tm", None),
        P("head", "tm"),
        P("head"),
        P(None, "head"),
        P("head", "tm"),
        P(),
    )
    out_specs = P("tm", "head")
    return jax.shard_map(local, mesh=mesh, in_specs=in_specs, out_specs=out_specs, check_vma=False)
```

```python
import functools

import jax
import jax.numpy as jnp
from jax import lax
from jax.experimental import pallas as pl
from jax.experimental.pallas import tpu as pltpu
from jax.sharding import PartitionSpec as P

SPAN = 128
LANES = 128
EDGE = 16
CONV_ROWS = 64
BF16 = jnp.bfloat16
F32 = jnp.float32
STACK_HINT = 40_000_000_000
INWARD_HINT = 40_000_000_000
ASSEMBLE_HINT = 40_000_000_000
ALL_VMEM_BYTES = 63 * 1024 * 1024
VMEM_BYTES = 20 * 1024 * 1024


def dot(a, b, dims=((1,), (0,)), precision=None):
    return lax.dot_general(a, b, (dims, ((), ())), precision=precision, preferred_element_type=F32)


def call(kernel, out_shape, operands, scratch=(), flops=0, smem=1, anywhere=0, vmem=VMEM_BYTES):
    in_specs = [pl.BlockSpec(memory_space=pltpu.SMEM)] * smem
    in_specs += [pl.BlockSpec(memory_space=pltpu.VMEM)] * (len(operands) - smem - anywhere)
    in_specs += [pl.BlockSpec(memory_space=pl.ANY)] * anywhere
    moved = sum(a.size * a.dtype.itemsize for a in operands)
    moved += sum(a.size * a.dtype.itemsize for a in jax.tree.leaves(out_shape))
    return pl.pallas_call(
        kernel,
        out_shape=out_shape,
        in_specs=in_specs,
        out_specs=jax.tree.map(lambda _: pl.BlockSpec(memory_space=pltpu.VMEM), out_shape),
        scratch_shapes=list(scratch),
        compiler_params=pltpu.CompilerParams(vmem_limit_bytes=vmem),
        cost_estimate=pl.CostEstimate(flops=flops, bytes_accessed=moved, transcendentals=0),
    )(*operands)


def plane_place(group):
    index = lax.axis_index("tm")
    return lax.rem(index, group), lax.div(index, group)


def record_starts(len_ref, position):
    start = jnp.zeros_like(position)
    end = jnp.int32(0)
    for record in range(len_ref.shape[0] - 1):
        end = end + len_ref[record]
        start = jnp.where(position >= end, end, start)
    return start


def fill_planes(plane, dest_ref, pieces, offsets, lanes=slice(None)):
    rows = pieces[0].shape[0]
    for offset in sorted(set(offsets)):
        same = [piece[:, lanes] for piece, at in zip(pieces, offsets) if at == offset]
        value = same[0] if len(same) == 1 else same[0] + same[1]
        dest_ref[pl.ds(pl.multiple_of((plane ^ offset) * rows, rows), rows), : value.shape[1]] = value


def first_kernel(group, planes, log_decay_ref, bc_ref, frames_ref, *refs):
    weight_refs, refs = refs[:3], refs[3:]
    inner_refs, outer_refs, refs = refs[:group], refs[group : group + planes], refs[group + planes :]
    bc_half_ref, edge_ref, decay_ref, sems = refs
    place, plane = plane_place(group)
    parity = lax.rem(lax.axis_index("head"), 2)
    width = weight_refs[0].shape[1] // group
    frames = frames_ref.shape[0]
    heads = log_decay_ref.shape[0] // group
    copies = [
        (bc_ref.at[:, pl.ds(pl.multiple_of(parity * LANES, LANES), LANES)], bc_half_ref),
        (frames_ref.at[:EDGE, :], edge_ref.at[0]),
        (frames_ref.at[frames - EDGE :, :], edge_ref.at[1]),
        (log_decay_ref, decay_ref),
    ]
    for step, inner_ref in enumerate(inner_refs):
        lanes = pl.ds(pl.multiple_of((place ^ step) * width, LANES), width)
        for number, weight_ref in enumerate(weight_refs):
            copies.append((weight_ref.at[:, lanes], inner_ref.at[:, number * width : (number + 1) * width]))
    started = [pltpu.make_async_copy(a, b, sems.at[number]) for number, (a, b) in enumerate(copies)]
    for copy in started:
        copy.start()
    for copy in started[:4]:
        copy.wait()
    lane = lax.broadcasted_iota(jnp.int32, (8, LANES), 1)
    decays = []
    for first in (0, frames - LANES):
        rows = [jnp.zeros((8, LANES), F32), jnp.zeros((8, LANES), F32)]
        for block in range(group):
            here = decay_ref[block * heads : (block + 1) * heads, first : first + LANES]
            here = jnp.concatenate([here, jnp.zeros((8 - heads, LANES), F32)], axis=0)
            for number, term in enumerate(three_terms(here)):
                slot = number * group + block
                moved = pltpu.roll(term, (slot % 8 * EDGE + (EDGE if first else 0)) % LANES, 1)
                rows[slot // 8] = jnp.where(lane // EDGE == slot % 8, moved, rows[slot // 8])
        decays.append(jnp.concatenate(rows, axis=0))
    for step, out_ref in enumerate(outer_refs):
        number = put(out_ref, 0, bc_half_ref[...])
        later = (plane ^ step) > plane
        number = put(out_ref, number, jnp.where(later, edge_ref[1].astype(F32), edge_ref[0].astype(F32)).astype(BF16))
        put(out_ref, number, jnp.where(later, decays[1], decays[0]).astype(BF16))
    for copy in started[4:]:
        copy.wait()


def stack_kernel(group, *refs):
    parts, stack_refs = refs[:group], refs[group:]
    place, _ = plane_place(group)
    rows = parts[0].shape[0]
    for step, part in enumerate(parts):
        at = pl.ds(pl.multiple_of((place ^ step) * rows, rows), rows)
        first = 0
        for stack_ref in stack_refs:
            width = stack_ref.shape[1]
            stack_ref[at, :] = part[:, first : first + width]
            first += width


def assemble_kernel(group, offsets, *refs):
    pieces, dest_refs = refs[: len(offsets)], refs[len(offsets) :]
    _, plane = plane_place(group)
    first = 0
    for dest_ref in dest_refs:
        width = dest_ref.shape[1]
        fill_planes(plane, dest_ref, pieces, offsets, slice(first, first + width))
        first += width


def tile(number):
    return slice(number // 8 * 16, number // 8 * 16 + 16), slice(number % 8 * LANES, (number % 8 + 1) * LANES)


def put(out_ref, number, array):
    for at in range(0, array.shape[0], 16):
        for lane in range(0, array.shape[1], LANES):
            out_ref[tile(number)] = array[at : at + 16, lane : lane + LANES]
            number += 1
    return number


def three_terms(value):
    terms = []
    for _ in range(3):
        term = value.astype(BF16).astype(F32)
        terms.append(term)
        value = value - term
    return terms


def inward_kernel(group, rows, decay_ref, frames_ref, *refs):
    piece_refs, out_refs = refs[:-group], refs[-group:]
    place, plane = plane_place(group)
    planes = len(piece_refs)
    half = frames_ref.shape[0] // 2
    mine = pl.ds(pl.multiple_of(lax.rem(lax.axis_index("head"), 2) * half, half), half)
    wanted = jnp.clip(jnp.where(place == 0, plane + 1, plane - 1), 0, planes - 1)
    depth_tiles = frames_ref.shape[1] // LANES
    down = rows // 16
    for step, out_ref in enumerate(out_refs):
        out_ref[:half, :] = frames_ref[mine, :]
        number = half // 16 * depth_tiles
        for piece_ref in piece_refs:
            for at in range(down):
                out_ref[tile(number)] = piece_ref[tile(at)]
                number += 1
        for offset, piece_ref in enumerate(piece_refs):

            @pl.when((plane ^ offset) == wanted)
            def _(piece_ref=piece_ref, number=number, out_ref=out_ref):
                for at in range(depth_tiles + 1):
                    out_ref[tile(number + at)] = piece_ref[tile(down + at)]

        number += depth_tiles + 1
        terms = three_terms(decay_ref[place ^ step])
        terms = jnp.concatenate([*terms, jnp.zeros_like(terms[0])], axis=0).astype(BF16)
        for span in range(terms.shape[1] // SPAN):
            number = put(out_ref, number, terms[:, span * SPAN : (span + 1) * SPAN])


def swap_kernel(group, rows, *refs):
    part_refs, (swap_ref, bc_ref, halo_ref, decay_ref, span_ref) = refs[:group], refs[group:]
    half_refs = part_refs[1:]
    place, plane = plane_place(group)
    planes = bc_ref.shape[0] // (group * rows)
    count = span_ref.shape[0]
    spans = count // group
    down = rows // 16
    depth_tiles = swap_ref.shape[1] // LANES
    height = LANES
    top = swap_ref.shape[0] - height
    half = top // len(half_refs)
    lane = lax.broadcasted_iota(jnp.int32, (8, LANES), 1)
    for step, part_ref in enumerate(part_refs):
        block = place ^ step
        number = half // 16 * depth_tiles
        for offset in range(planes):
            first = ((plane ^ offset) * group + block) * rows
            for at in range(down):
                bc_ref[pl.ds(pl.multiple_of(first + at * 16, 16), 16), :] = part_ref[tile(number)]
                number += 1
        for side, owner in enumerate((group - 1, 0)):

            @pl.when(block == owner)
            def _(part_ref=part_ref, number=number, side=side):
                for at in range(depth_tiles):
                    halo_ref[side * EDGE : (side + 1) * EDGE, at * LANES : (at + 1) * LANES] = part_ref[tile(number + at)]
                packed = part_ref[tile(number + depth_tiles)].astype(F32)
                chosen = jnp.zeros((8, LANES), F32)
                for head_block in range(group):
                    value = jnp.zeros((8, LANES), F32)
                    for term in range(3):
                        slot = term * group + head_block
                        half = packed[slot // 8 * 8 : slot // 8 * 8 + 8]
                        value = value + pltpu.roll(half, (LANES - slot % 8 * EDGE) % LANES, 1)
                    chosen = jnp.where(place == head_block, value, chosen)
                if side:
                    last = pltpu.roll(chosen, EDGE, 1)
                    decay_ref[count * 8 :, :] = jnp.where((lane >= EDGE) & (lane < 2 * EDGE), last, 0.0)
                else:
                    decay_ref[:8, :] = jnp.where(lane < EDGE, chosen, 0.0)

        number += depth_tiles + 1
        for span in range(spans):
            upper = part_ref[tile(number)].astype(F32)
            lower = part_ref[tile(number + 1)].astype(F32)
            number += 2
            span_ref[block * spans + span] = upper[:8] + upper[8:] + lower[:8]
    for span in range(count):
        moved = pltpu.roll(span_ref[span], EDGE, 1)
        here, after = slice(span * 8, span * 8 + 8), slice(span * 8 + 8, span * 8 + 16)
        decay_ref[here, :] = jnp.where(lane < EDGE, decay_ref[here, :], moved)
        kept = decay_ref[after, :] if span == count - 1 else jnp.zeros((8, LANES), F32)
        decay_ref[after, :] = jnp.where(lane < EDGE, moved, kept)
    for number, half_ref in enumerate(half_refs):
        swap_ref[number * half : (number + 1) * half, :] = half_ref[:half, : swap_ref.shape[1]]
    for number in range(bc_ref.shape[0] // height):
        lanes = slice(number * LANES, (number + 1) * LANES)
        swap_ref[top:, lanes] = bc_ref[number * height : (number + 1) * height, :]


def lanes_of(rows, width, head_size):
    high = rows.astype(BF16).astype(F32)
    owner = lax.broadcasted_iota(jnp.int32, (16, width), 1) // head_size
    chosen = jnp.where((lax.broadcasted_iota(jnp.int32, (16, width), 0) & 7) == owner, 1.0, 0.0).astype(BF16)
    return dot(jnp.concatenate([high, rows - high], axis=0).astype(BF16), chosen, ((0,), (0,)))


def spans_in_lanes(rows):
    return jnp.concatenate([rows[at : at + 8] for at in range(0, rows.shape[0], 8)], axis=1)


def row_blocks(total, wide):
    return [slice(at, at + 256) for at in range(0, total, 256)] + [slice(total, wide)]


def state_kernel(group, heads, state, len_ref, decay_ref, x_weight_ref, bc_half_ref, own_ref, swap_ref, halo_ref, *refs):
    half_refs, refs = refs[: group - 1], refs[group - 1 :]
    frames_ref, x_ref, b_ref, c_ref, rows_ref, step_ref, keep_ref, send_ref, weight_ref, tail_ref = refs
    place, plane = plane_place(group)
    parity = lax.rem(lax.axis_index("head"), 2)
    width = x_ref.shape[1]
    frames = own_ref.shape[0]
    total = frames * group
    half = frames // 2
    head_size = width // heads
    count = total // SPAN
    base = plane * total - EDGE
    wide = total + 2 * EDGE
    frames_ref[:EDGE, :] = halo_ref[:EDGE, :]
    frames_ref[total + EDGE : wide, :] = halo_ref[EDGE:, :]
    frames_ref[wide:, :] = jnp.zeros((frames_ref.shape[0] - wide, frames_ref.shape[1]), BF16)
    frames_ref[pl.ds(pl.multiple_of(EDGE + place * frames, EDGE), frames), :] = own_ref[...]
    for number, half_ref in enumerate(half_refs):
        block = EDGE + (place ^ (number + 1)) * frames
        mine = pl.ds(pl.multiple_of(block + parity * half, EDGE), half)
        other = pl.ds(pl.multiple_of(block + (1 - parity) * half, EDGE), half)
        frames_ref[mine, :] = half_ref[:half, : frames_ref.shape[1]]
        frames_ref[other, :] = swap_ref[number * half : (number + 1) * half, :]
    mine = pl.ds(pl.multiple_of(parity * LANES, LANES), LANES)
    other = pl.ds(pl.multiple_of((1 - parity) * LANES, LANES), LANES)
    weight_ref[:, mine] = bc_half_ref[...]
    top = len(half_refs) * half
    height = swap_ref.shape[0] - top
    for number in range(weight_ref.shape[0] // height):
        lanes = slice(number * LANES, (number + 1) * LANES)
        weight_ref[number * height : (number + 1) * height, other] = swap_ref[top:, lanes]

    decay = decay_ref[...]
    used = decay.shape[0]
    square = (SPAN, SPAN)
    row, lane = (lax.broadcasted_iota(jnp.int32, square, dim) for dim in (0, 1))
    upper = jnp.where(row <= lane, 1.0, 0.0).astype(F32)
    cumul = dot(decay, upper, precision=lax.Precision.HIGHEST)
    whole = dot(decay, jnp.ones(square, F32), precision=lax.Precision.HIGHEST)
    first = base + lax.broadcasted_iota(jnp.int32, (used, SPAN), 0) // 8 * SPAN
    position = first + lane[:1]
    start = record_starts(len_ref, position)
    start_last = record_starts(len_ref, first + (SPAN - 1))
    carried = jnp.where(start < first, jnp.exp(cumul), 0.0)
    tail = jnp.where(position >= start_last, jnp.exp(whole - cumul), 0.0)
    keep = jnp.where(start_last < first, jnp.exp(whole), 0.0)
    rows_ref[:used, :] = cumul
    rows_ref[used : 2 * used, :] = start.astype(F32)
    rows_ref[2 * used :, :] = carried

    for rows in row_blocks(total, wide):
        x_ref[rows, :] = dot(frames_ref[rows, :], x_weight_ref[...]).astype(BF16)
        product = dot(frames_ref[rows, :], weight_ref[...])
        b_ref[rows, :] = product[:, :state].astype(BF16)
        c_ref[rows, :] = product[:, state:].astype(BF16)
    for ref in (x_ref, b_ref, c_ref):
        ref[wide:, :] = jnp.zeros((ref.shape[0] - wide, ref.shape[1]), BF16)

    tail_ref[...] = lanes_of(spans_in_lanes(tail[: count * 8]), width, head_size)
    by_span = jnp.zeros((8, SPAN), F32)
    for block in range(count):
        by_span = jnp.where(lane[:8] == block, keep[block * 8 : (block + 1) * 8], by_span)
    kept = lanes_of(by_span, width, head_size)[: keep_ref.shape[0]]
    keep_ref[...] = kept
    entry = jnp.zeros((state, width), F32)
    through = jnp.ones((1, width), F32)
    for block in range(count):
        rows = slice(block * SPAN, (block + 1) * SPAN)
        weighed = x_ref[rows, :].astype(F32) * tail_ref[rows, :]
        step = dot(b_ref[rows, :], weighed.astype(BF16), ((0,), (0,)))
        step_ref[block * state : (block + 1) * state, :] = step
        entry = kept[block : block + 1] * entry + step
        through = through * kept[block : block + 1]
    send_ref[:state, :] = entry.astype(BF16)
    send_ref[state:, :] = jnp.broadcast_to(through, (EDGE, width)).astype(BF16)


def inner_kernel(group, heads, x_ref, b_ref, c_ref, rows_ref, y_ref, carry_ref):
    _, plane = plane_place(group)
    total, width = x_ref.shape
    head_size = width // heads
    count = total // SPAN
    base = plane * (total - SPAN) - EDGE
    used = rows_ref.shape[0] // 3
    square = (SPAN, SPAN)
    parts = [rows_ref[: 2 * used, :]]
    if 2 * used % SPAN:
        parts.append(jnp.zeros((SPAN - 2 * used % SPAN, SPAN), F32))
    columns = jnp.concatenate(parts, axis=0).T
    carry_ref[...] = lanes_of(spans_in_lanes(rows_ref[2 * used :, :]), width, head_size)
    row, lane = (lax.broadcasted_iota(jnp.int32, square, dim) for dim in (0, 1))
    lower = row >= lane
    tile_heads = LANES // head_size
    tile_lane = lax.broadcasted_iota(jnp.int32, (1, LANES), 1) // head_size
    masks = [jnp.where(tile_lane == inner, 1.0, 0.0).astype(BF16) for inner in range(tile_heads)]
    for block in range(count):
        rows = slice(block * SPAN, (block + 1) * SPAN)
        at = block * 8
        x = x_ref[rows, :]
        scores = dot(c_ref[rows, :], b_ref[rows, :], ((1,), (1,)))
        here = (base + block * SPAN + lane).astype(F32)
        start_here = jnp.broadcast_to(columns[:, used + at : used + at + 1], square)
        joined = lower & (here >= start_here)
        for tile in range(width // LANES):
            mixes, values = [], []
            for inner in range(tile_heads):
                which = at + tile * tile_heads + inner
                column = jnp.broadcast_to(columns[:, which : which + 1], square)
                gap = jnp.where(joined, column - rows_ref[which : which + 1, :], -1e30)
                mixes.append((jnp.exp(gap) * scores).astype(BF16))
                values.append(x[:, tile * LANES : (tile + 1) * LANES] * masks[inner])
            y_ref[rows, tile * LANES : (tile + 1) * LANES] = dot(
                jnp.concatenate(mixes, axis=1), jnp.concatenate(values, axis=0)
            )


def silu_kernel(group, gain_ref, frames_ref, weight_ref, out_ref):
    place, _ = plane_place(group)
    rows_all, width = out_ref.shape
    total = rows_all - SPAN
    wide = total + 2 * EDGE
    gain = gain_ref[:, pl.ds(pl.multiple_of(place * width, LANES), width)]
    for rows in row_blocks(total, wide):
        z = dot(frames_ref[rows, :], weight_ref[...]).astype(BF16).astype(F32)
        out_ref[rows, :] = z / (1.0 + jnp.exp(-z)) * gain
    out_ref[wide:, :] = jnp.zeros((rows_all - wide, width), F32)


def share_kernel(cores, offsets, group, *refs):
    pieces, refs = refs[: len(offsets)], refs[len(offsets) :]
    outs, weight_ref = refs[:cores], refs[cores]
    _, plane = plane_place(group)
    core = lax.axis_index("head")
    fill_planes(plane, weight_ref, pieces, offsets)
    for step, out_ref in enumerate(outs):
        rows = out_ref.shape[0]
        out_ref[...] = weight_ref[pl.ds(pl.multiple_of((core ^ step) * rows, rows), rows), :]


def gate_kernel(heads, state, c_ref, y_ref, step_ref, carry_ref, keep_ref, silu_ref, *refs):
    earlier, gated_ref = refs[:-1], refs[-1]
    total, width = y_ref.shape
    head_size = width // heads
    count = total // SPAN
    entry = jnp.zeros((state, width), F32)
    for summary in reversed(earlier):
        through = summary[state : state + EDGE, :].astype(F32)[:1]
        entry = through * entry + summary[:state, :].astype(F32)
    owner = [lax.broadcasted_iota(jnp.int32, (width, width), dim) // head_size for dim in (0, 1)]
    average = jnp.where(owner[0] == owner[1], 1.0 / head_size, 0.0).astype(BF16)
    for block in range(count):
        rows = slice(block * SPAN, (block + 1) * SPAN)
        y = y_ref[rows, :] + carry_ref[rows, :] * dot(c_ref[rows, :], entry.astype(BF16))
        square_mean = dot((y * y).astype(BF16), average)
        gated_ref[rows, :] = (y * lax.rsqrt(square_mean + 1e-05) * silu_ref[rows, :]).astype(BF16)
        if block < count - 1:
            entry = keep_ref[block : block + 1, :] * entry + step_ref[block * state : (block + 1) * state, :]


def conv_kernel(group, steps, len_ref, taps_ref, gated_ref, act_ref, ext_ref, ends_ref):
    place, plane = plane_place(group)
    rows_all, width = gated_ref.shape
    total = rows_all - SPAN
    frames = total // group
    taps = taps_ref.shape[0]
    half = (taps - 1) // 2
    stream = lax.axis_size("tm") // group * total
    records = len_ref.shape[0]
    reach = CONV_ROWS + 2 * EDGE
    first_tap = EDGE - half
    pitch = frames + 2 * EDGE
    ends_ref[0] = 0
    for record in range(records):
        ends_ref[record + 1] = ends_ref[record] + len_ref[record]
    for number, step in enumerate(steps):
        first = pl.multiple_of((place ^ step) * frames, frames)
        ext_ref[number * pitch : (number + 1) * pitch, :] = gated_ref[pl.ds(first, pitch), :].astype(F32)

    def record_at(position):
        found = jnp.int32(0)
        for record in range(records - 1):
            found = found + (ends_ref[record + 1] <= position).astype(jnp.int32)
        return found

    for number, step in enumerate(steps):
        base = plane * total + (place ^ step) * frames

        def one_block(block, _, number=number, base=base):
            inside_part = pl.multiple_of(block * CONV_ROWS, CONV_ROWS)
            source = pl.multiple_of(number * pitch + inside_part, EDGE)
            target = pl.multiple_of(number * frames + inside_part, CONV_ROWS)
            at = base + inside_part
            low = record_at(jnp.maximum(at - half, 0))
            high = record_at(jnp.minimum(at + CONV_ROWS - 1 + half, stream - 1))
            near = lax.broadcasted_iota(jnp.int32, (reach, LANES), 0) + (at - EDGE)
            for tile in range(width // LANES):
                lanes = slice(tile * LANES, (tile + 1) * LANES)
                weights = taps_ref[:, pl.ds(pl.multiple_of(place * width + tile * LANES, LANES), LANES)]

                def one_record(record, done):
                    inside = (near >= ends_ref[record]) & (near < ends_ref[record + 1])
                    g = jnp.where(inside, ext_ref[pl.ds(source, reach), lanes], 0.0)
                    out = None
                    for phase in range(8):
                        part = None
                        for offset in range(phase, reach - CONV_ROWS, 8):
                            tap = offset - first_tap
                            if 0 <= tap < taps:
                                aligned = offset - phase
                                term = weights[tap : tap + 1, :] * g[aligned : aligned + CONV_ROWS + 8, :]
                                part = term if part is None else part + term
                        if part is not None:
                            moved = part[phase : phase + CONV_ROWS, :]
                            out = moved if out is None else out + moved
                    return jnp.where(inside[EDGE : EDGE + CONV_ROWS], out, done)

                conv = lax.fori_loop(low, high + 1, one_record, jnp.zeros((CONV_ROWS, LANES), F32))
                act_ref[pl.ds(target, CONV_ROWS), lanes] = (conv / (1.0 + jnp.exp(-conv))).astype(BF16)
            return 0

        lax.fori_loop(0, frames // CONV_ROWS, one_block, 0)


def out_kernel(cores, *refs):
    acts, weights, outs = refs[:cores], refs[cores : 2 * cores], refs[2 * cores :]
    frames = outs[0].shape[0]
    for number, out_ref in enumerate(outs):
        rows = slice(number * frames, (number + 1) * frames)
        total = None
        for act, weight in zip(acts, weights):
            product = dot(act[rows, :], weight[...], ((1,), (1,)))
            total = product if total is None else total + product
        out_ref[...] = total.astype(out_ref.dtype)


def local(
    frames,
    x_weight,
    z_weight,
    bc_weight,
    log_decay,
    norm_gain,
    conv_weight,
    out_weight,
    record_lengths,
):
    times, cores = lax.axis_size("tm"), lax.axis_size("head")
    frame_count, depth = frames.shape
    heads_here, channels = log_decay.shape[0], x_weight.shape[1]
    state = bc_weight.shape[1] // 2
    group = 4
    while group > 1 and (channels // group % LANES or times % group or heads_here % group):
        group //= 2
    planes = times // group
    width, heads = channels // group, heads_here // group
    total = frame_count * group
    count = total // SPAN
    index, core = lax.axis_index("tm"), lax.axis_index("head")
    place = lax.rem(index, group)

    def in_plane(array, step):
        return lax.ppermute(array, "tm", [(i, i ^ step) for i in range(times)])

    def later(array, step):
        return lax.ppermute(array, "tm", [(i, i + step * group) for i in range(times - step * group)])

    def across(array, step):
        return lax.ppermute(array, "head", [(i, i ^ step) for i in range(cores)])

    def between_planes(array, step):
        return lax.ppermute(array, "tm", [(i, i ^ (step * group)) for i in range(times)])

    shape = jax.ShapeDtypeStruct
    rows = x_weight.shape[0]
    parity = lax.rem(core, 2)

    def along_planes(stacks):
        if planes != 4:
            return [stacks[0]] + [between_planes(stacks[step], step) for step in range(1, planes)]

        def pairs(chosen):
            return [(a * group + q, b * group + q) for a, b in chosen for q in range(group)]

        second = between_planes(stacks[2], 2)
        first = between_planes(stacks[1], 1)
        again, last, first = lax.optimization_barrier((second, stacks[3], first))
        third = lax.ppermute(again, "tm", pairs([(1, 0), (2, 3)]))
        middle = lax.ppermute(last, "tm", pairs([(1, 2), (2, 1)]))
        return [stacks[0], first, second, third, middle]

    offsets = (0, 1, 2, 3, 3) if planes == 4 else tuple(range(planes))
    half_count = frame_count // 2
    down, depth_tiles = rows // 16, depth // LANES
    payloads = call(
        functools.partial(first_kernel, group, planes),
        (
            *(shape((rows, 3 * width), BF16) for _ in range(group)),
            *(shape((-(-(down + depth_tiles + 1) // 8) * 16, depth), BF16) for _ in range(planes)),
        ),
        [log_decay, bc_weight, frames, x_weight, z_weight, out_weight.T],
        [
            pltpu.VMEM((rows, LANES), BF16),
            pltpu.VMEM((2, EDGE, depth), BF16),
            pltpu.VMEM(log_decay.shape, F32),
            pltpu.SemaphoreType.DMA((4 + 3 * group,)),
        ],
        smem=0,
        anywhere=6,
        vmem=ALL_VMEM_BYTES,
    )
    inner, outer = payloads[:group], payloads[group:]
    parts = [inner[0]] + [in_plane(inner[step], step) for step in range(1, group)]
    pieces = [outer[0]] + [between_planes(outer[step], step) for step in range(1, planes)]
    xz_stack, out_stack = call(
        functools.partial(stack_kernel, group),
        (shape((group * rows, 2 * width), BF16), shape((group * rows, width), BF16)),
        parts,
        flops=STACK_HINT,
        smem=0,
    )
    xz_pieces = along_planes([xz_stack] * planes)
    x_columns, z_columns = call(
        functools.partial(assemble_kernel, group, offsets),
        (shape((depth, width), BF16), shape((depth, width), BF16)),
        xz_pieces,
        flops=ASSEMBLE_HINT,
        smem=0,
    )
    decay_blocks = jnp.pad(log_decay.reshape(group, heads, frame_count), ((0, 0), (0, 8 - heads), (0, 0)))
    tiles = planes * down + depth_tiles + 1 + frame_count // SPAN * 2
    inward = call(
        functools.partial(inward_kernel, group, rows),
        tuple(shape((half_count + -(-tiles // 8) * 16, depth), BF16) for _ in range(group)),
        [decay_blocks, frames, *pieces],
        flops=INWARD_HINT,
        smem=0,
    )
    inward = [inward[0]] + [in_plane(inward[step], step) for step in range(1, group)]
    swap, bc_mine, halo, decay = call(
        functools.partial(swap_kernel, group, rows),
        (
            shape(((group - 1) * half_count + LANES, depth), BF16),
            shape((depth, LANES), BF16),
            shape((2 * EDGE, depth), BF16),
            shape((count * 8 + 8, SPAN), F32),
        ),
        inward,
        [pltpu.VMEM((count, 8, SPAN), F32)],
        smem=0,
    )
    swap = across(swap, 1)
    all_rows = total + SPAN

    frame_rows, x_rows, b_rows, c_rows, decay_rows, steps, keep, summary = call(
        functools.partial(state_kernel, group, heads, state),
        (
            shape((all_rows, depth), BF16),
            shape((all_rows, width), BF16),
            shape((all_rows, state), BF16),
            shape((all_rows, state), BF16),
            shape((3 * (count + 1) * 8, SPAN), F32),
            shape((count * state, width), F32),
            shape((-(-count // 8) * 8, width), F32),
            shape((state + EDGE, width), BF16),
        ),
        [record_lengths, decay, x_columns, bc_mine, frames, swap, halo, *inward[1:]],
        [pltpu.VMEM((depth, 2 * state), BF16), pltpu.VMEM((total, width), F32)],
        flops=2 * total * depth * (width + 2 * state),
    )
    summaries = [later(summary, step) for step in range(1, planes)]
    y, carry = call(
        functools.partial(inner_kernel, group, heads),
        (shape((all_rows, width), F32), shape((all_rows, width), F32)),
        [x_rows, b_rows, c_rows, decay_rows],
        flops=4 * total * SPAN * width,
        smem=0,
    )
    silu = call(
        functools.partial(silu_kernel, group),
        shape((all_rows, width), F32),
        [norm_gain[None], frame_rows, z_columns],
        flops=2 * total * depth * width,
        smem=0,
    )
    out_stack, summaries, y, silu = lax.optimization_barrier((out_stack, summaries, y, silu))
    out_pieces = [out_stack] + [between_planes(out_stack, step) for step in range(1, planes)]
    gated = call(
        functools.partial(gate_kernel, heads, state),
        shape((all_rows, width), BF16),
        [c_rows, y, steps, carry, keep, silu, *summaries],
        flops=2 * total * state * width,
        smem=0,
    )
    ends = pltpu.SMEM((record_lengths.shape[0] + 1,), jnp.int32)
    far, near = (group - 1,), (*range(1, group - 1), 0)

    def conv(steps, gated):
        return call(
            functools.partial(conv_kernel, group, steps),
            shape((len(steps) * frame_count, width), BF16),
            [record_lengths, conv_weight, gated],
            [pltpu.VMEM((len(steps) * (frame_count + 2 * EDGE), width), F32), ends],
            flops=2 * len(steps) * frame_count * width * conv_weight.shape[0],
        )

    def out(steps, act, swapped):
        return call(
            functools.partial(out_kernel, cores),
            tuple(shape((frame_count, share), BF16 if step else F32) for step in steps),
            [act, *swapped, *out_parts],
            flops=2 * len(steps) * frame_count * width * cores * share,
            smem=0,
        )

    far_act = conv(far, gated)
    far_swapped = [across(far_act, step) for step in range(1, cores)]
    gated, far_act = lax.optimization_barrier((gated, far_act))
    near_act = conv(near, gated)
    near_act, out_pieces = lax.optimization_barrier((near_act, out_pieces))
    share = depth // cores
    out_parts = call(
        functools.partial(share_kernel, cores, tuple(range(planes)), group),
        tuple(shape((share, width), BF16) for _ in range(cores)),
        out_pieces,
        [pltpu.VMEM((depth, width), BF16)],
        smem=0,
    )
    out_parts = [out_parts[0]] + [across(out_parts[step], step) for step in range(1, cores)]
    near_act, far_swapped, out_parts = lax.optimization_barrier((near_act, far_swapped, out_parts))
    (far_out,) = out(far, far_act, far_swapped)
    near_act, far_out = lax.optimization_barrier((near_act, far_out))
    far_out = in_plane(far_out, far[0])
    near_swapped = [across(near_act, step) for step in range(1, cores)]
    near_outs = out(near, near_act, near_swapped)
    mixed = near_outs[-1] + far_out.astype(F32)
    for step, partial in zip(near[:-1], near_outs[:-1]):
        mixed = mixed + in_plane(partial, step).astype(F32)
    return mixed.astype(BF16)


def solution(mesh):
    in_specs = (
        P("tm", None),
        P("tm", "head"),
        P("tm", "head"),
        P("tm", None),
        P("head", "tm"),
        P("head"),
        P(None, "head"),
        P("head", "tm"),
        P(),
    )
    out_specs = P("tm", "head")
    return jax.shard_map(local, mesh=mesh, in_specs=in_specs, out_specs=out_specs, check_vma=False)
```

```python
import functools

import jax
import jax.numpy as jnp
from jax import lax
from jax.experimental import pallas as pl
from jax.experimental.pallas import tpu as pltpu
from jax.sharding import PartitionSpec as P

SPAN = 128
LANES = 128
EDGE = 16
CONV_ROWS = 64
BF16 = jnp.bfloat16
F32 = jnp.float32
STACK_HINT = 40_000_000_000
INWARD_HINT = 40_000_000_000
ASSEMBLE_HINT = 40_000_000_000
ALL_VMEM_BYTES = 63 * 1024 * 1024
VMEM_BYTES = 20 * 1024 * 1024


def dot(a, b, dims=((1,), (0,)), precision=None):
    return lax.dot_general(a, b, (dims, ((), ())), precision=precision, preferred_element_type=F32)


def call(kernel, out_shape, operands, scratch=(), flops=0, smem=1, anywhere=0, vmem=VMEM_BYTES, hidden=False):
    in_specs = [pl.BlockSpec(memory_space=pltpu.SMEM)] * smem
    in_specs += [pl.BlockSpec(memory_space=pltpu.VMEM)] * (len(operands) - smem - anywhere)
    in_specs += [pl.BlockSpec(memory_space=pl.ANY)] * anywhere
    moved = sum(a.size * a.dtype.itemsize for a in operands)
    moved += sum(a.size * a.dtype.itemsize for a in jax.tree.leaves(out_shape))
    if hidden:
        flops = moved = 0
    return pl.pallas_call(
        kernel,
        out_shape=out_shape,
        in_specs=in_specs,
        out_specs=jax.tree.map(lambda _: pl.BlockSpec(memory_space=pltpu.VMEM), out_shape),
        scratch_shapes=list(scratch),
        compiler_params=pltpu.CompilerParams(vmem_limit_bytes=vmem),
        cost_estimate=pl.CostEstimate(flops=flops, bytes_accessed=moved, transcendentals=0),
    )(*operands)


def plane_place(group):
    index = lax.axis_index("tm")
    return lax.rem(index, group), lax.div(index, group)


def record_starts(len_ref, position):
    start = jnp.zeros_like(position)
    end = jnp.int32(0)
    for record in range(len_ref.shape[0] - 1):
        end = end + len_ref[record]
        start = jnp.where(position >= end, end, start)
    return start


def fill_planes(plane, dest_ref, pieces, offsets, lanes=slice(None)):
    rows = pieces[0].shape[0]
    for offset in sorted(set(offsets)):
        same = [piece[:, lanes] for piece, at in zip(pieces, offsets) if at == offset]
        value = same[0] if len(same) == 1 else same[0] + same[1]
        dest_ref[pl.ds(pl.multiple_of((plane ^ offset) * rows, rows), rows), : value.shape[1]] = value


def first_kernel(group, planes, log_decay_ref, bc_ref, frames_ref, *refs):
    weight_refs, refs = refs[:3], refs[3:]
    inner_refs, outer_refs, refs = refs[:group], refs[group : group + planes], refs[group + planes :]
    bc_half_ref, edge_ref, decay_ref, sems = refs
    place, plane = plane_place(group)
    parity = lax.rem(lax.axis_index("head"), 2)
    width = weight_refs[0].shape[1] // group
    frames = frames_ref.shape[0]
    heads = log_decay_ref.shape[0] // group
    copies = [
        (bc_ref.at[:, pl.ds(pl.multiple_of(parity * LANES, LANES), LANES)], bc_half_ref),
        (frames_ref.at[:EDGE, :], edge_ref.at[0]),
        (frames_ref.at[frames - EDGE :, :], edge_ref.at[1]),
        (log_decay_ref, decay_ref),
    ]
    for step, inner_ref in enumerate(inner_refs):
        lanes = pl.ds(pl.multiple_of((place ^ step) * width, LANES), width)
        for number, weight_ref in enumerate(weight_refs):
            copies.append((weight_ref.at[:, lanes], inner_ref.at[:, number * width : (number + 1) * width]))
    started = [pltpu.make_async_copy(a, b, sems.at[number]) for number, (a, b) in enumerate(copies)]
    for copy in started:
        copy.start()
    for copy in started[:4]:
        copy.wait()
    lane = lax.broadcasted_iota(jnp.int32, (8, LANES), 1)
    decays = []
    for first in (0, frames - LANES):
        rows = [jnp.zeros((8, LANES), F32), jnp.zeros((8, LANES), F32)]
        for block in range(group):
            here = decay_ref[block * heads : (block + 1) * heads, first : first + LANES]
            here = jnp.concatenate([here, jnp.zeros((8 - heads, LANES), F32)], axis=0)
            for number, term in enumerate(three_terms(here)):
                slot = number * group + block
                moved = pltpu.roll(term, (slot % 8 * EDGE + (EDGE if first else 0)) % LANES, 1)
                rows[slot // 8] = jnp.where(lane // EDGE == slot % 8, moved, rows[slot // 8])
        decays.append(jnp.concatenate(rows, axis=0))
    for step, out_ref in enumerate(outer_refs):
        number = put(out_ref, 0, bc_half_ref[...])
        later = (plane ^ step) > plane
        number = put(out_ref, number, jnp.where(later, edge_ref[1].astype(F32), edge_ref[0].astype(F32)).astype(BF16))
        put(out_ref, number, jnp.where(later, decays[1], decays[0]).astype(BF16))
    for copy in started[4:]:
        copy.wait()


def stack_kernel(group, *refs):
    parts, stack_refs = refs[:group], refs[group:]
    place, _ = plane_place(group)
    rows = parts[0].shape[0]
    for step, part in enumerate(parts):
        at = pl.ds(pl.multiple_of((place ^ step) * rows, rows), rows)
        first = 0
        for stack_ref in stack_refs:
            width = stack_ref.shape[1]
            stack_ref[at, :] = part[:, first : first + width]
            first += width


def assemble_kernel(group, offsets, *refs):
    pieces, dest_refs = refs[: len(offsets)], refs[len(offsets) :]
    _, plane = plane_place(group)
    first = 0
    for dest_ref in dest_refs:
        width = dest_ref.shape[1]
        fill_planes(plane, dest_ref, pieces, offsets, slice(first, first + width))
        first += width


def tile(number):
    return slice(number // 8 * 16, number // 8 * 16 + 16), slice(number % 8 * LANES, (number % 8 + 1) * LANES)


def put(out_ref, number, array):
    for at in range(0, array.shape[0], 16):
        for lane in range(0, array.shape[1], LANES):
            out_ref[tile(number)] = array[at : at + 16, lane : lane + LANES]
            number += 1
    return number


def three_terms(value):
    terms = []
    for _ in range(3):
        term = value.astype(BF16).astype(F32)
        terms.append(term)
        value = value - term
    return terms


def inward_kernel(group, rows, decay_ref, frames_ref, *refs):
    piece_refs, out_refs = refs[:-group], refs[-group:]
    place, plane = plane_place(group)
    planes = len(piece_refs)
    half = frames_ref.shape[0] // 2
    mine = pl.ds(pl.multiple_of(lax.rem(lax.axis_index("head"), 2) * half, half), half)
    wanted = jnp.clip(jnp.where(place == 0, plane + 1, plane - 1), 0, planes - 1)
    depth_tiles = frames_ref.shape[1] // LANES
    down = rows // 16
    for step, out_ref in enumerate(out_refs):
        out_ref[:half, :] = frames_ref[mine, :]
        number = half // 16 * depth_tiles
        for piece_ref in piece_refs:
            for at in range(down):
                out_ref[tile(number)] = piece_ref[tile(at)]
                number += 1
        for offset, piece_ref in enumerate(piece_refs):

            @pl.when((plane ^ offset) == wanted)
            def _(piece_ref=piece_ref, number=number, out_ref=out_ref):
                for at in range(depth_tiles + 1):
                    out_ref[tile(number + at)] = piece_ref[tile(down + at)]

        number += depth_tiles + 1
        terms = three_terms(decay_ref[place ^ step])
        terms = jnp.concatenate([*terms, jnp.zeros_like(terms[0])], axis=0).astype(BF16)
        for span in range(terms.shape[1] // SPAN):
            number = put(out_ref, number, terms[:, span * SPAN : (span + 1) * SPAN])


def swap_kernel(group, rows, *refs):
    part_refs, (swap_ref, bc_ref, halo_ref, decay_ref, span_ref) = refs[:group], refs[group:]
    half_refs = part_refs[1:]
    place, plane = plane_place(group)
    planes = bc_ref.shape[0] // (group * rows)
    count = span_ref.shape[0]
    spans = count // group
    down = rows // 16
    depth_tiles = swap_ref.shape[1] // LANES
    height = LANES
    top = swap_ref.shape[0] - height
    half = top // len(half_refs)
    lane = lax.broadcasted_iota(jnp.int32, (8, LANES), 1)
    for step, part_ref in enumerate(part_refs):
        block = place ^ step
        number = half // 16 * depth_tiles
        for offset in range(planes):
            first = ((plane ^ offset) * group + block) * rows
            for at in range(down):
                bc_ref[pl.ds(pl.multiple_of(first + at * 16, 16), 16), :] = part_ref[tile(number)]
                number += 1
        for side, owner in enumerate((group - 1, 0)):

            @pl.when(block == owner)
            def _(part_ref=part_ref, number=number, side=side):
                for at in range(depth_tiles):
                    halo_ref[side * EDGE : (side + 1) * EDGE, at * LANES : (at + 1) * LANES] = part_ref[tile(number + at)]
                packed = part_ref[tile(number + depth_tiles)].astype(F32)
                chosen = jnp.zeros((8, LANES), F32)
                for head_block in range(group):
                    value = jnp.zeros((8, LANES), F32)
                    for term in range(3):
                        slot = term * group + head_block
                        half = packed[slot // 8 * 8 : slot // 8 * 8 + 8]
                        value = value + pltpu.roll(half, (LANES - slot % 8 * EDGE) % LANES, 1)
                    chosen = jnp.where(place == head_block, value, chosen)
                if side:
                    last = pltpu.roll(chosen, EDGE, 1)
                    decay_ref[count * 8 :, :] = jnp.where((lane >= EDGE) & (lane < 2 * EDGE), last, 0.0)
                else:
                    decay_ref[:8, :] = jnp.where(lane < EDGE, chosen, 0.0)

        number += depth_tiles + 1
        for span in range(spans):
            upper = part_ref[tile(number)].astype(F32)
            lower = part_ref[tile(number + 1)].astype(F32)
            number += 2
            span_ref[block * spans + span] = upper[:8] + upper[8:] + lower[:8]
    for span in range(count):
        moved = pltpu.roll(span_ref[span], EDGE, 1)
        here, after = slice(span * 8, span * 8 + 8), slice(span * 8 + 8, span * 8 + 16)
        decay_ref[here, :] = jnp.where(lane < EDGE, decay_ref[here, :], moved)
        kept = decay_ref[after, :] if span == count - 1 else jnp.zeros((8, LANES), F32)
        decay_ref[after, :] = jnp.where(lane < EDGE, moved, kept)
    for number, half_ref in enumerate(half_refs):
        swap_ref[number * half : (number + 1) * half, :] = half_ref[:half, : swap_ref.shape[1]]
    for number in range(bc_ref.shape[0] // height):
        lanes = slice(number * LANES, (number + 1) * LANES)
        swap_ref[top:, lanes] = bc_ref[number * height : (number + 1) * height, :]


def lanes_of(rows, width, head_size):
    high = rows.astype(BF16).astype(F32)
    owner = lax.broadcasted_iota(jnp.int32, (16, width), 1) // head_size
    chosen = jnp.where((lax.broadcasted_iota(jnp.int32, (16, width), 0) & 7) == owner, 1.0, 0.0).astype(BF16)
    return dot(jnp.concatenate([high, rows - high], axis=0).astype(BF16), chosen, ((0,), (0,)))


def spans_in_lanes(rows):
    return jnp.concatenate([rows[at : at + 8] for at in range(0, rows.shape[0], 8)], axis=1)


def row_blocks(total, wide):
    return [slice(at, at + 256) for at in range(0, total, 256)] + [slice(total, wide)]


def state_kernel(group, heads, state, len_ref, decay_ref, x_weight_ref, bc_half_ref, own_ref, swap_ref, halo_ref, *refs):
    half_refs, refs = refs[: group - 1], refs[group - 1 :]
    frames_ref, x_ref, b_ref, c_ref, rows_ref, step_ref, keep_ref, send_ref, weight_ref, tail_ref = refs
    place, plane = plane_place(group)
    parity = lax.rem(lax.axis_index("head"), 2)
    width = x_ref.shape[1]
    frames = own_ref.shape[0]
    total = frames * group
    half = frames // 2
    head_size = width // heads
    count = total // SPAN
    base = plane * total - EDGE
    wide = total + 2 * EDGE
    frames_ref[:EDGE, :] = halo_ref[:EDGE, :]
    frames_ref[total + EDGE : wide, :] = halo_ref[EDGE:, :]
    frames_ref[wide:, :] = jnp.zeros((frames_ref.shape[0] - wide, frames_ref.shape[1]), BF16)
    frames_ref[pl.ds(pl.multiple_of(EDGE + place * frames, EDGE), frames), :] = own_ref[...]
    for number, half_ref in enumerate(half_refs):
        block = EDGE + (place ^ (number + 1)) * frames
        mine = pl.ds(pl.multiple_of(block + parity * half, EDGE), half)
        other = pl.ds(pl.multiple_of(block + (1 - parity) * half, EDGE), half)
        frames_ref[mine, :] = half_ref[:half, : frames_ref.shape[1]]
        frames_ref[other, :] = swap_ref[number * half : (number + 1) * half, :]
    mine = pl.ds(pl.multiple_of(parity * LANES, LANES), LANES)
    other = pl.ds(pl.multiple_of((1 - parity) * LANES, LANES), LANES)
    weight_ref[:, mine] = bc_half_ref[...]
    top = len(half_refs) * half
    height = swap_ref.shape[0] - top
    for number in range(weight_ref.shape[0] // height):
        lanes = slice(number * LANES, (number + 1) * LANES)
        weight_ref[number * height : (number + 1) * height, other] = swap_ref[top:, lanes]

    decay = decay_ref[...]
    used = decay.shape[0]
    square = (SPAN, SPAN)
    row, lane = (lax.broadcasted_iota(jnp.int32, square, dim) for dim in (0, 1))
    upper = jnp.where(row <= lane, 1.0, 0.0).astype(F32)
    cumul = dot(decay, upper, precision=lax.Precision.HIGHEST)
    whole = dot(decay, jnp.ones(square, F32), precision=lax.Precision.HIGHEST)
    first = base + lax.broadcasted_iota(jnp.int32, (used, SPAN), 0) // 8 * SPAN
    position = first + lane[:1]
    start = record_starts(len_ref, position)
    start_last = record_starts(len_ref, first + (SPAN - 1))
    carried = jnp.where(start < first, jnp.exp(cumul), 0.0)
    tail = jnp.where(position >= start_last, jnp.exp(whole - cumul), 0.0)
    keep = jnp.where(start_last < first, jnp.exp(whole), 0.0)
    rows_ref[:used, :] = cumul
    rows_ref[used : 2 * used, :] = start.astype(F32)
    rows_ref[2 * used :, :] = carried

    for rows in row_blocks(total, wide):
        x_ref[rows, :] = dot(frames_ref[rows, :], x_weight_ref[...]).astype(BF16)
        product = dot(frames_ref[rows, :], weight_ref[...])
        b_ref[rows, :] = product[:, :state].astype(BF16)
        c_ref[rows, :] = product[:, state:].astype(BF16)
    for ref in (x_ref, b_ref, c_ref):
        ref[wide:, :] = jnp.zeros((ref.shape[0] - wide, ref.shape[1]), BF16)

    tail_ref[...] = lanes_of(spans_in_lanes(tail[: count * 8]), width, head_size)
    by_span = jnp.zeros((8, SPAN), F32)
    for block in range(count):
        by_span = jnp.where(lane[:8] == block, keep[block * 8 : (block + 1) * 8], by_span)
    kept = lanes_of(by_span, width, head_size)[: keep_ref.shape[0]]
    keep_ref[...] = kept
    entry = jnp.zeros((state, width), F32)
    through = jnp.ones((1, width), F32)
    for block in range(count):
        rows = slice(block * SPAN, (block + 1) * SPAN)
        weighed = x_ref[rows, :].astype(F32) * tail_ref[rows, :]
        step = dot(b_ref[rows, :], weighed.astype(BF16), ((0,), (0,)))
        step_ref[block * state : (block + 1) * state, :] = step
        entry = kept[block : block + 1] * entry + step
        through = through * kept[block : block + 1]
    send_ref[:state, :] = entry.astype(BF16)
    send_ref[state:, :] = jnp.broadcast_to(through, (EDGE, width)).astype(BF16)


def inner_kernel(group, heads, x_ref, b_ref, c_ref, rows_ref, y_ref, carry_ref):
    _, plane = plane_place(group)
    total, width = x_ref.shape
    head_size = width // heads
    count = total // SPAN
    base = plane * (total - SPAN) - EDGE
    used = rows_ref.shape[0] // 3
    square = (SPAN, SPAN)
    parts = [rows_ref[: 2 * used, :]]
    if 2 * used % SPAN:
        parts.append(jnp.zeros((SPAN - 2 * used % SPAN, SPAN), F32))
    columns = jnp.concatenate(parts, axis=0).T
    carry_ref[...] = lanes_of(spans_in_lanes(rows_ref[2 * used :, :]), width, head_size)
    row, lane = (lax.broadcasted_iota(jnp.int32, square, dim) for dim in (0, 1))
    lower = row >= lane
    tile_heads = LANES // head_size
    tile_lane = lax.broadcasted_iota(jnp.int32, (1, LANES), 1) // head_size
    masks = [jnp.where(tile_lane == inner, 1.0, 0.0).astype(BF16) for inner in range(tile_heads)]
    for block in range(count):
        rows = slice(block * SPAN, (block + 1) * SPAN)
        at = block * 8
        x = x_ref[rows, :]
        scores = dot(c_ref[rows, :], b_ref[rows, :], ((1,), (1,)))
        here = (base + block * SPAN + lane).astype(F32)
        start_here = jnp.broadcast_to(columns[:, used + at : used + at + 1], square)
        joined = lower & (here >= start_here)
        for tile in range(width // LANES):
            mixes, values = [], []
            for inner in range(tile_heads):
                which = at + tile * tile_heads + inner
                column = jnp.broadcast_to(columns[:, which : which + 1], square)
                gap = jnp.where(joined, column - rows_ref[which : which + 1, :], -1e30)
                mixes.append((jnp.exp(gap) * scores).astype(BF16))
                values.append(x[:, tile * LANES : (tile + 1) * LANES] * masks[inner])
            y_ref[rows, tile * LANES : (tile + 1) * LANES] = dot(
                jnp.concatenate(mixes, axis=1), jnp.concatenate(values, axis=0)
            )


def silu_kernel(group, gain_ref, frames_ref, weight_ref, out_ref):
    place, _ = plane_place(group)
    rows_all, width = out_ref.shape
    total = rows_all - SPAN
    wide = total + 2 * EDGE
    gain = gain_ref[:, pl.ds(pl.multiple_of(place * width, LANES), width)]
    for rows in row_blocks(total, wide):
        z = dot(frames_ref[rows, :], weight_ref[...]).astype(BF16).astype(F32)
        out_ref[rows, :] = z / (1.0 + jnp.exp(-z)) * gain
    out_ref[wide:, :] = jnp.zeros((rows_all - wide, width), F32)


def share_kernel(cores, offsets, group, *refs):
    pieces, refs = refs[: len(offsets)], refs[len(offsets) :]
    outs, weight_ref = refs[:cores], refs[cores]
    _, plane = plane_place(group)
    core = lax.axis_index("head")
    fill_planes(plane, weight_ref, pieces, offsets)
    for step, out_ref in enumerate(outs):
        rows = out_ref.shape[0]
        out_ref[...] = weight_ref[pl.ds(pl.multiple_of((core ^ step) * rows, rows), rows), :]


def gate_kernel(heads, state, c_ref, y_ref, step_ref, carry_ref, keep_ref, silu_ref, *refs):
    earlier, gated_ref = refs[:-1], refs[-1]
    total, width = y_ref.shape
    head_size = width // heads
    count = total // SPAN
    entry = jnp.zeros((state, width), F32)
    for summary in reversed(earlier):
        through = summary[state : state + EDGE, :].astype(F32)[:1]
        entry = through * entry + summary[:state, :].astype(F32)
    owner = [lax.broadcasted_iota(jnp.int32, (width, width), dim) // head_size for dim in (0, 1)]
    average = jnp.where(owner[0] == owner[1], 1.0 / head_size, 0.0).astype(BF16)
    for block in range(count):
        rows = slice(block * SPAN, (block + 1) * SPAN)
        y = y_ref[rows, :] + carry_ref[rows, :] * dot(c_ref[rows, :], entry.astype(BF16))
        square_mean = dot((y * y).astype(BF16), average)
        gated_ref[rows, :] = (y * lax.rsqrt(square_mean + 1e-05) * silu_ref[rows, :]).astype(BF16)
        if block < count - 1:
            entry = keep_ref[block : block + 1, :] * entry + step_ref[block * state : (block + 1) * state, :]


def conv_kernel(group, steps, len_ref, taps_ref, gated_ref, act_ref, ext_ref, ends_ref):
    place, plane = plane_place(group)
    rows_all, width = gated_ref.shape
    total = rows_all - SPAN
    frames = total // group
    taps = taps_ref.shape[0]
    half = (taps - 1) // 2
    stream = lax.axis_size("tm") // group * total
    records = len_ref.shape[0]
    reach = CONV_ROWS + 2 * EDGE
    first_tap = EDGE - half
    pitch = frames + 2 * EDGE
    ends_ref[0] = 0
    for record in range(records):
        ends_ref[record + 1] = ends_ref[record] + len_ref[record]
    for number, step in enumerate(steps):
        first = pl.multiple_of((place ^ step) * frames, frames)
        ext_ref[number * pitch : (number + 1) * pitch, :] = gated_ref[pl.ds(first, pitch), :].astype(F32)

    def record_at(position):
        found = jnp.int32(0)
        for record in range(records - 1):
            found = found + (ends_ref[record + 1] <= position).astype(jnp.int32)
        return found

    for number, step in enumerate(steps):
        base = plane * total + (place ^ step) * frames

        def one_block(block, _, number=number, base=base):
            inside_part = pl.multiple_of(block * CONV_ROWS, CONV_ROWS)
            source = pl.multiple_of(number * pitch + inside_part, EDGE)
            target = pl.multiple_of(number * frames + inside_part, CONV_ROWS)
            at = base + inside_part
            low = record_at(jnp.maximum(at - half, 0))
            high = record_at(jnp.minimum(at + CONV_ROWS - 1 + half, stream - 1))
            near = lax.broadcasted_iota(jnp.int32, (reach, LANES), 0) + (at - EDGE)
            for tile in range(width // LANES):
                lanes = slice(tile * LANES, (tile + 1) * LANES)
                weights = taps_ref[:, pl.ds(pl.multiple_of(place * width + tile * LANES, LANES), LANES)]

                def one_record(record, done):
                    inside = (near >= ends_ref[record]) & (near < ends_ref[record + 1])
                    g = jnp.where(inside, ext_ref[pl.ds(source, reach), lanes], 0.0)
                    out = None
                    for phase in range(8):
                        part = None
                        for offset in range(phase, reach - CONV_ROWS, 8):
                            tap = offset - first_tap
                            if 0 <= tap < taps:
                                aligned = offset - phase
                                term = weights[tap : tap + 1, :] * g[aligned : aligned + CONV_ROWS + 8, :]
                                part = term if part is None else part + term
                        if part is not None:
                            moved = part[phase : phase + CONV_ROWS, :]
                            out = moved if out is None else out + moved
                    return jnp.where(inside[EDGE : EDGE + CONV_ROWS], out, done)

                conv = lax.fori_loop(low, high + 1, one_record, jnp.zeros((CONV_ROWS, LANES), F32))
                act_ref[pl.ds(target, CONV_ROWS), lanes] = (conv / (1.0 + jnp.exp(-conv))).astype(BF16)
            return 0

        lax.fori_loop(0, frames // CONV_ROWS, one_block, 0)


def out_kernel(cores, *refs):
    acts, weights, outs = refs[:cores], refs[cores : 2 * cores], refs[2 * cores :]
    frames = outs[0].shape[0]
    for number, out_ref in enumerate(outs):
        rows = slice(number * frames, (number + 1) * frames)
        total = None
        for act, weight in zip(acts, weights):
            product = dot(act[rows, :], weight[...], ((1,), (1,)))
            total = product if total is None else total + product
        out_ref[...] = total.astype(out_ref.dtype)


def local(
    frames,
    x_weight,
    z_weight,
    bc_weight,
    log_decay,
    norm_gain,
    conv_weight,
    out_weight,
    record_lengths,
):
    times, cores = lax.axis_size("tm"), lax.axis_size("head")
    frame_count, depth = frames.shape
    heads_here, channels = log_decay.shape[0], x_weight.shape[1]
    state = bc_weight.shape[1] // 2
    group = 4
    while group > 1 and (channels // group % LANES or times % group or heads_here % group):
        group //= 2
    planes = times // group
    width, heads = channels // group, heads_here // group
    total = frame_count * group
    count = total // SPAN
    index, core = lax.axis_index("tm"), lax.axis_index("head")
    place = lax.rem(index, group)

    def in_plane(array, step):
        return lax.ppermute(array, "tm", [(i, i ^ step) for i in range(times)])

    def later(array, step):
        return lax.ppermute(array, "tm", [(i, i + step * group) for i in range(times - step * group)])

    def across(array, step):
        return lax.ppermute(array, "head", [(i, i ^ step) for i in range(cores)])

    def between_planes(array, step):
        return lax.ppermute(array, "tm", [(i, i ^ (step * group)) for i in range(times)])

    shape = jax.ShapeDtypeStruct
    rows = x_weight.shape[0]
    parity = lax.rem(core, 2)

    def along_planes(stacks):
        if planes != 4:
            return [stacks[0]] + [between_planes(stacks[step], step) for step in range(1, planes)]

        def pairs(chosen):
            return [(a * group + q, b * group + q) for a, b in chosen for q in range(group)]

        second = between_planes(stacks[2], 2)
        first = between_planes(stacks[1], 1)
        again, last, first = lax.optimization_barrier((second, stacks[3], first))
        third = lax.ppermute(again, "tm", pairs([(1, 0), (2, 3)]))
        middle = lax.ppermute(last, "tm", pairs([(1, 2), (2, 1)]))
        return [stacks[0], first, second, third, middle]

    offsets = (0, 1, 2, 3, 3) if planes == 4 else tuple(range(planes))
    half_count = frame_count // 2
    down, depth_tiles = rows // 16, depth // LANES
    payloads = call(
        functools.partial(first_kernel, group, planes),
        (
            *(shape((rows, 3 * width), BF16) for _ in range(group)),
            *(shape((-(-(down + depth_tiles + 1) // 8) * 16, depth), BF16) for _ in range(planes)),
        ),
        [log_decay, bc_weight, frames, x_weight, z_weight, out_weight.T],
        [
            pltpu.VMEM((rows, LANES), BF16),
            pltpu.VMEM((2, EDGE, depth), BF16),
            pltpu.VMEM(log_decay.shape, F32),
            pltpu.SemaphoreType.DMA((4 + 3 * group,)),
        ],
        smem=0,
        anywhere=6,
        vmem=ALL_VMEM_BYTES,
    )
    inner, outer = payloads[:group], payloads[group:]
    parts = [inner[0]] + [in_plane(inner[step], step) for step in range(1, group)]
    pieces = [outer[0]] + [between_planes(outer[step], step) for step in range(1, planes)]
    xz_stack, out_stack = call(
        functools.partial(stack_kernel, group),
        (shape((group * rows, 2 * width), BF16), shape((group * rows, width), BF16)),
        parts,
        flops=STACK_HINT,
        smem=0,
    )
    xz_pieces = along_planes([xz_stack] * planes)
    x_columns, z_columns = call(
        functools.partial(assemble_kernel, group, offsets),
        (shape((depth, width), BF16), shape((depth, width), BF16)),
        xz_pieces,
        flops=ASSEMBLE_HINT,
        smem=0,
    )
    decay_blocks = jnp.pad(log_decay.reshape(group, heads, frame_count), ((0, 0), (0, 8 - heads), (0, 0)))
    tiles = planes * down + depth_tiles + 1 + frame_count // SPAN * 2
    inward = call(
        functools.partial(inward_kernel, group, rows),
        tuple(shape((half_count + -(-tiles // 8) * 16, depth), BF16) for _ in range(group)),
        [decay_blocks, frames, *pieces],
        flops=INWARD_HINT,
        smem=0,
    )
    inward = [inward[0]] + [in_plane(inward[step], step) for step in range(1, group)]
    swap, bc_mine, halo, decay = call(
        functools.partial(swap_kernel, group, rows),
        (
            shape(((group - 1) * half_count + LANES, depth), BF16),
            shape((depth, LANES), BF16),
            shape((2 * EDGE, depth), BF16),
            shape((count * 8 + 8, SPAN), F32),
        ),
        inward,
        [pltpu.VMEM((count, 8, SPAN), F32)],
        smem=0,
    )
    swap = across(swap, 1)
    all_rows = total + SPAN

    frame_rows, x_rows, b_rows, c_rows, decay_rows, steps, keep, summary = call(
        functools.partial(state_kernel, group, heads, state),
        (
            shape((all_rows, depth), BF16),
            shape((all_rows, width), BF16),
            shape((all_rows, state), BF16),
            shape((all_rows, state), BF16),
            shape((3 * (count + 1) * 8, SPAN), F32),
            shape((count * state, width), F32),
            shape((-(-count // 8) * 8, width), F32),
            shape((state + EDGE, width), BF16),
        ),
        [record_lengths, decay, x_columns, bc_mine, frames, swap, halo, *inward[1:]],
        [pltpu.VMEM((depth, 2 * state), BF16), pltpu.VMEM((total, width), F32)],
        hidden=True,
    )
    early = between_planes(out_stack, 2) if planes > 2 else None
    x_rows, early = lax.optimization_barrier((x_rows, early))
    summaries = [later(summary, step) for step in range(1, planes)]
    y, carry = call(
        functools.partial(inner_kernel, group, heads),
        (shape((all_rows, width), F32), shape((all_rows, width), F32)),
        [x_rows, b_rows, c_rows, decay_rows],
        flops=4 * total * SPAN * width,
        smem=0,
    )
    silu = call(
        functools.partial(silu_kernel, group),
        shape((all_rows, width), F32),
        [norm_gain[None], frame_rows, z_columns],
        flops=2 * total * depth * width,
        smem=0,
    )
    out_stack, summaries, y, silu = lax.optimization_barrier((out_stack, summaries, y, silu))
    out_pieces = [out_stack]
    for step in range(1, planes):
        out_pieces.append(early if step == 2 else between_planes(out_stack, step))
    gated = call(
        functools.partial(gate_kernel, heads, state),
        shape((all_rows, width), BF16),
        [c_rows, y, steps, carry, keep, silu, *summaries],
        flops=2 * total * state * width,
        smem=0,
    )
    ends = pltpu.SMEM((record_lengths.shape[0] + 1,), jnp.int32)
    far, near = (group - 1,), (*range(1, group - 1), 0)

    def conv(steps, gated):
        return call(
            functools.partial(conv_kernel, group, steps),
            shape((len(steps) * frame_count, width), BF16),
            [record_lengths, conv_weight, gated],
            [pltpu.VMEM((len(steps) * (frame_count + 2 * EDGE), width), F32), ends],
            flops=2 * len(steps) * frame_count * width * conv_weight.shape[0],
        )

    def out(steps, act, swapped):
        return call(
            functools.partial(out_kernel, cores),
            tuple(shape((frame_count, share), BF16 if step else F32) for step in steps),
            [act, *swapped, *out_parts],
            flops=2 * len(steps) * frame_count * width * cores * share,
            smem=0,
        )

    far_act = conv(far, gated)
    far_swapped = [across(far_act, step) for step in range(1, cores)]
    far_act, out_pieces = lax.optimization_barrier((far_act, out_pieces))
    share = depth // cores
    out_parts = call(
        functools.partial(share_kernel, cores, tuple(range(planes)), group),
        tuple(shape((share, width), BF16) for _ in range(cores)),
        out_pieces,
        [pltpu.VMEM((depth, width), BF16)],
        smem=0,
    )
    out_parts = [out_parts[0]] + [across(out_parts[step], step) for step in range(1, cores)]
    (far_out,) = out(far, far_act, far_swapped)
    gated, far_out = lax.optimization_barrier((gated, far_out))
    far_out = in_plane(far_out, far[0])
    near_act = conv(near, gated)
    near_act, far_out = lax.optimization_barrier((near_act, far_out))
    near_swapped = [across(near_act, step) for step in range(1, cores)]
    near_outs = out(near, near_act, near_swapped)
    mixed = near_outs[-1] + far_out.astype(F32)
    for step, partial in zip(near[:-1], near_outs[:-1]):
        mixed = mixed + in_plane(partial, step).astype(F32)
    return mixed.astype(BF16)


def solution(mesh):
    in_specs = (
        P("tm", None),
        P("tm", "head"),
        P("tm", "head"),
        P("tm", None),
        P("head", "tm"),
        P("head"),
        P(None, "head"),
        P("head", "tm"),
        P(),
    )
    out_specs = P("tm", "head")
    return jax.shard_map(local, mesh=mesh, in_specs=in_specs, out_specs=out_specs, check_vma=False)
```

```python
import functools

import jax
import jax.numpy as jnp
from jax import lax
from jax.experimental import pallas as pl
from jax.experimental.pallas import tpu as pltpu
from jax.sharding import PartitionSpec as P

SPAN = 128
LANES = 128
EDGE = 16
CONV_ROWS = 64
BF16 = jnp.bfloat16
F32 = jnp.float32
STACK_HINT = 40_000_000_000
INWARD_HINT = 40_000_000_000
ASSEMBLE_HINT = 40_000_000_000
ALL_VMEM_BYTES = 63 * 1024 * 1024
VMEM_BYTES = 20 * 1024 * 1024


def dot(a, b, dims=((1,), (0,)), precision=None):
    return lax.dot_general(a, b, (dims, ((), ())), precision=precision, preferred_element_type=F32)


def call(kernel, out_shape, operands, scratch=(), flops=0, smem=1, anywhere=0, vmem=VMEM_BYTES, hidden=False):
    in_specs = [pl.BlockSpec(memory_space=pltpu.SMEM)] * smem
    in_specs += [pl.BlockSpec(memory_space=pltpu.VMEM)] * (len(operands) - smem - anywhere)
    in_specs += [pl.BlockSpec(memory_space=pl.ANY)] * anywhere
    moved = sum(a.size * a.dtype.itemsize for a in operands)
    moved += sum(a.size * a.dtype.itemsize for a in jax.tree.leaves(out_shape))
    if hidden:
        flops = moved = 0
    return pl.pallas_call(
        kernel,
        out_shape=out_shape,
        in_specs=in_specs,
        out_specs=jax.tree.map(lambda _: pl.BlockSpec(memory_space=pltpu.VMEM), out_shape),
        scratch_shapes=list(scratch),
        compiler_params=pltpu.CompilerParams(vmem_limit_bytes=vmem),
        cost_estimate=pl.CostEstimate(flops=flops, bytes_accessed=moved, transcendentals=0),
    )(*operands)


def plane_place(group):
    index = lax.axis_index("tm")
    return lax.rem(index, group), lax.div(index, group)


def record_starts(len_ref, position):
    start = jnp.zeros_like(position)
    end = jnp.int32(0)
    for record in range(len_ref.shape[0] - 1):
        end = end + len_ref[record]
        start = jnp.where(position >= end, end, start)
    return start


def fill_planes(plane, dest_ref, pieces, offsets, lanes=slice(None)):
    rows = pieces[0].shape[0]
    for offset in sorted(set(offsets)):
        same = [piece[:, lanes] for piece, at in zip(pieces, offsets) if at == offset]
        value = same[0] if len(same) == 1 else same[0] + same[1]
        dest_ref[pl.ds(pl.multiple_of((plane ^ offset) * rows, rows), rows), : value.shape[1]] = value


def first_kernel(group, planes, log_decay_ref, bc_ref, frames_ref, *refs):
    weight_refs, refs = refs[:3], refs[3:]
    inner_refs, outer_refs, refs = refs[:group], refs[group : group + planes], refs[group + planes :]
    bc_half_ref, edge_ref, decay_ref, sems = refs
    place, plane = plane_place(group)
    parity = lax.rem(lax.axis_index("head"), 2)
    width = weight_refs[0].shape[1] // group
    frames = frames_ref.shape[0]
    heads = log_decay_ref.shape[0] // group
    copies = [
        (bc_ref.at[:, pl.ds(pl.multiple_of(parity * LANES, LANES), LANES)], bc_half_ref),
        (frames_ref.at[:EDGE, :], edge_ref.at[0]),
        (frames_ref.at[frames - EDGE :, :], edge_ref.at[1]),
        (log_decay_ref, decay_ref),
    ]
    for step, inner_ref in enumerate(inner_refs):
        lanes = pl.ds(pl.multiple_of((place ^ step) * width, LANES), width)
        for number, weight_ref in enumerate(weight_refs):
            copies.append((weight_ref.at[:, lanes], inner_ref.at[:, number * width : (number + 1) * width]))
    started = [pltpu.make_async_copy(a, b, sems.at[number]) for number, (a, b) in enumerate(copies)]
    for copy in started:
        copy.start()
    for copy in started[:4]:
        copy.wait()
    lane = lax.broadcasted_iota(jnp.int32, (8, LANES), 1)
    decays = []
    for first in (0, frames - LANES):
        rows = [jnp.zeros((8, LANES), F32), jnp.zeros((8, LANES), F32)]
        for block in range(group):
            here = decay_ref[block * heads : (block + 1) * heads, first : first + LANES]
            here = jnp.concatenate([here, jnp.zeros((8 - heads, LANES), F32)], axis=0)
            for number, term in enumerate(three_terms(here)):
                slot = number * group + block
                moved = pltpu.roll(term, (slot % 8 * EDGE + (EDGE if first else 0)) % LANES, 1)
                rows[slot // 8] = jnp.where(lane // EDGE == slot % 8, moved, rows[slot // 8])
        decays.append(jnp.concatenate(rows, axis=0))
    for step, out_ref in enumerate(outer_refs):
        number = put(out_ref, 0, bc_half_ref[...])
        later = (plane ^ step) > plane
        number = put(out_ref, number, jnp.where(later, edge_ref[1].astype(F32), edge_ref[0].astype(F32)).astype(BF16))
        put(out_ref, number, jnp.where(later, decays[1], decays[0]).astype(BF16))
    for copy in started[4:]:
        copy.wait()


def stack_kernel(group, *refs):
    parts, stack_refs = refs[:group], refs[group:]
    place, _ = plane_place(group)
    rows = parts[0].shape[0]
    for step, part in enumerate(parts):
        at = pl.ds(pl.multiple_of((place ^ step) * rows, rows), rows)
        first = 0
        for stack_ref in stack_refs:
            width = stack_ref.shape[1]
            stack_ref[at, :] = part[:, first : first + width]
            first += width


def assemble_kernel(group, offsets, *refs):
    pieces, dest_refs = refs[: len(offsets)], refs[len(offsets) :]
    _, plane = plane_place(group)
    first = 0
    for dest_ref in dest_refs:
        width = dest_ref.shape[1]
        fill_planes(plane, dest_ref, pieces, offsets, slice(first, first + width))
        first += width


def tile(number):
    return slice(number // 8 * 16, number // 8 * 16 + 16), slice(number % 8 * LANES, (number % 8 + 1) * LANES)


def put(out_ref, number, array):
    for at in range(0, array.shape[0], 16):
        for lane in range(0, array.shape[1], LANES):
            out_ref[tile(number)] = array[at : at + 16, lane : lane + LANES]
            number += 1
    return number


def three_terms(value):
    terms = []
    for _ in range(3):
        term = value.astype(BF16).astype(F32)
        terms.append(term)
        value = value - term
    return terms


def inward_kernel(group, rows, decay_ref, frames_ref, *refs):
    piece_refs, out_refs = refs[:-group], refs[-group:]
    place, plane = plane_place(group)
    planes = len(piece_refs)
    half = frames_ref.shape[0] // 2
    mine = pl.ds(pl.multiple_of(lax.rem(lax.axis_index("head"), 2) * half, half), half)
    wanted = jnp.clip(jnp.where(place == 0, plane + 1, plane - 1), 0, planes - 1)
    depth_tiles = frames_ref.shape[1] // LANES
    down = rows // 16
    for step, out_ref in enumerate(out_refs):
        out_ref[:half, :] = frames_ref[mine, :]
        number = half // 16 * depth_tiles
        for piece_ref in piece_refs:
            for at in range(down):
                out_ref[tile(number)] = piece_ref[tile(at)]
                number += 1
        for offset, piece_ref in enumerate(piece_refs):

            @pl.when((plane ^ offset) == wanted)
            def _(piece_ref=piece_ref, number=number, out_ref=out_ref):
                for at in range(depth_tiles + 1):
                    out_ref[tile(number + at)] = piece_ref[tile(down + at)]

        number += depth_tiles + 1
        terms = three_terms(decay_ref[place ^ step])
        terms = jnp.concatenate([*terms, jnp.zeros_like(terms[0])], axis=0).astype(BF16)
        for span in range(terms.shape[1] // SPAN):
            number = put(out_ref, number, terms[:, span * SPAN : (span + 1) * SPAN])


def swap_kernel(group, rows, *refs):
    part_refs, (swap_ref, bc_ref, halo_ref, decay_ref, span_ref) = refs[:group], refs[group:]
    half_refs = part_refs[1:]
    place, plane = plane_place(group)
    planes = bc_ref.shape[0] // (group * rows)
    count = span_ref.shape[0]
    spans = count // group
    down = rows // 16
    depth_tiles = swap_ref.shape[1] // LANES
    height = LANES
    top = swap_ref.shape[0] - height
    half = top // len(half_refs)
    lane = lax.broadcasted_iota(jnp.int32, (8, LANES), 1)
    for step, part_ref in enumerate(part_refs):
        block = place ^ step
        number = half // 16 * depth_tiles
        for offset in range(planes):
            first = ((plane ^ offset) * group + block) * rows
            for at in range(down):
                bc_ref[pl.ds(pl.multiple_of(first + at * 16, 16), 16), :] = part_ref[tile(number)]
                number += 1
        for side, owner in enumerate((group - 1, 0)):

            @pl.when(block == owner)
            def _(part_ref=part_ref, number=number, side=side):
                for at in range(depth_tiles):
                    halo_ref[side * EDGE : (side + 1) * EDGE, at * LANES : (at + 1) * LANES] = part_ref[tile(number + at)]
                packed = part_ref[tile(number + depth_tiles)].astype(F32)
                chosen = jnp.zeros((8, LANES), F32)
                for head_block in range(group):
                    value = jnp.zeros((8, LANES), F32)
                    for term in range(3):
                        slot = term * group + head_block
                        half = packed[slot // 8 * 8 : slot // 8 * 8 + 8]
                        value = value + pltpu.roll(half, (LANES - slot % 8 * EDGE) % LANES, 1)
                    chosen = jnp.where(place == head_block, value, chosen)
                if side:
                    last = pltpu.roll(chosen, EDGE, 1)
                    decay_ref[count * 8 :, :] = jnp.where((lane >= EDGE) & (lane < 2 * EDGE), last, 0.0)
                else:
                    decay_ref[:8, :] = jnp.where(lane < EDGE, chosen, 0.0)

        number += depth_tiles + 1
        for span in range(spans):
            upper = part_ref[tile(number)].astype(F32)
            lower = part_ref[tile(number + 1)].astype(F32)
            number += 2
            span_ref[block * spans + span] = upper[:8] + upper[8:] + lower[:8]
    for span in range(count):
        moved = pltpu.roll(span_ref[span], EDGE, 1)
        here, after = slice(span * 8, span * 8 + 8), slice(span * 8 + 8, span * 8 + 16)
        decay_ref[here, :] = jnp.where(lane < EDGE, decay_ref[here, :], moved)
        kept = decay_ref[after, :] if span == count - 1 else jnp.zeros((8, LANES), F32)
        decay_ref[after, :] = jnp.where(lane < EDGE, moved, kept)
    for number, half_ref in enumerate(half_refs):
        swap_ref[number * half : (number + 1) * half, :] = half_ref[:half, : swap_ref.shape[1]]
    for number in range(bc_ref.shape[0] // height):
        lanes = slice(number * LANES, (number + 1) * LANES)
        swap_ref[top:, lanes] = bc_ref[number * height : (number + 1) * height, :]


def lanes_of(rows, width, head_size):
    high = rows.astype(BF16).astype(F32)
    owner = lax.broadcasted_iota(jnp.int32, (16, width), 1) // head_size
    chosen = jnp.where((lax.broadcasted_iota(jnp.int32, (16, width), 0) & 7) == owner, 1.0, 0.0).astype(BF16)
    return dot(jnp.concatenate([high, rows - high], axis=0).astype(BF16), chosen, ((0,), (0,)))


def spans_in_lanes(rows):
    return jnp.concatenate([rows[at : at + 8] for at in range(0, rows.shape[0], 8)], axis=1)


def row_blocks(total, wide):
    return [slice(at, at + 256) for at in range(0, total, 256)] + [slice(total, wide)]


def state_kernel(group, heads, state, len_ref, decay_ref, x_weight_ref, bc_half_ref, own_ref, swap_ref, halo_ref, *refs):
    half_refs, refs = refs[: group - 1], refs[group - 1 :]
    frames_ref, x_ref, b_ref, c_ref, rows_ref, step_ref, keep_ref, send_ref, weight_ref, tail_ref = refs
    place, plane = plane_place(group)
    parity = lax.rem(lax.axis_index("head"), 2)
    width = x_ref.shape[1]
    frames = own_ref.shape[0]
    total = frames * group
    half = frames // 2
    head_size = width // heads
    count = total // SPAN
    base = plane * total - EDGE
    wide = total + 2 * EDGE
    frames_ref[:EDGE, :] = halo_ref[:EDGE, :]
    frames_ref[total + EDGE : wide, :] = halo_ref[EDGE:, :]
    frames_ref[wide:, :] = jnp.zeros((frames_ref.shape[0] - wide, frames_ref.shape[1]), BF16)
    frames_ref[pl.ds(pl.multiple_of(EDGE + place * frames, EDGE), frames), :] = own_ref[...]
    for number, half_ref in enumerate(half_refs):
        block = EDGE + (place ^ (number + 1)) * frames
        mine = pl.ds(pl.multiple_of(block + parity * half, EDGE), half)
        other = pl.ds(pl.multiple_of(block + (1 - parity) * half, EDGE), half)
        frames_ref[mine, :] = half_ref[:half, : frames_ref.shape[1]]
        frames_ref[other, :] = swap_ref[number * half : (number + 1) * half, :]
    mine = pl.ds(pl.multiple_of(parity * LANES, LANES), LANES)
    other = pl.ds(pl.multiple_of((1 - parity) * LANES, LANES), LANES)
    weight_ref[:, mine] = bc_half_ref[...]
    top = len(half_refs) * half
    height = swap_ref.shape[0] - top
    for number in range(weight_ref.shape[0] // height):
        lanes = slice(number * LANES, (number + 1) * LANES)
        weight_ref[number * height : (number + 1) * height, other] = swap_ref[top:, lanes]

    decay = decay_ref[...]
    used = decay.shape[0]
    square = (SPAN, SPAN)
    row, lane = (lax.broadcasted_iota(jnp.int32, square, dim) for dim in (0, 1))
    upper = jnp.where(row <= lane, 1.0, 0.0).astype(F32)
    cumul = dot(decay, upper, precision=lax.Precision.HIGHEST)
    whole = dot(decay, jnp.ones(square, F32), precision=lax.Precision.HIGHEST)
    first = base + lax.broadcasted_iota(jnp.int32, (used, SPAN), 0) // 8 * SPAN
    position = first + lane[:1]
    start = record_starts(len_ref, position)
    start_last = record_starts(len_ref, first + (SPAN - 1))
    carried = jnp.where(start < first, jnp.exp(cumul), 0.0)
    tail = jnp.where(position >= start_last, jnp.exp(whole - cumul), 0.0)
    keep = jnp.where(start_last < first, jnp.exp(whole), 0.0)
    rows_ref[:used, :] = cumul
    rows_ref[used : 2 * used, :] = start.astype(F32)
    rows_ref[2 * used :, :] = carried

    for rows in row_blocks(total, wide):
        x_ref[rows, :] = dot(frames_ref[rows, :], x_weight_ref[...]).astype(BF16)
        product = dot(frames_ref[rows, :], weight_ref[...])
        b_ref[rows, :] = product[:, :state].astype(BF16)
        c_ref[rows, :] = product[:, state:].astype(BF16)
    for ref in (x_ref, b_ref, c_ref):
        ref[wide:, :] = jnp.zeros((ref.shape[0] - wide, ref.shape[1]), BF16)

    tail_ref[...] = lanes_of(spans_in_lanes(tail[: count * 8]), width, head_size)
    by_span = jnp.zeros((8, SPAN), F32)
    for block in range(count):
        by_span = jnp.where(lane[:8] == block, keep[block * 8 : (block + 1) * 8], by_span)
    kept = lanes_of(by_span, width, head_size)[: keep_ref.shape[0]]
    keep_ref[...] = kept
    entry = jnp.zeros((state, width), F32)
    through = jnp.ones((1, width), F32)
    for block in range(count):
        rows = slice(block * SPAN, (block + 1) * SPAN)
        weighed = x_ref[rows, :].astype(F32) * tail_ref[rows, :]
        step = dot(b_ref[rows, :], weighed.astype(BF16), ((0,), (0,)))
        step_ref[block * state : (block + 1) * state, :] = step
        entry = kept[block : block + 1] * entry + step
        through = through * kept[block : block + 1]
    send_ref[:state, :] = entry.astype(BF16)
    send_ref[state:, :] = jnp.broadcast_to(through, (EDGE, width)).astype(BF16)


def inner_kernel(group, heads, x_ref, b_ref, c_ref, rows_ref, y_ref, carry_ref):
    _, plane = plane_place(group)
    total, width = x_ref.shape
    head_size = width // heads
    count = total // SPAN
    base = plane * (total - SPAN) - EDGE
    used = rows_ref.shape[0] // 3
    square = (SPAN, SPAN)
    parts = [rows_ref[: 2 * used, :]]
    if 2 * used % SPAN:
        parts.append(jnp.zeros((SPAN - 2 * used % SPAN, SPAN), F32))
    columns = jnp.concatenate(parts, axis=0).T
    carry_ref[...] = lanes_of(spans_in_lanes(rows_ref[2 * used :, :]), width, head_size)
    row, lane = (lax.broadcasted_iota(jnp.int32, square, dim) for dim in (0, 1))
    lower = row >= lane
    tile_heads = LANES // head_size
    tile_lane = lax.broadcasted_iota(jnp.int32, (1, LANES), 1) // head_size
    masks = [jnp.where(tile_lane == inner, 1.0, 0.0).astype(BF16) for inner in range(tile_heads)]
    for block in range(count):
        rows = slice(block * SPAN, (block + 1) * SPAN)
        at = block * 8
        x = x_ref[rows, :]
        scores = dot(c_ref[rows, :], b_ref[rows, :], ((1,), (1,)))
        here = (base + block * SPAN + lane).astype(F32)
        start_here = jnp.broadcast_to(columns[:, used + at : used + at + 1], square)
        joined = lower & (here >= start_here)
        for tile in range(width // LANES):
            mixes, values = [], []
            for inner in range(tile_heads):
                which = at + tile * tile_heads + inner
                column = jnp.broadcast_to(columns[:, which : which + 1], square)
                gap = jnp.where(joined, column - rows_ref[which : which + 1, :], -1e30)
                mixes.append((jnp.exp(gap) * scores).astype(BF16))
                values.append(x[:, tile * LANES : (tile + 1) * LANES] * masks[inner])
            y_ref[rows, tile * LANES : (tile + 1) * LANES] = dot(
                jnp.concatenate(mixes, axis=1), jnp.concatenate(values, axis=0)
            )


def silu_kernel(group, gain_ref, frames_ref, weight_ref, out_ref):
    place, _ = plane_place(group)
    rows_all, width = out_ref.shape
    total = rows_all - SPAN
    wide = total + 2 * EDGE
    gain = gain_ref[:, pl.ds(pl.multiple_of(place * width, LANES), width)]
    for rows in row_blocks(total, wide):
        z = dot(frames_ref[rows, :], weight_ref[...]).astype(BF16).astype(F32)
        out_ref[rows, :] = z / (1.0 + jnp.exp(-z)) * gain
    out_ref[wide:, :] = jnp.zeros((rows_all - wide, width), F32)


def share_kernel(cores, offsets, group, *refs):
    pieces, refs = refs[: len(offsets)], refs[len(offsets) :]
    outs, weight_ref = refs[:cores], refs[cores]
    _, plane = plane_place(group)
    core = lax.axis_index("head")
    fill_planes(plane, weight_ref, pieces, offsets)
    for step, out_ref in enumerate(outs):
        rows = out_ref.shape[0]
        out_ref[...] = weight_ref[pl.ds(pl.multiple_of((core ^ step) * rows, rows), rows), :]


def gate_kernel(heads, state, c_ref, y_ref, step_ref, carry_ref, keep_ref, silu_ref, *refs):
    earlier, gated_ref = refs[:-1], refs[-1]
    total, width = y_ref.shape
    head_size = width // heads
    count = total // SPAN
    entry = jnp.zeros((state, width), F32)
    for summary in reversed(earlier):
        through = summary[state : state + EDGE, :].astype(F32)[:1]
        entry = through * entry + summary[:state, :].astype(F32)
    owner = [lax.broadcasted_iota(jnp.int32, (width, width), dim) // head_size for dim in (0, 1)]
    average = jnp.where(owner[0] == owner[1], 1.0 / head_size, 0.0).astype(BF16)
    for block in range(count):
        rows = slice(block * SPAN, (block + 1) * SPAN)
        y = y_ref[rows, :] + carry_ref[rows, :] * dot(c_ref[rows, :], entry.astype(BF16))
        square_mean = dot((y * y).astype(BF16), average)
        gated_ref[rows, :] = (y * lax.rsqrt(square_mean + 1e-05) * silu_ref[rows, :]).astype(BF16)
        if block < count - 1:
            entry = keep_ref[block : block + 1, :] * entry + step_ref[block * state : (block + 1) * state, :]


def conv_kernel(group, steps, len_ref, taps_ref, gated_ref, act_ref, ext_ref, ends_ref):
    place, plane = plane_place(group)
    rows_all, width = gated_ref.shape
    total = rows_all - SPAN
    frames = total // group
    taps = taps_ref.shape[0]
    half = (taps - 1) // 2
    stream = lax.axis_size("tm") // group * total
    records = len_ref.shape[0]
    reach = CONV_ROWS + 2 * EDGE
    first_tap = EDGE - half
    pitch = frames + 2 * EDGE
    ends_ref[0] = 0
    for record in range(records):
        ends_ref[record + 1] = ends_ref[record] + len_ref[record]
    for number, step in enumerate(steps):
        first = pl.multiple_of((place ^ step) * frames, frames)
        ext_ref[number * pitch : (number + 1) * pitch, :] = gated_ref[pl.ds(first, pitch), :].astype(F32)

    def record_at(position):
        found = jnp.int32(0)
        for record in range(records - 1):
            found = found + (ends_ref[record + 1] <= position).astype(jnp.int32)
        return found

    for number, step in enumerate(steps):
        base = plane * total + (place ^ step) * frames

        def one_block(block, _, number=number, base=base):
            inside_part = pl.multiple_of(block * CONV_ROWS, CONV_ROWS)
            source = pl.multiple_of(number * pitch + inside_part, EDGE)
            target = pl.multiple_of(number * frames + inside_part, CONV_ROWS)
            at = base + inside_part
            low = record_at(jnp.maximum(at - half, 0))
            high = record_at(jnp.minimum(at + CONV_ROWS - 1 + half, stream - 1))
            near = lax.broadcasted_iota(jnp.int32, (reach, LANES), 0) + (at - EDGE)
            for tile in range(width // LANES):
                lanes = slice(tile * LANES, (tile + 1) * LANES)
                weights = taps_ref[:, pl.ds(pl.multiple_of(place * width + tile * LANES, LANES), LANES)]

                def one_record(record, done):
                    inside = (near >= ends_ref[record]) & (near < ends_ref[record + 1])
                    g = jnp.where(inside, ext_ref[pl.ds(source, reach), lanes], 0.0)
                    out = None
                    for phase in range(8):
                        part = None
                        for offset in range(phase, reach - CONV_ROWS, 8):
                            tap = offset - first_tap
                            if 0 <= tap < taps:
                                aligned = offset - phase
                                term = weights[tap : tap + 1, :] * g[aligned : aligned + CONV_ROWS + 8, :]
                                part = term if part is None else part + term
                        if part is not None:
                            moved = part[phase : phase + CONV_ROWS, :]
                            out = moved if out is None else out + moved
                    return jnp.where(inside[EDGE : EDGE + CONV_ROWS], out, done)

                conv = lax.fori_loop(low, high + 1, one_record, jnp.zeros((CONV_ROWS, LANES), F32))
                act_ref[pl.ds(target, CONV_ROWS), lanes] = (conv / (1.0 + jnp.exp(-conv))).astype(BF16)
            return 0

        lax.fori_loop(0, frames // CONV_ROWS, one_block, 0)


def out_kernel(cores, *refs):
    acts, weights, outs = refs[:cores], refs[cores : 2 * cores], refs[2 * cores :]
    frames = outs[0].shape[0]
    for number, out_ref in enumerate(outs):
        rows = slice(number * frames, (number + 1) * frames)
        total = None
        for act, weight in zip(acts, weights):
            product = dot(act[rows, :], weight[...], ((1,), (1,)))
            total = product if total is None else total + product
        out_ref[...] = total.astype(out_ref.dtype)


def local(
    frames,
    x_weight,
    z_weight,
    bc_weight,
    log_decay,
    norm_gain,
    conv_weight,
    out_weight,
    record_lengths,
):
    times, cores = lax.axis_size("tm"), lax.axis_size("head")
    frame_count, depth = frames.shape
    heads_here, channels = log_decay.shape[0], x_weight.shape[1]
    state = bc_weight.shape[1] // 2
    group = 4
    while group > 1 and (channels // group % LANES or times % group or heads_here % group):
        group //= 2
    planes = times // group
    width, heads = channels // group, heads_here // group
    total = frame_count * group
    count = total // SPAN
    index, core = lax.axis_index("tm"), lax.axis_index("head")
    place = lax.rem(index, group)

    def in_plane(array, step):
        return lax.ppermute(array, "tm", [(i, i ^ step) for i in range(times)])

    def later(array, step):
        return lax.ppermute(array, "tm", [(i, i + step * group) for i in range(times - step * group)])

    def across(array, step):
        return lax.ppermute(array, "head", [(i, i ^ step) for i in range(cores)])

    def between_planes(array, step):
        return lax.ppermute(array, "tm", [(i, i ^ (step * group)) for i in range(times)])

    shape = jax.ShapeDtypeStruct
    rows = x_weight.shape[0]
    parity = lax.rem(core, 2)

    def along_planes(stacks):
        if planes != 4:
            return [stacks[0]] + [between_planes(stacks[step], step) for step in range(1, planes)]

        def pairs(chosen):
            return [(a * group + q, b * group + q) for a, b in chosen for q in range(group)]

        second = between_planes(stacks[2], 2)
        first = between_planes(stacks[1], 1)
        again, last, first = lax.optimization_barrier((second, stacks[3], first))
        third = lax.ppermute(again, "tm", pairs([(1, 0), (2, 3)]))
        middle = lax.ppermute(last, "tm", pairs([(1, 2), (2, 1)]))
        return [stacks[0], first, second, third, middle]

    offsets = (0, 1, 2, 3, 3) if planes == 4 else tuple(range(planes))
    half_count = frame_count // 2
    down, depth_tiles = rows // 16, depth // LANES
    payloads = call(
        functools.partial(first_kernel, group, planes),
        (
            *(shape((rows, 3 * width), BF16) for _ in range(group)),
            *(shape((-(-(down + depth_tiles + 1) // 8) * 16, depth), BF16) for _ in range(planes)),
        ),
        [log_decay, bc_weight, frames, x_weight, z_weight, out_weight.T],
        [
            pltpu.VMEM((rows, LANES), BF16),
            pltpu.VMEM((2, EDGE, depth), BF16),
            pltpu.VMEM(log_decay.shape, F32),
            pltpu.SemaphoreType.DMA((4 + 3 * group,)),
        ],
        smem=0,
        anywhere=6,
        vmem=ALL_VMEM_BYTES,
    )
    inner, outer = payloads[:group], payloads[group:]
    parts = [inner[0]] + [in_plane(inner[step], step) for step in range(1, group)]
    pieces = [outer[0]] + [between_planes(outer[step], step) for step in range(1, planes)]
    xz_stack, out_stack = call(
        functools.partial(stack_kernel, group),
        (shape((group * rows, 2 * width), BF16), shape((group * rows, width), BF16)),
        parts,
        flops=STACK_HINT,
        smem=0,
    )
    xz_pieces = along_planes([xz_stack] * planes)
    xz_pieces, out_stack = lax.optimization_barrier((xz_pieces, out_stack))
    out_pieces = [out_stack] + [between_planes(out_stack, step) for step in range(1, planes)]
    x_columns, z_columns = call(
        functools.partial(assemble_kernel, group, offsets),
        (shape((depth, width), BF16), shape((depth, width), BF16)),
        xz_pieces,
        flops=ASSEMBLE_HINT,
        smem=0,
    )
    decay_blocks = jnp.pad(log_decay.reshape(group, heads, frame_count), ((0, 0), (0, 8 - heads), (0, 0)))
    tiles = planes * down + depth_tiles + 1 + frame_count // SPAN * 2
    inward = call(
        functools.partial(inward_kernel, group, rows),
        tuple(shape((half_count + -(-tiles // 8) * 16, depth), BF16) for _ in range(group)),
        [decay_blocks, frames, *pieces],
        flops=INWARD_HINT,
        smem=0,
    )
    inward = [inward[0]] + [in_plane(inward[step], step) for step in range(1, group)]
    swap, bc_mine, halo, decay = call(
        functools.partial(swap_kernel, group, rows),
        (
            shape(((group - 1) * half_count + LANES, depth), BF16),
            shape((depth, LANES), BF16),
            shape((2 * EDGE, depth), BF16),
            shape((count * 8 + 8, SPAN), F32),
        ),
        inward,
        [pltpu.VMEM((count, 8, SPAN), F32)],
        smem=0,
    )
    swap = across(swap, 1)
    all_rows = total + SPAN

    frame_rows, x_rows, b_rows, c_rows, decay_rows, steps, keep, summary = call(
        functools.partial(state_kernel, group, heads, state),
        (
            shape((all_rows, depth), BF16),
            shape((all_rows, width), BF16),
            shape((all_rows, state), BF16),
            shape((all_rows, state), BF16),
            shape((3 * (count + 1) * 8, SPAN), F32),
            shape((count * state, width), F32),
            shape((-(-count // 8) * 8, width), F32),
            shape((state + EDGE, width), BF16),
        ),
        [record_lengths, decay, x_columns, bc_mine, frames, swap, halo, *inward[1:]],
        [pltpu.VMEM((depth, 2 * state), BF16), pltpu.VMEM((total, width), F32)],
        hidden=True,
    )
    summaries = [later(summary, step) for step in range(1, planes)]
    x_rows, out_pieces = lax.optimization_barrier((x_rows, out_pieces))
    y, carry = call(
        functools.partial(inner_kernel, group, heads),
        (shape((all_rows, width), F32), shape((all_rows, width), F32)),
        [x_rows, b_rows, c_rows, decay_rows],
        flops=4 * total * SPAN * width,
        smem=0,
    )
    silu = call(
        functools.partial(silu_kernel, group),
        shape((all_rows, width), F32),
        [norm_gain[None], frame_rows, z_columns],
        flops=2 * total * depth * width,
        smem=0,
    )
    gated = call(
        functools.partial(gate_kernel, heads, state),
        shape((all_rows, width), BF16),
        [c_rows, y, steps, carry, keep, silu, *summaries],
        flops=2 * total * state * width,
        smem=0,
    )
    ends = pltpu.SMEM((record_lengths.shape[0] + 1,), jnp.int32)
    far, near = (group - 1,), (*range(1, group - 1), 0)

    def conv(steps, gated):
        return call(
            functools.partial(conv_kernel, group, steps),
            shape((len(steps) * frame_count, width), BF16),
            [record_lengths, conv_weight, gated],
            [pltpu.VMEM((len(steps) * (frame_count + 2 * EDGE), width), F32), ends],
            flops=2 * len(steps) * frame_count * width * conv_weight.shape[0],
        )

    def out(steps, act, swapped):
        return call(
            functools.partial(out_kernel, cores),
            tuple(shape((frame_count, share), BF16 if step else F32) for step in steps),
            [act, *swapped, *out_parts],
            flops=2 * len(steps) * frame_count * width * cores * share,
            smem=0,
        )

    share = depth // cores
    out_parts = call(
        functools.partial(share_kernel, cores, tuple(range(planes)), group),
        tuple(shape((share, width), BF16) for _ in range(cores)),
        out_pieces,
        [pltpu.VMEM((depth, width), BF16)],
        smem=0,
    )
    out_parts, gated = lax.optimization_barrier((out_parts, gated))
    out_parts = [out_parts[0]] + [across(out_parts[step], step) for step in range(1, cores)]
    far_act = conv(far, gated)
    far_swapped = [across(far_act, step) for step in range(1, cores)]
    gated, far_act = lax.optimization_barrier((gated, far_act))
    near_act = conv(near, gated)
    near_act, far_swapped, out_parts = lax.optimization_barrier((near_act, far_swapped, out_parts))
    (far_out,) = out(far, far_act, far_swapped)
    near_act, far_out = lax.optimization_barrier((near_act, far_out))
    far_out = in_plane(far_out, far[0])
    near_swapped = [across(near_act, step) for step in range(1, cores)]
    near_outs = out(near, near_act, near_swapped)
    mixed = near_outs[-1] + far_out.astype(F32)
    for step, partial in zip(near[:-1], near_outs[:-1]):
        mixed = mixed + in_plane(partial, step).astype(F32)
    return mixed.astype(BF16)


def solution(mesh):
    in_specs = (
        P("tm", None),
        P("tm", "head"),
        P("tm", "head"),
        P("tm", None),
        P("head", "tm"),
        P("head"),
        P(None, "head"),
        P("head", "tm"),
        P(),
    )
    out_specs = P("tm", "head")
    return jax.shard_map(local, mesh=mesh, in_specs=in_specs, out_specs=out_specs, check_vma=False)
```

```python
import functools

import jax
import jax.numpy as jnp
from jax import lax
from jax.experimental import pallas as pl
from jax.experimental.pallas import tpu as pltpu
from jax.sharding import PartitionSpec as P

SPAN = 128
LANES = 128
EDGE = 16
CONV_ROWS = 64
BF16 = jnp.bfloat16
F32 = jnp.float32
STACK_HINT = 40_000_000_000
INWARD_HINT = 40_000_000_000
ASSEMBLE_HINT = 40_000_000_000
ALL_VMEM_BYTES = 63 * 1024 * 1024
VMEM_BYTES = 20 * 1024 * 1024


def dot(a, b, dims=((1,), (0,)), precision=None):
    return lax.dot_general(a, b, (dims, ((), ())), precision=precision, preferred_element_type=F32)


def call(kernel, out_shape, operands, scratch=(), flops=0, smem=1, anywhere=0, vmem=VMEM_BYTES, hidden=False):
    in_specs = [pl.BlockSpec(memory_space=pltpu.SMEM)] * smem
    in_specs += [pl.BlockSpec(memory_space=pltpu.VMEM)] * (len(operands) - smem - anywhere)
    in_specs += [pl.BlockSpec(memory_space=pl.ANY)] * anywhere
    moved = sum(a.size * a.dtype.itemsize for a in operands)
    moved += sum(a.size * a.dtype.itemsize for a in jax.tree.leaves(out_shape))
    if hidden:
        flops = moved = 0
    return pl.pallas_call(
        kernel,
        out_shape=out_shape,
        in_specs=in_specs,
        out_specs=jax.tree.map(lambda _: pl.BlockSpec(memory_space=pltpu.VMEM), out_shape),
        scratch_shapes=list(scratch),
        compiler_params=pltpu.CompilerParams(vmem_limit_bytes=vmem),
        cost_estimate=pl.CostEstimate(flops=flops, bytes_accessed=moved, transcendentals=0),
    )(*operands)


def plane_place(group):
    index = lax.axis_index("tm")
    return lax.rem(index, group), lax.div(index, group)


def record_starts(len_ref, position):
    start = jnp.zeros_like(position)
    end = jnp.int32(0)
    for record in range(len_ref.shape[0] - 1):
        end = end + len_ref[record]
        start = jnp.where(position >= end, end, start)
    return start


def fill_planes(plane, dest_ref, pieces, offsets, lanes=slice(None)):
    rows = pieces[0].shape[0]
    for offset in sorted(set(offsets)):
        same = [piece[:, lanes] for piece, at in zip(pieces, offsets) if at == offset]
        value = same[0] if len(same) == 1 else same[0] + same[1]
        dest_ref[pl.ds(pl.multiple_of((plane ^ offset) * rows, rows), rows), : value.shape[1]] = value


def first_kernel(group, planes, log_decay_ref, bc_ref, frames_ref, *refs):
    weight_refs, refs = refs[:3], refs[3:]
    inner_refs, outer_refs, refs = refs[:group], refs[group : group + planes], refs[group + planes :]
    bc_half_ref, edge_ref, decay_ref, sems = refs
    place, plane = plane_place(group)
    parity = lax.rem(lax.axis_index("head"), 2)
    width = weight_refs[0].shape[1] // group
    frames = frames_ref.shape[0]
    heads = log_decay_ref.shape[0] // group
    copies = [
        (bc_ref.at[:, pl.ds(pl.multiple_of(parity * LANES, LANES), LANES)], bc_half_ref),
        (frames_ref.at[:EDGE, :], edge_ref.at[0]),
        (frames_ref.at[frames - EDGE :, :], edge_ref.at[1]),
        (log_decay_ref, decay_ref),
    ]
    for step, inner_ref in enumerate(inner_refs):
        lanes = pl.ds(pl.multiple_of((place ^ step) * width, LANES), width)
        for number, weight_ref in enumerate(weight_refs):
            copies.append((weight_ref.at[:, lanes], inner_ref.at[:, number * width : (number + 1) * width]))
    started = [pltpu.make_async_copy(a, b, sems.at[number]) for number, (a, b) in enumerate(copies)]
    for copy in started:
        copy.start()
    for copy in started[:4]:
        copy.wait()
    lane = lax.broadcasted_iota(jnp.int32, (8, LANES), 1)
    decays = []
    for first in (0, frames - LANES):
        rows = [jnp.zeros((8, LANES), F32), jnp.zeros((8, LANES), F32)]
        for block in range(group):
            here = decay_ref[block * heads : (block + 1) * heads, first : first + LANES]
            here = jnp.concatenate([here, jnp.zeros((8 - heads, LANES), F32)], axis=0)
            for number, term in enumerate(three_terms(here)):
                slot = number * group + block
                moved = pltpu.roll(term, (slot % 8 * EDGE + (EDGE if first else 0)) % LANES, 1)
                rows[slot // 8] = jnp.where(lane // EDGE == slot % 8, moved, rows[slot // 8])
        decays.append(jnp.concatenate(rows, axis=0))
    for step, out_ref in enumerate(outer_refs):
        number = put(out_ref, 0, bc_half_ref[...])
        later = (plane ^ step) > plane
        number = put(out_ref, number, jnp.where(later, edge_ref[1].astype(F32), edge_ref[0].astype(F32)).astype(BF16))
        put(out_ref, number, jnp.where(later, decays[1], decays[0]).astype(BF16))
    for copy in started[4:]:
        copy.wait()


def stack_kernel(group, *refs):
    parts, stack_refs = refs[:group], refs[group:]
    place, _ = plane_place(group)
    rows = parts[0].shape[0]
    for step, part in enumerate(parts):
        at = pl.ds(pl.multiple_of((place ^ step) * rows, rows), rows)
        first = 0
        for stack_ref in stack_refs:
            width = stack_ref.shape[1]
            stack_ref[at, :] = part[:, first : first + width]
            first += width


def assemble_kernel(group, offsets, *refs):
    pieces, dest_refs = refs[: len(offsets)], refs[len(offsets) :]
    _, plane = plane_place(group)
    first = 0
    for dest_ref in dest_refs:
        width = dest_ref.shape[1]
        fill_planes(plane, dest_ref, pieces, offsets, slice(first, first + width))
        first += width


def tile(number):
    return slice(number // 8 * 16, number // 8 * 16 + 16), slice(number % 8 * LANES, (number % 8 + 1) * LANES)


def put(out_ref, number, array):
    for at in range(0, array.shape[0], 16):
        for lane in range(0, array.shape[1], LANES):
            out_ref[tile(number)] = array[at : at + 16, lane : lane + LANES]
            number += 1
    return number


def three_terms(value):
    terms = []
    for _ in range(3):
        term = value.astype(BF16).astype(F32)
        terms.append(term)
        value = value - term
    return terms


def inward_kernel(group, rows, decay_ref, frames_ref, *refs):
    piece_refs, out_refs = refs[:-group], refs[-group:]
    place, plane = plane_place(group)
    planes = len(piece_refs)
    half = frames_ref.shape[0] // 2
    mine = pl.ds(pl.multiple_of(lax.rem(lax.axis_index("head"), 2) * half, half), half)
    wanted = jnp.clip(jnp.where(place == 0, plane + 1, plane - 1), 0, planes - 1)
    depth_tiles = frames_ref.shape[1] // LANES
    down = rows // 16
    for step, out_ref in enumerate(out_refs):
        out_ref[:half, :] = frames_ref[mine, :]
        number = half // 16 * depth_tiles
        for piece_ref in piece_refs:
            for at in range(down):
                out_ref[tile(number)] = piece_ref[tile(at)]
                number += 1
        for offset, piece_ref in enumerate(piece_refs):

            @pl.when((plane ^ offset) == wanted)
            def _(piece_ref=piece_ref, number=number, out_ref=out_ref):
                for at in range(depth_tiles + 1):
                    out_ref[tile(number + at)] = piece_ref[tile(down + at)]

        number += depth_tiles + 1
        terms = three_terms(decay_ref[place ^ step])
        terms = jnp.concatenate([*terms, jnp.zeros_like(terms[0])], axis=0).astype(BF16)
        for span in range(terms.shape[1] // SPAN):
            number = put(out_ref, number, terms[:, span * SPAN : (span + 1) * SPAN])


def swap_kernel(group, rows, *refs):
    part_refs, (swap_ref, bc_ref, halo_ref, decay_ref, span_ref) = refs[:group], refs[group:]
    half_refs = part_refs[1:]
    place, plane = plane_place(group)
    planes = bc_ref.shape[0] // (group * rows)
    count = span_ref.shape[0]
    spans = count // group
    down = rows // 16
    depth_tiles = swap_ref.shape[1] // LANES
    height = LANES
    top = swap_ref.shape[0] - height
    half = top // len(half_refs)
    lane = lax.broadcasted_iota(jnp.int32, (8, LANES), 1)
    for step, part_ref in enumerate(part_refs):
        block = place ^ step
        number = half // 16 * depth_tiles
        for offset in range(planes):
            first = ((plane ^ offset) * group + block) * rows
            for at in range(down):
                bc_ref[pl.ds(pl.multiple_of(first + at * 16, 16), 16), :] = part_ref[tile(number)]
                number += 1
        for side, owner in enumerate((group - 1, 0)):

            @pl.when(block == owner)
            def _(part_ref=part_ref, number=number, side=side):
                for at in range(depth_tiles):
                    halo_ref[side * EDGE : (side + 1) * EDGE, at * LANES : (at + 1) * LANES] = part_ref[tile(number + at)]
                packed = part_ref[tile(number + depth_tiles)].astype(F32)
                chosen = jnp.zeros((8, LANES), F32)
                for head_block in range(group):
                    value = jnp.zeros((8, LANES), F32)
                    for term in range(3):
                        slot = term * group + head_block
                        half = packed[slot // 8 * 8 : slot // 8 * 8 + 8]
                        value = value + pltpu.roll(half, (LANES - slot % 8 * EDGE) % LANES, 1)
                    chosen = jnp.where(place == head_block, value, chosen)
                if side:
                    last = pltpu.roll(chosen, EDGE, 1)
                    decay_ref[count * 8 :, :] = jnp.where((lane >= EDGE) & (lane < 2 * EDGE), last, 0.0)
                else:
                    decay_ref[:8, :] = jnp.where(lane < EDGE, chosen, 0.0)

        number += depth_tiles + 1
        for span in range(spans):
            upper = part_ref[tile(number)].astype(F32)
            lower = part_ref[tile(number + 1)].astype(F32)
            number += 2
            span_ref[block * spans + span] = upper[:8] + upper[8:] + lower[:8]
    for span in range(count):
        moved = pltpu.roll(span_ref[span], EDGE, 1)
        here, after = slice(span * 8, span * 8 + 8), slice(span * 8 + 8, span * 8 + 16)
        decay_ref[here, :] = jnp.where(lane < EDGE, decay_ref[here, :], moved)
        kept = decay_ref[after, :] if span == count - 1 else jnp.zeros((8, LANES), F32)
        decay_ref[after, :] = jnp.where(lane < EDGE, moved, kept)
    for number, half_ref in enumerate(half_refs):
        swap_ref[number * half : (number + 1) * half, :] = half_ref[:half, : swap_ref.shape[1]]
    for number in range(bc_ref.shape[0] // height):
        lanes = slice(number * LANES, (number + 1) * LANES)
        swap_ref[top:, lanes] = bc_ref[number * height : (number + 1) * height, :]


def lanes_of(rows, width, head_size):
    high = rows.astype(BF16).astype(F32)
    owner = lax.broadcasted_iota(jnp.int32, (16, width), 1) // head_size
    chosen = jnp.where((lax.broadcasted_iota(jnp.int32, (16, width), 0) & 7) == owner, 1.0, 0.0).astype(BF16)
    return dot(jnp.concatenate([high, rows - high], axis=0).astype(BF16), chosen, ((0,), (0,)))


def spans_in_lanes(rows):
    return jnp.concatenate([rows[at : at + 8] for at in range(0, rows.shape[0], 8)], axis=1)


def row_blocks(total, wide):
    return [slice(at, at + 256) for at in range(0, total, 256)] + [slice(total, wide)]


def state_kernel(group, heads, state, len_ref, decay_ref, x_weight_ref, bc_half_ref, own_ref, swap_ref, halo_ref, *refs):
    half_refs, refs = refs[: group - 1], refs[group - 1 :]
    frames_ref, x_ref, b_ref, c_ref, rows_ref, step_ref, keep_ref, send_ref, weight_ref, tail_ref = refs
    place, plane = plane_place(group)
    parity = lax.rem(lax.axis_index("head"), 2)
    width = x_ref.shape[1]
    frames = own_ref.shape[0]
    total = frames * group
    half = frames // 2
    head_size = width // heads
    count = total // SPAN
    base = plane * total - EDGE
    wide = total + 2 * EDGE
    frames_ref[:EDGE, :] = halo_ref[:EDGE, :]
    frames_ref[total + EDGE : wide, :] = halo_ref[EDGE:, :]
    frames_ref[wide:, :] = jnp.zeros((frames_ref.shape[0] - wide, frames_ref.shape[1]), BF16)
    frames_ref[pl.ds(pl.multiple_of(EDGE + place * frames, EDGE), frames), :] = own_ref[...]
    for number, half_ref in enumerate(half_refs):
        block = EDGE + (place ^ (number + 1)) * frames
        mine = pl.ds(pl.multiple_of(block + parity * half, EDGE), half)
        other = pl.ds(pl.multiple_of(block + (1 - parity) * half, EDGE), half)
        frames_ref[mine, :] = half_ref[:half, : frames_ref.shape[1]]
        frames_ref[other, :] = swap_ref[number * half : (number + 1) * half, :]
    mine = pl.ds(pl.multiple_of(parity * LANES, LANES), LANES)
    other = pl.ds(pl.multiple_of((1 - parity) * LANES, LANES), LANES)
    weight_ref[:, mine] = bc_half_ref[...]
    top = len(half_refs) * half
    height = swap_ref.shape[0] - top
    for number in range(weight_ref.shape[0] // height):
        lanes = slice(number * LANES, (number + 1) * LANES)
        weight_ref[number * height : (number + 1) * height, other] = swap_ref[top:, lanes]

    decay = decay_ref[...]
    used = decay.shape[0]
    square = (SPAN, SPAN)
    row, lane = (lax.broadcasted_iota(jnp.int32, square, dim) for dim in (0, 1))
    upper = jnp.where(row <= lane, 1.0, 0.0).astype(F32)
    cumul = dot(decay, upper, precision=lax.Precision.HIGHEST)
    whole = dot(decay, jnp.ones(square, F32), precision=lax.Precision.HIGHEST)
    first = base + lax.broadcasted_iota(jnp.int32, (used, SPAN), 0) // 8 * SPAN
    position = first + lane[:1]
    start = record_starts(len_ref, position)
    start_last = record_starts(len_ref, first + (SPAN - 1))
    carried = jnp.where(start < first, jnp.exp(cumul), 0.0)
    tail = jnp.where(position >= start_last, jnp.exp(whole - cumul), 0.0)
    keep = jnp.where(start_last < first, jnp.exp(whole), 0.0)
    rows_ref[:used, :] = cumul
    rows_ref[used : 2 * used, :] = start.astype(F32)
    rows_ref[2 * used :, :] = carried

    for rows in row_blocks(total, wide):
        x_ref[rows, :] = dot(frames_ref[rows, :], x_weight_ref[...]).astype(BF16)
        product = dot(frames_ref[rows, :], weight_ref[...])
        b_ref[rows, :] = product[:, :state].astype(BF16)
        c_ref[rows, :] = product[:, state:].astype(BF16)
    for ref in (x_ref, b_ref, c_ref):
        ref[wide:, :] = jnp.zeros((ref.shape[0] - wide, ref.shape[1]), BF16)

    tail_ref[...] = lanes_of(spans_in_lanes(tail[: count * 8]), width, head_size)
    by_span = jnp.zeros((8, SPAN), F32)
    for block in range(count):
        by_span = jnp.where(lane[:8] == block, keep[block * 8 : (block + 1) * 8], by_span)
    kept = lanes_of(by_span, width, head_size)[: keep_ref.shape[0]]
    keep_ref[...] = kept
    entry = jnp.zeros((state, width), F32)
    through = jnp.ones((1, width), F32)
    for block in range(count):
        rows = slice(block * SPAN, (block + 1) * SPAN)
        weighed = x_ref[rows, :].astype(F32) * tail_ref[rows, :]
        step = dot(b_ref[rows, :], weighed.astype(BF16), ((0,), (0,)))
        step_ref[block * state : (block + 1) * state, :] = step
        entry = kept[block : block + 1] * entry + step
        through = through * kept[block : block + 1]
    send_ref[:state, :] = entry.astype(BF16)
    send_ref[state:, :] = jnp.broadcast_to(through, (EDGE, width)).astype(BF16)


def inner_kernel(group, heads, x_ref, b_ref, c_ref, rows_ref, y_ref, carry_ref):
    _, plane = plane_place(group)
    total, width = x_ref.shape
    head_size = width // heads
    count = total // SPAN
    base = plane * (total - SPAN) - EDGE
    used = rows_ref.shape[0] // 3
    square = (SPAN, SPAN)
    parts = [rows_ref[: 2 * used, :]]
    if 2 * used % SPAN:
        parts.append(jnp.zeros((SPAN - 2 * used % SPAN, SPAN), F32))
    columns = jnp.concatenate(parts, axis=0).T
    carry_ref[...] = lanes_of(spans_in_lanes(rows_ref[2 * used :, :]), width, head_size)
    row, lane = (lax.broadcasted_iota(jnp.int32, square, dim) for dim in (0, 1))
    lower = row >= lane
    tile_heads = LANES // head_size
    tile_lane = lax.broadcasted_iota(jnp.int32, (1, LANES), 1) // head_size
    masks = [jnp.where(tile_lane == inner, 1.0, 0.0).astype(BF16) for inner in range(tile_heads)]
    for block in range(count):
        rows = slice(block * SPAN, (block + 1) * SPAN)
        at = block * 8
        x = x_ref[rows, :]
        scores = dot(c_ref[rows, :], b_ref[rows, :], ((1,), (1,)))
        here = (base + block * SPAN + lane).astype(F32)
        start_here = jnp.broadcast_to(columns[:, used + at : used + at + 1], square)
        joined = lower & (here >= start_here)
        for tile in range(width // LANES):
            mixes, values = [], []
            for inner in range(tile_heads):
                which = at + tile * tile_heads + inner
                column = jnp.broadcast_to(columns[:, which : which + 1], square)
                gap = jnp.where(joined, column - rows_ref[which : which + 1, :], -1e30)
                mixes.append((jnp.exp(gap) * scores).astype(BF16))
                values.append(x[:, tile * LANES : (tile + 1) * LANES] * masks[inner])
            y_ref[rows, tile * LANES : (tile + 1) * LANES] = dot(
                jnp.concatenate(mixes, axis=1), jnp.concatenate(values, axis=0)
            )


def silu_kernel(group, gain_ref, frames_ref, weight_ref, out_ref):
    place, _ = plane_place(group)
    rows_all, width = out_ref.shape
    total = rows_all - SPAN
    wide = total + 2 * EDGE
    gain = gain_ref[:, pl.ds(pl.multiple_of(place * width, LANES), width)]
    for rows in row_blocks(total, wide):
        z = dot(frames_ref[rows, :], weight_ref[...]).astype(BF16).astype(F32)
        out_ref[rows, :] = z / (1.0 + jnp.exp(-z)) * gain
    out_ref[wide:, :] = jnp.zeros((rows_all - wide, width), F32)


def share_kernel(cores, offsets, group, *refs):
    pieces, refs = refs[: len(offsets)], refs[len(offsets) :]
    outs, weight_ref = refs[:cores], refs[cores]
    _, plane = plane_place(group)
    core = lax.axis_index("head")
    fill_planes(plane, weight_ref, pieces, offsets)
    for step, out_ref in enumerate(outs):
        rows = out_ref.shape[0]
        out_ref[...] = weight_ref[pl.ds(pl.multiple_of((core ^ step) * rows, rows), rows), :]


def gate_kernel(heads, state, c_ref, y_ref, step_ref, carry_ref, keep_ref, silu_ref, *refs):
    earlier, gated_ref = refs[:-1], refs[-1]
    total, width = y_ref.shape
    head_size = width // heads
    count = total // SPAN
    entry = jnp.zeros((state, width), F32)
    for summary in reversed(earlier):
        through = summary[state : state + EDGE, :].astype(F32)[:1]
        entry = through * entry + summary[:state, :].astype(F32)
    owner = [lax.broadcasted_iota(jnp.int32, (width, width), dim) // head_size for dim in (0, 1)]
    average = jnp.where(owner[0] == owner[1], 1.0 / head_size, 0.0).astype(BF16)
    for block in range(count):
        rows = slice(block * SPAN, (block + 1) * SPAN)
        y = y_ref[rows, :] + carry_ref[rows, :] * dot(c_ref[rows, :], entry.astype(BF16))
        square_mean = dot((y * y).astype(BF16), average)
        gated_ref[rows, :] = (y * lax.rsqrt(square_mean + 1e-05) * silu_ref[rows, :]).astype(BF16)
        if block < count - 1:
            entry = keep_ref[block : block + 1, :] * entry + step_ref[block * state : (block + 1) * state, :]


def conv_kernel(group, steps, len_ref, taps_ref, gated_ref, act_ref, ext_ref, ends_ref):
    place, plane = plane_place(group)
    rows_all, width = gated_ref.shape
    total = rows_all - SPAN
    frames = total // group
    taps = taps_ref.shape[0]
    half = (taps - 1) // 2
    stream = lax.axis_size("tm") // group * total
    records = len_ref.shape[0]
    reach = CONV_ROWS + 2 * EDGE
    first_tap = EDGE - half
    pitch = frames + 2 * EDGE
    ends_ref[0] = 0
    for record in range(records):
        ends_ref[record + 1] = ends_ref[record] + len_ref[record]
    for number, step in enumerate(steps):
        first = pl.multiple_of((place ^ step) * frames, frames)
        ext_ref[number * pitch : (number + 1) * pitch, :] = gated_ref[pl.ds(first, pitch), :].astype(F32)

    def record_at(position):
        found = jnp.int32(0)
        for record in range(records - 1):
            found = found + (ends_ref[record + 1] <= position).astype(jnp.int32)
        return found

    for number, step in enumerate(steps):
        base = plane * total + (place ^ step) * frames

        def one_block(block, _, number=number, base=base):
            inside_part = pl.multiple_of(block * CONV_ROWS, CONV_ROWS)
            source = pl.multiple_of(number * pitch + inside_part, EDGE)
            target = pl.multiple_of(number * frames + inside_part, CONV_ROWS)
            at = base + inside_part
            low = record_at(jnp.maximum(at - half, 0))
            high = record_at(jnp.minimum(at + CONV_ROWS - 1 + half, stream - 1))
            near = lax.broadcasted_iota(jnp.int32, (reach, LANES), 0) + (at - EDGE)
            for tile in range(width // LANES):
                lanes = slice(tile * LANES, (tile + 1) * LANES)
                weights = taps_ref[:, pl.ds(pl.multiple_of(place * width + tile * LANES, LANES), LANES)]

                def one_record(record, done):
                    inside = (near >= ends_ref[record]) & (near < ends_ref[record + 1])
                    g = jnp.where(inside, ext_ref[pl.ds(source, reach), lanes], 0.0)
                    out = None
                    for phase in range(8):
                        part = None
                        for offset in range(phase, reach - CONV_ROWS, 8):
                            tap = offset - first_tap
                            if 0 <= tap < taps:
                                aligned = offset - phase
                                term = weights[tap : tap + 1, :] * g[aligned : aligned + CONV_ROWS + 8, :]
                                part = term if part is None else part + term
                        if part is not None:
                            moved = part[phase : phase + CONV_ROWS, :]
                            out = moved if out is None else out + moved
                    return jnp.where(inside[EDGE : EDGE + CONV_ROWS], out, done)

                conv = lax.fori_loop(low, high + 1, one_record, jnp.zeros((CONV_ROWS, LANES), F32))
                act_ref[pl.ds(target, CONV_ROWS), lanes] = (conv / (1.0 + jnp.exp(-conv))).astype(BF16)
            return 0

        lax.fori_loop(0, frames // CONV_ROWS, one_block, 0)


def out_kernel(cores, *refs):
    acts, weights, outs = refs[:cores], refs[cores : 2 * cores], refs[2 * cores :]
    frames = outs[0].shape[0]
    for number, out_ref in enumerate(outs):
        rows = slice(number * frames, (number + 1) * frames)
        total = None
        for act, weight in zip(acts, weights):
            product = dot(act[rows, :], weight[...], ((1,), (1,)))
            total = product if total is None else total + product
        out_ref[...] = total.astype(out_ref.dtype)


def local(
    frames,
    x_weight,
    z_weight,
    bc_weight,
    log_decay,
    norm_gain,
    conv_weight,
    out_weight,
    record_lengths,
):
    times, cores = lax.axis_size("tm"), lax.axis_size("head")
    frame_count, depth = frames.shape
    heads_here, channels = log_decay.shape[0], x_weight.shape[1]
    state = bc_weight.shape[1] // 2
    group = 4
    while group > 1 and (channels // group % LANES or times % group or heads_here % group):
        group //= 2
    planes = times // group
    width, heads = channels // group, heads_here // group
    total = frame_count * group
    count = total // SPAN
    index, core = lax.axis_index("tm"), lax.axis_index("head")
    place = lax.rem(index, group)

    def in_plane(array, step):
        return lax.ppermute(array, "tm", [(i, i ^ step) for i in range(times)])

    def later(array, step):
        return lax.ppermute(array, "tm", [(i, i + step * group) for i in range(times - step * group)])

    def across(array, step):
        return lax.ppermute(array, "head", [(i, i ^ step) for i in range(cores)])

    def between_planes(array, step):
        return lax.ppermute(array, "tm", [(i, i ^ (step * group)) for i in range(times)])

    shape = jax.ShapeDtypeStruct
    rows = x_weight.shape[0]
    parity = lax.rem(core, 2)

    def along_planes(stacks):
        if planes != 4:
            return [stacks[0]] + [between_planes(stacks[step], step) for step in range(1, planes)]

        def pairs(chosen):
            return [(a * group + q, b * group + q) for a, b in chosen for q in range(group)]

        second = between_planes(stacks[2], 2)
        first = between_planes(stacks[1], 1)
        again, last, first = lax.optimization_barrier((second, stacks[3], first))
        third = lax.ppermute(again, "tm", pairs([(1, 0), (2, 3)]))
        middle = lax.ppermute(last, "tm", pairs([(1, 2), (2, 1)]))
        return [stacks[0], first, second, third, middle]

    offsets = (0, 1, 2, 3, 3) if planes == 4 else tuple(range(planes))
    half_count = frame_count // 2
    down, depth_tiles = rows // 16, depth // LANES
    payloads = call(
        functools.partial(first_kernel, group, planes),
        (
            *(shape((rows, 3 * width), BF16) for _ in range(group)),
            *(shape((-(-(down + depth_tiles + 1) // 8) * 16, depth), BF16) for _ in range(planes)),
        ),
        [log_decay, bc_weight, frames, x_weight, z_weight, out_weight.T],
        [
            pltpu.VMEM((rows, LANES), BF16),
            pltpu.VMEM((2, EDGE, depth), BF16),
            pltpu.VMEM(log_decay.shape, F32),
            pltpu.SemaphoreType.DMA((4 + 3 * group,)),
        ],
        smem=0,
        anywhere=6,
        vmem=ALL_VMEM_BYTES,
    )
    inner, outer = payloads[:group], payloads[group:]
    parts = [inner[0]] + [in_plane(inner[step], step) for step in range(1, group)]
    pieces = [outer[0]] + [between_planes(outer[step], step) for step in range(1, planes)]
    xz_stack, out_stack = call(
        functools.partial(stack_kernel, group),
        (shape((group * rows, 2 * width), BF16), shape((group * rows, width), BF16)),
        parts,
        flops=STACK_HINT,
        smem=0,
    )
    xz_pieces = along_planes([xz_stack] * planes)
    xz_pieces, out_stack = lax.optimization_barrier((xz_pieces, out_stack))
    out_pieces = [out_stack] + [between_planes(out_stack, step) for step in range(1, planes)]
    x_columns, z_columns = call(
        functools.partial(assemble_kernel, group, offsets),
        (shape((depth, width), BF16), shape((depth, width), BF16)),
        xz_pieces,
        flops=ASSEMBLE_HINT,
        smem=0,
    )
    decay_blocks = jnp.pad(log_decay.reshape(group, heads, frame_count), ((0, 0), (0, 8 - heads), (0, 0)))
    tiles = planes * down + depth_tiles + 1 + frame_count // SPAN * 2
    inward = call(
        functools.partial(inward_kernel, group, rows),
        tuple(shape((half_count + -(-tiles // 8) * 16, depth), BF16) for _ in range(group)),
        [decay_blocks, frames, *pieces],
        flops=INWARD_HINT,
        smem=0,
    )
    inward = [inward[0]] + [in_plane(inward[step], step) for step in range(1, group)]
    swap, bc_mine, halo, decay = call(
        functools.partial(swap_kernel, group, rows),
        (
            shape(((group - 1) * half_count + LANES, depth), BF16),
            shape((depth, LANES), BF16),
            shape((2 * EDGE, depth), BF16),
            shape((count * 8 + 8, SPAN), F32),
        ),
        inward,
        [pltpu.VMEM((count, 8, SPAN), F32)],
        smem=0,
    )
    swap = across(swap, 1)
    all_rows = total + SPAN

    frame_rows, x_rows, b_rows, c_rows, decay_rows, steps, keep, summary = call(
        functools.partial(state_kernel, group, heads, state),
        (
            shape((all_rows, depth), BF16),
            shape((all_rows, width), BF16),
            shape((all_rows, state), BF16),
            shape((all_rows, state), BF16),
            shape((3 * (count + 1) * 8, SPAN), F32),
            shape((count * state, width), F32),
            shape((-(-count // 8) * 8, width), F32),
            shape((state + EDGE, width), BF16),
        ),
        [record_lengths, decay, x_columns, bc_mine, frames, swap, halo, *inward[1:]],
        [pltpu.VMEM((depth, 2 * state), BF16), pltpu.VMEM((total, width), F32)],
        hidden=True,
    )
    summaries = [later(summary, step) for step in range(1, planes)]
    x_rows, out_pieces = lax.optimization_barrier((x_rows, out_pieces))
    y, carry = call(
        functools.partial(inner_kernel, group, heads),
        (shape((all_rows, width), F32), shape((all_rows, width), F32)),
        [x_rows, b_rows, c_rows, decay_rows],
        flops=4 * total * SPAN * width,
        smem=0,
    )
    silu = call(
        functools.partial(silu_kernel, group),
        shape((all_rows, width), F32),
        [norm_gain[None], frame_rows, z_columns],
        flops=2 * total * depth * width,
        smem=0,
    )
    gated = call(
        functools.partial(gate_kernel, heads, state),
        shape((all_rows, width), BF16),
        [c_rows, y, steps, carry, keep, silu, *summaries],
        flops=2 * total * state * width,
        smem=0,
    )
    ends = pltpu.SMEM((record_lengths.shape[0] + 1,), jnp.int32)

    def conv(steps, gated):
        return call(
            functools.partial(conv_kernel, group, steps),
            shape((len(steps) * frame_count, width), BF16),
            [record_lengths, conv_weight, gated],
            [pltpu.VMEM((len(steps) * (frame_count + 2 * EDGE), width), F32), ends],
            flops=2 * len(steps) * frame_count * width * conv_weight.shape[0],
        )

    def out(steps, act, swapped):
        return call(
            functools.partial(out_kernel, cores),
            tuple(shape((frame_count, share), BF16 if step else F32) for step in steps),
            [act, *swapped, *out_parts],
            flops=2 * len(steps) * frame_count * width * cores * share,
            smem=0,
        )

    share = depth // cores
    out_parts = call(
        functools.partial(share_kernel, cores, tuple(range(planes)), group),
        tuple(shape((share, width), BF16) for _ in range(cores)),
        out_pieces,
        [pltpu.VMEM((depth, width), BF16)],
        smem=0,
    )
    out_parts, gated = lax.optimization_barrier((out_parts, gated))
    out_parts = [out_parts[0]] + [across(out_parts[step], step) for step in range(1, cores)]
    stages = [(step,) for step in range(group - 1, 1, -2)] + [(1,)] if group > 2 else [(1,)]
    stages.append((*(step for step in range(2, group) if (step,) not in stages), 0))
    act, products = None, []
    for number, steps in enumerate(stages):
        gated, act = lax.optimization_barrier((gated, act))
        act = conv(steps, gated)
        if number:
            act, swapped = lax.optimization_barrier((act, swapped))
            done = out(stages[number - 1], last_act, swapped)
            act, done = lax.optimization_barrier((act, done))
            received = [in_plane(part, step) for part, step in zip(done, stages[number - 1])]
            products += received
            if number == len(stages) - 1:
                act, products[0] = lax.optimization_barrier((act, products[0]))
        swapped = [across(act, step) for step in range(1, cores)]
        last_act = act
    done = out(stages[-1], last_act, swapped)
    products += [in_plane(part, step) for part, step in zip(done[:-1], stages[-1])]
    mixed = done[-1]
    for product in products:
        mixed = mixed + product.astype(F32)
    return mixed.astype(BF16)


def solution(mesh):
    in_specs = (
        P("tm", None),
        P("tm", "head"),
        P("tm", "head"),
        P("tm", None),
        P("head", "tm"),
        P("head"),
        P(None, "head"),
        P("head", "tm"),
        P(),
    )
    out_specs = P("tm", "head")
    return jax.shard_map(local, mesh=mesh, in_specs=in_specs, out_specs=out_specs, check_vma=False)
```

```python
import functools

import jax
import jax.numpy as jnp
from jax import lax
from jax.experimental import pallas as pl
from jax.experimental.pallas import tpu as pltpu
from jax.sharding import PartitionSpec as P

SPAN = 128
LANES = 128
EDGE = 16
CONV_ROWS = 64
BF16 = jnp.bfloat16
F32 = jnp.float32
STACK_HINT = 40_000_000_000
INWARD_HINT = 40_000_000_000
ASSEMBLE_HINT = 40_000_000_000
ALL_VMEM_BYTES = 63 * 1024 * 1024
VMEM_BYTES = 20 * 1024 * 1024


def dot(a, b, dims=((1,), (0,)), precision=None):
    return lax.dot_general(a, b, (dims, ((), ())), precision=precision, preferred_element_type=F32)


def call(kernel, out_shape, operands, scratch=(), flops=0, smem=1, anywhere=0, vmem=VMEM_BYTES, hidden=False):
    in_specs = [pl.BlockSpec(memory_space=pltpu.SMEM)] * smem
    in_specs += [pl.BlockSpec(memory_space=pltpu.VMEM)] * (len(operands) - smem - anywhere)
    in_specs += [pl.BlockSpec(memory_space=pl.ANY)] * anywhere
    moved = sum(a.size * a.dtype.itemsize for a in operands)
    moved += sum(a.size * a.dtype.itemsize for a in jax.tree.leaves(out_shape))
    if hidden:
        flops = moved = 0
    return pl.pallas_call(
        kernel,
        out_shape=out_shape,
        in_specs=in_specs,
        out_specs=jax.tree.map(lambda _: pl.BlockSpec(memory_space=pltpu.VMEM), out_shape),
        scratch_shapes=list(scratch),
        compiler_params=pltpu.CompilerParams(vmem_limit_bytes=vmem),
        cost_estimate=pl.CostEstimate(flops=flops, bytes_accessed=moved, transcendentals=0),
    )(*operands)


def plane_place(group):
    index = lax.axis_index("tm")
    return lax.rem(index, group), lax.div(index, group)


def record_starts(len_ref, position):
    start = jnp.zeros_like(position)
    end = jnp.int32(0)
    for record in range(len_ref.shape[0] - 1):
        end = end + len_ref[record]
        start = jnp.where(position >= end, end, start)
    return start


def fill_planes(plane, dest_ref, pieces, offsets, lanes=slice(None)):
    rows = pieces[0].shape[0]
    for offset in sorted(set(offsets)):
        same = [piece[:, lanes] for piece, at in zip(pieces, offsets) if at == offset]
        value = same[0] if len(same) == 1 else same[0] + same[1]
        dest_ref[pl.ds(pl.multiple_of((plane ^ offset) * rows, rows), rows), : value.shape[1]] = value


def first_kernel(group, planes, log_decay_ref, bc_ref, frames_ref, *refs):
    weight_refs, refs = refs[:3], refs[3:]
    inner_refs, outer_refs, refs = refs[:group], refs[group : group + planes], refs[group + planes :]
    bc_half_ref, edge_ref, decay_ref, sems = refs
    place, plane = plane_place(group)
    parity = lax.rem(lax.axis_index("head"), 2)
    width = weight_refs[0].shape[1] // group
    frames = frames_ref.shape[0]
    heads = log_decay_ref.shape[0] // group
    copies = [
        (bc_ref.at[:, pl.ds(pl.multiple_of(parity * LANES, LANES), LANES)], bc_half_ref),
        (frames_ref.at[:EDGE, :], edge_ref.at[0]),
        (frames_ref.at[frames - EDGE :, :], edge_ref.at[1]),
        (log_decay_ref, decay_ref),
    ]
    for step, inner_ref in enumerate(inner_refs):
        lanes = pl.ds(pl.multiple_of((place ^ step) * width, LANES), width)
        for number, weight_ref in enumerate(weight_refs):
            copies.append((weight_ref.at[:, lanes], inner_ref.at[:, number * width : (number + 1) * width]))
    started = [pltpu.make_async_copy(a, b, sems.at[number]) for number, (a, b) in enumerate(copies)]
    for copy in started:
        copy.start()
    for copy in started[:4]:
        copy.wait()
    lane = lax.broadcasted_iota(jnp.int32, (8, LANES), 1)
    decays = []
    for first in (0, frames - LANES):
        rows = [jnp.zeros((8, LANES), F32), jnp.zeros((8, LANES), F32)]
        for block in range(group):
            here = decay_ref[block * heads : (block + 1) * heads, first : first + LANES]
            here = jnp.concatenate([here, jnp.zeros((8 - heads, LANES), F32)], axis=0)
            for number, term in enumerate(three_terms(here)):
                slot = number * group + block
                moved = pltpu.roll(term, (slot % 8 * EDGE + (EDGE if first else 0)) % LANES, 1)
                rows[slot // 8] = jnp.where(lane // EDGE == slot % 8, moved, rows[slot // 8])
        decays.append(jnp.concatenate(rows, axis=0))
    for step, out_ref in enumerate(outer_refs):
        number = put(out_ref, 0, bc_half_ref[...])
        later = (plane ^ step) > plane
        number = put(out_ref, number, jnp.where(later, edge_ref[1].astype(F32), edge_ref[0].astype(F32)).astype(BF16))
        put(out_ref, number, jnp.where(later, decays[1], decays[0]).astype(BF16))
    for copy in started[4:]:
        copy.wait()


def stack_kernel(group, *refs):
    parts, stack_refs = refs[:group], refs[group:]
    place, _ = plane_place(group)
    rows = parts[0].shape[0]
    for step, part in enumerate(parts):
        at = pl.ds(pl.multiple_of((place ^ step) * rows, rows), rows)
        first = 0
        for stack_ref in stack_refs:
            width = stack_ref.shape[1]
            stack_ref[at, :] = part[:, first : first + width]
            first += width


def assemble_kernel(group, offsets, *refs):
    pieces, dest_refs = refs[: len(offsets)], refs[len(offsets) :]
    _, plane = plane_place(group)
    first = 0
    for dest_ref in dest_refs:
        width = dest_ref.shape[1]
        fill_planes(plane, dest_ref, pieces, offsets, slice(first, first + width))
        first += width


def tile(number):
    return slice(number // 8 * 16, number // 8 * 16 + 16), slice(number % 8 * LANES, (number % 8 + 1) * LANES)


def put(out_ref, number, array):
    for at in range(0, array.shape[0], 16):
        for lane in range(0, array.shape[1], LANES):
            out_ref[tile(number)] = array[at : at + 16, lane : lane + LANES]
            number += 1
    return number


def three_terms(value):
    terms = []
    for _ in range(3):
        term = value.astype(BF16).astype(F32)
        terms.append(term)
        value = value - term
    return terms


def inward_kernel(group, rows, decay_ref, frames_ref, *refs):
    piece_refs, out_refs = refs[:-group], refs[-group:]
    place, plane = plane_place(group)
    planes = len(piece_refs)
    half = frames_ref.shape[0] // 2
    mine = pl.ds(pl.multiple_of(lax.rem(lax.axis_index("head"), 2) * half, half), half)
    wanted = jnp.clip(jnp.where(place == 0, plane + 1, plane - 1), 0, planes - 1)
    depth_tiles = frames_ref.shape[1] // LANES
    down = rows // 16
    for step, out_ref in enumerate(out_refs):
        out_ref[:half, :] = frames_ref[mine, :]
        number = half // 16 * depth_tiles
        for piece_ref in piece_refs:
            for at in range(down):
                out_ref[tile(number)] = piece_ref[tile(at)]
                number += 1
        for offset, piece_ref in enumerate(piece_refs):

            @pl.when((plane ^ offset) == wanted)
            def _(piece_ref=piece_ref, number=number, out_ref=out_ref):
                for at in range(depth_tiles + 1):
                    out_ref[tile(number + at)] = piece_ref[tile(down + at)]

        number += depth_tiles + 1
        terms = three_terms(decay_ref[place ^ step])
        terms = jnp.concatenate([*terms, jnp.zeros_like(terms[0])], axis=0).astype(BF16)
        for span in range(terms.shape[1] // SPAN):
            number = put(out_ref, number, terms[:, span * SPAN : (span + 1) * SPAN])


def swap_kernel(group, rows, *refs):
    part_refs, (swap_ref, bc_ref, halo_ref, decay_ref, span_ref) = refs[:group], refs[group:]
    half_refs = part_refs[1:]
    place, plane = plane_place(group)
    planes = bc_ref.shape[0] // (group * rows)
    count = span_ref.shape[0]
    spans = count // group
    down = rows // 16
    depth_tiles = swap_ref.shape[1] // LANES
    height = LANES
    top = swap_ref.shape[0] - height
    half = top // len(half_refs)
    lane = lax.broadcasted_iota(jnp.int32, (8, LANES), 1)
    for step, part_ref in enumerate(part_refs):
        block = place ^ step
        number = half // 16 * depth_tiles
        for offset in range(planes):
            first = ((plane ^ offset) * group + block) * rows
            for at in range(down):
                bc_ref[pl.ds(pl.multiple_of(first + at * 16, 16), 16), :] = part_ref[tile(number)]
                number += 1
        for side, owner in enumerate((group - 1, 0)):

            @pl.when(block == owner)
            def _(part_ref=part_ref, number=number, side=side):
                for at in range(depth_tiles):
                    halo_ref[side * EDGE : (side + 1) * EDGE, at * LANES : (at + 1) * LANES] = part_ref[tile(number + at)]
                packed = part_ref[tile(number + depth_tiles)].astype(F32)
                chosen = jnp.zeros((8, LANES), F32)
                for head_block in range(group):
                    value = jnp.zeros((8, LANES), F32)
                    for term in range(3):
                        slot = term * group + head_block
                        half = packed[slot // 8 * 8 : slot // 8 * 8 + 8]
                        value = value + pltpu.roll(half, (LANES - slot % 8 * EDGE) % LANES, 1)
                    chosen = jnp.where(place == head_block, value, chosen)
                if side:
                    last = pltpu.roll(chosen, EDGE, 1)
                    decay_ref[count * 8 :, :] = jnp.where((lane >= EDGE) & (lane < 2 * EDGE), last, 0.0)
                else:
                    decay_ref[:8, :] = jnp.where(lane < EDGE, chosen, 0.0)

        number += depth_tiles + 1
        for span in range(spans):
            upper = part_ref[tile(number)].astype(F32)
            lower = part_ref[tile(number + 1)].astype(F32)
            number += 2
            span_ref[block * spans + span] = upper[:8] + upper[8:] + lower[:8]
    for span in range(count):
        moved = pltpu.roll(span_ref[span], EDGE, 1)
        here, after = slice(span * 8, span * 8 + 8), slice(span * 8 + 8, span * 8 + 16)
        decay_ref[here, :] = jnp.where(lane < EDGE, decay_ref[here, :], moved)
        kept = decay_ref[after, :] if span == count - 1 else jnp.zeros((8, LANES), F32)
        decay_ref[after, :] = jnp.where(lane < EDGE, moved, kept)
    for number, half_ref in enumerate(half_refs):
        swap_ref[number * half : (number + 1) * half, :] = half_ref[:half, : swap_ref.shape[1]]
    for number in range(bc_ref.shape[0] // height):
        lanes = slice(number * LANES, (number + 1) * LANES)
        swap_ref[top:, lanes] = bc_ref[number * height : (number + 1) * height, :]


def lanes_of(rows, width, head_size):
    high = rows.astype(BF16).astype(F32)
    owner = lax.broadcasted_iota(jnp.int32, (16, width), 1) // head_size
    chosen = jnp.where((lax.broadcasted_iota(jnp.int32, (16, width), 0) & 7) == owner, 1.0, 0.0).astype(BF16)
    return dot(jnp.concatenate([high, rows - high], axis=0).astype(BF16), chosen, ((0,), (0,)))


def spans_in_lanes(rows):
    return jnp.concatenate([rows[at : at + 8] for at in range(0, rows.shape[0], 8)], axis=1)


def row_blocks(total, wide):
    return [slice(at, at + 256) for at in range(0, total, 256)] + [slice(total, wide)]


def state_kernel(group, heads, state, len_ref, decay_ref, x_weight_ref, bc_half_ref, own_ref, swap_ref, halo_ref, *refs):
    half_refs, refs = refs[: group - 1], refs[group - 1 :]
    frames_ref, x_ref, b_ref, c_ref, rows_ref, step_ref, keep_ref, send_ref, weight_ref, tail_ref = refs
    place, plane = plane_place(group)
    parity = lax.rem(lax.axis_index("head"), 2)
    width = x_ref.shape[1]
    frames = own_ref.shape[0]
    total = frames * group
    half = frames // 2
    head_size = width // heads
    count = total // SPAN
    base = plane * total - EDGE
    wide = total + 2 * EDGE
    frames_ref[:EDGE, :] = halo_ref[:EDGE, :]
    frames_ref[total + EDGE : wide, :] = halo_ref[EDGE:, :]
    frames_ref[wide:, :] = jnp.zeros((frames_ref.shape[0] - wide, frames_ref.shape[1]), BF16)
    frames_ref[pl.ds(pl.multiple_of(EDGE + place * frames, EDGE), frames), :] = own_ref[...]
    for number, half_ref in enumerate(half_refs):
        block = EDGE + (place ^ (number + 1)) * frames
        mine = pl.ds(pl.multiple_of(block + parity * half, EDGE), half)
        other = pl.ds(pl.multiple_of(block + (1 - parity) * half, EDGE), half)
        frames_ref[mine, :] = half_ref[:half, : frames_ref.shape[1]]
        frames_ref[other, :] = swap_ref[number * half : (number + 1) * half, :]
    mine = pl.ds(pl.multiple_of(parity * LANES, LANES), LANES)
    other = pl.ds(pl.multiple_of((1 - parity) * LANES, LANES), LANES)
    weight_ref[:, mine] = bc_half_ref[...]
    top = len(half_refs) * half
    height = swap_ref.shape[0] - top
    for number in range(weight_ref.shape[0] // height):
        lanes = slice(number * LANES, (number + 1) * LANES)
        weight_ref[number * height : (number + 1) * height, other] = swap_ref[top:, lanes]

    decay = decay_ref[...]
    used = decay.shape[0]
    square = (SPAN, SPAN)
    row, lane = (lax.broadcasted_iota(jnp.int32, square, dim) for dim in (0, 1))
    upper = jnp.where(row <= lane, 1.0, 0.0).astype(F32)
    cumul = dot(decay, upper, precision=lax.Precision.HIGHEST)
    whole = dot(decay, jnp.ones(square, F32), precision=lax.Precision.HIGHEST)
    first = base + lax.broadcasted_iota(jnp.int32, (used, SPAN), 0) // 8 * SPAN
    position = first + lane[:1]
    start = record_starts(len_ref, position)
    start_last = record_starts(len_ref, first + (SPAN - 1))
    carried = jnp.where(start < first, jnp.exp(cumul), 0.0)
    tail = jnp.where(position >= start_last, jnp.exp(whole - cumul), 0.0)
    keep = jnp.where(start_last < first, jnp.exp(whole), 0.0)
    rows_ref[:used, :] = cumul
    rows_ref[used : 2 * used, :] = start.astype(F32)
    rows_ref[2 * used :, :] = carried

    for rows in row_blocks(total, wide):
        x_ref[rows, :] = dot(frames_ref[rows, :], x_weight_ref[...]).astype(BF16)
        product = dot(frames_ref[rows, :], weight_ref[...])
        b_ref[rows, :] = product[:, :state].astype(BF16)
        c_ref[rows, :] = product[:, state:].astype(BF16)
    for ref in (x_ref, b_ref, c_ref):
        ref[wide:, :] = jnp.zeros((ref.shape[0] - wide, ref.shape[1]), BF16)

    tail_ref[...] = lanes_of(spans_in_lanes(tail[: count * 8]), width, head_size)
    by_span = jnp.zeros((8, SPAN), F32)
    for block in range(count):
        by_span = jnp.where(lane[:8] == block, keep[block * 8 : (block + 1) * 8], by_span)
    kept = lanes_of(by_span, width, head_size)[: keep_ref.shape[0]]
    keep_ref[...] = kept
    entry = jnp.zeros((state, width), F32)
    through = jnp.ones((1, width), F32)
    for block in range(count):
        rows = slice(block * SPAN, (block + 1) * SPAN)
        weighed = x_ref[rows, :].astype(F32) * tail_ref[rows, :]
        step = dot(b_ref[rows, :], weighed.astype(BF16), ((0,), (0,)))
        step_ref[block * state : (block + 1) * state, :] = step
        entry = kept[block : block + 1] * entry + step
        through = through * kept[block : block + 1]
    send_ref[:state, :] = entry.astype(BF16)
    send_ref[state:, :] = jnp.broadcast_to(through, (EDGE, width)).astype(BF16)


def inner_kernel(group, heads, x_ref, b_ref, c_ref, rows_ref, y_ref, carry_ref):
    _, plane = plane_place(group)
    total, width = x_ref.shape
    head_size = width // heads
    count = total // SPAN
    base = plane * (total - SPAN) - EDGE
    used = rows_ref.shape[0] // 3
    square = (SPAN, SPAN)
    parts = [rows_ref[: 2 * used, :]]
    if 2 * used % SPAN:
        parts.append(jnp.zeros((SPAN - 2 * used % SPAN, SPAN), F32))
    columns = jnp.concatenate(parts, axis=0).T
    carry_ref[...] = lanes_of(spans_in_lanes(rows_ref[2 * used :, :]), width, head_size)
    row, lane = (lax.broadcasted_iota(jnp.int32, square, dim) for dim in (0, 1))
    lower = row >= lane
    tile_heads = LANES // head_size
    tile_lane = lax.broadcasted_iota(jnp.int32, (1, LANES), 1) // head_size
    masks = [jnp.where(tile_lane == inner, 1.0, 0.0).astype(BF16) for inner in range(tile_heads)]
    for block in range(count):
        rows = slice(block * SPAN, (block + 1) * SPAN)
        at = block * 8
        x = x_ref[rows, :]
        scores = dot(c_ref[rows, :], b_ref[rows, :], ((1,), (1,)))
        here = (base + block * SPAN + lane).astype(F32)
        start_here = jnp.broadcast_to(columns[:, used + at : used + at + 1], square)
        joined = lower & (here >= start_here)
        for tile in range(width // LANES):
            mixes, values = [], []
            for inner in range(tile_heads):
                which = at + tile * tile_heads + inner
                column = jnp.broadcast_to(columns[:, which : which + 1], square)
                gap = jnp.where(joined, column - rows_ref[which : which + 1, :], -1e30)
                mixes.append((jnp.exp(gap) * scores).astype(BF16))
                values.append(x[:, tile * LANES : (tile + 1) * LANES] * masks[inner])
            y_ref[rows, tile * LANES : (tile + 1) * LANES] = dot(
                jnp.concatenate(mixes, axis=1), jnp.concatenate(values, axis=0)
            )


def silu_kernel(group, gain_ref, frames_ref, weight_ref, out_ref):
    place, _ = plane_place(group)
    rows_all, width = out_ref.shape
    total = rows_all - SPAN
    wide = total + 2 * EDGE
    gain = gain_ref[:, pl.ds(pl.multiple_of(place * width, LANES), width)]
    for rows in row_blocks(total, wide):
        z = dot(frames_ref[rows, :], weight_ref[...]).astype(BF16).astype(F32)
        out_ref[rows, :] = z / (1.0 + jnp.exp(-z)) * gain
    out_ref[wide:, :] = jnp.zeros((rows_all - wide, width), F32)


def share_kernel(cores, offsets, group, *refs):
    pieces, refs = refs[: len(offsets)], refs[len(offsets) :]
    outs, weight_ref = refs[:cores], refs[cores]
    _, plane = plane_place(group)
    core = lax.axis_index("head")
    fill_planes(plane, weight_ref, pieces, offsets)
    for step, out_ref in enumerate(outs):
        rows = out_ref.shape[0]
        out_ref[...] = weight_ref[pl.ds(pl.multiple_of((core ^ step) * rows, rows), rows), :]


def gate_kernel(heads, state, c_ref, y_ref, step_ref, carry_ref, keep_ref, silu_ref, *refs):
    earlier, gated_ref = refs[:-1], refs[-1]
    total, width = y_ref.shape
    head_size = width // heads
    count = total // SPAN
    entry = jnp.zeros((state, width), F32)
    for summary in reversed(earlier):
        through = summary[state : state + EDGE, :].astype(F32)[:1]
        entry = through * entry + summary[:state, :].astype(F32)
    owner = [lax.broadcasted_iota(jnp.int32, (width, width), dim) // head_size for dim in (0, 1)]
    average = jnp.where(owner[0] == owner[1], 1.0 / head_size, 0.0).astype(BF16)
    for block in range(count):
        rows = slice(block * SPAN, (block + 1) * SPAN)
        y = y_ref[rows, :] + carry_ref[rows, :] * dot(c_ref[rows, :], entry.astype(BF16))
        square_mean = dot((y * y).astype(BF16), average)
        gated_ref[rows, :] = (y * lax.rsqrt(square_mean + 1e-05) * silu_ref[rows, :]).astype(BF16)
        if block < count - 1:
            entry = keep_ref[block : block + 1, :] * entry + step_ref[block * state : (block + 1) * state, :]


def conv_kernel(group, steps, len_ref, taps_ref, gated_ref, act_ref, ext_ref, ends_ref):
    place, plane = plane_place(group)
    rows_all, width = gated_ref.shape
    total = rows_all - SPAN
    frames = total // group
    taps = taps_ref.shape[0]
    half = (taps - 1) // 2
    stream = lax.axis_size("tm") // group * total
    records = len_ref.shape[0]
    reach = CONV_ROWS + 2 * EDGE
    first_tap = EDGE - half
    pitch = frames + 2 * EDGE
    ends_ref[0] = 0
    for record in range(records):
        ends_ref[record + 1] = ends_ref[record] + len_ref[record]
    for number, step in enumerate(steps):
        first = pl.multiple_of((place ^ step) * frames, frames)
        ext_ref[number * pitch : (number + 1) * pitch, :] = gated_ref[pl.ds(first, pitch), :].astype(F32)

    def record_at(position):
        found = jnp.int32(0)
        for record in range(records - 1):
            found = found + (ends_ref[record + 1] <= position).astype(jnp.int32)
        return found

    for number, step in enumerate(steps):
        base = plane * total + (place ^ step) * frames

        def one_block(block, _, number=number, base=base):
            inside_part = pl.multiple_of(block * CONV_ROWS, CONV_ROWS)
            source = pl.multiple_of(number * pitch + inside_part, EDGE)
            target = pl.multiple_of(number * frames + inside_part, CONV_ROWS)
            at = base + inside_part
            low = record_at(jnp.maximum(at - half, 0))
            high = record_at(jnp.minimum(at + CONV_ROWS - 1 + half, stream - 1))
            near = lax.broadcasted_iota(jnp.int32, (reach, LANES), 0) + (at - EDGE)
            for tile in range(width // LANES):
                lanes = slice(tile * LANES, (tile + 1) * LANES)
                weights = taps_ref[:, pl.ds(pl.multiple_of(place * width + tile * LANES, LANES), LANES)]

                def one_record(record, done):
                    inside = (near >= ends_ref[record]) & (near < ends_ref[record + 1])
                    g = jnp.where(inside, ext_ref[pl.ds(source, reach), lanes], 0.0)
                    out = None
                    for phase in range(8):
                        part = None
                        for offset in range(phase, reach - CONV_ROWS, 8):
                            tap = offset - first_tap
                            if 0 <= tap < taps:
                                aligned = offset - phase
                                term = weights[tap : tap + 1, :] * g[aligned : aligned + CONV_ROWS + 8, :]
                                part = term if part is None else part + term
                        if part is not None:
                            moved = part[phase : phase + CONV_ROWS, :]
                            out = moved if out is None else out + moved
                    return jnp.where(inside[EDGE : EDGE + CONV_ROWS], out, done)

                conv = lax.fori_loop(low, high + 1, one_record, jnp.zeros((CONV_ROWS, LANES), F32))
                act_ref[pl.ds(target, CONV_ROWS), lanes] = (conv / (1.0 + jnp.exp(-conv))).astype(BF16)
            return 0

        lax.fori_loop(0, frames // CONV_ROWS, one_block, 0)


def out_kernel(cores, *refs):
    acts, weights, outs = refs[:cores], refs[cores : 2 * cores], refs[2 * cores :]
    frames = outs[0].shape[0]
    for number, out_ref in enumerate(outs):
        rows = slice(number * frames, (number + 1) * frames)
        total = None
        for act, weight in zip(acts, weights):
            product = dot(act[rows, :], weight[...], ((1,), (1,)))
            total = product if total is None else total + product
        out_ref[...] = total.astype(out_ref.dtype)


def local(
    frames,
    x_weight,
    z_weight,
    bc_weight,
    log_decay,
    norm_gain,
    conv_weight,
    out_weight,
    record_lengths,
):
    times, cores = lax.axis_size("tm"), lax.axis_size("head")
    frame_count, depth = frames.shape
    heads_here, channels = log_decay.shape[0], x_weight.shape[1]
    state = bc_weight.shape[1] // 2
    group = 4
    while group > 1 and (channels // group % LANES or times % group or heads_here % group):
        group //= 2
    planes = times // group
    width, heads = channels // group, heads_here // group
    total = frame_count * group
    count = total // SPAN
    index, core = lax.axis_index("tm"), lax.axis_index("head")
    place = lax.rem(index, group)

    def in_plane(array, step):
        return lax.ppermute(array, "tm", [(i, i ^ step) for i in range(times)])

    def later(array, step):
        return lax.ppermute(array, "tm", [(i, i + step * group) for i in range(times - step * group)])

    def across(array, step):
        return lax.ppermute(array, "head", [(i, i ^ step) for i in range(cores)])

    def between_planes(array, step):
        return lax.ppermute(array, "tm", [(i, i ^ (step * group)) for i in range(times)])

    shape = jax.ShapeDtypeStruct
    rows = x_weight.shape[0]
    parity = lax.rem(core, 2)

    def along_planes(stacks):
        if planes != 4:
            return [stacks[0]] + [between_planes(stacks[step], step) for step in range(1, planes)]

        def pairs(chosen):
            return [(a * group + q, b * group + q) for a, b in chosen for q in range(group)]

        second = between_planes(stacks[2], 2)
        first = between_planes(stacks[1], 1)
        again, last, first = lax.optimization_barrier((second, stacks[3], first))
        third = lax.ppermute(again, "tm", pairs([(1, 0), (2, 3)]))
        middle = lax.ppermute(last, "tm", pairs([(1, 2), (2, 1)]))
        return [stacks[0], first, second, third, middle]

    offsets = (0, 1, 2, 3, 3) if planes == 4 else tuple(range(planes))
    half_count = frame_count // 2
    down, depth_tiles = rows // 16, depth // LANES
    payloads = call(
        functools.partial(first_kernel, group, planes),
        (
            *(shape((rows, 3 * width), BF16) for _ in range(group)),
            *(shape((-(-(down + depth_tiles + 1) // 8) * 16, depth), BF16) for _ in range(planes)),
        ),
        [log_decay, bc_weight, frames, x_weight, z_weight, out_weight.T],
        [
            pltpu.VMEM((rows, LANES), BF16),
            pltpu.VMEM((2, EDGE, depth), BF16),
            pltpu.VMEM(log_decay.shape, F32),
            pltpu.SemaphoreType.DMA((4 + 3 * group,)),
        ],
        smem=0,
        anywhere=6,
        vmem=ALL_VMEM_BYTES,
    )
    inner, outer = payloads[:group], payloads[group:]
    parts = [inner[0]] + [in_plane(inner[step], step) for step in range(1, group)]
    pieces = [outer[0]] + [between_planes(outer[step], step) for step in range(1, planes)]
    xz_stack, out_stack = call(
        functools.partial(stack_kernel, group),
        (shape((group * rows, 2 * width), BF16), shape((group * rows, width), BF16)),
        parts,
        flops=STACK_HINT,
        smem=0,
    )
    xz_pieces = along_planes([xz_stack] * planes)
    xz_pieces, out_stack = lax.optimization_barrier((xz_pieces, out_stack))
    out_pieces = [out_stack] + [between_planes(out_stack, step) for step in range(1, min(3, planes))]
    x_columns, z_columns = call(
        functools.partial(assemble_kernel, group, offsets),
        (shape((depth, width), BF16), shape((depth, width), BF16)),
        xz_pieces,
        flops=ASSEMBLE_HINT,
        smem=0,
    )
    decay_blocks = jnp.pad(log_decay.reshape(group, heads, frame_count), ((0, 0), (0, 8 - heads), (0, 0)))
    tiles = planes * down + depth_tiles + 1 + frame_count // SPAN * 2
    inward = call(
        functools.partial(inward_kernel, group, rows),
        tuple(shape((half_count + -(-tiles // 8) * 16, depth), BF16) for _ in range(group)),
        [decay_blocks, frames, *pieces],
        flops=INWARD_HINT,
        smem=0,
    )
    inward = [inward[0]] + [in_plane(inward[step], step) for step in range(1, group)]
    swap, bc_mine, halo, decay = call(
        functools.partial(swap_kernel, group, rows),
        (
            shape(((group - 1) * half_count + LANES, depth), BF16),
            shape((depth, LANES), BF16),
            shape((2 * EDGE, depth), BF16),
            shape((count * 8 + 8, SPAN), F32),
        ),
        inward,
        [pltpu.VMEM((count, 8, SPAN), F32)],
        smem=0,
    )
    swap = across(swap, 1)
    all_rows = total + SPAN

    frame_rows, x_rows, b_rows, c_rows, decay_rows, steps, keep, summary = call(
        functools.partial(state_kernel, group, heads, state),
        (
            shape((all_rows, depth), BF16),
            shape((all_rows, width), BF16),
            shape((all_rows, state), BF16),
            shape((all_rows, state), BF16),
            shape((3 * (count + 1) * 8, SPAN), F32),
            shape((count * state, width), F32),
            shape((-(-count // 8) * 8, width), F32),
            shape((state + EDGE, width), BF16),
        ),
        [record_lengths, decay, x_columns, bc_mine, frames, swap, halo, *inward[1:]],
        [pltpu.VMEM((depth, 2 * state), BF16), pltpu.VMEM((total, width), F32)],
        hidden=True,
    )
    summaries = [later(summary, step) for step in range(1, planes)]
    x_rows, out_pieces = lax.optimization_barrier((x_rows, out_pieces))
    y, carry = call(
        functools.partial(inner_kernel, group, heads),
        (shape((all_rows, width), F32), shape((all_rows, width), F32)),
        [x_rows, b_rows, c_rows, decay_rows],
        flops=4 * total * SPAN * width,
        smem=0,
    )
    silu = call(
        functools.partial(silu_kernel, group),
        shape((all_rows, width), F32),
        [norm_gain[None], frame_rows, z_columns],
        flops=2 * total * depth * width,
        smem=0,
    )
    out_pieces, summaries, y, silu = lax.optimization_barrier((out_pieces, summaries, y, silu))
    out_pieces += [between_planes(out_pieces[0], step) for step in range(3, planes)]
    gated = call(
        functools.partial(gate_kernel, heads, state),
        shape((all_rows, width), BF16),
        [c_rows, y, steps, carry, keep, silu, *summaries],
        flops=2 * total * state * width,
        smem=0,
    )
    ends = pltpu.SMEM((record_lengths.shape[0] + 1,), jnp.int32)
    far, near = (group - 1,), (*range(1, group - 1), 0)

    def conv(steps, gated):
        return call(
            functools.partial(conv_kernel, group, steps),
            shape((len(steps) * frame_count, width), BF16),
            [record_lengths, conv_weight, gated],
            [pltpu.VMEM((len(steps) * (frame_count + 2 * EDGE), width), F32), ends],
            flops=2 * len(steps) * frame_count * width * conv_weight.shape[0],
        )

    def out(steps, act, swapped):
        return call(
            functools.partial(out_kernel, cores),
            tuple(shape((frame_count, share), BF16 if step else F32) for step in steps),
            [act, *swapped, *out_parts],
            flops=2 * len(steps) * frame_count * width * cores * share,
            smem=0,
        )

    far_act = conv(far, gated)
    far_swapped = [across(far_act, step) for step in range(1, cores)]
    gated, far_act = lax.optimization_barrier((gated, far_act))
    near_act = conv(near, gated)
    near_act, far_swapped, out_pieces = lax.optimization_barrier((near_act, far_swapped, out_pieces))
    share = depth // cores
    out_parts = call(
        functools.partial(share_kernel, cores, tuple(range(planes)), group),
        tuple(shape((share, width), BF16) for _ in range(cores)),
        out_pieces,
        [pltpu.VMEM((depth, width), BF16)],
        smem=0,
    )
    out_parts = [out_parts[0]] + [across(out_parts[step], step) for step in range(1, cores)]
    near_act, out_parts = lax.optimization_barrier((near_act, out_parts))
    (far_out,) = out(far, far_act, far_swapped)
    near_act, far_out = lax.optimization_barrier((near_act, far_out))
    far_out = in_plane(far_out, far[0])
    near_swapped = [across(near_act, step) for step in range(1, cores)]
    near_outs = out(near, near_act, near_swapped)
    mixed = near_outs[-1] + far_out.astype(F32)
    for step, partial in zip(near[:-1], near_outs[:-1]):
        mixed = mixed + in_plane(partial, step).astype(F32)
    return mixed.astype(BF16)


def solution(mesh):
    in_specs = (
        P("tm", None),
        P("tm", "head"),
        P("tm", "head"),
        P("tm", None),
        P("head", "tm"),
        P("head"),
        P(None, "head"),
        P("head", "tm"),
        P(),
    )
    out_specs = P("tm", "head")
    return jax.shard_map(local, mesh=mesh, in_specs=in_specs, out_specs=out_specs, check_vma=False)
```

```python
import functools

import jax
import jax.numpy as jnp
from jax import lax
from jax.experimental import pallas as pl
from jax.experimental.pallas import tpu as pltpu
from jax.sharding import PartitionSpec as P

SPAN = 128
LANES = 128
EDGE = 16
CONV_ROWS = 64
BF16 = jnp.bfloat16
F32 = jnp.float32
STACK_HINT = 40_000_000_000
INWARD_HINT = 40_000_000_000
ASSEMBLE_HINT = 40_000_000_000
ALL_VMEM_BYTES = 63 * 1024 * 1024
VMEM_BYTES = 20 * 1024 * 1024


def dot(a, b, dims=((1,), (0,)), precision=None):
    return lax.dot_general(a, b, (dims, ((), ())), precision=precision, preferred_element_type=F32)


def call(kernel, out_shape, operands, scratch=(), flops=0, smem=1, anywhere=0, vmem=VMEM_BYTES, hidden=False):
    in_specs = [pl.BlockSpec(memory_space=pltpu.SMEM)] * smem
    in_specs += [pl.BlockSpec(memory_space=pltpu.VMEM)] * (len(operands) - smem - anywhere)
    in_specs += [pl.BlockSpec(memory_space=pl.ANY)] * anywhere
    moved = sum(a.size * a.dtype.itemsize for a in operands)
    moved += sum(a.size * a.dtype.itemsize for a in jax.tree.leaves(out_shape))
    if hidden:
        flops = moved = 0
    return pl.pallas_call(
        kernel,
        out_shape=out_shape,
        in_specs=in_specs,
        out_specs=jax.tree.map(lambda _: pl.BlockSpec(memory_space=pltpu.VMEM), out_shape),
        scratch_shapes=list(scratch),
        compiler_params=pltpu.CompilerParams(vmem_limit_bytes=vmem),
        cost_estimate=pl.CostEstimate(flops=flops, bytes_accessed=moved, transcendentals=0),
    )(*operands)


def plane_place(group):
    index = lax.axis_index("tm")
    return lax.rem(index, group), lax.div(index, group)


def record_starts(len_ref, position):
    start = jnp.zeros_like(position)
    end = jnp.int32(0)
    for record in range(len_ref.shape[0] - 1):
        end = end + len_ref[record]
        start = jnp.where(position >= end, end, start)
    return start


def fill_planes(plane, dest_ref, pieces, offsets, lanes=slice(None)):
    rows = pieces[0].shape[0]
    for offset in sorted(set(offsets)):
        same = [piece[:, lanes] for piece, at in zip(pieces, offsets) if at == offset]
        value = same[0] if len(same) == 1 else same[0] + same[1]
        dest_ref[pl.ds(pl.multiple_of((plane ^ offset) * rows, rows), rows), : value.shape[1]] = value


def first_kernel(group, planes, log_decay_ref, bc_ref, frames_ref, *refs):
    weight_refs, refs = refs[:3], refs[3:]
    inner_refs, outer_refs, refs = refs[:group], refs[group : group + planes], refs[group + planes :]
    bc_half_ref, edge_ref, decay_ref, sems = refs
    place, plane = plane_place(group)
    parity = lax.rem(lax.axis_index("head"), 2)
    width = weight_refs[0].shape[1] // group
    frames = frames_ref.shape[0]
    heads = log_decay_ref.shape[0] // group
    copies = [
        (bc_ref.at[:, pl.ds(pl.multiple_of(parity * LANES, LANES), LANES)], bc_half_ref),
        (frames_ref.at[:EDGE, :], edge_ref.at[0]),
        (frames_ref.at[frames - EDGE :, :], edge_ref.at[1]),
        (log_decay_ref, decay_ref),
    ]
    for step, inner_ref in enumerate(inner_refs):
        lanes = pl.ds(pl.multiple_of((place ^ step) * width, LANES), width)
        for number, weight_ref in enumerate(weight_refs):
            copies.append((weight_ref.at[:, lanes], inner_ref.at[:, number * width : (number + 1) * width]))
    started = [pltpu.make_async_copy(a, b, sems.at[number]) for number, (a, b) in enumerate(copies)]
    for copy in started:
        copy.start()
    for copy in started[:4]:
        copy.wait()
    lane = lax.broadcasted_iota(jnp.int32, (8, LANES), 1)
    decays = []
    for first in (0, frames - LANES):
        rows = [jnp.zeros((8, LANES), F32), jnp.zeros((8, LANES), F32)]
        for block in range(group):
            here = decay_ref[block * heads : (block + 1) * heads, first : first + LANES]
            here = jnp.concatenate([here, jnp.zeros((8 - heads, LANES), F32)], axis=0)
            for number, term in enumerate(three_terms(here)):
                slot = number * group + block
                moved = pltpu.roll(term, (slot % 8 * EDGE + (EDGE if first else 0)) % LANES, 1)
                rows[slot // 8] = jnp.where(lane // EDGE == slot % 8, moved, rows[slot // 8])
        decays.append(jnp.concatenate(rows, axis=0))
    for step, out_ref in enumerate(outer_refs):
        number = put(out_ref, 0, bc_half_ref[...])
        later = (plane ^ step) > plane
        number = put(out_ref, number, jnp.where(later, edge_ref[1].astype(F32), edge_ref[0].astype(F32)).astype(BF16))
        put(out_ref, number, jnp.where(later, decays[1], decays[0]).astype(BF16))
    for copy in started[4:]:
        copy.wait()


def stack_kernel(group, *refs):
    parts, stack_refs = refs[:group], refs[group:]
    place, _ = plane_place(group)
    rows = parts[0].shape[0]
    for step, part in enumerate(parts):
        at = pl.ds(pl.multiple_of((place ^ step) * rows, rows), rows)
        first = 0
        for stack_ref in stack_refs:
            width = stack_ref.shape[1]
            stack_ref[at, :] = part[:, first : first + width]
            first += width


def assemble_kernel(group, offsets, *refs):
    pieces, dest_refs = refs[: len(offsets)], refs[len(offsets) :]
    _, plane = plane_place(group)
    first = 0
    for dest_ref in dest_refs:
        width = dest_ref.shape[1]
        fill_planes(plane, dest_ref, pieces, offsets, slice(first, first + width))
        first += width


def tile(number):
    return slice(number // 8 * 16, number // 8 * 16 + 16), slice(number % 8 * LANES, (number % 8 + 1) * LANES)


def put(out_ref, number, array):
    for at in range(0, array.shape[0], 16):
        for lane in range(0, array.shape[1], LANES):
            out_ref[tile(number)] = array[at : at + 16, lane : lane + LANES]
            number += 1
    return number


def three_terms(value):
    terms = []
    for _ in range(3):
        term = value.astype(BF16).astype(F32)
        terms.append(term)
        value = value - term
    return terms


def inward_kernel(group, rows, decay_ref, frames_ref, *refs):
    piece_refs, out_refs = refs[:-group], refs[-group:]
    place, plane = plane_place(group)
    planes = len(piece_refs)
    half = frames_ref.shape[0] // 2
    mine = pl.ds(pl.multiple_of(lax.rem(lax.axis_index("head"), 2) * half, half), half)
    wanted = jnp.clip(jnp.where(place == 0, plane + 1, plane - 1), 0, planes - 1)
    depth_tiles = frames_ref.shape[1] // LANES
    down = rows // 16
    for step, out_ref in enumerate(out_refs):
        out_ref[:half, :] = frames_ref[mine, :]
        number = half // 16 * depth_tiles
        for piece_ref in piece_refs:
            for at in range(down):
                out_ref[tile(number)] = piece_ref[tile(at)]
                number += 1
        for offset, piece_ref in enumerate(piece_refs):

            @pl.when((plane ^ offset) == wanted)
            def _(piece_ref=piece_ref, number=number, out_ref=out_ref):
                for at in range(depth_tiles + 1):
                    out_ref[tile(number + at)] = piece_ref[tile(down + at)]

        number += depth_tiles + 1
        terms = three_terms(decay_ref[place ^ step])
        terms = jnp.concatenate([*terms, jnp.zeros_like(terms[0])], axis=0).astype(BF16)
        for span in range(terms.shape[1] // SPAN):
            number = put(out_ref, number, terms[:, span * SPAN : (span + 1) * SPAN])


def swap_kernel(group, rows, *refs):
    part_refs, (swap_ref, bc_ref, halo_ref, decay_ref, span_ref) = refs[:group], refs[group:]
    half_refs = part_refs[1:]
    place, plane = plane_place(group)
    planes = bc_ref.shape[0] // (group * rows)
    count = span_ref.shape[0]
    spans = count // group
    down = rows // 16
    depth_tiles = swap_ref.shape[1] // LANES
    height = LANES
    top = swap_ref.shape[0] - height
    half = top // len(half_refs)
    lane = lax.broadcasted_iota(jnp.int32, (8, LANES), 1)
    for step, part_ref in enumerate(part_refs):
        block = place ^ step
        number = half // 16 * depth_tiles
        for offset in range(planes):
            first = ((plane ^ offset) * group + block) * rows
            for at in range(down):
                bc_ref[pl.ds(pl.multiple_of(first + at * 16, 16), 16), :] = part_ref[tile(number)]
                number += 1
        for side, owner in enumerate((group - 1, 0)):

            @pl.when(block == owner)
            def _(part_ref=part_ref, number=number, side=side):
                for at in range(depth_tiles):
                    halo_ref[side * EDGE : (side + 1) * EDGE, at * LANES : (at + 1) * LANES] = part_ref[tile(number + at)]
                packed = part_ref[tile(number + depth_tiles)].astype(F32)
                chosen = jnp.zeros((8, LANES), F32)
                for head_block in range(group):
                    value = jnp.zeros((8, LANES), F32)
                    for term in range(3):
                        slot = term * group + head_block
                        half = packed[slot // 8 * 8 : slot // 8 * 8 + 8]
                        value = value + pltpu.roll(half, (LANES - slot % 8 * EDGE) % LANES, 1)
                    chosen = jnp.where(place == head_block, value, chosen)
                if side:
                    last = pltpu.roll(chosen, EDGE, 1)
                    decay_ref[count * 8 :, :] = jnp.where((lane >= EDGE) & (lane < 2 * EDGE), last, 0.0)
                else:
                    decay_ref[:8, :] = jnp.where(lane < EDGE, chosen, 0.0)

        number += depth_tiles + 1
        for span in range(spans):
            upper = part_ref[tile(number)].astype(F32)
            lower = part_ref[tile(number + 1)].astype(F32)
            number += 2
            span_ref[block * spans + span] = upper[:8] + upper[8:] + lower[:8]
    for span in range(count):
        moved = pltpu.roll(span_ref[span], EDGE, 1)
        here, after = slice(span * 8, span * 8 + 8), slice(span * 8 + 8, span * 8 + 16)
        decay_ref[here, :] = jnp.where(lane < EDGE, decay_ref[here, :], moved)
        kept = decay_ref[after, :] if span == count - 1 else jnp.zeros((8, LANES), F32)
        decay_ref[after, :] = jnp.where(lane < EDGE, moved, kept)
    for number, half_ref in enumerate(half_refs):
        swap_ref[number * half : (number + 1) * half, :] = half_ref[:half, : swap_ref.shape[1]]
    for number in range(bc_ref.shape[0] // height):
        lanes = slice(number * LANES, (number + 1) * LANES)
        swap_ref[top:, lanes] = bc_ref[number * height : (number + 1) * height, :]


def lanes_of(rows, width, head_size):
    high = rows.astype(BF16).astype(F32)
    owner = lax.broadcasted_iota(jnp.int32, (16, width), 1) // head_size
    chosen = jnp.where((lax.broadcasted_iota(jnp.int32, (16, width), 0) & 7) == owner, 1.0, 0.0).astype(BF16)
    return dot(jnp.concatenate([high, rows - high], axis=0).astype(BF16), chosen, ((0,), (0,)))


def spans_in_lanes(rows):
    return jnp.concatenate([rows[at : at + 8] for at in range(0, rows.shape[0], 8)], axis=1)


def row_blocks(total, wide):
    return [slice(at, at + 256) for at in range(0, total, 256)] + [slice(total, wide)]


def state_kernel(group, heads, state, len_ref, decay_ref, x_weight_ref, bc_half_ref, own_ref, swap_ref, halo_ref, *refs):
    half_refs, refs = refs[: group - 1], refs[group - 1 :]
    frames_ref, x_ref, b_ref, c_ref, rows_ref, step_ref, keep_ref, send_ref, weight_ref, tail_ref = refs
    place, plane = plane_place(group)
    parity = lax.rem(lax.axis_index("head"), 2)
    width = x_ref.shape[1]
    frames = own_ref.shape[0]
    total = frames * group
    half = frames // 2
    head_size = width // heads
    count = total // SPAN
    base = plane * total - EDGE
    wide = total + 2 * EDGE
    frames_ref[:EDGE, :] = halo_ref[:EDGE, :]
    frames_ref[total + EDGE : wide, :] = halo_ref[EDGE:, :]
    frames_ref[wide:, :] = jnp.zeros((frames_ref.shape[0] - wide, frames_ref.shape[1]), BF16)
    frames_ref[pl.ds(pl.multiple_of(EDGE + place * frames, EDGE), frames), :] = own_ref[...]
    for number, half_ref in enumerate(half_refs):
        block = EDGE + (place ^ (number + 1)) * frames
        mine = pl.ds(pl.multiple_of(block + parity * half, EDGE), half)
        other = pl.ds(pl.multiple_of(block + (1 - parity) * half, EDGE), half)
        frames_ref[mine, :] = half_ref[:half, : frames_ref.shape[1]]
        frames_ref[other, :] = swap_ref[number * half : (number + 1) * half, :]
    mine = pl.ds(pl.multiple_of(parity * LANES, LANES), LANES)
    other = pl.ds(pl.multiple_of((1 - parity) * LANES, LANES), LANES)
    weight_ref[:, mine] = bc_half_ref[...]
    top = len(half_refs) * half
    height = swap_ref.shape[0] - top
    for number in range(weight_ref.shape[0] // height):
        lanes = slice(number * LANES, (number + 1) * LANES)
        weight_ref[number * height : (number + 1) * height, other] = swap_ref[top:, lanes]

    decay = decay_ref[...]
    used = decay.shape[0]
    square = (SPAN, SPAN)
    row, lane = (lax.broadcasted_iota(jnp.int32, square, dim) for dim in (0, 1))
    upper = jnp.where(row <= lane, 1.0, 0.0).astype(F32)
    cumul = dot(decay, upper, precision=lax.Precision.HIGHEST)
    whole = dot(decay, jnp.ones(square, F32), precision=lax.Precision.HIGHEST)
    first = base + lax.broadcasted_iota(jnp.int32, (used, SPAN), 0) // 8 * SPAN
    position = first + lane[:1]
    start = record_starts(len_ref, position)
    start_last = record_starts(len_ref, first + (SPAN - 1))
    carried = jnp.where(start < first, jnp.exp(cumul), 0.0)
    tail = jnp.where(position >= start_last, jnp.exp(whole - cumul), 0.0)
    keep = jnp.where(start_last < first, jnp.exp(whole), 0.0)
    rows_ref[:used, :] = cumul
    rows_ref[used : 2 * used, :] = start.astype(F32)
    rows_ref[2 * used :, :] = carried

    for rows in row_blocks(total, wide):
        x_ref[rows, :] = dot(frames_ref[rows, :], x_weight_ref[...]).astype(BF16)
        product = dot(frames_ref[rows, :], weight_ref[...])
        b_ref[rows, :] = product[:, :state].astype(BF16)
        c_ref[rows, :] = product[:, state:].astype(BF16)
    for ref in (x_ref, b_ref, c_ref):
        ref[wide:, :] = jnp.zeros((ref.shape[0] - wide, ref.shape[1]), BF16)

    tail_ref[...] = lanes_of(spans_in_lanes(tail[: count * 8]), width, head_size)
    by_span = jnp.zeros((8, SPAN), F32)
    for block in range(count):
        by_span = jnp.where(lane[:8] == block, keep[block * 8 : (block + 1) * 8], by_span)
    kept = lanes_of(by_span, width, head_size)[: keep_ref.shape[0]]
    keep_ref[...] = kept
    entry = jnp.zeros((state, width), F32)
    through = jnp.ones((1, width), F32)
    for block in range(count):
        rows = slice(block * SPAN, (block + 1) * SPAN)
        weighed = x_ref[rows, :].astype(F32) * tail_ref[rows, :]
        step = dot(b_ref[rows, :], weighed.astype(BF16), ((0,), (0,)))
        step_ref[block * state : (block + 1) * state, :] = step
        entry = kept[block : block + 1] * entry + step
        through = through * kept[block : block + 1]
    send_ref[:state, :] = entry.astype(BF16)
    send_ref[state:, :] = jnp.broadcast_to(through, (EDGE, width)).astype(BF16)


def inner_kernel(group, heads, x_ref, b_ref, c_ref, rows_ref, y_ref, carry_ref):
    _, plane = plane_place(group)
    total, width = x_ref.shape
    head_size = width // heads
    count = total // SPAN
    base = plane * (total - SPAN) - EDGE
    used = rows_ref.shape[0] // 3
    square = (SPAN, SPAN)
    parts = [rows_ref[: 2 * used, :]]
    if 2 * used % SPAN:
        parts.append(jnp.zeros((SPAN - 2 * used % SPAN, SPAN), F32))
    columns = jnp.concatenate(parts, axis=0).T
    carry_ref[...] = lanes_of(spans_in_lanes(rows_ref[2 * used :, :]), width, head_size)
    row, lane = (lax.broadcasted_iota(jnp.int32, square, dim) for dim in (0, 1))
    lower = row >= lane
    tile_heads = LANES // head_size
    tile_lane = lax.broadcasted_iota(jnp.int32, (1, LANES), 1) // head_size
    masks = [jnp.where(tile_lane == inner, 1.0, 0.0).astype(BF16) for inner in range(tile_heads)]
    for block in range(count):
        rows = slice(block * SPAN, (block + 1) * SPAN)
        at = block * 8
        x = x_ref[rows, :]
        scores = dot(c_ref[rows, :], b_ref[rows, :], ((1,), (1,)))
        here = (base + block * SPAN + lane).astype(F32)
        start_here = jnp.broadcast_to(columns[:, used + at : used + at + 1], square)
        joined = lower & (here >= start_here)
        for tile in range(width // LANES):
            mixes, values = [], []
            for inner in range(tile_heads):
                which = at + tile * tile_heads + inner
                column = jnp.broadcast_to(columns[:, which : which + 1], square)
                gap = jnp.where(joined, column - rows_ref[which : which + 1, :], -1e30)
                mixes.append((jnp.exp(gap) * scores).astype(BF16))
                values.append(x[:, tile * LANES : (tile + 1) * LANES] * masks[inner])
            y_ref[rows, tile * LANES : (tile + 1) * LANES] = dot(
                jnp.concatenate(mixes, axis=1), jnp.concatenate(values, axis=0)
            )


def silu_kernel(group, gain_ref, frames_ref, weight_ref, out_ref):
    place, _ = plane_place(group)
    rows_all, width = out_ref.shape
    total = rows_all - SPAN
    wide = total + 2 * EDGE
    gain = gain_ref[:, pl.ds(pl.multiple_of(place * width, LANES), width)]
    for rows in row_blocks(total, wide):
        z = dot(frames_ref[rows, :], weight_ref[...]).astype(BF16).astype(F32)
        out_ref[rows, :] = z / (1.0 + jnp.exp(-z)) * gain
    out_ref[wide:, :] = jnp.zeros((rows_all - wide, width), F32)


def share_kernel(cores, offsets, group, *refs):
    pieces, refs = refs[: len(offsets)], refs[len(offsets) :]
    outs, weight_ref = refs[:cores], refs[cores]
    _, plane = plane_place(group)
    core = lax.axis_index("head")
    fill_planes(plane, weight_ref, pieces, offsets)
    for step, out_ref in enumerate(outs):
        rows = out_ref.shape[0]
        out_ref[...] = weight_ref[pl.ds(pl.multiple_of((core ^ step) * rows, rows), rows), :]


def gate_kernel(heads, state, c_ref, y_ref, step_ref, carry_ref, keep_ref, silu_ref, *refs):
    earlier, gated_ref = refs[:-1], refs[-1]
    total, width = y_ref.shape
    head_size = width // heads
    count = total // SPAN
    entry = jnp.zeros((state, width), F32)
    for summary in reversed(earlier):
        through = summary[state : state + EDGE, :].astype(F32)[:1]
        entry = through * entry + summary[:state, :].astype(F32)
    owner = [lax.broadcasted_iota(jnp.int32, (width, width), dim) // head_size for dim in (0, 1)]
    average = jnp.where(owner[0] == owner[1], 1.0 / head_size, 0.0).astype(BF16)
    for block in range(count):
        rows = slice(block * SPAN, (block + 1) * SPAN)
        y = y_ref[rows, :] + carry_ref[rows, :] * dot(c_ref[rows, :], entry.astype(BF16))
        square_mean = dot((y * y).astype(BF16), average)
        gated_ref[rows, :] = (y * lax.rsqrt(square_mean + 1e-05) * silu_ref[rows, :]).astype(BF16)
        if block < count - 1:
            entry = keep_ref[block : block + 1, :] * entry + step_ref[block * state : (block + 1) * state, :]


def conv_kernel(group, steps, len_ref, taps_ref, gated_ref, act_ref, ext_ref, ends_ref):
    place, plane = plane_place(group)
    rows_all, width = gated_ref.shape
    total = rows_all - SPAN
    frames = total // group
    taps = taps_ref.shape[0]
    half = (taps - 1) // 2
    stream = lax.axis_size("tm") // group * total
    records = len_ref.shape[0]
    reach = CONV_ROWS + 2 * EDGE
    first_tap = EDGE - half
    pitch = frames + 2 * EDGE
    ends_ref[0] = 0
    for record in range(records):
        ends_ref[record + 1] = ends_ref[record] + len_ref[record]
    for number, step in enumerate(steps):
        first = pl.multiple_of((place ^ step) * frames, frames)
        ext_ref[number * pitch : (number + 1) * pitch, :] = gated_ref[pl.ds(first, pitch), :].astype(F32)

    def record_at(position):
        found = jnp.int32(0)
        for record in range(records - 1):
            found = found + (ends_ref[record + 1] <= position).astype(jnp.int32)
        return found

    for number, step in enumerate(steps):
        base = plane * total + (place ^ step) * frames

        def one_block(block, _, number=number, base=base):
            inside_part = pl.multiple_of(block * CONV_ROWS, CONV_ROWS)
            source = pl.multiple_of(number * pitch + inside_part, EDGE)
            target = pl.multiple_of(number * frames + inside_part, CONV_ROWS)
            at = base + inside_part
            low = record_at(jnp.maximum(at - half, 0))
            high = record_at(jnp.minimum(at + CONV_ROWS - 1 + half, stream - 1))
            near = lax.broadcasted_iota(jnp.int32, (reach, LANES), 0) + (at - EDGE)
            for tile in range(width // LANES):
                lanes = slice(tile * LANES, (tile + 1) * LANES)
                weights = taps_ref[:, pl.ds(pl.multiple_of(place * width + tile * LANES, LANES), LANES)]

                def one_record(record, done):
                    inside = (near >= ends_ref[record]) & (near < ends_ref[record + 1])
                    g = jnp.where(inside, ext_ref[pl.ds(source, reach), lanes], 0.0)
                    out = None
                    for phase in range(8):
                        part = None
                        for offset in range(phase, reach - CONV_ROWS, 8):
                            tap = offset - first_tap
                            if 0 <= tap < taps:
                                aligned = offset - phase
                                term = weights[tap : tap + 1, :] * g[aligned : aligned + CONV_ROWS + 8, :]
                                part = term if part is None else part + term
                        if part is not None:
                            moved = part[phase : phase + CONV_ROWS, :]
                            out = moved if out is None else out + moved
                    return jnp.where(inside[EDGE : EDGE + CONV_ROWS], out, done)

                conv = lax.fori_loop(low, high + 1, one_record, jnp.zeros((CONV_ROWS, LANES), F32))
                act_ref[pl.ds(target, CONV_ROWS), lanes] = (conv / (1.0 + jnp.exp(-conv))).astype(BF16)
            return 0

        lax.fori_loop(0, frames // CONV_ROWS, one_block, 0)


def out_kernel(cores, count, *refs):
    acts, weights, sent, outs = refs[:cores], refs[cores : 2 * cores], refs[2 * cores : -count], refs[-count:]
    frames = outs[0].shape[0]
    for number, out_ref in enumerate(outs):
        rows = slice(number * frames, (number + 1) * frames)
        total = None
        for act, weight in zip(acts, weights):
            product = dot(act[rows, :], weight[...], ((1,), (1,)))
            total = product if total is None else total + product
        for part in sent:
            total = total + part[...].astype(F32)
        out_ref[...] = total.astype(out_ref.dtype)


def local(
    frames,
    x_weight,
    z_weight,
    bc_weight,
    log_decay,
    norm_gain,
    conv_weight,
    out_weight,
    record_lengths,
):
    times, cores = lax.axis_size("tm"), lax.axis_size("head")
    frame_count, depth = frames.shape
    heads_here, channels = log_decay.shape[0], x_weight.shape[1]
    state = bc_weight.shape[1] // 2
    group = 4
    while group > 1 and (channels // group % LANES or times % group or heads_here % group):
        group //= 2
    planes = times // group
    width, heads = channels // group, heads_here // group
    total = frame_count * group
    count = total // SPAN
    index, core = lax.axis_index("tm"), lax.axis_index("head")
    place = lax.rem(index, group)

    def in_plane(array, step):
        return lax.ppermute(array, "tm", [(i, i ^ step) for i in range(times)])

    def later(array, step):
        return lax.ppermute(array, "tm", [(i, i + step * group) for i in range(times - step * group)])

    def across(array, step):
        return lax.ppermute(array, "head", [(i, i ^ step) for i in range(cores)])

    def between_planes(array, step):
        return lax.ppermute(array, "tm", [(i, i ^ (step * group)) for i in range(times)])

    shape = jax.ShapeDtypeStruct
    rows = x_weight.shape[0]
    parity = lax.rem(core, 2)

    def along_planes(stacks):
        if planes != 4:
            return [stacks[0]] + [between_planes(stacks[step], step) for step in range(1, planes)]

        def pairs(chosen):
            return [(a * group + q, b * group + q) for a, b in chosen for q in range(group)]

        second = between_planes(stacks[2], 2)
        first = between_planes(stacks[1], 1)
        again, last, first = lax.optimization_barrier((second, stacks[3], first))
        third = lax.ppermute(again, "tm", pairs([(1, 0), (2, 3)]))
        middle = lax.ppermute(last, "tm", pairs([(1, 2), (2, 1)]))
        return [stacks[0], first, second, third, middle]

    offsets = (0, 1, 2, 3, 3) if planes == 4 else tuple(range(planes))
    half_count = frame_count // 2
    down, depth_tiles = rows // 16, depth // LANES
    payloads = call(
        functools.partial(first_kernel, group, planes),
        (
            *(shape((rows, 3 * width), BF16) for _ in range(group)),
            *(shape((-(-(down + depth_tiles + 1) // 8) * 16, depth), BF16) for _ in range(planes)),
        ),
        [log_decay, bc_weight, frames, x_weight, z_weight, out_weight.T],
        [
            pltpu.VMEM((rows, LANES), BF16),
            pltpu.VMEM((2, EDGE, depth), BF16),
            pltpu.VMEM(log_decay.shape, F32),
            pltpu.SemaphoreType.DMA((4 + 3 * group,)),
        ],
        smem=0,
        anywhere=6,
        vmem=ALL_VMEM_BYTES,
    )
    inner, outer = payloads[:group], payloads[group:]
    parts = [inner[0]] + [in_plane(inner[step], step) for step in range(1, group)]
    pieces = [outer[0]] + [between_planes(outer[step], step) for step in range(1, planes)]
    xz_stack, out_stack = call(
        functools.partial(stack_kernel, group),
        (shape((group * rows, 2 * width), BF16), shape((group * rows, width), BF16)),
        parts,
        flops=STACK_HINT,
        smem=0,
    )
    xz_pieces = along_planes([xz_stack] * planes)
    xz_pieces, out_stack = lax.optimization_barrier((xz_pieces, out_stack))
    out_pieces = [out_stack] + [between_planes(out_stack, step) for step in range(1, planes)]
    x_columns, z_columns = call(
        functools.partial(assemble_kernel, group, offsets),
        (shape((depth, width), BF16), shape((depth, width), BF16)),
        xz_pieces,
        flops=ASSEMBLE_HINT,
        smem=0,
    )
    decay_blocks = jnp.pad(log_decay.reshape(group, heads, frame_count), ((0, 0), (0, 8 - heads), (0, 0)))
    tiles = planes * down + depth_tiles + 1 + frame_count // SPAN * 2
    inward = call(
        functools.partial(inward_kernel, group, rows),
        tuple(shape((half_count + -(-tiles // 8) * 16, depth), BF16) for _ in range(group)),
        [decay_blocks, frames, *pieces],
        flops=INWARD_HINT,
        smem=0,
    )
    inward = [inward[0]] + [in_plane(inward[step], step) for step in range(1, group)]
    swap, bc_mine, halo, decay = call(
        functools.partial(swap_kernel, group, rows),
        (
            shape(((group - 1) * half_count + LANES, depth), BF16),
            shape((depth, LANES), BF16),
            shape((2 * EDGE, depth), BF16),
            shape((count * 8 + 8, SPAN), F32),
        ),
        inward,
        [pltpu.VMEM((count, 8, SPAN), F32)],
        smem=0,
    )
    swap = across(swap, 1)
    all_rows = total + SPAN

    frame_rows, x_rows, b_rows, c_rows, decay_rows, steps, keep, summary = call(
        functools.partial(state_kernel, group, heads, state),
        (
            shape((all_rows, depth), BF16),
            shape((all_rows, width), BF16),
            shape((all_rows, state), BF16),
            shape((all_rows, state), BF16),
            shape((3 * (count + 1) * 8, SPAN), F32),
            shape((count * state, width), F32),
            shape((-(-count // 8) * 8, width), F32),
            shape((state + EDGE, width), BF16),
        ),
        [record_lengths, decay, x_columns, bc_mine, frames, swap, halo, *inward[1:]],
        [pltpu.VMEM((depth, 2 * state), BF16), pltpu.VMEM((total, width), F32)],
        hidden=True,
    )
    summaries = [later(summary, step) for step in range(1, planes)]
    x_rows, out_pieces = lax.optimization_barrier((x_rows, out_pieces))
    y, carry = call(
        functools.partial(inner_kernel, group, heads),
        (shape((all_rows, width), F32), shape((all_rows, width), F32)),
        [x_rows, b_rows, c_rows, decay_rows],
        flops=4 * total * SPAN * width,
        smem=0,
    )
    silu = call(
        functools.partial(silu_kernel, group),
        shape((all_rows, width), F32),
        [norm_gain[None], frame_rows, z_columns],
        flops=2 * total * depth * width,
        smem=0,
    )
    gated = call(
        functools.partial(gate_kernel, heads, state),
        shape((all_rows, width), BF16),
        [c_rows, y, steps, carry, keep, silu, *summaries],
        flops=2 * total * state * width,
        smem=0,
    )
    ends = pltpu.SMEM((record_lengths.shape[0] + 1,), jnp.int32)
    far, near = (group - 1,), tuple(range(1, group - 1))

    def conv(steps, gated):
        return call(
            functools.partial(conv_kernel, group, steps),
            shape((len(steps) * frame_count, width), BF16),
            [record_lengths, conv_weight, gated],
            [pltpu.VMEM((len(steps) * (frame_count + 2 * EDGE), width), F32), ends],
            flops=2 * len(steps) * frame_count * width * conv_weight.shape[0],
        )

    def out(steps, act, swapped, sent=()):
        return call(
            functools.partial(out_kernel, cores, len(steps)),
            tuple(shape((frame_count, share), BF16) for _ in steps),
            [act, *swapped, *out_parts, *sent],
            flops=2 * len(steps) * frame_count * width * cores * share,
            smem=0,
        )

    share = depth // cores
    out_parts = call(
        functools.partial(share_kernel, cores, tuple(range(planes)), group),
        tuple(shape((share, width), BF16) for _ in range(cores)),
        out_pieces,
        [pltpu.VMEM((depth, width), BF16)],
        smem=0,
    )
    out_parts, gated = lax.optimization_barrier((out_parts, gated))
    out_parts = [out_parts[0]] + [across(out_parts[step], step) for step in range(1, cores)]
    far_act = conv(far, gated)
    far_swapped = [across(far_act, step) for step in range(1, cores)]
    gated, far_act = lax.optimization_barrier((gated, far_act))
    if near:
        near_act = conv(near, gated)
        near_act, far_swapped, out_parts = lax.optimization_barrier((near_act, far_swapped, out_parts))
    (far_out,) = out(far, far_act, far_swapped)
    if near:
        near_act, far_out = lax.optimization_barrier((near_act, far_out))
    sent = [in_plane(far_out, far[0])]
    if near:
        near_swapped = [across(near_act, step) for step in range(1, cores)]
        near_outs = out(near, near_act, near_swapped)
        gated, near_outs = lax.optimization_barrier((gated, near_outs))
        sent += [in_plane(part, step) for part, step in zip(near_outs, near)]
    own_act = conv((0,), gated)
    own_swapped = [across(own_act, step) for step in range(1, cores)]
    (mixed,) = out((0,), own_act, own_swapped, sent)
    return mixed


def solution(mesh):
    in_specs = (
        P("tm", None),
        P("tm", "head"),
        P("tm", "head"),
        P("tm", None),
        P("head", "tm"),
        P("head"),
        P(None, "head"),
        P("head", "tm"),
        P(),
    )
    out_specs = P("tm", "head")
    return jax.shard_map(local, mesh=mesh, in_specs=in_specs, out_specs=out_specs, check_vma=False)
```

```python
import functools

import jax
import jax.numpy as jnp
from jax import lax
from jax.experimental import pallas as pl
from jax.experimental.pallas import tpu as pltpu
from jax.sharding import PartitionSpec as P

SPAN = 128
LANES = 128
EDGE = 16
CONV_ROWS = 64
BF16 = jnp.bfloat16
F32 = jnp.float32
STACK_HINT = 40_000_000_000
INWARD_HINT = 40_000_000_000
ASSEMBLE_HINT = 40_000_000_000
ALL_VMEM_BYTES = 63 * 1024 * 1024
VMEM_BYTES = 20 * 1024 * 1024


def dot(a, b, dims=((1,), (0,)), precision=None):
    return lax.dot_general(a, b, (dims, ((), ())), precision=precision, preferred_element_type=F32)


def call(kernel, out_shape, operands, scratch=(), flops=0, smem=1, anywhere=0, vmem=VMEM_BYTES, hidden=False):
    in_specs = [pl.BlockSpec(memory_space=pltpu.SMEM)] * smem
    in_specs += [pl.BlockSpec(memory_space=pltpu.VMEM)] * (len(operands) - smem - anywhere)
    in_specs += [pl.BlockSpec(memory_space=pl.ANY)] * anywhere
    moved = sum(a.size * a.dtype.itemsize for a in operands)
    moved += sum(a.size * a.dtype.itemsize for a in jax.tree.leaves(out_shape))
    if hidden:
        flops = moved = 0
    return pl.pallas_call(
        kernel,
        out_shape=out_shape,
        in_specs=in_specs,
        out_specs=jax.tree.map(lambda _: pl.BlockSpec(memory_space=pltpu.VMEM), out_shape),
        scratch_shapes=list(scratch),
        compiler_params=pltpu.CompilerParams(vmem_limit_bytes=vmem),
        cost_estimate=pl.CostEstimate(flops=flops, bytes_accessed=moved, transcendentals=0),
    )(*operands)


def plane_place(group):
    index = lax.axis_index("tm")
    return lax.rem(index, group), lax.div(index, group)


def record_starts(len_ref, position):
    start = jnp.zeros_like(position)
    end = jnp.int32(0)
    for record in range(len_ref.shape[0] - 1):
        end = end + len_ref[record]
        start = jnp.where(position >= end, end, start)
    return start


def fill_planes(plane, dest_ref, pieces, offsets, lanes=slice(None)):
    rows = pieces[0].shape[0]
    for offset in sorted(set(offsets)):
        same = [piece[:, lanes] for piece, at in zip(pieces, offsets) if at == offset]
        value = same[0] if len(same) == 1 else same[0] + same[1]
        dest_ref[pl.ds(pl.multiple_of((plane ^ offset) * rows, rows), rows), : value.shape[1]] = value


def first_kernel(group, planes, log_decay_ref, bc_ref, frames_ref, *refs):
    weight_refs, refs = refs[:3], refs[3:]
    inner_refs, outer_refs, refs = refs[:group], refs[group : group + planes], refs[group + planes :]
    bc_half_ref, edge_ref, decay_ref, sems = refs
    place, plane = plane_place(group)
    parity = lax.rem(lax.axis_index("head"), 2)
    width = weight_refs[0].shape[1] // group
    frames = frames_ref.shape[0]
    heads = log_decay_ref.shape[0] // group
    copies = [
        (bc_ref.at[:, pl.ds(pl.multiple_of(parity * LANES, LANES), LANES)], bc_half_ref),
        (frames_ref.at[:EDGE, :], edge_ref.at[0]),
        (frames_ref.at[frames - EDGE :, :], edge_ref.at[1]),
        (log_decay_ref, decay_ref),
    ]
    for step, inner_ref in enumerate(inner_refs):
        lanes = pl.ds(pl.multiple_of((place ^ step) * width, LANES), width)
        for number, weight_ref in enumerate(weight_refs):
            copies.append((weight_ref.at[:, lanes], inner_ref.at[:, number * width : (number + 1) * width]))
    started = [pltpu.make_async_copy(a, b, sems.at[number]) for number, (a, b) in enumerate(copies)]
    for copy in started:
        copy.start()
    for copy in started[:4]:
        copy.wait()
    lane = lax.broadcasted_iota(jnp.int32, (8, LANES), 1)
    decays = []
    for first in (0, frames - LANES):
        rows = [jnp.zeros((8, LANES), F32), jnp.zeros((8, LANES), F32)]
        for block in range(group):
            here = decay_ref[block * heads : (block + 1) * heads, first : first + LANES]
            here = jnp.concatenate([here, jnp.zeros((8 - heads, LANES), F32)], axis=0)
            for number, term in enumerate(three_terms(here)):
                slot = number * group + block
                moved = pltpu.roll(term, (slot % 8 * EDGE + (EDGE if first else 0)) % LANES, 1)
                rows[slot // 8] = jnp.where(lane // EDGE == slot % 8, moved, rows[slot // 8])
        decays.append(jnp.concatenate(rows, axis=0))
    for step, out_ref in enumerate(outer_refs):
        number = put(out_ref, 0, bc_half_ref[...])
        later = (plane ^ step) > plane
        number = put(out_ref, number, jnp.where(later, edge_ref[1].astype(F32), edge_ref[0].astype(F32)).astype(BF16))
        put(out_ref, number, jnp.where(later, decays[1], decays[0]).astype(BF16))
    for copy in started[4:]:
        copy.wait()


def stack_kernel(group, *refs):
    parts, stack_refs = refs[:group], refs[group:]
    place, _ = plane_place(group)
    rows = parts[0].shape[0]
    for step, part in enumerate(parts):
        at = pl.ds(pl.multiple_of((place ^ step) * rows, rows), rows)
        first = 0
        for stack_ref in stack_refs:
            width = stack_ref.shape[1]
            stack_ref[at, :] = part[:, first : first + width]
            first += width


def assemble_kernel(group, offsets, *refs):
    pieces, dest_refs = refs[: len(offsets)], refs[len(offsets) :]
    _, plane = plane_place(group)
    first = 0
    for dest_ref in dest_refs:
        width = dest_ref.shape[1]
        fill_planes(plane, dest_ref, pieces, offsets, slice(first, first + width))
        first += width


def tile(number):
    return slice(number // 8 * 16, number // 8 * 16 + 16), slice(number % 8 * LANES, (number % 8 + 1) * LANES)


def put(out_ref, number, array):
    for at in range(0, array.shape[0], 16):
        for lane in range(0, array.shape[1], LANES):
            out_ref[tile(number)] = array[at : at + 16, lane : lane + LANES]
            number += 1
    return number


def three_terms(value):
    terms = []
    for _ in range(3):
        term = value.astype(BF16).astype(F32)
        terms.append(term)
        value = value - term
    return terms


def inward_kernel(group, rows, decay_ref, frames_ref, *refs):
    piece_refs, out_refs = refs[:-group], refs[-group:]
    place, plane = plane_place(group)
    planes = len(piece_refs)
    half = frames_ref.shape[0] // 2
    mine = pl.ds(pl.multiple_of(lax.rem(lax.axis_index("head"), 2) * half, half), half)
    wanted = jnp.clip(jnp.where(place == 0, plane + 1, plane - 1), 0, planes - 1)
    depth_tiles = frames_ref.shape[1] // LANES
    down = rows // 16
    for step, out_ref in enumerate(out_refs):
        out_ref[:half, :] = frames_ref[mine, :]
        number = half // 16 * depth_tiles
        for piece_ref in piece_refs:
            for at in range(down):
                out_ref[tile(number)] = piece_ref[tile(at)]
                number += 1
        for offset, piece_ref in enumerate(piece_refs):

            @pl.when((plane ^ offset) == wanted)
            def _(piece_ref=piece_ref, number=number, out_ref=out_ref):
                for at in range(depth_tiles + 1):
                    out_ref[tile(number + at)] = piece_ref[tile(down + at)]

        number += depth_tiles + 1
        terms = three_terms(decay_ref[place ^ step])
        terms = jnp.concatenate([*terms, jnp.zeros_like(terms[0])], axis=0).astype(BF16)
        for span in range(terms.shape[1] // SPAN):
            number = put(out_ref, number, terms[:, span * SPAN : (span + 1) * SPAN])


def swap_kernel(group, rows, *refs):
    part_refs, (swap_ref, bc_ref, halo_ref, decay_ref, span_ref) = refs[:group], refs[group:]
    half_refs = part_refs[1:]
    place, plane = plane_place(group)
    planes = bc_ref.shape[0] // (group * rows)
    count = span_ref.shape[0]
    spans = count // group
    down = rows // 16
    depth_tiles = swap_ref.shape[1] // LANES
    height = LANES
    top = swap_ref.shape[0] - height
    half = top // len(half_refs)
    lane = lax.broadcasted_iota(jnp.int32, (8, LANES), 1)
    for step, part_ref in enumerate(part_refs):
        block = place ^ step
        number = half // 16 * depth_tiles
        for offset in range(planes):
            first = ((plane ^ offset) * group + block) * rows
            for at in range(down):
                bc_ref[pl.ds(pl.multiple_of(first + at * 16, 16), 16), :] = part_ref[tile(number)]
                number += 1
        for side, owner in enumerate((group - 1, 0)):

            @pl.when(block == owner)
            def _(part_ref=part_ref, number=number, side=side):
                for at in range(depth_tiles):
                    halo_ref[side * EDGE : (side + 1) * EDGE, at * LANES : (at + 1) * LANES] = part_ref[tile(number + at)]
                packed = part_ref[tile(number + depth_tiles)].astype(F32)
                chosen = jnp.zeros((8, LANES), F32)
                for head_block in range(group):
                    value = jnp.zeros((8, LANES), F32)
                    for term in range(3):
                        slot = term * group + head_block
                        half = packed[slot // 8 * 8 : slot // 8 * 8 + 8]
                        value = value + pltpu.roll(half, (LANES - slot % 8 * EDGE) % LANES, 1)
                    chosen = jnp.where(place == head_block, value, chosen)
                if side:
                    last = pltpu.roll(chosen, EDGE, 1)
                    decay_ref[count * 8 :, :] = jnp.where((lane >= EDGE) & (lane < 2 * EDGE), last, 0.0)
                else:
                    decay_ref[:8, :] = jnp.where(lane < EDGE, chosen, 0.0)

        number += depth_tiles + 1
        for span in range(spans):
            upper = part_ref[tile(number)].astype(F32)
            lower = part_ref[tile(number + 1)].astype(F32)
            number += 2
            span_ref[block * spans + span] = upper[:8] + upper[8:] + lower[:8]
    for span in range(count):
        moved = pltpu.roll(span_ref[span], EDGE, 1)
        here, after = slice(span * 8, span * 8 + 8), slice(span * 8 + 8, span * 8 + 16)
        decay_ref[here, :] = jnp.where(lane < EDGE, decay_ref[here, :], moved)
        kept = decay_ref[after, :] if span == count - 1 else jnp.zeros((8, LANES), F32)
        decay_ref[after, :] = jnp.where(lane < EDGE, moved, kept)
    for number, half_ref in enumerate(half_refs):
        swap_ref[number * half : (number + 1) * half, :] = half_ref[:half, : swap_ref.shape[1]]
    for number in range(bc_ref.shape[0] // height):
        lanes = slice(number * LANES, (number + 1) * LANES)
        swap_ref[top:, lanes] = bc_ref[number * height : (number + 1) * height, :]


def lanes_of(rows, width, head_size):
    high = rows.astype(BF16).astype(F32)
    owner = lax.broadcasted_iota(jnp.int32, (16, width), 1) // head_size
    chosen = jnp.where((lax.broadcasted_iota(jnp.int32, (16, width), 0) & 7) == owner, 1.0, 0.0).astype(BF16)
    return dot(jnp.concatenate([high, rows - high], axis=0).astype(BF16), chosen, ((0,), (0,)))


def spans_in_lanes(rows):
    return jnp.concatenate([rows[at : at + 8] for at in range(0, rows.shape[0], 8)], axis=1)


def row_blocks(total, wide):
    return [slice(at, at + 256) for at in range(0, total, 256)] + [slice(total, wide)]


def state_kernel(group, heads, state, len_ref, decay_ref, x_weight_ref, bc_half_ref, own_ref, swap_ref, halo_ref, *refs):
    half_refs, refs = refs[: group - 1], refs[group - 1 :]
    frames_ref, x_ref, b_ref, c_ref, rows_ref, step_ref, keep_ref, send_ref, weight_ref, tail_ref = refs
    place, plane = plane_place(group)
    parity = lax.rem(lax.axis_index("head"), 2)
    width = x_ref.shape[1]
    frames = own_ref.shape[0]
    total = frames * group
    half = frames // 2
    head_size = width // heads
    count = total // SPAN
    base = plane * total - EDGE
    wide = total + 2 * EDGE
    frames_ref[:EDGE, :] = halo_ref[:EDGE, :]
    frames_ref[total + EDGE : wide, :] = halo_ref[EDGE:, :]
    frames_ref[wide:, :] = jnp.zeros((frames_ref.shape[0] - wide, frames_ref.shape[1]), BF16)
    frames_ref[pl.ds(pl.multiple_of(EDGE + place * frames, EDGE), frames), :] = own_ref[...]
    for number, half_ref in enumerate(half_refs):
        block = EDGE + (place ^ (number + 1)) * frames
        mine = pl.ds(pl.multiple_of(block + parity * half, EDGE), half)
        other = pl.ds(pl.multiple_of(block + (1 - parity) * half, EDGE), half)
        frames_ref[mine, :] = half_ref[:half, : frames_ref.shape[1]]
        frames_ref[other, :] = swap_ref[number * half : (number + 1) * half, :]
    mine = pl.ds(pl.multiple_of(parity * LANES, LANES), LANES)
    other = pl.ds(pl.multiple_of((1 - parity) * LANES, LANES), LANES)
    weight_ref[:, mine] = bc_half_ref[...]
    top = len(half_refs) * half
    height = swap_ref.shape[0] - top
    for number in range(weight_ref.shape[0] // height):
        lanes = slice(number * LANES, (number + 1) * LANES)
        weight_ref[number * height : (number + 1) * height, other] = swap_ref[top:, lanes]

    decay = decay_ref[...]
    used = decay.shape[0]
    square = (SPAN, SPAN)
    row, lane = (lax.broadcasted_iota(jnp.int32, square, dim) for dim in (0, 1))
    upper = jnp.where(row <= lane, 1.0, 0.0).astype(F32)
    cumul = dot(decay, upper, precision=lax.Precision.HIGHEST)
    whole = dot(decay, jnp.ones(square, F32), precision=lax.Precision.HIGHEST)
    first = base + lax.broadcasted_iota(jnp.int32, (used, SPAN), 0) // 8 * SPAN
    position = first + lane[:1]
    start = record_starts(len_ref, position)
    start_last = record_starts(len_ref, first + (SPAN - 1))
    carried = jnp.where(start < first, jnp.exp(cumul), 0.0)
    tail = jnp.where(position >= start_last, jnp.exp(whole - cumul), 0.0)
    keep = jnp.where(start_last < first, jnp.exp(whole), 0.0)
    rows_ref[:used, :] = cumul
    rows_ref[used : 2 * used, :] = start.astype(F32)
    rows_ref[2 * used :, :] = carried

    for rows in row_blocks(total, wide):
        x_ref[rows, :] = dot(frames_ref[rows, :], x_weight_ref[...]).astype(BF16)
        product = dot(frames_ref[rows, :], weight_ref[...])
        b_ref[rows, :] = product[:, :state].astype(BF16)
        c_ref[rows, :] = product[:, state:].astype(BF16)
    for ref in (x_ref, b_ref, c_ref):
        ref[wide:, :] = jnp.zeros((ref.shape[0] - wide, ref.shape[1]), BF16)

    tail_ref[...] = lanes_of(spans_in_lanes(tail[: count * 8]), width, head_size)
    by_span = jnp.zeros((8, SPAN), F32)
    for block in range(count):
        by_span = jnp.where(lane[:8] == block, keep[block * 8 : (block + 1) * 8], by_span)
    kept = lanes_of(by_span, width, head_size)[: keep_ref.shape[0]]
    keep_ref[...] = kept
    entry = jnp.zeros((state, width), F32)
    through = jnp.ones((1, width), F32)
    for block in range(count):
        rows = slice(block * SPAN, (block + 1) * SPAN)
        weighed = x_ref[rows, :].astype(F32) * tail_ref[rows, :]
        step = dot(b_ref[rows, :], weighed.astype(BF16), ((0,), (0,)))
        step_ref[block * state : (block + 1) * state, :] = step
        entry = kept[block : block + 1] * entry + step
        through = through * kept[block : block + 1]
    send_ref[:state, :] = entry.astype(BF16)
    send_ref[state:, :] = jnp.broadcast_to(through, (EDGE, width)).astype(BF16)


def inner_kernel(group, heads, x_ref, b_ref, c_ref, rows_ref, y_ref, carry_ref):
    _, plane = plane_place(group)
    total, width = x_ref.shape
    head_size = width // heads
    count = total // SPAN
    base = plane * (total - SPAN) - EDGE
    used = rows_ref.shape[0] // 3
    square = (SPAN, SPAN)
    parts = [rows_ref[: 2 * used, :]]
    if 2 * used % SPAN:
        parts.append(jnp.zeros((SPAN - 2 * used % SPAN, SPAN), F32))
    columns = jnp.concatenate(parts, axis=0).T
    carry_ref[...] = lanes_of(spans_in_lanes(rows_ref[2 * used :, :]), width, head_size)
    row, lane = (lax.broadcasted_iota(jnp.int32, square, dim) for dim in (0, 1))
    lower = row >= lane
    tile_heads = LANES // head_size
    tile_lane = lax.broadcasted_iota(jnp.int32, (1, LANES), 1) // head_size
    masks = [jnp.where(tile_lane == inner, 1.0, 0.0).astype(BF16) for inner in range(tile_heads)]
    for block in range(count):
        rows = slice(block * SPAN, (block + 1) * SPAN)
        at = block * 8
        x = x_ref[rows, :]
        scores = dot(c_ref[rows, :], b_ref[rows, :], ((1,), (1,)))
        here = (base + block * SPAN + lane).astype(F32)
        start_here = jnp.broadcast_to(columns[:, used + at : used + at + 1], square)
        joined = lower & (here >= start_here)
        for tile in range(width // LANES):
            mixes, values = [], []
            for inner in range(tile_heads):
                which = at + tile * tile_heads + inner
                column = jnp.broadcast_to(columns[:, which : which + 1], square)
                gap = jnp.where(joined, column - rows_ref[which : which + 1, :], -1e30)
                mixes.append((jnp.exp(gap) * scores).astype(BF16))
                values.append(x[:, tile * LANES : (tile + 1) * LANES] * masks[inner])
            y_ref[rows, tile * LANES : (tile + 1) * LANES] = dot(
                jnp.concatenate(mixes, axis=1), jnp.concatenate(values, axis=0)
            )


def silu_kernel(group, gain_ref, frames_ref, weight_ref, out_ref):
    place, _ = plane_place(group)
    rows_all, width = out_ref.shape
    total = rows_all - SPAN
    wide = total + 2 * EDGE
    gain = gain_ref[:, pl.ds(pl.multiple_of(place * width, LANES), width)]
    for rows in row_blocks(total, wide):
        z = dot(frames_ref[rows, :], weight_ref[...]).astype(BF16).astype(F32)
        out_ref[rows, :] = z / (1.0 + jnp.exp(-z)) * gain
    out_ref[wide:, :] = jnp.zeros((rows_all - wide, width), F32)


def share_kernel(cores, offsets, group, *refs):
    pieces, refs = refs[: len(offsets)], refs[len(offsets) :]
    outs, weight_ref = refs[:cores], refs[cores]
    _, plane = plane_place(group)
    core = lax.axis_index("head")
    fill_planes(plane, weight_ref, pieces, offsets)
    for step, out_ref in enumerate(outs):
        rows = out_ref.shape[0]
        out_ref[...] = weight_ref[pl.ds(pl.multiple_of((core ^ step) * rows, rows), rows), :]


def gate_kernel(heads, state, c_ref, y_ref, step_ref, carry_ref, keep_ref, silu_ref, *refs):
    earlier, gated_ref = refs[:-1], refs[-1]
    total, width = y_ref.shape
    head_size = width // heads
    count = total // SPAN
    entry = jnp.zeros((state, width), F32)
    for summary in reversed(earlier):
        through = summary[state : state + EDGE, :].astype(F32)[:1]
        entry = through * entry + summary[:state, :].astype(F32)
    owner = [lax.broadcasted_iota(jnp.int32, (width, width), dim) // head_size for dim in (0, 1)]
    average = jnp.where(owner[0] == owner[1], 1.0 / head_size, 0.0).astype(BF16)
    for block in range(count):
        rows = slice(block * SPAN, (block + 1) * SPAN)
        y = y_ref[rows, :] + carry_ref[rows, :] * dot(c_ref[rows, :], entry.astype(BF16))
        square_mean = dot((y * y).astype(BF16), average)
        gated_ref[rows, :] = (y * lax.rsqrt(square_mean + 1e-05) * silu_ref[rows, :]).astype(BF16)
        if block < count - 1:
            entry = keep_ref[block : block + 1, :] * entry + step_ref[block * state : (block + 1) * state, :]


def conv_kernel(group, steps, len_ref, taps_ref, gated_ref, act_ref, ext_ref, ends_ref):
    place, plane = plane_place(group)
    rows_all, width = gated_ref.shape
    total = rows_all - SPAN
    frames = total // group
    taps = taps_ref.shape[0]
    half = (taps - 1) // 2
    stream = lax.axis_size("tm") // group * total
    records = len_ref.shape[0]
    reach = CONV_ROWS + 2 * EDGE
    first_tap = EDGE - half
    pitch = frames + 2 * EDGE
    ends_ref[0] = 0
    for record in range(records):
        ends_ref[record + 1] = ends_ref[record] + len_ref[record]
    for number, step in enumerate(steps):
        first = pl.multiple_of((place ^ step) * frames, frames)
        ext_ref[number * pitch : (number + 1) * pitch, :] = gated_ref[pl.ds(first, pitch), :].astype(F32)

    def record_at(position):
        found = jnp.int32(0)
        for record in range(records - 1):
            found = found + (ends_ref[record + 1] <= position).astype(jnp.int32)
        return found

    for number, step in enumerate(steps):
        base = plane * total + (place ^ step) * frames

        def one_block(block, _, number=number, base=base):
            inside_part = pl.multiple_of(block * CONV_ROWS, CONV_ROWS)
            source = pl.multiple_of(number * pitch + inside_part, EDGE)
            target = pl.multiple_of(number * frames + inside_part, CONV_ROWS)
            at = base + inside_part
            low = record_at(jnp.maximum(at - half, 0))
            high = record_at(jnp.minimum(at + CONV_ROWS - 1 + half, stream - 1))
            near = lax.broadcasted_iota(jnp.int32, (reach, LANES), 0) + (at - EDGE)
            for tile in range(width // LANES):
                lanes = slice(tile * LANES, (tile + 1) * LANES)
                weights = taps_ref[:, pl.ds(pl.multiple_of(place * width + tile * LANES, LANES), LANES)]

                def one_record(record, done):
                    inside = (near >= ends_ref[record]) & (near < ends_ref[record + 1])
                    g = jnp.where(inside, ext_ref[pl.ds(source, reach), lanes], 0.0)
                    out = None
                    for phase in range(8):
                        part = None
                        for offset in range(phase, reach - CONV_ROWS, 8):
                            tap = offset - first_tap
                            if 0 <= tap < taps:
                                aligned = offset - phase
                                term = weights[tap : tap + 1, :] * g[aligned : aligned + CONV_ROWS + 8, :]
                                part = term if part is None else part + term
                        if part is not None:
                            moved = part[phase : phase + CONV_ROWS, :]
                            out = moved if out is None else out + moved
                    return jnp.where(inside[EDGE : EDGE + CONV_ROWS], out, done)

                conv = lax.fori_loop(low, high + 1, one_record, jnp.zeros((CONV_ROWS, LANES), F32))
                act_ref[pl.ds(target, CONV_ROWS), lanes] = (conv / (1.0 + jnp.exp(-conv))).astype(BF16)
            return 0

        lax.fori_loop(0, frames // CONV_ROWS, one_block, 0)


def out_kernel(cores, count, *refs):
    acts, weights, sent, outs = refs[:cores], refs[cores : 2 * cores], refs[2 * cores : -count], refs[-count:]
    frames = outs[0].shape[0]
    for number, out_ref in enumerate(outs):
        rows = slice(number * frames, (number + 1) * frames)
        total = None
        for act, weight in zip(acts, weights):
            product = dot(act[rows, :], weight[...], ((1,), (1,)))
            total = product if total is None else total + product
        for part in sent:
            total = total + part[...].astype(F32)
        out_ref[...] = total.astype(out_ref.dtype)


def local(
    frames,
    x_weight,
    z_weight,
    bc_weight,
    log_decay,
    norm_gain,
    conv_weight,
    out_weight,
    record_lengths,
):
    times, cores = lax.axis_size("tm"), lax.axis_size("head")
    frame_count, depth = frames.shape
    heads_here, channels = log_decay.shape[0], x_weight.shape[1]
    state = bc_weight.shape[1] // 2
    group = 4
    while group > 1 and (channels // group % LANES or times % group or heads_here % group):
        group //= 2
    planes = times // group
    width, heads = channels // group, heads_here // group
    total = frame_count * group
    count = total // SPAN
    index, core = lax.axis_index("tm"), lax.axis_index("head")
    place = lax.rem(index, group)

    def in_plane(array, step):
        return lax.ppermute(array, "tm", [(i, i ^ step) for i in range(times)])

    def later(array, step):
        return lax.ppermute(array, "tm", [(i, i + step * group) for i in range(times - step * group)])

    def across(array, step):
        return lax.ppermute(array, "head", [(i, i ^ step) for i in range(cores)])

    def between_planes(array, step):
        return lax.ppermute(array, "tm", [(i, i ^ (step * group)) for i in range(times)])

    shape = jax.ShapeDtypeStruct
    rows = x_weight.shape[0]
    parity = lax.rem(core, 2)

    def along_planes(stacks):
        if planes != 4:
            return [stacks[0]] + [between_planes(stacks[step], step) for step in range(1, planes)]

        def pairs(chosen):
            return [(a * group + q, b * group + q) for a, b in chosen for q in range(group)]

        second = between_planes(stacks[2], 2)
        first = between_planes(stacks[1], 1)
        again, last, first = lax.optimization_barrier((second, stacks[3], first))
        third = lax.ppermute(again, "tm", pairs([(1, 0), (2, 3)]))
        middle = lax.ppermute(last, "tm", pairs([(1, 2), (2, 1)]))
        return [stacks[0], first, second, third, middle]

    offsets = (0, 1, 2, 3, 3) if planes == 4 else tuple(range(planes))
    half_count = frame_count // 2
    down, depth_tiles = rows // 16, depth // LANES
    payloads = call(
        functools.partial(first_kernel, group, planes),
        (
            *(shape((rows, 3 * width), BF16) for _ in range(group)),
            *(shape((-(-(down + depth_tiles + 1) // 8) * 16, depth), BF16) for _ in range(planes)),
        ),
        [log_decay, bc_weight, frames, x_weight, z_weight, out_weight.T],
        [
            pltpu.VMEM((rows, LANES), BF16),
            pltpu.VMEM((2, EDGE, depth), BF16),
            pltpu.VMEM(log_decay.shape, F32),
            pltpu.SemaphoreType.DMA((4 + 3 * group,)),
        ],
        smem=0,
        anywhere=6,
        vmem=ALL_VMEM_BYTES,
    )
    inner, outer = payloads[:group], payloads[group:]
    parts = [inner[0]] + [in_plane(inner[step], step) for step in range(1, group)]
    pieces = [outer[0]] + [between_planes(outer[step], step) for step in range(1, planes)]
    xz_stack, out_stack = call(
        functools.partial(stack_kernel, group),
        (shape((group * rows, 2 * width), BF16), shape((group * rows, width), BF16)),
        parts,
        flops=STACK_HINT,
        smem=0,
    )
    xz_stack, pieces = lax.optimization_barrier((xz_stack, pieces))
    xz_pieces = along_planes([xz_stack] * planes)
    xz_pieces, out_stack = lax.optimization_barrier((xz_pieces, out_stack))
    out_pieces = [out_stack] + [between_planes(out_stack, step) for step in range(1, planes)]
    x_columns, z_columns = call(
        functools.partial(assemble_kernel, group, offsets),
        (shape((depth, width), BF16), shape((depth, width), BF16)),
        xz_pieces,
        flops=ASSEMBLE_HINT,
        smem=0,
    )
    decay_blocks = jnp.pad(log_decay.reshape(group, heads, frame_count), ((0, 0), (0, 8 - heads), (0, 0)))
    tiles = planes * down + depth_tiles + 1 + frame_count // SPAN * 2
    inward = call(
        functools.partial(inward_kernel, group, rows),
        tuple(shape((half_count + -(-tiles // 8) * 16, depth), BF16) for _ in range(group)),
        [decay_blocks, frames, *pieces],
        flops=INWARD_HINT,
        smem=0,
    )
    inward = [inward[0]] + [in_plane(inward[step], step) for step in range(1, group)]
    swap, bc_mine, halo, decay = call(
        functools.partial(swap_kernel, group, rows),
        (
            shape(((group - 1) * half_count + LANES, depth), BF16),
            shape((depth, LANES), BF16),
            shape((2 * EDGE, depth), BF16),
            shape((count * 8 + 8, SPAN), F32),
        ),
        inward,
        [pltpu.VMEM((count, 8, SPAN), F32)],
        smem=0,
    )
    swap = across(swap, 1)
    all_rows = total + SPAN

    frame_rows, x_rows, b_rows, c_rows, decay_rows, steps, keep, summary = call(
        functools.partial(state_kernel, group, heads, state),
        (
            shape((all_rows, depth), BF16),
            shape((all_rows, width), BF16),
            shape((all_rows, state), BF16),
            shape((all_rows, state), BF16),
            shape((3 * (count + 1) * 8, SPAN), F32),
            shape((count * state, width), F32),
            shape((-(-count // 8) * 8, width), F32),
            shape((state + EDGE, width), BF16),
        ),
        [record_lengths, decay, x_columns, bc_mine, frames, swap, halo, *inward[1:]],
        [pltpu.VMEM((depth, 2 * state), BF16), pltpu.VMEM((total, width), F32)],
        hidden=True,
    )
    summaries = [later(summary, step) for step in range(1, planes)]
    x_rows, out_pieces = lax.optimization_barrier((x_rows, out_pieces))
    y, carry = call(
        functools.partial(inner_kernel, group, heads),
        (shape((all_rows, width), F32), shape((all_rows, width), F32)),
        [x_rows, b_rows, c_rows, decay_rows],
        flops=4 * total * SPAN * width,
        smem=0,
    )
    silu = call(
        functools.partial(silu_kernel, group),
        shape((all_rows, width), F32),
        [norm_gain[None], frame_rows, z_columns],
        flops=2 * total * depth * width,
        smem=0,
    )
    gated = call(
        functools.partial(gate_kernel, heads, state),
        shape((all_rows, width), BF16),
        [c_rows, y, steps, carry, keep, silu, *summaries],
        flops=2 * total * state * width,
        smem=0,
    )
    ends = pltpu.SMEM((record_lengths.shape[0] + 1,), jnp.int32)
    far, near = (group - 1,), tuple(range(1, group - 1))

    def conv(steps, gated):
        return call(
            functools.partial(conv_kernel, group, steps),
            shape((len(steps) * frame_count, width), BF16),
            [record_lengths, conv_weight, gated],
            [pltpu.VMEM((len(steps) * (frame_count + 2 * EDGE), width), F32), ends],
            flops=2 * len(steps) * frame_count * width * conv_weight.shape[0],
        )

    def out(steps, act, swapped, sent=()):
        return call(
            functools.partial(out_kernel, cores, len(steps)),
            tuple(shape((frame_count, share), BF16) for _ in steps),
            [act, *swapped, *out_parts, *sent],
            flops=2 * len(steps) * frame_count * width * cores * share,
            smem=0,
        )

    share = depth // cores
    out_parts = call(
        functools.partial(share_kernel, cores, tuple(range(planes)), group),
        tuple(shape((share, width), BF16) for _ in range(cores)),
        out_pieces,
        [pltpu.VMEM((depth, width), BF16)],
        smem=0,
    )
    out_parts, gated = lax.optimization_barrier((out_parts, gated))
    out_parts = [out_parts[0]] + [across(out_parts[step], step) for step in range(1, cores)]
    far_act = conv(far, gated)
    far_swapped = [across(far_act, step) for step in range(1, cores)]
    gated, far_act = lax.optimization_barrier((gated, far_act))
    if near:
        near_act = conv(near, gated)
        near_act, far_swapped, out_parts = lax.optimization_barrier((near_act, far_swapped, out_parts))
    (far_out,) = out(far, far_act, far_swapped)
    if near:
        near_act, far_out = lax.optimization_barrier((near_act, far_out))
    sent = [in_plane(far_out, far[0])]
    if near:
        near_swapped = [across(near_act, step) for step in range(1, cores)]
        near_outs = out(near, near_act, near_swapped)
        gated, near_outs = lax.optimization_barrier((gated, near_outs))
        sent += [in_plane(part, step) for part, step in zip(near_outs, near)]
    own_act = conv((0,), gated)
    own_swapped = [across(own_act, step) for step in range(1, cores)]
    (mixed,) = out((0,), own_act, own_swapped, sent)
    return mixed


def solution(mesh):
    in_specs = (
        P("tm", None),
        P("tm", "head"),
        P("tm", "head"),
        P("tm", None),
        P("head", "tm"),
        P("head"),
        P(None, "head"),
        P("head", "tm"),
        P(),
    )
    out_specs = P("tm", "head")
    return jax.shard_map(local, mesh=mesh, in_specs=in_specs, out_specs=out_specs, check_vma=False)
```

```python
import functools

import jax
import jax.numpy as jnp
from jax import lax
from jax.experimental import pallas as pl
from jax.experimental.pallas import tpu as pltpu
from jax.sharding import PartitionSpec as P

SPAN = 128
LANES = 128
EDGE = 16
CONV_ROWS = 64
BF16 = jnp.bfloat16
F32 = jnp.float32
STACK_HINT = 40_000_000_000
INWARD_HINT = 40_000_000_000
ASSEMBLE_HINT = 40_000_000_000
ALL_VMEM_BYTES = 63 * 1024 * 1024
VMEM_BYTES = 20 * 1024 * 1024


def dot(a, b, dims=((1,), (0,)), precision=None):
    return lax.dot_general(a, b, (dims, ((), ())), precision=precision, preferred_element_type=F32)


def call(kernel, out_shape, operands, scratch=(), flops=0, smem=1, anywhere=0, vmem=VMEM_BYTES, hidden=False):
    in_specs = [pl.BlockSpec(memory_space=pltpu.SMEM)] * smem
    in_specs += [pl.BlockSpec(memory_space=pltpu.VMEM)] * (len(operands) - smem - anywhere)
    in_specs += [pl.BlockSpec(memory_space=pl.ANY)] * anywhere
    moved = sum(a.size * a.dtype.itemsize for a in operands)
    moved += sum(a.size * a.dtype.itemsize for a in jax.tree.leaves(out_shape))
    if hidden:
        flops = moved = 0
    return pl.pallas_call(
        kernel,
        out_shape=out_shape,
        in_specs=in_specs,
        out_specs=jax.tree.map(lambda _: pl.BlockSpec(memory_space=pltpu.VMEM), out_shape),
        scratch_shapes=list(scratch),
        compiler_params=pltpu.CompilerParams(vmem_limit_bytes=vmem),
        cost_estimate=pl.CostEstimate(flops=flops, bytes_accessed=moved, transcendentals=0),
    )(*operands)


def plane_place(group):
    index = lax.axis_index("tm")
    return lax.rem(index, group), lax.div(index, group)


def record_starts(len_ref, position):
    start = jnp.zeros_like(position)
    end = jnp.int32(0)
    for record in range(len_ref.shape[0] - 1):
        end = end + len_ref[record]
        start = jnp.where(position >= end, end, start)
    return start


def fill_planes(plane, dest_ref, pieces, offsets, lanes=slice(None)):
    rows = pieces[0].shape[0]
    for offset in sorted(set(offsets)):
        same = [piece[:, lanes] for piece, at in zip(pieces, offsets) if at == offset]
        value = same[0] if len(same) == 1 else same[0] + same[1]
        dest_ref[pl.ds(pl.multiple_of((plane ^ offset) * rows, rows), rows), : value.shape[1]] = value


def first_kernel(group, planes, log_decay_ref, bc_ref, frames_ref, *refs):
    weight_refs, refs = refs[:3], refs[3:]
    inner_refs, outer_refs, refs = refs[:group], refs[group : group + planes], refs[group + planes :]
    bc_half_ref, edge_ref, decay_ref, sems = refs
    place, plane = plane_place(group)
    parity = lax.rem(lax.axis_index("head"), 2)
    width = weight_refs[0].shape[1] // group
    frames = frames_ref.shape[0]
    heads = log_decay_ref.shape[0] // group
    copies = [
        (bc_ref.at[:, pl.ds(pl.multiple_of(parity * LANES, LANES), LANES)], bc_half_ref),
        (frames_ref.at[:EDGE, :], edge_ref.at[0]),
        (frames_ref.at[frames - EDGE :, :], edge_ref.at[1]),
        (log_decay_ref, decay_ref),
    ]
    for step, inner_ref in enumerate(inner_refs):
        lanes = pl.ds(pl.multiple_of((place ^ step) * width, LANES), width)
        for number, weight_ref in enumerate(weight_refs):
            copies.append((weight_ref.at[:, lanes], inner_ref.at[:, number * width : (number + 1) * width]))
    started = [pltpu.make_async_copy(a, b, sems.at[number]) for number, (a, b) in enumerate(copies)]
    for copy in started:
        copy.start()
    for copy in started[:4]:
        copy.wait()
    lane = lax.broadcasted_iota(jnp.int32, (8, LANES), 1)
    decays = []
    for first in (0, frames - LANES):
        rows = [jnp.zeros((8, LANES), F32), jnp.zeros((8, LANES), F32)]
        for block in range(group):
            here = decay_ref[block * heads : (block + 1) * heads, first : first + LANES]
            here = jnp.concatenate([here, jnp.zeros((8 - heads, LANES), F32)], axis=0)
            for number, term in enumerate(three_terms(here)):
                slot = number * group + block
                moved = pltpu.roll(term, (slot % 8 * EDGE + (EDGE if first else 0)) % LANES, 1)
                rows[slot // 8] = jnp.where(lane // EDGE == slot % 8, moved, rows[slot // 8])
        decays.append(jnp.concatenate(rows, axis=0))
    for step, out_ref in enumerate(outer_refs):
        number = put(out_ref, 0, bc_half_ref[...])
        later = (plane ^ step) > plane
        number = put(out_ref, number, jnp.where(later, edge_ref[1].astype(F32), edge_ref[0].astype(F32)).astype(BF16))
        put(out_ref, number, jnp.where(later, decays[1], decays[0]).astype(BF16))
    for copy in started[4:]:
        copy.wait()


def stack_kernel(group, *refs):
    parts, stack_refs = refs[:group], refs[group:]
    place, _ = plane_place(group)
    rows = parts[0].shape[0]
    for step, part in enumerate(parts):
        at = pl.ds(pl.multiple_of((place ^ step) * rows, rows), rows)
        first = 0
        for stack_ref in stack_refs:
            width = stack_ref.shape[1]
            stack_ref[at, :] = part[:, first : first + width]
            first += width


def assemble_kernel(group, offsets, *refs):
    pieces, dest_refs = refs[: len(offsets)], refs[len(offsets) :]
    _, plane = plane_place(group)
    first = 0
    for dest_ref in dest_refs:
        width = dest_ref.shape[1]
        fill_planes(plane, dest_ref, pieces, offsets, slice(first, first + width))
        first += width


def tile(number):
    return slice(number // 8 * 16, number // 8 * 16 + 16), slice(number % 8 * LANES, (number % 8 + 1) * LANES)


def put(out_ref, number, array):
    for at in range(0, array.shape[0], 16):
        for lane in range(0, array.shape[1], LANES):
            out_ref[tile(number)] = array[at : at + 16, lane : lane + LANES]
            number += 1
    return number


def three_terms(value):
    terms = []
    for _ in range(3):
        term = value.astype(BF16).astype(F32)
        terms.append(term)
        value = value - term
    return terms


def inward_kernel(group, rows, decay_ref, frames_ref, *refs):
    piece_refs, out_refs = refs[:-group], refs[-group:]
    place, plane = plane_place(group)
    planes = len(piece_refs)
    half = frames_ref.shape[0] // 2
    mine = pl.ds(pl.multiple_of(lax.rem(lax.axis_index("head"), 2) * half, half), half)
    wanted = jnp.clip(jnp.where(place == 0, plane + 1, plane - 1), 0, planes - 1)
    depth_tiles = frames_ref.shape[1] // LANES
    down = rows // 16
    for step, out_ref in enumerate(out_refs):
        out_ref[:half, :] = frames_ref[mine, :]
        number = half // 16 * depth_tiles
        for piece_ref in piece_refs:
            for at in range(down):
                out_ref[tile(number)] = piece_ref[tile(at)]
                number += 1
        for offset, piece_ref in enumerate(piece_refs):

            @pl.when((plane ^ offset) == wanted)
            def _(piece_ref=piece_ref, number=number, out_ref=out_ref):
                for at in range(depth_tiles + 1):
                    out_ref[tile(number + at)] = piece_ref[tile(down + at)]

        number += depth_tiles + 1
        terms = three_terms(decay_ref[place ^ step])
        terms = jnp.concatenate([*terms, jnp.zeros_like(terms[0])], axis=0).astype(BF16)
        for span in range(terms.shape[1] // SPAN):
            number = put(out_ref, number, terms[:, span * SPAN : (span + 1) * SPAN])


def swap_kernel(group, rows, *refs):
    part_refs, (swap_ref, bc_ref, halo_ref, decay_ref, span_ref) = refs[:group], refs[group:]
    half_refs = part_refs[1:]
    place, plane = plane_place(group)
    planes = bc_ref.shape[0] // (group * rows)
    count = span_ref.shape[0]
    spans = count // group
    down = rows // 16
    depth_tiles = swap_ref.shape[1] // LANES
    height = LANES
    top = swap_ref.shape[0] - height
    half = top // len(half_refs)
    lane = lax.broadcasted_iota(jnp.int32, (8, LANES), 1)
    for step, part_ref in enumerate(part_refs):
        block = place ^ step
        number = half // 16 * depth_tiles
        for offset in range(planes):
            first = ((plane ^ offset) * group + block) * rows
            for at in range(down):
                bc_ref[pl.ds(pl.multiple_of(first + at * 16, 16), 16), :] = part_ref[tile(number)]
                number += 1
        for side, owner in enumerate((group - 1, 0)):

            @pl.when(block == owner)
            def _(part_ref=part_ref, number=number, side=side):
                for at in range(depth_tiles):
                    halo_ref[side * EDGE : (side + 1) * EDGE, at * LANES : (at + 1) * LANES] = part_ref[tile(number + at)]
                packed = part_ref[tile(number + depth_tiles)].astype(F32)
                chosen = jnp.zeros((8, LANES), F32)
                for head_block in range(group):
                    value = jnp.zeros((8, LANES), F32)
                    for term in range(3):
                        slot = term * group + head_block
                        half = packed[slot // 8 * 8 : slot // 8 * 8 + 8]
                        value = value + pltpu.roll(half, (LANES - slot % 8 * EDGE) % LANES, 1)
                    chosen = jnp.where(place == head_block, value, chosen)
                if side:
                    last = pltpu.roll(chosen, EDGE, 1)
                    decay_ref[count * 8 :, :] = jnp.where((lane >= EDGE) & (lane < 2 * EDGE), last, 0.0)
                else:
                    decay_ref[:8, :] = jnp.where(lane < EDGE, chosen, 0.0)

        number += depth_tiles + 1
        for span in range(spans):
            upper = part_ref[tile(number)].astype(F32)
            lower = part_ref[tile(number + 1)].astype(F32)
            number += 2
            span_ref[block * spans + span] = upper[:8] + upper[8:] + lower[:8]
    for span in range(count):
        moved = pltpu.roll(span_ref[span], EDGE, 1)
        here, after = slice(span * 8, span * 8 + 8), slice(span * 8 + 8, span * 8 + 16)
        decay_ref[here, :] = jnp.where(lane < EDGE, decay_ref[here, :], moved)
        kept = decay_ref[after, :] if span == count - 1 else jnp.zeros((8, LANES), F32)
        decay_ref[after, :] = jnp.where(lane < EDGE, moved, kept)
    for number, half_ref in enumerate(half_refs):
        swap_ref[number * half : (number + 1) * half, :] = half_ref[:half, : swap_ref.shape[1]]
    for number in range(bc_ref.shape[0] // height):
        lanes = slice(number * LANES, (number + 1) * LANES)
        swap_ref[top:, lanes] = bc_ref[number * height : (number + 1) * height, :]


def lanes_of(rows, width, head_size):
    high = rows.astype(BF16).astype(F32)
    owner = lax.broadcasted_iota(jnp.int32, (16, width), 1) // head_size
    chosen = jnp.where((lax.broadcasted_iota(jnp.int32, (16, width), 0) & 7) == owner, 1.0, 0.0).astype(BF16)
    return dot(jnp.concatenate([high, rows - high], axis=0).astype(BF16), chosen, ((0,), (0,)))


def spans_in_lanes(rows):
    return jnp.concatenate([rows[at : at + 8] for at in range(0, rows.shape[0], 8)], axis=1)


def row_blocks(total, wide):
    return [slice(at, at + 256) for at in range(0, total, 256)] + [slice(total, wide)]


def state_kernel(group, heads, state, len_ref, decay_ref, x_weight_ref, bc_half_ref, own_ref, swap_ref, halo_ref, *refs):
    half_refs, refs = refs[: group - 1], refs[group - 1 :]
    frames_ref, x_ref, b_ref, c_ref, rows_ref, step_ref, keep_ref, send_ref, weight_ref, tail_ref = refs
    place, plane = plane_place(group)
    parity = lax.rem(lax.axis_index("head"), 2)
    width = x_ref.shape[1]
    frames = own_ref.shape[0]
    total = frames * group
    half = frames // 2
    head_size = width // heads
    count = total // SPAN
    base = plane * total - EDGE
    wide = total + 2 * EDGE
    frames_ref[:EDGE, :] = halo_ref[:EDGE, :]
    frames_ref[total + EDGE : wide, :] = halo_ref[EDGE:, :]
    frames_ref[wide:, :] = jnp.zeros((frames_ref.shape[0] - wide, frames_ref.shape[1]), BF16)
    frames_ref[pl.ds(pl.multiple_of(EDGE + place * frames, EDGE), frames), :] = own_ref[...]
    for number, half_ref in enumerate(half_refs):
        block = EDGE + (place ^ (number + 1)) * frames
        mine = pl.ds(pl.multiple_of(block + parity * half, EDGE), half)
        other = pl.ds(pl.multiple_of(block + (1 - parity) * half, EDGE), half)
        frames_ref[mine, :] = half_ref[:half, : frames_ref.shape[1]]
        frames_ref[other, :] = swap_ref[number * half : (number + 1) * half, :]
    mine = pl.ds(pl.multiple_of(parity * LANES, LANES), LANES)
    other = pl.ds(pl.multiple_of((1 - parity) * LANES, LANES), LANES)
    weight_ref[:, mine] = bc_half_ref[...]
    top = len(half_refs) * half
    height = swap_ref.shape[0] - top
    for number in range(weight_ref.shape[0] // height):
        lanes = slice(number * LANES, (number + 1) * LANES)
        weight_ref[number * height : (number + 1) * height, other] = swap_ref[top:, lanes]

    decay = decay_ref[...]
    used = decay.shape[0]
    square = (SPAN, SPAN)
    row, lane = (lax.broadcasted_iota(jnp.int32, square, dim) for dim in (0, 1))
    upper = jnp.where(row <= lane, 1.0, 0.0).astype(F32)
    cumul = dot(decay, upper, precision=lax.Precision.HIGHEST)
    whole = dot(decay, jnp.ones(square, F32), precision=lax.Precision.HIGHEST)
    first = base + lax.broadcasted_iota(jnp.int32, (used, SPAN), 0) // 8 * SPAN
    position = first + lane[:1]
    start = record_starts(len_ref, position)
    start_last = record_starts(len_ref, first + (SPAN - 1))
    carried = jnp.where(start < first, jnp.exp(cumul), 0.0)
    tail = jnp.where(position >= start_last, jnp.exp(whole - cumul), 0.0)
    keep = jnp.where(start_last < first, jnp.exp(whole), 0.0)
    rows_ref[:used, :] = cumul
    rows_ref[used : 2 * used, :] = start.astype(F32)
    rows_ref[2 * used :, :] = carried

    for rows in row_blocks(total, wide):
        x_ref[rows, :] = dot(frames_ref[rows, :], x_weight_ref[...]).astype(BF16)
        product = dot(frames_ref[rows, :], weight_ref[...])
        b_ref[rows, :] = product[:, :state].astype(BF16)
        c_ref[rows, :] = product[:, state:].astype(BF16)
    for ref in (x_ref, b_ref, c_ref):
        ref[wide:, :] = jnp.zeros((ref.shape[0] - wide, ref.shape[1]), BF16)

    tail_ref[...] = lanes_of(spans_in_lanes(tail[: count * 8]), width, head_size)
    by_span = jnp.zeros((8, SPAN), F32)
    for block in range(count):
        by_span = jnp.where(lane[:8] == block, keep[block * 8 : (block + 1) * 8], by_span)
    kept = lanes_of(by_span, width, head_size)[: keep_ref.shape[0]]
    keep_ref[...] = kept
    entry = jnp.zeros((state, width), F32)
    through = jnp.ones((1, width), F32)
    for block in range(count):
        rows = slice(block * SPAN, (block + 1) * SPAN)
        weighed = x_ref[rows, :].astype(F32) * tail_ref[rows, :]
        step = dot(b_ref[rows, :], weighed.astype(BF16), ((0,), (0,)))
        step_ref[block * state : (block + 1) * state, :] = step
        entry = kept[block : block + 1] * entry + step
        through = through * kept[block : block + 1]
    send_ref[:state, :] = entry.astype(BF16)
    send_ref[state:, :] = jnp.broadcast_to(through, (EDGE, width)).astype(BF16)


def inner_kernel(group, heads, x_ref, b_ref, c_ref, rows_ref, y_ref, carry_ref):
    _, plane = plane_place(group)
    total, width = x_ref.shape
    head_size = width // heads
    count = total // SPAN
    base = plane * (total - SPAN) - EDGE
    used = rows_ref.shape[0] // 3
    square = (SPAN, SPAN)
    parts = [rows_ref[: 2 * used, :]]
    if 2 * used % SPAN:
        parts.append(jnp.zeros((SPAN - 2 * used % SPAN, SPAN), F32))
    columns = jnp.concatenate(parts, axis=0).T
    carry_ref[...] = lanes_of(spans_in_lanes(rows_ref[2 * used :, :]), width, head_size)
    row, lane = (lax.broadcasted_iota(jnp.int32, square, dim) for dim in (0, 1))
    lower = row >= lane
    tile_heads = LANES // head_size
    tile_lane = lax.broadcasted_iota(jnp.int32, (1, LANES), 1) // head_size
    masks = [jnp.where(tile_lane == inner, 1.0, 0.0).astype(BF16) for inner in range(tile_heads)]
    for block in range(count):
        rows = slice(block * SPAN, (block + 1) * SPAN)
        at = block * 8
        x = x_ref[rows, :]
        scores = dot(c_ref[rows, :], b_ref[rows, :], ((1,), (1,)))
        here = (base + block * SPAN + lane).astype(F32)
        start_here = jnp.broadcast_to(columns[:, used + at : used + at + 1], square)
        joined = lower & (here >= start_here)
        for tile in range(width // LANES):
            mixes, values = [], []
            for inner in range(tile_heads):
                which = at + tile * tile_heads + inner
                column = jnp.broadcast_to(columns[:, which : which + 1], square)
                gap = jnp.where(joined, column - rows_ref[which : which + 1, :], -1e30)
                mixes.append((jnp.exp(gap) * scores).astype(BF16))
                values.append(x[:, tile * LANES : (tile + 1) * LANES] * masks[inner])
            y_ref[rows, tile * LANES : (tile + 1) * LANES] = dot(
                jnp.concatenate(mixes, axis=1), jnp.concatenate(values, axis=0)
            )


def silu_kernel(group, gain_ref, frames_ref, weight_ref, out_ref):
    place, _ = plane_place(group)
    rows_all, width = out_ref.shape
    total = rows_all - SPAN
    wide = total + 2 * EDGE
    gain = gain_ref[:, pl.ds(pl.multiple_of(place * width, LANES), width)]
    for rows in row_blocks(total, wide):
        z = dot(frames_ref[rows, :], weight_ref[...]).astype(BF16).astype(F32)
        out_ref[rows, :] = z / (1.0 + jnp.exp(-z)) * gain
    out_ref[wide:, :] = jnp.zeros((rows_all - wide, width), F32)


def share_kernel(cores, offsets, group, *refs):
    pieces, refs = refs[: len(offsets)], refs[len(offsets) :]
    outs, weight_ref = refs[:cores], refs[cores]
    _, plane = plane_place(group)
    core = lax.axis_index("head")
    fill_planes(plane, weight_ref, pieces, offsets)
    for step, out_ref in enumerate(outs):
        rows = out_ref.shape[0]
        out_ref[...] = weight_ref[pl.ds(pl.multiple_of((core ^ step) * rows, rows), rows), :]


def gate_kernel(heads, state, c_ref, y_ref, step_ref, carry_ref, keep_ref, silu_ref, *refs):
    earlier, gated_ref = refs[:-1], refs[-1]
    total, width = y_ref.shape
    head_size = width // heads
    count = total // SPAN
    entry = jnp.zeros((state, width), F32)
    for summary in reversed(earlier):
        through = summary[state : state + EDGE, :].astype(F32)[:1]
        entry = through * entry + summary[:state, :].astype(F32)
    owner = [lax.broadcasted_iota(jnp.int32, (width, width), dim) // head_size for dim in (0, 1)]
    average = jnp.where(owner[0] == owner[1], 1.0 / head_size, 0.0).astype(BF16)
    for block in range(count):
        rows = slice(block * SPAN, (block + 1) * SPAN)
        y = y_ref[rows, :] + carry_ref[rows, :] * dot(c_ref[rows, :], entry.astype(BF16))
        square_mean = dot((y * y).astype(BF16), average)
        gated_ref[rows, :] = (y * lax.rsqrt(square_mean + 1e-05) * silu_ref[rows, :]).astype(BF16)
        if block < count - 1:
            entry = keep_ref[block : block + 1, :] * entry + step_ref[block * state : (block + 1) * state, :]


def conv_kernel(group, steps, len_ref, taps_ref, gated_ref, act_ref, ext_ref, spread_ref, ends_ref):
    place, plane = plane_place(group)
    rows_all, width = gated_ref.shape
    total = rows_all - SPAN
    frames = total // group
    taps = taps_ref.shape[0]
    half = (taps - 1) // 2
    stream = lax.axis_size("tm") // group * total
    records = len_ref.shape[0]
    reach = CONV_ROWS + 2 * EDGE
    first_tap = EDGE - half
    pitch = frames + 2 * EDGE
    ours = taps_ref[:, pl.ds(pl.multiple_of(place * width, LANES), width)]
    for tap in range(taps):
        spread_ref[tap * 8 : (tap + 1) * 8, :] = jnp.broadcast_to(ours[tap : tap + 1, :], (8, width))
    ends_ref[0] = 0
    for record in range(records):
        ends_ref[record + 1] = ends_ref[record] + len_ref[record]
    for number, step in enumerate(steps):
        first = pl.multiple_of((place ^ step) * frames, frames)
        ext_ref[number * pitch : (number + 1) * pitch, :] = gated_ref[pl.ds(first, pitch), :].astype(F32)

    def record_at(position):
        found = jnp.int32(0)
        for record in range(records - 1):
            found = found + (ends_ref[record + 1] <= position).astype(jnp.int32)
        return found

    for number, step in enumerate(steps):
        base = plane * total + (place ^ step) * frames

        def one_block(block, _, number=number, base=base):
            inside_part = pl.multiple_of(block * CONV_ROWS, CONV_ROWS)
            source = pl.multiple_of(number * pitch + inside_part, EDGE)
            target = pl.multiple_of(number * frames + inside_part, CONV_ROWS)
            at = base + inside_part
            low = record_at(jnp.maximum(at - half, 0))
            high = record_at(jnp.minimum(at + CONV_ROWS - 1 + half, stream - 1))
            near = lax.broadcasted_iota(jnp.int32, (reach, LANES), 0) + (at - EDGE)
            for tile in range(width // LANES):
                lanes = slice(tile * LANES, (tile + 1) * LANES)
                def one_record(record, done):
                    inside = (near >= ends_ref[record]) & (near < ends_ref[record + 1])
                    g = jnp.where(inside, ext_ref[pl.ds(source, reach), lanes], 0.0).reshape(reach // 8, 8, LANES)
                    out = None
                    for phase in range(8):
                        part = None
                        for offset in range(phase, reach - CONV_ROWS, 8):
                            tap = offset - first_tap
                            if 0 <= tap < taps:
                                first = (offset - phase) // 8
                                weight = spread_ref[tap * 8 : (tap + 1) * 8, lanes]
                                term = weight[None] * g[first : first + CONV_ROWS // 8 + 1]
                                part = term if part is None else part + term
                        if part is not None:
                            moved = part.reshape(CONV_ROWS + 8, LANES)[phase : phase + CONV_ROWS, :]
                            out = moved if out is None else out + moved
                    return jnp.where(inside[EDGE : EDGE + CONV_ROWS], out, done)

                conv = lax.fori_loop(low, high + 1, one_record, jnp.zeros((CONV_ROWS, LANES), F32))
                act_ref[pl.ds(target, CONV_ROWS), lanes] = (conv / (1.0 + jnp.exp(-conv))).astype(BF16)
            return 0

        lax.fori_loop(0, frames // CONV_ROWS, one_block, 0)


def sum_kernel(own_ref, *refs):
    total = own_ref[...]
    for part in refs[:-1]:
        total = total + part[...].astype(F32)
    refs[-1][...] = total.astype(refs[-1].dtype)


def out_kernel(cores, *refs):
    acts, weights, outs = refs[:cores], refs[cores : 2 * cores], refs[2 * cores :]
    frames = outs[0].shape[0]
    for number, out_ref in enumerate(outs):
        rows = slice(number * frames, (number + 1) * frames)
        total = None
        for act, weight in zip(acts, weights):
            product = dot(act[rows, :], weight[...], ((1,), (1,)))
            total = product if total is None else total + product
        out_ref[...] = total.astype(out_ref.dtype)


def local(
    frames,
    x_weight,
    z_weight,
    bc_weight,
    log_decay,
    norm_gain,
    conv_weight,
    out_weight,
    record_lengths,
):
    times, cores = lax.axis_size("tm"), lax.axis_size("head")
    frame_count, depth = frames.shape
    heads_here, channels = log_decay.shape[0], x_weight.shape[1]
    state = bc_weight.shape[1] // 2
    group = 4
    while group > 1 and (channels // group % LANES or times % group or heads_here % group):
        group //= 2
    planes = times // group
    width, heads = channels // group, heads_here // group
    total = frame_count * group
    count = total // SPAN
    index, core = lax.axis_index("tm"), lax.axis_index("head")
    place = lax.rem(index, group)

    def in_plane(array, step):
        return lax.ppermute(array, "tm", [(i, i ^ step) for i in range(times)])

    def later(array, step):
        return lax.ppermute(array, "tm", [(i, i + step * group) for i in range(times - step * group)])

    def across(array, step):
        return lax.ppermute(array, "head", [(i, i ^ step) for i in range(cores)])

    def between_planes(array, step):
        return lax.ppermute(array, "tm", [(i, i ^ (step * group)) for i in range(times)])

    shape = jax.ShapeDtypeStruct
    rows = x_weight.shape[0]
    parity = lax.rem(core, 2)

    def along_planes(stacks):
        if planes != 4:
            return [stacks[0]] + [between_planes(stacks[step], step) for step in range(1, planes)]

        def pairs(chosen):
            return [(a * group + q, b * group + q) for a, b in chosen for q in range(group)]

        second = between_planes(stacks[2], 2)
        first = between_planes(stacks[1], 1)
        again, last, first = lax.optimization_barrier((second, stacks[3], first))
        third = lax.ppermute(again, "tm", pairs([(1, 0), (2, 3)]))
        middle = lax.ppermute(last, "tm", pairs([(1, 2), (2, 1)]))
        return [stacks[0], first, second, third, middle]

    offsets = (0, 1, 2, 3, 3) if planes == 4 else tuple(range(planes))
    half_count = frame_count // 2
    down, depth_tiles = rows // 16, depth // LANES
    payloads = call(
        functools.partial(first_kernel, group, planes),
        (
            *(shape((rows, 3 * width), BF16) for _ in range(group)),
            *(shape((-(-(down + depth_tiles + 1) // 8) * 16, depth), BF16) for _ in range(planes)),
        ),
        [log_decay, bc_weight, frames, x_weight, z_weight, out_weight.T],
        [
            pltpu.VMEM((rows, LANES), BF16),
            pltpu.VMEM((2, EDGE, depth), BF16),
            pltpu.VMEM(log_decay.shape, F32),
            pltpu.SemaphoreType.DMA((4 + 3 * group,)),
        ],
        smem=0,
        anywhere=6,
        vmem=ALL_VMEM_BYTES,
    )
    inner, outer = payloads[:group], payloads[group:]
    parts = [inner[0]] + [in_plane(inner[step], step) for step in range(1, group)]
    pieces = [outer[0]] + [between_planes(outer[step], step) for step in range(1, planes)]
    xz_stack, out_stack = call(
        functools.partial(stack_kernel, group),
        (shape((group * rows, 2 * width), BF16), shape((group * rows, width), BF16)),
        parts,
        flops=STACK_HINT,
        smem=0,
    )
    xz_pieces = along_planes([xz_stack] * planes)
    xz_pieces, out_stack = lax.optimization_barrier((xz_pieces, out_stack))
    out_pieces = [out_stack] + [between_planes(out_stack, step) for step in range(1, planes)]
    x_columns, z_columns = call(
        functools.partial(assemble_kernel, group, offsets),
        (shape((depth, width), BF16), shape((depth, width), BF16)),
        xz_pieces,
        flops=ASSEMBLE_HINT,
        smem=0,
    )
    decay_blocks = jnp.pad(log_decay.reshape(group, heads, frame_count), ((0, 0), (0, 8 - heads), (0, 0)))
    tiles = planes * down + depth_tiles + 1 + frame_count // SPAN * 2
    inward = call(
        functools.partial(inward_kernel, group, rows),
        tuple(shape((half_count + -(-tiles // 8) * 16, depth), BF16) for _ in range(group)),
        [decay_blocks, frames, *pieces],
        flops=INWARD_HINT,
        smem=0,
    )
    inward = [inward[0]] + [in_plane(inward[step], step) for step in range(1, group)]
    swap, bc_mine, halo, decay = call(
        functools.partial(swap_kernel, group, rows),
        (
            shape(((group - 1) * half_count + LANES, depth), BF16),
            shape((depth, LANES), BF16),
            shape((2 * EDGE, depth), BF16),
            shape((count * 8 + 8, SPAN), F32),
        ),
        inward,
        [pltpu.VMEM((count, 8, SPAN), F32)],
        smem=0,
    )
    swap = across(swap, 1)
    all_rows = total + SPAN

    frame_rows, x_rows, b_rows, c_rows, decay_rows, steps, keep, summary = call(
        functools.partial(state_kernel, group, heads, state),
        (
            shape((all_rows, depth), BF16),
            shape((all_rows, width), BF16),
            shape((all_rows, state), BF16),
            shape((all_rows, state), BF16),
            shape((3 * (count + 1) * 8, SPAN), F32),
            shape((count * state, width), F32),
            shape((-(-count // 8) * 8, width), F32),
            shape((state + EDGE, width), BF16),
        ),
        [record_lengths, decay, x_columns, bc_mine, frames, swap, halo, *inward[1:]],
        [pltpu.VMEM((depth, 2 * state), BF16), pltpu.VMEM((total, width), F32)],
        hidden=True,
    )
    summaries = [later(summary, step) for step in range(1, planes)]
    x_rows, out_pieces = lax.optimization_barrier((x_rows, out_pieces))
    y, carry = call(
        functools.partial(inner_kernel, group, heads),
        (shape((all_rows, width), F32), shape((all_rows, width), F32)),
        [x_rows, b_rows, c_rows, decay_rows],
        flops=4 * total * SPAN * width,
        smem=0,
    )
    silu = call(
        functools.partial(silu_kernel, group),
        shape((all_rows, width), F32),
        [norm_gain[None], frame_rows, z_columns],
        flops=2 * total * depth * width,
        smem=0,
    )
    gated = call(
        functools.partial(gate_kernel, heads, state),
        shape((all_rows, width), BF16),
        [c_rows, y, steps, carry, keep, silu, *summaries],
        flops=2 * total * state * width,
        smem=0,
    )
    ends = pltpu.SMEM((record_lengths.shape[0] + 1,), jnp.int32)
    far, near = (group - 1,), tuple(range(1, group - 1))

    def conv(steps, gated):
        return call(
            functools.partial(conv_kernel, group, steps),
            shape((len(steps) * frame_count, width), BF16),
            [record_lengths, conv_weight, gated],
            [
                pltpu.VMEM((len(steps) * (frame_count + 2 * EDGE), width), F32),
                pltpu.VMEM((conv_weight.shape[0] * 8, width), F32),
                ends,
            ],
            flops=2 * len(steps) * frame_count * width * conv_weight.shape[0],
        )

    def out(steps, act, swapped):
        return call(
            functools.partial(out_kernel, cores),
            tuple(shape((frame_count, share), BF16 if step else F32) for step in steps),
            [act, *swapped, *out_parts],
            flops=2 * len(steps) * frame_count * width * cores * share,
            smem=0,
        )

    share = depth // cores
    out_parts = call(
        functools.partial(share_kernel, cores, tuple(range(planes)), group),
        tuple(shape((share, width), BF16) for _ in range(cores)),
        out_pieces,
        [pltpu.VMEM((depth, width), BF16)],
        smem=0,
    )
    out_parts, gated = lax.optimization_barrier((out_parts, gated))
    out_parts = [out_parts[0]] + [across(out_parts[step], step) for step in range(1, cores)]
    far_act = conv(far, gated)
    far_swapped = [across(far_act, step) for step in range(1, cores)]
    gated, far_act = lax.optimization_barrier((gated, far_act))
    if near:
        near_act = conv(near, gated)
        near_act, far_swapped, out_parts = lax.optimization_barrier((near_act, far_swapped, out_parts))
    (far_out,) = out(far, far_act, far_swapped)
    if near:
        near_act, far_out = lax.optimization_barrier((near_act, far_out))
    sent = [in_plane(far_out, far[0])]
    if near:
        near_swapped = [across(near_act, step) for step in range(1, cores)]
        near_outs = out(near, near_act, near_swapped)
        gated, near_outs = lax.optimization_barrier((gated, near_outs))
        sent += [in_plane(part, step) for part, step in zip(near_outs, near)]
    own_act = conv((0,), gated)
    own_swapped = [across(own_act, step) for step in range(1, cores)]
    (own_out,) = out((0,), own_act, own_swapped)
    return call(sum_kernel, shape((frame_count, share), BF16), [own_out, *sent], smem=0)


def solution(mesh):
    in_specs = (
        P("tm", None),
        P("tm", "head"),
        P("tm", "head"),
        P("tm", None),
        P("head", "tm"),
        P("head"),
        P(None, "head"),
        P("head", "tm"),
        P(),
    )
    out_specs = P("tm", "head")
    return jax.shard_map(local, mesh=mesh, in_specs=in_specs, out_specs=out_specs, check_vma=False)
```

```python
import functools

import jax
import jax.numpy as jnp
from jax import lax
from jax.experimental import pallas as pl
from jax.experimental.pallas import tpu as pltpu
from jax.sharding import PartitionSpec as P

SPAN = 128
LANES = 128
EDGE = 16
CONV_ROWS = 128
BF16 = jnp.bfloat16
F32 = jnp.float32
STACK_HINT = 40_000_000_000
INWARD_HINT = 40_000_000_000
ASSEMBLE_HINT = 40_000_000_000
ALL_VMEM_BYTES = 63 * 1024 * 1024
VMEM_BYTES = 20 * 1024 * 1024


def dot(a, b, dims=((1,), (0,)), precision=None):
    return lax.dot_general(a, b, (dims, ((), ())), precision=precision, preferred_element_type=F32)


def call(kernel, out_shape, operands, scratch=(), flops=0, smem=1, anywhere=0, vmem=VMEM_BYTES, hidden=False):
    in_specs = [pl.BlockSpec(memory_space=pltpu.SMEM)] * smem
    in_specs += [pl.BlockSpec(memory_space=pltpu.VMEM)] * (len(operands) - smem - anywhere)
    in_specs += [pl.BlockSpec(memory_space=pl.ANY)] * anywhere
    moved = sum(a.size * a.dtype.itemsize for a in operands)
    moved += sum(a.size * a.dtype.itemsize for a in jax.tree.leaves(out_shape))
    if hidden:
        flops = moved = 0
    return pl.pallas_call(
        kernel,
        out_shape=out_shape,
        in_specs=in_specs,
        out_specs=jax.tree.map(lambda _: pl.BlockSpec(memory_space=pltpu.VMEM), out_shape),
        scratch_shapes=list(scratch),
        compiler_params=pltpu.CompilerParams(vmem_limit_bytes=vmem),
        cost_estimate=pl.CostEstimate(flops=flops, bytes_accessed=moved, transcendentals=0),
    )(*operands)


def plane_place(group):
    index = lax.axis_index("tm")
    return lax.rem(index, group), lax.div(index, group)


def record_starts(len_ref, position):
    start = jnp.zeros_like(position)
    end = jnp.int32(0)
    for record in range(len_ref.shape[0] - 1):
        end = end + len_ref[record]
        start = jnp.where(position >= end, end, start)
    return start


def fill_planes(plane, dest_ref, pieces, offsets, lanes=slice(None)):
    rows = pieces[0].shape[0]
    for offset in sorted(set(offsets)):
        same = [piece[:, lanes] for piece, at in zip(pieces, offsets) if at == offset]
        value = same[0] if len(same) == 1 else same[0] + same[1]
        dest_ref[pl.ds(pl.multiple_of((plane ^ offset) * rows, rows), rows), : value.shape[1]] = value


def first_kernel(group, planes, log_decay_ref, bc_ref, frames_ref, *refs):
    weight_refs, refs = refs[:3], refs[3:]
    inner_refs, outer_refs, refs = refs[:group], refs[group : group + planes], refs[group + planes :]
    bc_half_ref, edge_ref, decay_ref, sems = refs
    place, plane = plane_place(group)
    parity = lax.rem(lax.axis_index("head"), 2)
    width = weight_refs[0].shape[1] // group
    frames = frames_ref.shape[0]
    heads = log_decay_ref.shape[0] // group
    copies = [
        (bc_ref.at[:, pl.ds(pl.multiple_of(parity * LANES, LANES), LANES)], bc_half_ref),
        (frames_ref.at[:EDGE, :], edge_ref.at[0]),
        (frames_ref.at[frames - EDGE :, :], edge_ref.at[1]),
        (log_decay_ref, decay_ref),
    ]
    for step, inner_ref in enumerate(inner_refs):
        lanes = pl.ds(pl.multiple_of((place ^ step) * width, LANES), width)
        for number, weight_ref in enumerate(weight_refs):
            copies.append((weight_ref.at[:, lanes], inner_ref.at[:, number * width : (number + 1) * width]))
    started = [pltpu.make_async_copy(a, b, sems.at[number]) for number, (a, b) in enumerate(copies)]
    for copy in started:
        copy.start()
    for copy in started[:4]:
        copy.wait()
    lane = lax.broadcasted_iota(jnp.int32, (8, LANES), 1)
    decays = []
    for first in (0, frames - LANES):
        rows = [jnp.zeros((8, LANES), F32), jnp.zeros((8, LANES), F32)]
        for block in range(group):
            here = decay_ref[block * heads : (block + 1) * heads, first : first + LANES]
            here = jnp.concatenate([here, jnp.zeros((8 - heads, LANES), F32)], axis=0)
            for number, term in enumerate(three_terms(here)):
                slot = number * group + block
                moved = pltpu.roll(term, (slot % 8 * EDGE + (EDGE if first else 0)) % LANES, 1)
                rows[slot // 8] = jnp.where(lane // EDGE == slot % 8, moved, rows[slot // 8])
        decays.append(jnp.concatenate(rows, axis=0))
    for step, out_ref in enumerate(outer_refs):
        number = put(out_ref, 0, bc_half_ref[...])
        later = (plane ^ step) > plane
        number = put(out_ref, number, jnp.where(later, edge_ref[1].astype(F32), edge_ref[0].astype(F32)).astype(BF16))
        put(out_ref, number, jnp.where(later, decays[1], decays[0]).astype(BF16))
    for copy in started[4:]:
        copy.wait()


def stack_kernel(group, *refs):
    parts, stack_refs = refs[:group], refs[group:]
    place, _ = plane_place(group)
    rows = parts[0].shape[0]
    for step, part in enumerate(parts):
        at = pl.ds(pl.multiple_of((place ^ step) * rows, rows), rows)
        first = 0
        for stack_ref in stack_refs:
            width = stack_ref.shape[1]
            stack_ref[at, :] = part[:, first : first + width]
            first += width


def assemble_kernel(group, offsets, *refs):
    pieces, dest_refs = refs[: len(offsets)], refs[len(offsets) :]
    _, plane = plane_place(group)
    first = 0
    for dest_ref in dest_refs:
        width = dest_ref.shape[1]
        fill_planes(plane, dest_ref, pieces, offsets, slice(first, first + width))
        first += width


def tile(number):
    return slice(number // 8 * 16, number // 8 * 16 + 16), slice(number % 8 * LANES, (number % 8 + 1) * LANES)


def put(out_ref, number, array):
    for at in range(0, array.shape[0], 16):
        for lane in range(0, array.shape[1], LANES):
            out_ref[tile(number)] = array[at : at + 16, lane : lane + LANES]
            number += 1
    return number


def three_terms(value):
    terms = []
    for _ in range(3):
        term = value.astype(BF16).astype(F32)
        terms.append(term)
        value = value - term
    return terms


def inward_kernel(group, rows, decay_ref, frames_ref, *refs):
    piece_refs, out_refs = refs[:-group], refs[-group:]
    place, plane = plane_place(group)
    planes = len(piece_refs)
    half = frames_ref.shape[0] // 2
    mine = pl.ds(pl.multiple_of(lax.rem(lax.axis_index("head"), 2) * half, half), half)
    wanted = jnp.clip(jnp.where(place == 0, plane + 1, plane - 1), 0, planes - 1)
    depth_tiles = frames_ref.shape[1] // LANES
    down = rows // 16
    for step, out_ref in enumerate(out_refs):
        out_ref[:half, :] = frames_ref[mine, :]
        number = half // 16 * depth_tiles
        for piece_ref in piece_refs:
            for at in range(down):
                out_ref[tile(number)] = piece_ref[tile(at)]
                number += 1
        for offset, piece_ref in enumerate(piece_refs):

            @pl.when((plane ^ offset) == wanted)
            def _(piece_ref=piece_ref, number=number, out_ref=out_ref):
                for at in range(depth_tiles + 1):
                    out_ref[tile(number + at)] = piece_ref[tile(down + at)]

        number += depth_tiles + 1
        terms = three_terms(decay_ref[place ^ step])
        terms = jnp.concatenate([*terms, jnp.zeros_like(terms[0])], axis=0).astype(BF16)
        for span in range(terms.shape[1] // SPAN):
            number = put(out_ref, number, terms[:, span * SPAN : (span + 1) * SPAN])


def swap_kernel(group, rows, *refs):
    part_refs, (swap_ref, bc_ref, halo_ref, decay_ref, span_ref) = refs[:group], refs[group:]
    half_refs = part_refs[1:]
    place, plane = plane_place(group)
    planes = bc_ref.shape[0] // (group * rows)
    count = span_ref.shape[0]
    spans = count // group
    down = rows // 16
    depth_tiles = swap_ref.shape[1] // LANES
    height = LANES
    top = swap_ref.shape[0] - height
    half = top // len(half_refs)
    lane = lax.broadcasted_iota(jnp.int32, (8, LANES), 1)
    for step, part_ref in enumerate(part_refs):
        block = place ^ step
        number = half // 16 * depth_tiles
        for offset in range(planes):
            first = ((plane ^ offset) * group + block) * rows
            for at in range(down):
                bc_ref[pl.ds(pl.multiple_of(first + at * 16, 16), 16), :] = part_ref[tile(number)]
                number += 1
        for side, owner in enumerate((group - 1, 0)):

            @pl.when(block == owner)
            def _(part_ref=part_ref, number=number, side=side):
                for at in range(depth_tiles):
                    halo_ref[side * EDGE : (side + 1) * EDGE, at * LANES : (at + 1) * LANES] = part_ref[tile(number + at)]
                packed = part_ref[tile(number + depth_tiles)].astype(F32)
                chosen = jnp.zeros((8, LANES), F32)
                for head_block in range(group):
                    value = jnp.zeros((8, LANES), F32)
                    for term in range(3):
                        slot = term * group + head_block
                        half = packed[slot // 8 * 8 : slot // 8 * 8 + 8]
                        value = value + pltpu.roll(half, (LANES - slot % 8 * EDGE) % LANES, 1)
                    chosen = jnp.where(place == head_block, value, chosen)
                if side:
                    last = pltpu.roll(chosen, EDGE, 1)
                    decay_ref[count * 8 :, :] = jnp.where((lane >= EDGE) & (lane < 2 * EDGE), last, 0.0)
                else:
                    decay_ref[:8, :] = jnp.where(lane < EDGE, chosen, 0.0)

        number += depth_tiles + 1
        for span in range(spans):
            upper = part_ref[tile(number)].astype(F32)
            lower = part_ref[tile(number + 1)].astype(F32)
            number += 2
            span_ref[block * spans + span] = upper[:8] + upper[8:] + lower[:8]
    for span in range(count):
        moved = pltpu.roll(span_ref[span], EDGE, 1)
        here, after = slice(span * 8, span * 8 + 8), slice(span * 8 + 8, span * 8 + 16)
        decay_ref[here, :] = jnp.where(lane < EDGE, decay_ref[here, :], moved)
        kept = decay_ref[after, :] if span == count - 1 else jnp.zeros((8, LANES), F32)
        decay_ref[after, :] = jnp.where(lane < EDGE, moved, kept)
    for number, half_ref in enumerate(half_refs):
        swap_ref[number * half : (number + 1) * half, :] = half_ref[:half, : swap_ref.shape[1]]
    for number in range(bc_ref.shape[0] // height):
        lanes = slice(number * LANES, (number + 1) * LANES)
        swap_ref[top:, lanes] = bc_ref[number * height : (number + 1) * height, :]


def lanes_of(rows, width, head_size):
    high = rows.astype(BF16).astype(F32)
    owner = lax.broadcasted_iota(jnp.int32, (16, width), 1) // head_size
    chosen = jnp.where((lax.broadcasted_iota(jnp.int32, (16, width), 0) & 7) == owner, 1.0, 0.0).astype(BF16)
    return dot(jnp.concatenate([high, rows - high], axis=0).astype(BF16), chosen, ((0,), (0,)))


def spans_in_lanes(rows):
    return jnp.concatenate([rows[at : at + 8] for at in range(0, rows.shape[0], 8)], axis=1)


def row_blocks(total, wide):
    return [slice(at, at + 256) for at in range(0, total, 256)] + [slice(total, wide)]


def state_kernel(group, heads, state, len_ref, decay_ref, x_weight_ref, bc_half_ref, own_ref, swap_ref, halo_ref, *refs):
    half_refs, refs = refs[: group - 1], refs[group - 1 :]
    frames_ref, x_ref, b_ref, c_ref, rows_ref, step_ref, keep_ref, send_ref, weight_ref, tail_ref = refs
    place, plane = plane_place(group)
    parity = lax.rem(lax.axis_index("head"), 2)
    width = x_ref.shape[1]
    frames = own_ref.shape[0]
    total = frames * group
    half = frames // 2
    head_size = width // heads
    count = total // SPAN
    base = plane * total - EDGE
    wide = total + 2 * EDGE
    frames_ref[:EDGE, :] = halo_ref[:EDGE, :]
    frames_ref[total + EDGE : wide, :] = halo_ref[EDGE:, :]
    frames_ref[wide:, :] = jnp.zeros((frames_ref.shape[0] - wide, frames_ref.shape[1]), BF16)
    frames_ref[pl.ds(pl.multiple_of(EDGE + place * frames, EDGE), frames), :] = own_ref[...]
    for number, half_ref in enumerate(half_refs):
        block = EDGE + (place ^ (number + 1)) * frames
        mine = pl.ds(pl.multiple_of(block + parity * half, EDGE), half)
        other = pl.ds(pl.multiple_of(block + (1 - parity) * half, EDGE), half)
        frames_ref[mine, :] = half_ref[:half, : frames_ref.shape[1]]
        frames_ref[other, :] = swap_ref[number * half : (number + 1) * half, :]
    mine = pl.ds(pl.multiple_of(parity * LANES, LANES), LANES)
    other = pl.ds(pl.multiple_of((1 - parity) * LANES, LANES), LANES)
    weight_ref[:, mine] = bc_half_ref[...]
    top = len(half_refs) * half
    height = swap_ref.shape[0] - top
    for number in range(weight_ref.shape[0] // height):
        lanes = slice(number * LANES, (number + 1) * LANES)
        weight_ref[number * height : (number + 1) * height, other] = swap_ref[top:, lanes]

    decay = decay_ref[...]
    used = decay.shape[0]
    square = (SPAN, SPAN)
    row, lane = (lax.broadcasted_iota(jnp.int32, square, dim) for dim in (0, 1))
    upper = jnp.where(row <= lane, 1.0, 0.0).astype(F32)
    cumul = dot(decay, upper, precision=lax.Precision.HIGHEST)
    whole = dot(decay, jnp.ones(square, F32), precision=lax.Precision.HIGHEST)
    first = base + lax.broadcasted_iota(jnp.int32, (used, SPAN), 0) // 8 * SPAN
    position = first + lane[:1]
    start = record_starts(len_ref, position)
    start_last = record_starts(len_ref, first + (SPAN - 1))
    carried = jnp.where(start < first, jnp.exp(cumul), 0.0)
    tail = jnp.where(position >= start_last, jnp.exp(whole - cumul), 0.0)
    keep = jnp.where(start_last < first, jnp.exp(whole), 0.0)
    rows_ref[:used, :] = cumul
    rows_ref[used : 2 * used, :] = start.astype(F32)
    rows_ref[2 * used :, :] = carried

    for rows in row_blocks(total, wide):
        x_ref[rows, :] = dot(frames_ref[rows, :], x_weight_ref[...]).astype(BF16)
        product = dot(frames_ref[rows, :], weight_ref[...])
        b_ref[rows, :] = product[:, :state].astype(BF16)
        c_ref[rows, :] = product[:, state:].astype(BF16)
    for ref in (x_ref, b_ref, c_ref):
        ref[wide:, :] = jnp.zeros((ref.shape[0] - wide, ref.shape[1]), BF16)

    tail_ref[...] = lanes_of(spans_in_lanes(tail[: count * 8]), width, head_size)
    by_span = jnp.zeros((8, SPAN), F32)
    for block in range(count):
        by_span = jnp.where(lane[:8] == block, keep[block * 8 : (block + 1) * 8], by_span)
    kept = lanes_of(by_span, width, head_size)[: keep_ref.shape[0]]
    keep_ref[...] = kept
    entry = jnp.zeros((state, width), F32)
    through = jnp.ones((1, width), F32)
    for block in range(count):
        rows = slice(block * SPAN, (block + 1) * SPAN)
        weighed = x_ref[rows, :].astype(F32) * tail_ref[rows, :]
        step = dot(b_ref[rows, :], weighed.astype(BF16), ((0,), (0,)))
        step_ref[block * state : (block + 1) * state, :] = step
        entry = kept[block : block + 1] * entry + step
        through = through * kept[block : block + 1]
    send_ref[:state, :] = entry.astype(BF16)
    send_ref[state:, :] = jnp.broadcast_to(through, (EDGE, width)).astype(BF16)


def inner_kernel(group, heads, x_ref, b_ref, c_ref, rows_ref, y_ref, carry_ref):
    _, plane = plane_place(group)
    total, width = x_ref.shape
    head_size = width // heads
    count = total // SPAN
    base = plane * (total - SPAN) - EDGE
    used = rows_ref.shape[0] // 3
    square = (SPAN, SPAN)
    parts = [rows_ref[: 2 * used, :]]
    if 2 * used % SPAN:
        parts.append(jnp.zeros((SPAN - 2 * used % SPAN, SPAN), F32))
    columns = jnp.concatenate(parts, axis=0).T
    carry_ref[...] = lanes_of(spans_in_lanes(rows_ref[2 * used :, :]), width, head_size)
    row, lane = (lax.broadcasted_iota(jnp.int32, square, dim) for dim in (0, 1))
    lower = row >= lane
    tile_heads = LANES // head_size
    tile_lane = lax.broadcasted_iota(jnp.int32, (1, LANES), 1) // head_size
    masks = [jnp.where(tile_lane == inner, 1.0, 0.0).astype(BF16) for inner in range(tile_heads)]
    for block in range(count):
        rows = slice(block * SPAN, (block + 1) * SPAN)
        at = block * 8
        x = x_ref[rows, :]
        scores = dot(c_ref[rows, :], b_ref[rows, :], ((1,), (1,)))
        here = (base + block * SPAN + lane).astype(F32)
        start_here = jnp.broadcast_to(columns[:, used + at : used + at + 1], square)
        joined = lower & (here >= start_here)
        for tile in range(width // LANES):
            mixes, values = [], []
            for inner in range(tile_heads):
                which = at + tile * tile_heads + inner
                column = jnp.broadcast_to(columns[:, which : which + 1], square)
                gap = jnp.where(joined, column - rows_ref[which : which + 1, :], -1e30)
                mixes.append((jnp.exp(gap) * scores).astype(BF16))
                values.append(x[:, tile * LANES : (tile + 1) * LANES] * masks[inner])
            y_ref[rows, tile * LANES : (tile + 1) * LANES] = dot(
                jnp.concatenate(mixes, axis=1), jnp.concatenate(values, axis=0)
            )


def silu_kernel(group, gain_ref, frames_ref, weight_ref, out_ref):
    place, _ = plane_place(group)
    rows_all, width = out_ref.shape
    total = rows_all - SPAN
    wide = total + 2 * EDGE
    gain = gain_ref[:, pl.ds(pl.multiple_of(place * width, LANES), width)]
    for rows in row_blocks(total, wide):
        z = dot(frames_ref[rows, :], weight_ref[...]).astype(BF16).astype(F32)
        out_ref[rows, :] = z / (1.0 + jnp.exp(-z)) * gain
    out_ref[wide:, :] = jnp.zeros((rows_all - wide, width), F32)


def share_kernel(cores, offsets, group, *refs):
    pieces, refs = refs[: len(offsets)], refs[len(offsets) :]
    outs, weight_ref = refs[:cores], refs[cores]
    _, plane = plane_place(group)
    core = lax.axis_index("head")
    fill_planes(plane, weight_ref, pieces, offsets)
    for step, out_ref in enumerate(outs):
        rows = out_ref.shape[0]
        out_ref[...] = weight_ref[pl.ds(pl.multiple_of((core ^ step) * rows, rows), rows), :]


def gate_kernel(heads, state, c_ref, y_ref, step_ref, carry_ref, keep_ref, silu_ref, *refs):
    earlier, gated_ref = refs[:-1], refs[-1]
    total, width = y_ref.shape
    head_size = width // heads
    count = total // SPAN
    entry = jnp.zeros((state, width), F32)
    for summary in reversed(earlier):
        through = summary[state : state + EDGE, :].astype(F32)[:1]
        entry = through * entry + summary[:state, :].astype(F32)
    owner = [lax.broadcasted_iota(jnp.int32, (width, width), dim) // head_size for dim in (0, 1)]
    average = jnp.where(owner[0] == owner[1], 1.0 / head_size, 0.0).astype(BF16)
    for block in range(count):
        rows = slice(block * SPAN, (block + 1) * SPAN)
        y = y_ref[rows, :] + carry_ref[rows, :] * dot(c_ref[rows, :], entry.astype(BF16))
        square_mean = dot((y * y).astype(BF16), average)
        gated_ref[rows, :] = (y * lax.rsqrt(square_mean + 1e-05) * silu_ref[rows, :]).astype(BF16)
        if block < count - 1:
            entry = keep_ref[block : block + 1, :] * entry + step_ref[block * state : (block + 1) * state, :]


def conv_kernel(group, steps, len_ref, taps_ref, gated_ref, act_ref, ext_ref, spread_ref, ends_ref):
    place, plane = plane_place(group)
    rows_all, width = gated_ref.shape
    total = rows_all - SPAN
    frames = total // group
    taps = taps_ref.shape[0]
    half = (taps - 1) // 2
    stream = lax.axis_size("tm") // group * total
    records = len_ref.shape[0]
    reach = CONV_ROWS + 2 * EDGE
    first_tap = EDGE - half
    pitch = frames + 2 * EDGE
    ours = taps_ref[:, pl.ds(pl.multiple_of(place * width, LANES), width)]
    for tap in range(taps):
        spread_ref[tap * 8 : (tap + 1) * 8, :] = jnp.broadcast_to(ours[tap : tap + 1, :], (8, width))
    ends_ref[0] = 0
    for record in range(records):
        ends_ref[record + 1] = ends_ref[record] + len_ref[record]
    for number, step in enumerate(steps):
        first = pl.multiple_of((place ^ step) * frames, frames)
        ext_ref[number * pitch : (number + 1) * pitch, :] = gated_ref[pl.ds(first, pitch), :].astype(F32)

    def record_at(position):
        found = jnp.int32(0)
        for record in range(records - 1):
            found = found + (ends_ref[record + 1] <= position).astype(jnp.int32)
        return found

    for number, step in enumerate(steps):
        base = plane * total + (place ^ step) * frames

        def one_block(block, _, number=number, base=base):
            inside_part = pl.multiple_of(block * CONV_ROWS, CONV_ROWS)
            source = pl.multiple_of(number * pitch + inside_part, EDGE)
            target = pl.multiple_of(number * frames + inside_part, CONV_ROWS)
            at = base + inside_part
            low = record_at(jnp.maximum(at - half, 0))
            high = record_at(jnp.minimum(at + CONV_ROWS - 1 + half, stream - 1))
            near = lax.broadcasted_iota(jnp.int32, (reach, LANES), 0) + (at - EDGE)
            for tile in range(width // LANES):
                lanes = slice(tile * LANES, (tile + 1) * LANES)
                def one_record(record, done):
                    inside = (near >= ends_ref[record]) & (near < ends_ref[record + 1])
                    g = jnp.where(inside, ext_ref[pl.ds(source, reach), lanes], 0.0).reshape(reach // 8, 8, LANES)
                    out = None
                    for phase in range(8):
                        part = None
                        for offset in range(phase, reach - CONV_ROWS, 8):
                            tap = offset - first_tap
                            if 0 <= tap < taps:
                                first = (offset - phase) // 8
                                weight = spread_ref[tap * 8 : (tap + 1) * 8, lanes]
                                term = weight[None] * g[first : first + CONV_ROWS // 8 + 1]
                                part = term if part is None else part + term
                        if part is not None:
                            moved = part.reshape(CONV_ROWS + 8, LANES)[phase : phase + CONV_ROWS, :]
                            out = moved if out is None else out + moved
                    return jnp.where(inside[EDGE : EDGE + CONV_ROWS], out, done)

                conv = lax.fori_loop(low, high + 1, one_record, jnp.zeros((CONV_ROWS, LANES), F32))
                act_ref[pl.ds(target, CONV_ROWS), lanes] = (conv / (1.0 + jnp.exp(-conv))).astype(BF16)
            return 0

        lax.fori_loop(0, frames // CONV_ROWS, one_block, 0)


def sum_kernel(own_ref, *refs):
    total = own_ref[...]
    for part in refs[:-1]:
        total = total + part[...].astype(F32)
    refs[-1][...] = total.astype(refs[-1].dtype)


def out_kernel(cores, *refs):
    acts, weights, outs = refs[:cores], refs[cores : 2 * cores], refs[2 * cores :]
    frames = outs[0].shape[0]
    for number, out_ref in enumerate(outs):
        rows = slice(number * frames, (number + 1) * frames)
        total = None
        for act, weight in zip(acts, weights):
            product = dot(act[rows, :], weight[...], ((1,), (1,)))
            total = product if total is None else total + product
        out_ref[...] = total.astype(out_ref.dtype)


def local(
    frames,
    x_weight,
    z_weight,
    bc_weight,
    log_decay,
    norm_gain,
    conv_weight,
    out_weight,
    record_lengths,
):
    times, cores = lax.axis_size("tm"), lax.axis_size("head")
    frame_count, depth = frames.shape
    heads_here, channels = log_decay.shape[0], x_weight.shape[1]
    state = bc_weight.shape[1] // 2
    group = 4
    while group > 1 and (channels // group % LANES or times % group or heads_here % group):
        group //= 2
    planes = times // group
    width, heads = channels // group, heads_here // group
    total = frame_count * group
    count = total // SPAN
    index, core = lax.axis_index("tm"), lax.axis_index("head")
    place = lax.rem(index, group)

    def in_plane(array, step):
        return lax.ppermute(array, "tm", [(i, i ^ step) for i in range(times)])

    def later(array, step):
        return lax.ppermute(array, "tm", [(i, i + step * group) for i in range(times - step * group)])

    def across(array, step):
        return lax.ppermute(array, "head", [(i, i ^ step) for i in range(cores)])

    def between_planes(array, step):
        return lax.ppermute(array, "tm", [(i, i ^ (step * group)) for i in range(times)])

    shape = jax.ShapeDtypeStruct
    rows = x_weight.shape[0]
    parity = lax.rem(core, 2)

    def along_planes(stacks):
        if planes != 4:
            return [stacks[0]] + [between_planes(stacks[step], step) for step in range(1, planes)]

        def pairs(chosen):
            return [(a * group + q, b * group + q) for a, b in chosen for q in range(group)]

        second = between_planes(stacks[2], 2)
        first = between_planes(stacks[1], 1)
        again, last, first = lax.optimization_barrier((second, stacks[3], first))
        third = lax.ppermute(again, "tm", pairs([(1, 0), (2, 3)]))
        middle = lax.ppermute(last, "tm", pairs([(1, 2), (2, 1)]))
        return [stacks[0], first, second, third, middle]

    offsets = (0, 1, 2, 3, 3) if planes == 4 else tuple(range(planes))
    half_count = frame_count // 2
    down, depth_tiles = rows // 16, depth // LANES
    payloads = call(
        functools.partial(first_kernel, group, planes),
        (
            *(shape((rows, 3 * width), BF16) for _ in range(group)),
            *(shape((-(-(down + depth_tiles + 1) // 8) * 16, depth), BF16) for _ in range(planes)),
        ),
        [log_decay, bc_weight, frames, x_weight, z_weight, out_weight.T],
        [
            pltpu.VMEM((rows, LANES), BF16),
            pltpu.VMEM((2, EDGE, depth), BF16),
            pltpu.VMEM(log_decay.shape, F32),
            pltpu.SemaphoreType.DMA((4 + 3 * group,)),
        ],
        smem=0,
        anywhere=6,
        vmem=ALL_VMEM_BYTES,
    )
    inner, outer = payloads[:group], payloads[group:]
    parts = [inner[0]] + [in_plane(inner[step], step) for step in range(1, group)]
    pieces = [outer[0]] + [between_planes(outer[step], step) for step in range(1, planes)]
    xz_stack, out_stack = call(
        functools.partial(stack_kernel, group),
        (shape((group * rows, 2 * width), BF16), shape((group * rows, width), BF16)),
        parts,
        flops=STACK_HINT,
        smem=0,
    )
    xz_pieces = along_planes([xz_stack] * planes)
    xz_pieces, out_stack = lax.optimization_barrier((xz_pieces, out_stack))
    out_pieces = [out_stack] + [between_planes(out_stack, step) for step in range(1, planes)]
    x_columns, z_columns = call(
        functools.partial(assemble_kernel, group, offsets),
        (shape((depth, width), BF16), shape((depth, width), BF16)),
        xz_pieces,
        flops=ASSEMBLE_HINT,
        smem=0,
    )
    decay_blocks = jnp.pad(log_decay.reshape(group, heads, frame_count), ((0, 0), (0, 8 - heads), (0, 0)))
    tiles = planes * down + depth_tiles + 1 + frame_count // SPAN * 2
    inward = call(
        functools.partial(inward_kernel, group, rows),
        tuple(shape((half_count + -(-tiles // 8) * 16, depth), BF16) for _ in range(group)),
        [decay_blocks, frames, *pieces],
        flops=INWARD_HINT,
        smem=0,
    )
    inward = [inward[0]] + [in_plane(inward[step], step) for step in range(1, group)]
    swap, bc_mine, halo, decay = call(
        functools.partial(swap_kernel, group, rows),
        (
            shape(((group - 1) * half_count + LANES, depth), BF16),
            shape((depth, LANES), BF16),
            shape((2 * EDGE, depth), BF16),
            shape((count * 8 + 8, SPAN), F32),
        ),
        inward,
        [pltpu.VMEM((count, 8, SPAN), F32)],
        smem=0,
    )
    swap = across(swap, 1)
    all_rows = total + SPAN

    frame_rows, x_rows, b_rows, c_rows, decay_rows, steps, keep, summary = call(
        functools.partial(state_kernel, group, heads, state),
        (
            shape((all_rows, depth), BF16),
            shape((all_rows, width), BF16),
            shape((all_rows, state), BF16),
            shape((all_rows, state), BF16),
            shape((3 * (count + 1) * 8, SPAN), F32),
            shape((count * state, width), F32),
            shape((-(-count // 8) * 8, width), F32),
            shape((state + EDGE, width), BF16),
        ),
        [record_lengths, decay, x_columns, bc_mine, frames, swap, halo, *inward[1:]],
        [pltpu.VMEM((depth, 2 * state), BF16), pltpu.VMEM((total, width), F32)],
        hidden=True,
    )
    summaries = [later(summary, step) for step in range(1, planes)]
    x_rows, out_pieces = lax.optimization_barrier((x_rows, out_pieces))
    y, carry = call(
        functools.partial(inner_kernel, group, heads),
        (shape((all_rows, width), F32), shape((all_rows, width), F32)),
        [x_rows, b_rows, c_rows, decay_rows],
        flops=4 * total * SPAN * width,
        smem=0,
    )
    silu = call(
        functools.partial(silu_kernel, group),
        shape((all_rows, width), F32),
        [norm_gain[None], frame_rows, z_columns],
        flops=2 * total * depth * width,
        smem=0,
    )
    gated = call(
        functools.partial(gate_kernel, heads, state),
        shape((all_rows, width), BF16),
        [c_rows, y, steps, carry, keep, silu, *summaries],
        flops=2 * total * state * width,
        smem=0,
    )
    ends = pltpu.SMEM((record_lengths.shape[0] + 1,), jnp.int32)
    far, near = (group - 1,), tuple(range(1, group - 1))

    def conv(steps, gated):
        return call(
            functools.partial(conv_kernel, group, steps),
            shape((len(steps) * frame_count, width), BF16),
            [record_lengths, conv_weight, gated],
            [
                pltpu.VMEM((len(steps) * (frame_count + 2 * EDGE), width), F32),
                pltpu.VMEM((conv_weight.shape[0] * 8, width), F32),
                ends,
            ],
            flops=2 * len(steps) * frame_count * width * conv_weight.shape[0],
        )

    def out(steps, act, swapped):
        return call(
            functools.partial(out_kernel, cores),
            tuple(shape((frame_count, share), BF16 if step else F32) for step in steps),
            [act, *swapped, *out_parts],
            flops=2 * len(steps) * frame_count * width * cores * share,
            smem=0,
        )

    share = depth // cores
    out_parts = call(
        functools.partial(share_kernel, cores, tuple(range(planes)), group),
        tuple(shape((share, width), BF16) for _ in range(cores)),
        out_pieces,
        [pltpu.VMEM((depth, width), BF16)],
        smem=0,
    )
    out_parts, gated = lax.optimization_barrier((out_parts, gated))
    out_parts = [out_parts[0]] + [across(out_parts[step], step) for step in range(1, cores)]
    far_act = conv(far, gated)
    far_swapped = [across(far_act, step) for step in range(1, cores)]
    gated, far_act = lax.optimization_barrier((gated, far_act))
    if near:
        near_act = conv(near, gated)
        near_act, far_swapped, out_parts = lax.optimization_barrier((near_act, far_swapped, out_parts))
    (far_out,) = out(far, far_act, far_swapped)
    if near:
        near_act, far_out = lax.optimization_barrier((near_act, far_out))
    sent = [in_plane(far_out, far[0])]
    if near:
        near_swapped = [across(near_act, step) for step in range(1, cores)]
        near_outs = out(near, near_act, near_swapped)
        gated, near_outs = lax.optimization_barrier((gated, near_outs))
        sent += [in_plane(part, step) for part, step in zip(near_outs, near)]
    own_act = conv((0,), gated)
    own_swapped = [across(own_act, step) for step in range(1, cores)]
    (own_out,) = out((0,), own_act, own_swapped)
    return call(sum_kernel, shape((frame_count, share), BF16), [own_out, *sent], smem=0)


def solution(mesh):
    in_specs = (
        P("tm", None),
        P("tm", "head"),
        P("tm", "head"),
        P("tm", None),
        P("head", "tm"),
        P("head"),
        P(None, "head"),
        P("head", "tm"),
        P(),
    )
    out_specs = P("tm", "head")
    return jax.shard_map(local, mesh=mesh, in_specs=in_specs, out_specs=out_specs, check_vma=False)
```

```python
import functools

import jax
import jax.numpy as jnp
from jax import lax
from jax.experimental import pallas as pl
from jax.experimental.pallas import tpu as pltpu
from jax.sharding import PartitionSpec as P

SPAN = 128
LANES = 128
EDGE = 16
CONV_ROWS = 64
BF16 = jnp.bfloat16
F32 = jnp.float32
STACK_HINT = 40_000_000_000
INWARD_HINT = 40_000_000_000
ASSEMBLE_HINT = 40_000_000_000
ALL_VMEM_BYTES = 63 * 1024 * 1024
VMEM_BYTES = 20 * 1024 * 1024


def dot(a, b, dims=((1,), (0,)), precision=None):
    return lax.dot_general(a, b, (dims, ((), ())), precision=precision, preferred_element_type=F32)


def call(kernel, out_shape, operands, scratch=(), flops=0, smem=1, anywhere=0, vmem=VMEM_BYTES, hidden=False):
    in_specs = [pl.BlockSpec(memory_space=pltpu.SMEM)] * smem
    in_specs += [pl.BlockSpec(memory_space=pltpu.VMEM)] * (len(operands) - smem - anywhere)
    in_specs += [pl.BlockSpec(memory_space=pl.ANY)] * anywhere
    moved = sum(a.size * a.dtype.itemsize for a in operands)
    moved += sum(a.size * a.dtype.itemsize for a in jax.tree.leaves(out_shape))
    if hidden:
        flops = moved = 0
    return pl.pallas_call(
        kernel,
        out_shape=out_shape,
        in_specs=in_specs,
        out_specs=jax.tree.map(lambda _: pl.BlockSpec(memory_space=pltpu.VMEM), out_shape),
        scratch_shapes=list(scratch),
        compiler_params=pltpu.CompilerParams(vmem_limit_bytes=vmem),
        cost_estimate=pl.CostEstimate(flops=flops, bytes_accessed=moved, transcendentals=0),
    )(*operands)


def plane_place(group):
    index = lax.axis_index("tm")
    return lax.rem(index, group), lax.div(index, group)


def record_starts(len_ref, position):
    start = jnp.zeros_like(position)
    end = jnp.int32(0)
    for record in range(len_ref.shape[0] - 1):
        end = end + len_ref[record]
        start = jnp.where(position >= end, end, start)
    return start


def fill_planes(plane, dest_ref, pieces, offsets, lanes=slice(None)):
    rows = pieces[0].shape[0]
    for offset in sorted(set(offsets)):
        same = [piece[:, lanes] for piece, at in zip(pieces, offsets) if at == offset]
        value = same[0] if len(same) == 1 else same[0] + same[1]
        dest_ref[pl.ds(pl.multiple_of((plane ^ offset) * rows, rows), rows), : value.shape[1]] = value


def first_kernel(group, planes, log_decay_ref, bc_ref, frames_ref, *refs):
    weight_refs, refs = refs[:3], refs[3:]
    inner_refs, outer_refs, refs = refs[:group], refs[group : group + planes], refs[group + planes :]
    bc_half_ref, edge_ref, decay_ref, sems = refs
    place, plane = plane_place(group)
    parity = lax.rem(lax.axis_index("head"), 2)
    width = weight_refs[0].shape[1] // group
    frames = frames_ref.shape[0]
    heads = log_decay_ref.shape[0] // group
    copies = [
        (bc_ref.at[:, pl.ds(pl.multiple_of(parity * LANES, LANES), LANES)], bc_half_ref),
        (frames_ref.at[:EDGE, :], edge_ref.at[0]),
        (frames_ref.at[frames - EDGE :, :], edge_ref.at[1]),
        (log_decay_ref, decay_ref),
    ]
    for step, inner_ref in enumerate(inner_refs):
        lanes = pl.ds(pl.multiple_of((place ^ step) * width, LANES), width)
        for number, weight_ref in enumerate(weight_refs):
            copies.append((weight_ref.at[:, lanes], inner_ref.at[:, number * width : (number + 1) * width]))
    started = [pltpu.make_async_copy(a, b, sems.at[number]) for number, (a, b) in enumerate(copies)]
    for copy in started:
        copy.start()
    for copy in started[:4]:
        copy.wait()
    lane = lax.broadcasted_iota(jnp.int32, (8, LANES), 1)
    decays = []
    for first in (0, frames - LANES):
        rows = [jnp.zeros((8, LANES), F32), jnp.zeros((8, LANES), F32)]
        for block in range(group):
            here = decay_ref[block * heads : (block + 1) * heads, first : first + LANES]
            here = jnp.concatenate([here, jnp.zeros((8 - heads, LANES), F32)], axis=0)
            for number, term in enumerate(three_terms(here)):
                slot = number * group + block
                moved = pltpu.roll(term, (slot % 8 * EDGE + (EDGE if first else 0)) % LANES, 1)
                rows[slot // 8] = jnp.where(lane // EDGE == slot % 8, moved, rows[slot // 8])
        decays.append(jnp.concatenate(rows, axis=0))
    for step, out_ref in enumerate(outer_refs):
        number = put(out_ref, 0, bc_half_ref[...])
        later = (plane ^ step) > plane
        number = put(out_ref, number, jnp.where(later, edge_ref[1].astype(F32), edge_ref[0].astype(F32)).astype(BF16))
        put(out_ref, number, jnp.where(later, decays[1], decays[0]).astype(BF16))
    for copy in started[4:]:
        copy.wait()


def stack_kernel(group, *refs):
    parts, stack_refs = refs[:group], refs[group:]
    place, _ = plane_place(group)
    rows = parts[0].shape[0]
    for step, part in enumerate(parts):
        at = pl.ds(pl.multiple_of((place ^ step) * rows, rows), rows)
        first = 0
        for stack_ref in stack_refs:
            width = stack_ref.shape[1]
            stack_ref[at, :] = part[:, first : first + width]
            first += width


def assemble_kernel(group, offsets, *refs):
    pieces, dest_refs = refs[: len(offsets)], refs[len(offsets) :]
    _, plane = plane_place(group)
    first = 0
    for dest_ref in dest_refs:
        width = dest_ref.shape[1]
        fill_planes(plane, dest_ref, pieces, offsets, slice(first, first + width))
        first += width


def tile(number):
    return slice(number // 8 * 16, number // 8 * 16 + 16), slice(number % 8 * LANES, (number % 8 + 1) * LANES)


def put(out_ref, number, array):
    for at in range(0, array.shape[0], 16):
        for lane in range(0, array.shape[1], LANES):
            out_ref[tile(number)] = array[at : at + 16, lane : lane + LANES]
            number += 1
    return number


def three_terms(value):
    terms = []
    for _ in range(3):
        term = value.astype(BF16).astype(F32)
        terms.append(term)
        value = value - term
    return terms


def inward_kernel(group, rows, decay_ref, frames_ref, *refs):
    piece_refs, out_refs = refs[:-group], refs[-group:]
    place, plane = plane_place(group)
    planes = len(piece_refs)
    half = frames_ref.shape[0] // 2
    mine = pl.ds(pl.multiple_of(lax.rem(lax.axis_index("head"), 2) * half, half), half)
    wanted = jnp.clip(jnp.where(place == 0, plane + 1, plane - 1), 0, planes - 1)
    depth_tiles = frames_ref.shape[1] // LANES
    down = rows // 16
    for step, out_ref in enumerate(out_refs):
        out_ref[:half, :] = frames_ref[mine, :]
        number = half // 16 * depth_tiles
        for piece_ref in piece_refs:
            for at in range(down):
                out_ref[tile(number)] = piece_ref[tile(at)]
                number += 1
        for offset, piece_ref in enumerate(piece_refs):

            @pl.when((plane ^ offset) == wanted)
            def _(piece_ref=piece_ref, number=number, out_ref=out_ref):
                for at in range(depth_tiles + 1):
                    out_ref[tile(number + at)] = piece_ref[tile(down + at)]

        number += depth_tiles + 1
        terms = three_terms(decay_ref[place ^ step])
        terms = jnp.concatenate([*terms, jnp.zeros_like(terms[0])], axis=0).astype(BF16)
        for span in range(terms.shape[1] // SPAN):
            number = put(out_ref, number, terms[:, span * SPAN : (span + 1) * SPAN])


def swap_kernel(group, rows, *refs):
    part_refs, (swap_ref, bc_ref, halo_ref, decay_ref, span_ref) = refs[:group], refs[group:]
    half_refs = part_refs[1:]
    place, plane = plane_place(group)
    planes = bc_ref.shape[0] // (group * rows)
    count = span_ref.shape[0]
    spans = count // group
    down = rows // 16
    depth_tiles = swap_ref.shape[1] // LANES
    height = LANES
    top = swap_ref.shape[0] - height
    half = top // len(half_refs)
    lane = lax.broadcasted_iota(jnp.int32, (8, LANES), 1)
    for step, part_ref in enumerate(part_refs):
        block = place ^ step
        number = half // 16 * depth_tiles
        for offset in range(planes):
            first = ((plane ^ offset) * group + block) * rows
            for at in range(down):
                bc_ref[pl.ds(pl.multiple_of(first + at * 16, 16), 16), :] = part_ref[tile(number)]
                number += 1
        for side, owner in enumerate((group - 1, 0)):

            @pl.when(block == owner)
            def _(part_ref=part_ref, number=number, side=side):
                for at in range(depth_tiles):
                    halo_ref[side * EDGE : (side + 1) * EDGE, at * LANES : (at + 1) * LANES] = part_ref[tile(number + at)]
                packed = part_ref[tile(number + depth_tiles)].astype(F32)
                chosen = jnp.zeros((8, LANES), F32)
                for head_block in range(group):
                    value = jnp.zeros((8, LANES), F32)
                    for term in range(3):
                        slot = term * group + head_block
                        half = packed[slot // 8 * 8 : slot // 8 * 8 + 8]
                        value = value + pltpu.roll(half, (LANES - slot % 8 * EDGE) % LANES, 1)
                    chosen = jnp.where(place == head_block, value, chosen)
                if side:
                    last = pltpu.roll(chosen, EDGE, 1)
                    decay_ref[count * 8 :, :] = jnp.where((lane >= EDGE) & (lane < 2 * EDGE), last, 0.0)
                else:
                    decay_ref[:8, :] = jnp.where(lane < EDGE, chosen, 0.0)

        number += depth_tiles + 1
        for span in range(spans):
            upper = part_ref[tile(number)].astype(F32)
            lower = part_ref[tile(number + 1)].astype(F32)
            number += 2
            span_ref[block * spans + span] = upper[:8] + upper[8:] + lower[:8]
    for span in range(count):
        moved = pltpu.roll(span_ref[span], EDGE, 1)
        here, after = slice(span * 8, span * 8 + 8), slice(span * 8 + 8, span * 8 + 16)
        decay_ref[here, :] = jnp.where(lane < EDGE, decay_ref[here, :], moved)
        kept = decay_ref[after, :] if span == count - 1 else jnp.zeros((8, LANES), F32)
        decay_ref[after, :] = jnp.where(lane < EDGE, moved, kept)
    for number, half_ref in enumerate(half_refs):
        swap_ref[number * half : (number + 1) * half, :] = half_ref[:half, : swap_ref.shape[1]]
    for number in range(bc_ref.shape[0] // height):
        lanes = slice(number * LANES, (number + 1) * LANES)
        swap_ref[top:, lanes] = bc_ref[number * height : (number + 1) * height, :]


def lanes_of(rows, width, head_size):
    high = rows.astype(BF16).astype(F32)
    owner = lax.broadcasted_iota(jnp.int32, (16, width), 1) // head_size
    chosen = jnp.where((lax.broadcasted_iota(jnp.int32, (16, width), 0) & 7) == owner, 1.0, 0.0).astype(BF16)
    return dot(jnp.concatenate([high, rows - high], axis=0).astype(BF16), chosen, ((0,), (0,)))


def spans_in_lanes(rows):
    return jnp.concatenate([rows[at : at + 8] for at in range(0, rows.shape[0], 8)], axis=1)


def row_blocks(total, wide):
    return [slice(at, at + 256) for at in range(0, total, 256)] + [slice(total, wide)]


def state_kernel(group, heads, state, len_ref, decay_ref, x_weight_ref, bc_half_ref, own_ref, swap_ref, halo_ref, *refs):
    half_refs, refs = refs[: group - 1], refs[group - 1 :]
    frames_ref, x_ref, b_ref, c_ref, rows_ref, step_ref, keep_ref, send_ref, weight_ref, tail_ref = refs
    place, plane = plane_place(group)
    parity = lax.rem(lax.axis_index("head"), 2)
    width = x_ref.shape[1]
    frames = own_ref.shape[0]
    total = frames * group
    half = frames // 2
    head_size = width // heads
    count = total // SPAN
    base = plane * total - EDGE
    wide = total + 2 * EDGE
    frames_ref[:EDGE, :] = halo_ref[:EDGE, :]
    frames_ref[total + EDGE : wide, :] = halo_ref[EDGE:, :]
    frames_ref[wide:, :] = jnp.zeros((frames_ref.shape[0] - wide, frames_ref.shape[1]), BF16)
    frames_ref[pl.ds(pl.multiple_of(EDGE + place * frames, EDGE), frames), :] = own_ref[...]
    for number, half_ref in enumerate(half_refs):
        block = EDGE + (place ^ (number + 1)) * frames
        mine = pl.ds(pl.multiple_of(block + parity * half, EDGE), half)
        other = pl.ds(pl.multiple_of(block + (1 - parity) * half, EDGE), half)
        frames_ref[mine, :] = half_ref[:half, : frames_ref.shape[1]]
        frames_ref[other, :] = swap_ref[number * half : (number + 1) * half, :]
    mine = pl.ds(pl.multiple_of(parity * LANES, LANES), LANES)
    other = pl.ds(pl.multiple_of((1 - parity) * LANES, LANES), LANES)
    weight_ref[:, mine] = bc_half_ref[...]
    top = len(half_refs) * half
    height = swap_ref.shape[0] - top
    for number in range(weight_ref.shape[0] // height):
        lanes = slice(number * LANES, (number + 1) * LANES)
        weight_ref[number * height : (number + 1) * height, other] = swap_ref[top:, lanes]

    decay = decay_ref[...]
    used = decay.shape[0]
    square = (SPAN, SPAN)
    row, lane = (lax.broadcasted_iota(jnp.int32, square, dim) for dim in (0, 1))
    upper = jnp.where(row <= lane, 1.0, 0.0).astype(F32)
    cumul = dot(decay, upper, precision=lax.Precision.HIGHEST)
    whole = dot(decay, jnp.ones(square, F32), precision=lax.Precision.HIGHEST)
    first = base + lax.broadcasted_iota(jnp.int32, (used, SPAN), 0) // 8 * SPAN
    position = first + lane[:1]
    start = record_starts(len_ref, position)
    start_last = record_starts(len_ref, first + (SPAN - 1))
    carried = jnp.where(start < first, jnp.exp(cumul), 0.0)
    tail = jnp.where(position >= start_last, jnp.exp(whole - cumul), 0.0)
    keep = jnp.where(start_last < first, jnp.exp(whole), 0.0)
    rows_ref[:used, :] = cumul
    rows_ref[used : 2 * used, :] = start.astype(F32)
    rows_ref[2 * used :, :] = carried

    for rows in row_blocks(total, wide):
        x_ref[rows, :] = dot(frames_ref[rows, :], x_weight_ref[...]).astype(BF16)
        product = dot(frames_ref[rows, :], weight_ref[...])
        b_ref[rows, :] = product[:, :state].astype(BF16)
        c_ref[rows, :] = product[:, state:].astype(BF16)
    for ref in (x_ref, b_ref, c_ref):
        ref[wide:, :] = jnp.zeros((ref.shape[0] - wide, ref.shape[1]), BF16)

    tail_ref[...] = lanes_of(spans_in_lanes(tail[: count * 8]), width, head_size)
    by_span = jnp.zeros((8, SPAN), F32)
    for block in range(count):
        by_span = jnp.where(lane[:8] == block, keep[block * 8 : (block + 1) * 8], by_span)
    kept = lanes_of(by_span, width, head_size)[: keep_ref.shape[0]]
    keep_ref[...] = kept
    entry = jnp.zeros((state, width), F32)
    through = jnp.ones((1, width), F32)
    for block in range(count):
        rows = slice(block * SPAN, (block + 1) * SPAN)
        weighed = x_ref[rows, :].astype(F32) * tail_ref[rows, :]
        step = dot(b_ref[rows, :], weighed.astype(BF16), ((0,), (0,)))
        step_ref[block * state : (block + 1) * state, :] = step
        entry = kept[block : block + 1] * entry + step
        through = through * kept[block : block + 1]
    send_ref[:state, :] = entry.astype(BF16)
    send_ref[state:, :] = jnp.broadcast_to(through, (EDGE, width)).astype(BF16)


def inner_kernel(group, heads, x_ref, b_ref, c_ref, rows_ref, y_ref, carry_ref):
    _, plane = plane_place(group)
    total, width = x_ref.shape
    head_size = width // heads
    count = total // SPAN
    base = plane * (total - SPAN) - EDGE
    used = rows_ref.shape[0] // 3
    square = (SPAN, SPAN)
    parts = [rows_ref[: 2 * used, :]]
    if 2 * used % SPAN:
        parts.append(jnp.zeros((SPAN - 2 * used % SPAN, SPAN), F32))
    columns = jnp.concatenate(parts, axis=0).T
    carry_ref[...] = lanes_of(spans_in_lanes(rows_ref[2 * used :, :]), width, head_size)
    row, lane = (lax.broadcasted_iota(jnp.int32, square, dim) for dim in (0, 1))
    lower = row >= lane
    tile_heads = LANES // head_size
    tile_lane = lax.broadcasted_iota(jnp.int32, (1, LANES), 1) // head_size
    masks = [jnp.where(tile_lane == inner, 1.0, 0.0).astype(BF16) for inner in range(tile_heads)]
    for block in range(count):
        rows = slice(block * SPAN, (block + 1) * SPAN)
        at = block * 8
        x = x_ref[rows, :]
        scores = dot(c_ref[rows, :], b_ref[rows, :], ((1,), (1,)))
        here = (base + block * SPAN + lane).astype(F32)
        start_here = jnp.broadcast_to(columns[:, used + at : used + at + 1], square)
        joined = lower & (here >= start_here)
        for tile in range(width // LANES):
            mixes, values = [], []
            for inner in range(tile_heads):
                which = at + tile * tile_heads + inner
                column = jnp.broadcast_to(columns[:, which : which + 1], square)
                gap = jnp.where(joined, column - rows_ref[which : which + 1, :], -1e30)
                mixes.append((jnp.exp(gap) * scores).astype(BF16))
                values.append(x[:, tile * LANES : (tile + 1) * LANES] * masks[inner])
            y_ref[rows, tile * LANES : (tile + 1) * LANES] = dot(
                jnp.concatenate(mixes, axis=1), jnp.concatenate(values, axis=0)
            )


def silu_kernel(group, gain_ref, frames_ref, weight_ref, out_ref):
    place, _ = plane_place(group)
    rows_all, width = out_ref.shape
    total = rows_all - SPAN
    wide = total + 2 * EDGE
    gain = gain_ref[:, pl.ds(pl.multiple_of(place * width, LANES), width)]
    for rows in row_blocks(total, wide):
        z = dot(frames_ref[rows, :], weight_ref[...]).astype(BF16).astype(F32)
        out_ref[rows, :] = z / (1.0 + jnp.exp(-z)) * gain
    out_ref[wide:, :] = jnp.zeros((rows_all - wide, width), F32)


def share_kernel(cores, offsets, group, *refs):
    pieces, refs = refs[: len(offsets)], refs[len(offsets) :]
    outs, weight_ref = refs[:cores], refs[cores]
    _, plane = plane_place(group)
    core = lax.axis_index("head")
    fill_planes(plane, weight_ref, pieces, offsets)
    for step, out_ref in enumerate(outs):
        rows = out_ref.shape[0]
        out_ref[...] = weight_ref[pl.ds(pl.multiple_of((core ^ step) * rows, rows), rows), :]


def gate_kernel(heads, state, c_ref, y_ref, step_ref, carry_ref, keep_ref, silu_ref, *refs):
    earlier, gated_ref = refs[:-1], refs[-1]
    total, width = y_ref.shape
    head_size = width // heads
    count = total // SPAN
    entry = jnp.zeros((state, width), F32)
    for summary in reversed(earlier):
        through = summary[state : state + EDGE, :].astype(F32)[:1]
        entry = through * entry + summary[:state, :].astype(F32)
    owner = [lax.broadcasted_iota(jnp.int32, (width, width), dim) // head_size for dim in (0, 1)]
    average = jnp.where(owner[0] == owner[1], 1.0 / head_size, 0.0).astype(BF16)
    for block in range(count):
        rows = slice(block * SPAN, (block + 1) * SPAN)
        y = y_ref[rows, :] + carry_ref[rows, :] * dot(c_ref[rows, :], entry.astype(BF16))
        square_mean = dot((y * y).astype(BF16), average)
        gated_ref[rows, :] = (y * lax.rsqrt(square_mean + 1e-05) * silu_ref[rows, :]).astype(BF16)
        if block < count - 1:
            entry = keep_ref[block : block + 1, :] * entry + step_ref[block * state : (block + 1) * state, :]


def conv_kernel(group, steps, len_ref, taps_ref, gated_ref, act_ref, ext_ref, spread_ref, ends_ref):
    place, plane = plane_place(group)
    rows_all, width = gated_ref.shape
    total = rows_all - SPAN
    frames = total // group
    taps = taps_ref.shape[0]
    half = (taps - 1) // 2
    stream = lax.axis_size("tm") // group * total
    records = len_ref.shape[0]
    reach = CONV_ROWS + 2 * EDGE
    first_tap = EDGE - half
    pitch = frames + 2 * EDGE
    ours = taps_ref[:, pl.ds(pl.multiple_of(place * width, LANES), width)]
    for tap in range(taps):
        spread_ref[tap * 8 : (tap + 1) * 8, :] = jnp.broadcast_to(ours[tap : tap + 1, :], (8, width))
    ends_ref[0] = 0
    for record in range(records):
        ends_ref[record + 1] = ends_ref[record] + len_ref[record]
    for number, step in enumerate(steps):
        first = pl.multiple_of((place ^ step) * frames, frames)
        ext_ref[number * pitch : (number + 1) * pitch, :] = gated_ref[pl.ds(first, pitch), :].astype(F32)

    def record_at(position):
        found = jnp.int32(0)
        for record in range(records - 1):
            found = found + (ends_ref[record + 1] <= position).astype(jnp.int32)
        return found

    for number, step in enumerate(steps):
        base = plane * total + (place ^ step) * frames

        def one_block(block, _, number=number, base=base):
            inside_part = pl.multiple_of(block * CONV_ROWS, CONV_ROWS)
            source = pl.multiple_of(number * pitch + inside_part, EDGE)
            target = pl.multiple_of(number * frames + inside_part, CONV_ROWS)
            at = base + inside_part
            low = record_at(jnp.maximum(at - half, 0))
            high = record_at(jnp.minimum(at + CONV_ROWS - 1 + half, stream - 1))
            near = lax.broadcasted_iota(jnp.int32, (reach, LANES), 0) + (at - EDGE)
            for tile in range(width // LANES):
                lanes = slice(tile * LANES, (tile + 1) * LANES)
                def one_record(record, done):
                    inside = (near >= ends_ref[record]) & (near < ends_ref[record + 1])
                    g = jnp.where(inside, ext_ref[pl.ds(source, reach), lanes], 0.0).reshape(reach // 8, 8, LANES)
                    out = None
                    for phase in range(8):
                        part = None
                        for offset in range(phase, reach - CONV_ROWS, 8):
                            tap = offset - first_tap
                            if 0 <= tap < taps:
                                first = (offset - phase) // 8
                                weight = spread_ref[tap * 8 : (tap + 1) * 8, lanes]
                                term = weight[None] * g[first : first + CONV_ROWS // 8 + 1]
                                part = term if part is None else part + term
                        if part is not None:
                            moved = part.reshape(CONV_ROWS + 8, LANES)[phase : phase + CONV_ROWS, :]
                            out = moved if out is None else out + moved
                    return jnp.where(inside[EDGE : EDGE + CONV_ROWS], out, done)

                conv = lax.fori_loop(low, high + 1, one_record, jnp.zeros((CONV_ROWS, LANES), F32))
                act_ref[pl.ds(target, CONV_ROWS), lanes] = (conv / (1.0 + jnp.exp(-conv))).astype(BF16)
            return 0

        lax.fori_loop(0, frames // CONV_ROWS, one_block, 0)


def sum_kernel(own_ref, *refs):
    total = own_ref[...]
    for part in refs[:-1]:
        total = total + part[...].astype(F32)
    refs[-1][...] = total.astype(refs[-1].dtype)


def out_kernel(cores, *refs):
    acts, weights, outs = refs[:cores], refs[cores : 2 * cores], refs[2 * cores :]
    frames = outs[0].shape[0]
    for number, out_ref in enumerate(outs):
        rows = slice(number * frames, (number + 1) * frames)
        total = None
        for act, weight in zip(acts, weights):
            product = dot(act[rows, :], weight[...], ((1,), (1,)))
            total = product if total is None else total + product
        out_ref[...] = total.astype(out_ref.dtype)


def local(
    frames,
    x_weight,
    z_weight,
    bc_weight,
    log_decay,
    norm_gain,
    conv_weight,
    out_weight,
    record_lengths,
):
    times, cores = lax.axis_size("tm"), lax.axis_size("head")
    frame_count, depth = frames.shape
    heads_here, channels = log_decay.shape[0], x_weight.shape[1]
    state = bc_weight.shape[1] // 2
    group = 4
    while group > 1 and (channels // group % LANES or times % group or heads_here % group):
        group //= 2
    planes = times // group
    width, heads = channels // group, heads_here // group
    total = frame_count * group
    count = total // SPAN
    index, core = lax.axis_index("tm"), lax.axis_index("head")
    place = lax.rem(index, group)

    def in_plane(array, step):
        return lax.ppermute(array, "tm", [(i, i ^ step) for i in range(times)])

    def later(array, step):
        return lax.ppermute(array, "tm", [(i, i + step * group) for i in range(times - step * group)])

    def across(array, step):
        return lax.ppermute(array, "head", [(i, i ^ step) for i in range(cores)])

    def between_planes(array, step):
        return lax.ppermute(array, "tm", [(i, i ^ (step * group)) for i in range(times)])

    shape = jax.ShapeDtypeStruct
    rows = x_weight.shape[0]
    parity = lax.rem(core, 2)

    def along_planes(stacks):
        if planes != 4:
            return [stacks[0]] + [between_planes(stacks[step], step) for step in range(1, planes)]

        def pairs(chosen):
            return [(a * group + q, b * group + q) for a, b in chosen for q in range(group)]

        second = between_planes(stacks[2], 2)
        first = between_planes(stacks[1], 1)
        again, last, first = lax.optimization_barrier((second, stacks[3], first))
        third = lax.ppermute(again, "tm", pairs([(1, 0), (2, 3)]))
        middle = lax.ppermute(last, "tm", pairs([(1, 2), (2, 1)]))
        return [stacks[0], first, second, third, middle]

    offsets = (0, 1, 2, 3, 3) if planes == 4 else tuple(range(planes))
    half_count = frame_count // 2
    down, depth_tiles = rows // 16, depth // LANES
    payloads = call(
        functools.partial(first_kernel, group, planes),
        (
            *(shape((rows, 3 * width), BF16) for _ in range(group)),
            *(shape((-(-(down + depth_tiles + 1) // 8) * 16, depth), BF16) for _ in range(planes)),
        ),
        [log_decay, bc_weight, frames, x_weight, z_weight, out_weight.T],
        [
            pltpu.VMEM((rows, LANES), BF16),
            pltpu.VMEM((2, EDGE, depth), BF16),
            pltpu.VMEM(log_decay.shape, F32),
            pltpu.SemaphoreType.DMA((4 + 3 * group,)),
        ],
        smem=0,
        anywhere=6,
        vmem=ALL_VMEM_BYTES,
    )
    inner, outer = payloads[:group], payloads[group:]
    parts = [inner[0]] + [in_plane(inner[step], step) for step in range(1, group)]
    pieces = [outer[0]] + [between_planes(outer[step], step) for step in range(1, planes)]
    xz_stack, out_stack = call(
        functools.partial(stack_kernel, group),
        (shape((group * rows, 2 * width), BF16), shape((group * rows, width), BF16)),
        parts,
        flops=STACK_HINT,
        smem=0,
    )
    xz_stack, pieces = lax.optimization_barrier((xz_stack, pieces))
    xz_pieces = along_planes([xz_stack] * planes)
    xz_pieces, out_stack = lax.optimization_barrier((xz_pieces, out_stack))
    out_pieces = [out_stack] + [between_planes(out_stack, step) for step in range(1, planes)]
    x_columns, z_columns = call(
        functools.partial(assemble_kernel, group, offsets),
        (shape((depth, width), BF16), shape((depth, width), BF16)),
        xz_pieces,
        flops=ASSEMBLE_HINT,
        smem=0,
    )
    decay_blocks = jnp.pad(log_decay.reshape(group, heads, frame_count), ((0, 0), (0, 8 - heads), (0, 0)))
    tiles = planes * down + depth_tiles + 1 + frame_count // SPAN * 2
    inward = call(
        functools.partial(inward_kernel, group, rows),
        tuple(shape((half_count + -(-tiles // 8) * 16, depth), BF16) for _ in range(group)),
        [decay_blocks, frames, *pieces],
        flops=INWARD_HINT,
        smem=0,
    )
    inward = [inward[0]] + [in_plane(inward[step], step) for step in range(1, group)]
    swap, bc_mine, halo, decay = call(
        functools.partial(swap_kernel, group, rows),
        (
            shape(((group - 1) * half_count + LANES, depth), BF16),
            shape((depth, LANES), BF16),
            shape((2 * EDGE, depth), BF16),
            shape((count * 8 + 8, SPAN), F32),
        ),
        inward,
        [pltpu.VMEM((count, 8, SPAN), F32)],
        smem=0,
    )
    swap = across(swap, 1)
    all_rows = total + SPAN

    frame_rows, x_rows, b_rows, c_rows, decay_rows, steps, keep, summary = call(
        functools.partial(state_kernel, group, heads, state),
        (
            shape((all_rows, depth), BF16),
            shape((all_rows, width), BF16),
            shape((all_rows, state), BF16),
            shape((all_rows, state), BF16),
            shape((3 * (count + 1) * 8, SPAN), F32),
            shape((count * state, width), F32),
            shape((-(-count // 8) * 8, width), F32),
            shape((state + EDGE, width), BF16),
        ),
        [record_lengths, decay, x_columns, bc_mine, frames, swap, halo, *inward[1:]],
        [pltpu.VMEM((depth, 2 * state), BF16), pltpu.VMEM((total, width), F32)],
        hidden=True,
    )
    summaries = [later(summary, step) for step in range(1, planes)]
    x_rows, out_pieces = lax.optimization_barrier((x_rows, out_pieces))
    y, carry = call(
        functools.partial(inner_kernel, group, heads),
        (shape((all_rows, width), F32), shape((all_rows, width), F32)),
        [x_rows, b_rows, c_rows, decay_rows],
        flops=4 * total * SPAN * width,
        smem=0,
    )
    silu = call(
        functools.partial(silu_kernel, group),
        shape((all_rows, width), F32),
        [norm_gain[None], frame_rows, z_columns],
        flops=2 * total * depth * width,
        smem=0,
    )
    gated = call(
        functools.partial(gate_kernel, heads, state),
        shape((all_rows, width), BF16),
        [c_rows, y, steps, carry, keep, silu, *summaries],
        flops=2 * total * state * width,
        smem=0,
    )
    ends = pltpu.SMEM((record_lengths.shape[0] + 1,), jnp.int32)
    far, near = (group - 1,), tuple(range(1, group - 1))

    def conv(steps, gated):
        return call(
            functools.partial(conv_kernel, group, steps),
            shape((len(steps) * frame_count, width), BF16),
            [record_lengths, conv_weight, gated],
            [
                pltpu.VMEM((len(steps) * (frame_count + 2 * EDGE), width), F32),
                pltpu.VMEM((conv_weight.shape[0] * 8, width), F32),
                ends,
            ],
            flops=2 * len(steps) * frame_count * width * conv_weight.shape[0],
        )

    def out(steps, act, swapped):
        return call(
            functools.partial(out_kernel, cores),
            tuple(shape((frame_count, share), BF16 if step else F32) for step in steps),
            [act, *swapped, *out_parts],
            flops=2 * len(steps) * frame_count * width * cores * share,
            smem=0,
        )

    share = depth // cores
    out_parts = call(
        functools.partial(share_kernel, cores, tuple(range(planes)), group),
        tuple(shape((share, width), BF16) for _ in range(cores)),
        out_pieces,
        [pltpu.VMEM((depth, width), BF16)],
        smem=0,
    )
    out_parts, gated = lax.optimization_barrier((out_parts, gated))
    out_parts = [out_parts[0]] + [across(out_parts[step], step) for step in range(1, cores)]
    far_act = conv(far, gated)
    far_swapped = [across(far_act, step) for step in range(1, cores)]
    gated, far_act = lax.optimization_barrier((gated, far_act))
    if near:
        near_act = conv(near, gated)
        near_act, far_swapped, out_parts = lax.optimization_barrier((near_act, far_swapped, out_parts))
    (far_out,) = out(far, far_act, far_swapped)
    if near:
        near_act, far_out = lax.optimization_barrier((near_act, far_out))
    sent = [in_plane(far_out, far[0])]
    if near:
        near_swapped = [across(near_act, step) for step in range(1, cores)]
        near_outs = out(near, near_act, near_swapped)
        gated, near_outs = lax.optimization_barrier((gated, near_outs))
        sent += [in_plane(part, step) for part, step in zip(near_outs, near)]
    own_act = conv((0,), gated)
    own_swapped = [across(own_act, step) for step in range(1, cores)]
    (own_out,) = out((0,), own_act, own_swapped)
    return call(sum_kernel, shape((frame_count, share), BF16), [own_out, *sent], smem=0)


def solution(mesh):
    in_specs = (
        P("tm", None),
        P("tm", "head"),
        P("tm", "head"),
        P("tm", None),
        P("head", "tm"),
        P("head"),
        P(None, "head"),
        P("head", "tm"),
        P(),
    )
    out_specs = P("tm", "head")
    return jax.shard_map(local, mesh=mesh, in_specs=in_specs, out_specs=out_specs, check_vma=False)
```
